32 devices in a mesh: section: 2 (over core), dp: 4 (over z), expert: 4 (over y, x).
Axes of the slice: x: 2, y: 2, z: 4, core: 2. Of those that a mesh axis runs over, the one named last changes fastest.
Arguments:
- layer_input: bfloat16 [2, 1024, 1024], P(None, ('dp', 'expert')), may hold values from -6 to 6
- cotangent: bfloat16 [2, 1024, 1024], P(None, ('dp', 'expert')), may hold values from -6 to 6
- positions: int32 [2, 1024], P(None, ('dp', 'expert')), may hold values from 0 to 63, as said below
- routes: int32 [2, 2, 1024, 8], P('section', None, ('dp', 'expert')), may hold values from 0 to 31, all different within a row; in each aligned block of 64 rows (0 to 63, 64 to 127, ..., all dimensions but the last counted through in order) at most 32 rows name the same one
- gain_one: float32 [2, 1024], P('section'), may hold values from 0.5 to 1.5
- attn_in: bfloat16 [2, 1024, 2048], P('section', 'dp'), may hold values from -0.1875 to 0.1875
- attn_out: bfloat16 [2, 1024, 1024], P('section', 'dp'), may hold values from -1 to 1
- gain_two: float32 [2, 1024], P('section'), may hold values from 0.5 to 1.5
- router: bfloat16 [2, 1024, 32], P('section'), may hold values from -0.09375 to 0.09375
- experts_in: bfloat16 [2, 32, 1024, 1024], P('section', 'expert'), may hold values from -0.1875 to 0.1875
- experts_out: bfloat16 [2, 32, 512, 1024], P('section', 'expert'), may hold values from -1.5 to 1.5
Outputs:
- hidden: bfloat16 [2, 2, 1024, 1024], P('section', None, ('dp', 'expert'))
- input_grad: bfloat16 [2, 2, 1024, 1024], P('section', None, ('dp', 'expert'))
- grad_gain_one: float32 [2, 1024], P('section')
- grad_attn_in: float32 [2, 1024, 2048], P('section', ('dp', 'expert'))
- grad_attn_out: float32 [2, 1024, 1024], P('section', ('dp', 'expert'))
- grad_gain_two: float32 [2, 1024], P('section')
- grad_router: float32 [2, 1024, 32], P('section')
- grad_experts_in: float32 [2, 32, 1024, 1024], P('section', 'expert', 'dp')
- grad_experts_out: float32 [2, 32, 512, 1024], P('section', 'expert', 'dp')
The draws below stay inside these ranges and needn't reach their ends.
Inputs may be any that keep to these rules, and one draw needn't show every extreme that they name: `routes`: each token names 8 different experts of 32. Among the 64 tokens of one sequence in one layer, no expert is named more than 32 times, and in some sequences one is named exactly 32 times. `positions`: within each sequence of 64 tokens a position is 0 at the first token and at the start of each packed document, and one more than the previous token's elsewhere.
All inputs are finite; a program needn't handle non-finite values.
Results may differ from the reference program's by a relative error of at most 0.025.
Values may be sent and summed in bfloat16 or wider, within the bound.
A program may use at most 320 MiB of HBM per device.

```python
import math
import jax
import jax.numpy as jnp
import numpy as np
from jax import lax

MODEL_WIDTH = 1024
QUERY_HEADS = 16
KEY_VALUE_HEADS = 8
HEAD_SIZE = 64
FF = 512
EXPERTS = 32
TOPK = 8
SEQUENCE_TOKENS = 64
MICRO = 2
LAYER_COUNT = 2
TOKENS = 1024
CAP = 32


def draw_positions(key, part):
    count_seqs = TOKENS // SEQUENCE_TOKENS
    breaks = jax.random.randint(key, (MICRO, count_seqs, SEQUENCE_TOKENS), 0, max(2, SEQUENCE_TOKENS // 4)) == 0
    token_index = jnp.arange(SEQUENCE_TOKENS, dtype=jnp.int32)
    starts = (token_index == 0)[None, None, :]
    keep_whole = (jnp.arange(count_seqs)[None, :, None] == 0) & (jnp.arange(MICRO)[:, None, None] == 0)
    breaks = breaks & jnp.logical_not(keep_whole) | starts
    last_start = lax.cummax(jnp.where(breaks, token_index[None, None, :], 0), axis=2)
    return (token_index[None, None, :] - last_start).reshape(MICRO, TOKENS).astype(jnp.int32)


def block_levels(key, shape, pieces, low, high):
    def one(axis_at, blocks):
        draws = jax.random.uniform(jax.random.fold_in(jax.random.fold_in(key, 6), axis_at), (blocks,), jnp.float32, low / len(pieces), high / len(pieces))
        return jnp.repeat(jnp.exp(draws), shape[axis_at] // blocks).reshape((-1,) + (1,) * (len(shape) - axis_at - 1))

    loudness = one(*pieces[0])
    for cut in pieces[1:]:
        loudness = loudness * one(*cut)
    return loudness


def routed_block(stream_key, own, number, rows, count, top, limit, slope):
    order = jax.random.permutation(stream_key, count)
    crowded, common = portions_of(count, rows * top, limit, slope, True), portions_of(count, rows * top, limit, slope, False)
    places = jnp.arange(count)

    def named(tallies, rotation):
        used = int((tallies > 0).sum())
        fixed = max(1, used // 4)
        moved = fixed + (places - fixed + rotation * (used - fixed)) % max(1, count - fixed)
        return jnp.zeros((count,), jnp.int32).at[order[jnp.where(places < fixed, places, moved)]].set(jnp.asarray(tallies, jnp.int32))

    tallies = jnp.where(number % 4 == 0, named(crowded, number // 4), named(common, number - number // 4 - 1))
    mixed = jax.random.permutation(jax.random.fold_in(own, 3), count)
    source_of, taker = mixed[0:count // 2 * 2:2], mixed[1:count // 2 * 2:2]
    slack = jnp.minimum(tallies[source_of] - 1, limit - tallies[taker]) // 2
    slack = jnp.where((source_of == order[0]) | (taker == order[0]) | (tallies[taker] == 0), 0, jnp.maximum(slack, 0))
    moved = jax.random.randint(jax.random.fold_in(own, 4), (count // 2,), 0, 1 << 20) % (slack + 1)
    tallies = tallies.at[source_of].add(-moved).at[taker].add(moved)
    items = jnp.searchsorted(jnp.cumsum(tallies), jnp.arange(rows * top), side="right").astype(jnp.int32)
    table = items.reshape(top, rows).T
    table = table[jax.random.permutation(jax.random.fold_in(own, 1), rows)]
    rotation = jax.random.randint(jax.random.fold_in(own, 2), (rows, 1), 0, top)
    return jnp.take_along_axis(table, (jnp.arange(top)[None, :] + rotation) % top, axis=1)


def portions_of(amount, total, limit, skew, full):
    portions = [(1 << 20) // math.isqrt(grade ** skew) + 1 for grade in range(1, amount + 1)]
    largest = limit if full else min(limit, max(-(-total // amount), total * portions[0] // sum(portions)))
    least = 1 if total - largest >= amount - 1 else 0
    holding, rest = [largest] + [least] * (amount - 1), total - largest - least * (amount - 1)
    while rest > 0:
        movable = [i for i in range(1, amount) if holding[i] < largest] or [i for i in range(1, amount) if holding[i] < limit]
        mass, budget = sum([portions[i] for i in movable]), rest
        for i in movable:
            addition = min(limit - holding[i], max(1, budget * portions[i] // mass), rest)
            holding[i] = holding[i] + addition
            rest = rest - addition
    return np.array(holding)


def normal_values(stream_key, dims, deviation, limit, split=(), kind=jnp.bfloat16):
    loudness = block_levels(stream_key, dims, split, -0.22, 0.18) if split else 1.0
    drawn = jax.random.normal(stream_key, dims, jnp.float32) * deviation * loudness
    return jnp.minimum(jnp.maximum(drawn, -limit), limit).astype(kind)


def setup_inputs(seed: int = 0) -> dict:
    arg_keys = jax.random.split(jax.random.key(seed), 12)
    layer_input = normal_values(arg_keys[0], (MICRO, TOKENS, MODEL_WIDTH), 1.0, 6.0, ((1, 16),))
    cotangent = normal_values(arg_keys[1], (MICRO, TOKENS, MODEL_WIDTH), 1.0, 6.0, ((1, 16),))
    positions = draw_positions(jax.random.fold_in(arg_keys[11], 71), 0)
    routes_keys = jax.random.split(jax.random.fold_in(arg_keys[3], 1), LAYER_COUNT * MICRO * TOKENS // SEQUENCE_TOKENS)
    routes_turns = jax.random.permutation(jax.random.fold_in(arg_keys[3], 3), LAYER_COUNT * MICRO * TOKENS // SEQUENCE_TOKENS)
    routes = jax.vmap(lambda own, number: routed_block(jax.random.fold_in(arg_keys[3], 2), own, number, SEQUENCE_TOKENS, EXPERTS, TOPK, CAP, 2))(routes_keys, routes_turns).reshape((LAYER_COUNT, MICRO, TOKENS, TOPK))
    gain_one = jnp.clip(1.0 + 0.1 * jax.random.normal(arg_keys[4], (LAYER_COUNT, MODEL_WIDTH), jnp.float32), 0.5, 1.5)
    attn_in = normal_values(arg_keys[5], (LAYER_COUNT, MODEL_WIDTH, (QUERY_HEADS + 2 * KEY_VALUE_HEADS) * HEAD_SIZE), MODEL_WIDTH ** -0.5, 0.1875, ((0, 2), (1, 4)))
    attn_out = normal_values(arg_keys[6], (LAYER_COUNT, QUERY_HEADS * HEAD_SIZE, MODEL_WIDTH), (max(1, 2 * QUERY_HEADS * HEAD_SIZE // SEQUENCE_TOKENS)) ** -0.5, 1.0, ((0, 2), (1, 4)))
    gain_two = jnp.clip(1.0 + 0.1 * jax.random.normal(arg_keys[7], (LAYER_COUNT, MODEL_WIDTH), jnp.float32), 0.5, 1.5)
    router = normal_values(arg_keys[8], (LAYER_COUNT, MODEL_WIDTH, EXPERTS), (4 * MODEL_WIDTH) ** -0.5, 0.09375, ((0, 2),))
    experts_in = normal_values(arg_keys[9], (LAYER_COUNT, EXPERTS, MODEL_WIDTH, 2 * FF), MODEL_WIDTH ** -0.5, 0.1875, ((0, 2), (1, 4)))
    experts_out = normal_values(arg_keys[10], (LAYER_COUNT, EXPERTS, FF, MODEL_WIDTH), (max(1, FF // 32)) ** -0.5, 1.5, ((0, 2), (1, 4)))
    return dict(layer_input=layer_input, cotangent=cotangent, positions=positions, routes=routes, gain_one=gain_one, attn_in=attn_in, attn_out=attn_out, gain_two=gain_two, router=router, experts_in=experts_in, experts_out=experts_out)


epsilon = 1e-06
rotary_base = 10000.0

def rms_scale(values):
    return lax.rsqrt(lax.optimization_barrier(jnp.mean(values * values, axis=-1, keepdims=True)) + epsilon)

def norm_back(grad_normed, inputs, scale):
    return scale * grad_normed - inputs * (scale * scale * scale) * lax.optimization_barrier(jnp.mean(grad_normed * inputs, axis=-1, keepdims=True))

def rotary_tables(place_now):
    half_size = HEAD_SIZE // 2
    frequency = jnp.power(rotary_base, -(jnp.arange(half_size, dtype=jnp.float32) * (2.0 / HEAD_SIZE)))
    angles = place_now.astype(jnp.float32)[:, None] * frequency[None, :]
    cosine_table = jnp.concatenate([jnp.cos(angles), jnp.cos(angles)], axis=-1)[:, None, :]
    sine_table = jnp.concatenate([jnp.sin(angles), jnp.sin(angles)], axis=-1)[:, None, :]
    return (cosine_table, sine_table)

def apply_rotary(values, cosine_table, sine_table):
    half_size = HEAD_SIZE // 2
    turned = jnp.concatenate([-values[..., half_size:], values[..., :half_size]], axis=-1)
    return values * cosine_table + turned * sine_table

def invert_rotary(incoming_grad, cosine_table, sine_table):
    half_size = HEAD_SIZE // 2
    times_sine = incoming_grad * sine_table
    turned_back = jnp.concatenate([times_sine[..., half_size:], -times_sine[..., :half_size]], axis=-1)
    return incoming_grad * cosine_table + turned_back

def split_heads(projection_output, cosine_table, sine_table):
    sequence_length = projection_output.shape[0]
    query_width = QUERY_HEADS * HEAD_SIZE
    key_width = KEY_VALUE_HEADS * HEAD_SIZE
    query_rows = apply_rotary(projection_output[:, :query_width].reshape(sequence_length, QUERY_HEADS, HEAD_SIZE), cosine_table, sine_table).astype(jnp.bfloat16)
    rotated_keys = apply_rotary(projection_output[:, query_width:query_width + key_width].reshape(sequence_length, KEY_VALUE_HEADS, HEAD_SIZE), cosine_table, sine_table).astype(jnp.bfloat16)
    value_rows_full = projection_output[:, query_width + key_width:].reshape(sequence_length, KEY_VALUE_HEADS, HEAD_SIZE).astype(jnp.bfloat16)
    return (query_rows, rotated_keys, value_rows_full)

def join_heads(gradient_query_rows, gradient_key_rows, gradient_value_rows, cosine_table, sine_table):
    sequence_length = gradient_query_rows.shape[0]
    return jnp.concatenate([invert_rotary(gradient_query_rows, cosine_table, sine_table).reshape(sequence_length, QUERY_HEADS * HEAD_SIZE), invert_rotary(gradient_key_rows, cosine_table, sine_table).reshape(sequence_length, KEY_VALUE_HEADS * HEAD_SIZE), gradient_value_rows.reshape(sequence_length, KEY_VALUE_HEADS * HEAD_SIZE)], axis=-1).astype(jnp.bfloat16)

def attention_scores(query_rows, rotated_keys):
    sequence_length = query_rows.shape[0]
    head_grouped = query_rows.reshape(sequence_length, KEY_VALUE_HEADS, QUERY_HEADS // KEY_VALUE_HEADS, HEAD_SIZE)
    scores = jnp.einsum('qkgd,skd->kgqs', head_grouped, rotated_keys, preferred_element_type=jnp.float32) * HEAD_SIZE ** (-0.5)
    allowed = jnp.arange(sequence_length)[:, None] >= jnp.arange(sequence_length)[None, :]
    return jnp.where(allowed, scores, -1e+30)

def attention_forward(query_rows, rotated_keys, value_rows_full):
    sequence_length = query_rows.shape[0]
    scores = attention_scores(query_rows, rotated_keys)
    row_top = lax.optimization_barrier(jnp.max(scores, axis=-1, keepdims=True))
    logarithm_total = row_top + jnp.log(lax.optimization_barrier(jnp.sum(jnp.exp(scores - row_top), axis=-1, keepdims=True)))
    weights = jnp.exp(scores - logarithm_total).astype(jnp.bfloat16)
    attention_result = jnp.einsum('kgqs,skd->qkgd', weights, value_rows_full, preferred_element_type=jnp.float32)
    return (attention_result.reshape(sequence_length, QUERY_HEADS * HEAD_SIZE).astype(jnp.bfloat16), logarithm_total)

def attention_backward(query_rows, rotated_keys, value_rows_full, attention_result, logarithm_total, gradient_attention_result):
    sequence_length = query_rows.shape[0]
    query_groups = QUERY_HEADS // KEY_VALUE_HEADS
    scores = attention_scores(query_rows, rotated_keys)
    probabilities = jnp.exp(scores - logarithm_total)
    gradient_quad = gradient_attention_result.reshape(sequence_length, KEY_VALUE_HEADS, query_groups, HEAD_SIZE)
    attention_quad = attention_result.reshape(sequence_length, KEY_VALUE_HEADS, query_groups, HEAD_SIZE)
    row_delta = jnp.einsum('qkgd,qkgd->kgq', gradient_quad, attention_quad, preferred_element_type=jnp.float32)
    grad_probs = jnp.einsum('qkgd,skd->kgqs', gradient_quad, value_rows_full, preferred_element_type=jnp.float32)
    grad_scores = (probabilities * (grad_probs - row_delta[..., None])).astype(jnp.bfloat16)
    head_grouped = query_rows.reshape(sequence_length, KEY_VALUE_HEADS, query_groups, HEAD_SIZE)
    gradient_query_rows = jnp.einsum('kgqs,skd->qkgd', grad_scores, rotated_keys, preferred_element_type=jnp.float32).reshape(sequence_length, QUERY_HEADS, HEAD_SIZE) * HEAD_SIZE ** (-0.5)
    gradient_key_rows = jnp.einsum('kgqs,qkgd->skd', grad_scores, head_grouped, preferred_element_type=jnp.float32) * HEAD_SIZE ** (-0.5)
    gradient_value_rows = jnp.einsum('kgqs,qkgd->skd', probabilities.astype(jnp.bfloat16), gradient_quad, preferred_element_type=jnp.float32)
    return (gradient_query_rows, gradient_key_rows, gradient_value_rows)

def expert_forward(arrived, expert_in, expert_out):
    hidden_pair = jnp.einsum('erd,edf->erf', arrived, expert_in, preferred_element_type=jnp.float32)
    gate_part = hidden_pair[..., :FF]
    up_part = hidden_pair[..., FF:]
    activated = (gate_part * jax.nn.sigmoid(gate_part) * up_part).astype(jnp.bfloat16)
    return jnp.einsum('erf,efd->erd', activated, expert_out, preferred_element_type=jnp.float32).astype(jnp.bfloat16)

def expert_backward(arrived, arrived_grads, expert_in, expert_out):
    hidden_pair = jnp.einsum('erd,edf->erf', arrived, expert_in, preferred_element_type=jnp.float32)
    gate_part = hidden_pair[..., :FF]
    up_part = hidden_pair[..., FF:]
    sigmoid_gate = jax.nn.sigmoid(gate_part)
    silu_gate = gate_part * sigmoid_gate
    activated = (silu_gate * up_part).astype(jnp.bfloat16)
    grad_act = jnp.einsum('erd,efd->erf', arrived_grads, expert_out, preferred_element_type=jnp.float32)
    delta_out = jnp.einsum('erf,erd->efd', activated, arrived_grads, preferred_element_type=jnp.float32)
    grad_gate = grad_act * up_part * sigmoid_gate * (1.0 + gate_part * (1.0 - sigmoid_gate))
    grad_up = grad_act * silu_gate
    grad_pair = jnp.concatenate([grad_gate, grad_up], axis=-1).astype(jnp.bfloat16)
    delta_in = jnp.einsum('erd,erf->edf', arrived, grad_pair, preferred_element_type=jnp.float32)
    back_rows = jnp.einsum('erf,edf->erd', grad_pair, expert_in, preferred_element_type=jnp.float32).astype(jnp.bfloat16)
    return (back_rows, delta_in, delta_out)

def expert_block(item_tuple):
    return expert_forward(item_tuple[0][None], item_tuple[1][None], item_tuple[2][None])[0]

def expert_back_block(item_tuple):
    back_rows, delta_in, delta_out = expert_backward(item_tuple[0][None], item_tuple[1][None], item_tuple[2][None], item_tuple[3][None])
    return (back_rows[0], delta_in[0], delta_out[0])

def attention_layer_block(item_tuple):
    return attention_forward(item_tuple[0], item_tuple[1], item_tuple[2])

def attention_reverse_block(item_tuple):
    return attention_backward(item_tuple[0], item_tuple[1], item_tuple[2], item_tuple[3], item_tuple[4], item_tuple[5])

def global_slots(choices):
    row_count = choices.shape[0]
    block_list = row_count // SEQUENCE_TOKENS
    per_block = choices.reshape(block_list, SEQUENCE_TOKENS * TOPK)
    onehot_table = (per_block[:, :, None] == jnp.arange(EXPERTS, dtype=jnp.int32)[None, None, :]).astype(jnp.int32)
    slot_rank = lax.optimization_barrier(jnp.sum((jnp.cumsum(onehot_table, axis=1) - 1) * onehot_table, axis=2))
    slot_column = (jnp.arange(block_list, dtype=jnp.int32)[:, None] * CAP + slot_rank).reshape(-1).astype(jnp.int32)
    table_three = onehot_table.reshape(row_count, TOPK, EXPERTS).astype(jnp.float32)
    return (table_three, choices.reshape(-1).astype(jnp.int32), slot_column)

def layer_forward(entering, choices, place_now, params):
    gain_first, weights_in, weights_out, gain_second, router_weights, expert_in, expert_out = params
    row_count = entering.shape[0]
    block_list = row_count // SEQUENCE_TOKENS
    residual = entering.astype(jnp.float32)
    scale_first = rms_scale(residual)
    normed_first = (residual * scale_first * gain_first).astype(jnp.bfloat16)
    projection_output = jnp.dot(normed_first, weights_in, preferred_element_type=jnp.float32)
    cosine_table, sine_table = rotary_tables(place_now)
    query_rows, rotated_keys, value_rows_full = split_heads(projection_output, cosine_table, sine_table)
    attention_result, logarithm_total = lax.map(attention_layer_block, (query_rows.reshape(block_list, SEQUENCE_TOKENS, QUERY_HEADS, HEAD_SIZE), rotated_keys.reshape(block_list, SEQUENCE_TOKENS, KEY_VALUE_HEADS, HEAD_SIZE), value_rows_full.reshape(block_list, SEQUENCE_TOKENS, KEY_VALUE_HEADS, HEAD_SIZE)))
    attention_result = attention_result.reshape(row_count, QUERY_HEADS * HEAD_SIZE)
    middle = residual + jnp.dot(attention_result, weights_out, preferred_element_type=jnp.float32)
    scale_second = rms_scale(middle)
    normed_second = (middle * scale_second * gain_second).astype(jnp.bfloat16)
    logits = jnp.dot(normed_second, router_weights, preferred_element_type=jnp.float32)
    table_three, expert_ids, slot_column = global_slots(choices)
    picked = lax.optimization_barrier(jnp.sum(table_three * logits[:, None, :], axis=-1))
    gate_probs = jax.nn.softmax(picked, axis=-1)
    copies = jnp.repeat(normed_second, TOPK, axis=0)
    outgoing = jnp.zeros((EXPERTS, block_list * CAP, MODEL_WIDTH), jnp.bfloat16).at[expert_ids, slot_column].set(copies)
    produced = lax.map(expert_block, (outgoing, expert_in, expert_out))
    picked_rows = produced[expert_ids, slot_column]
    mixture = jnp.einsum('skd,sk->sd', picked_rows.reshape(row_count, TOPK, MODEL_WIDTH), gate_probs, preferred_element_type=jnp.float32)
    leaving = (middle + mixture).astype(jnp.bfloat16)
    kept_state = (residual, scale_first, normed_first, query_rows, rotated_keys, value_rows_full, attention_result, logarithm_total, middle, scale_second, normed_second, table_three, gate_probs, expert_ids, slot_column, outgoing, picked_rows, cosine_table, sine_table)
    return (leaving, kept_state)

def layer_backward(kept_state, arriving, params):
    residual, scale_first, normed_first, query_rows, rotated_keys, value_rows_full, attention_result, logarithm_total, middle, scale_second, normed_second, table_three, gate_probs, expert_ids, slot_column, outgoing, picked_rows, cosine_table, sine_table = kept_state
    gain_first, weights_in, weights_out, gain_second, router_weights, expert_in, expert_out = params
    row_count = arriving.shape[0]
    block_list = row_count // SEQUENCE_TOKENS
    upstream = arriving.astype(jnp.float32)
    row_three = picked_rows.reshape(row_count, TOPK, MODEL_WIDTH)
    grad_gates = jnp.einsum('skd,sd->sk', row_three, upstream, preferred_element_type=jnp.float32)
    row_grads = (gate_probs[:, :, None] * upstream[:, None, :]).astype(jnp.bfloat16).reshape(row_count * TOPK, MODEL_WIDTH)
    grad_buffer = jnp.zeros((EXPERTS, block_list * CAP, MODEL_WIDTH), jnp.bfloat16).at[expert_ids, slot_column].set(row_grads)
    back_rows, delta_in, delta_out = lax.map(expert_back_block, (outgoing, grad_buffer, expert_in, expert_out))
    grad_second = lax.optimization_barrier(jnp.sum(back_rows[expert_ids, slot_column].reshape(row_count, TOPK, MODEL_WIDTH), axis=1, dtype=jnp.float32))
    grad_picked = gate_probs * (grad_gates - lax.optimization_barrier(jnp.sum(gate_probs * grad_gates, axis=-1, keepdims=True)))
    grad_logits = lax.optimization_barrier(jnp.sum(table_three * grad_picked[:, :, None], axis=1)).astype(jnp.bfloat16)
    delta_router = jnp.dot(normed_second.T, grad_logits, preferred_element_type=jnp.float32)
    grad_second = grad_second + jnp.dot(grad_logits, router_weights.T, preferred_element_type=jnp.float32)
    delta_gain_second = lax.optimization_barrier(jnp.sum(grad_second * middle * scale_second, axis=0))
    grad_middle = upstream + norm_back(grad_second * gain_second, middle, scale_second)
    grad_middle_low = grad_middle.astype(jnp.bfloat16)
    delta_attn_out = jnp.dot(attention_result.T, grad_middle_low, preferred_element_type=jnp.float32)
    gradient_attention_result = jnp.dot(grad_middle_low, weights_out.T, preferred_element_type=jnp.float32).astype(jnp.bfloat16)
    gradient_query_rows, gradient_key_rows, gradient_value_rows = lax.map(attention_reverse_block, (query_rows.reshape(block_list, SEQUENCE_TOKENS, QUERY_HEADS, HEAD_SIZE), rotated_keys.reshape(block_list, SEQUENCE_TOKENS, KEY_VALUE_HEADS, HEAD_SIZE), value_rows_full.reshape(block_list, SEQUENCE_TOKENS, KEY_VALUE_HEADS, HEAD_SIZE), attention_result.reshape(block_list, SEQUENCE_TOKENS, QUERY_HEADS * HEAD_SIZE), logarithm_total, gradient_attention_result.reshape(block_list, SEQUENCE_TOKENS, QUERY_HEADS * HEAD_SIZE)))
    gradient_projection_output = join_heads(gradient_query_rows.reshape(row_count, QUERY_HEADS, HEAD_SIZE), gradient_key_rows.reshape(row_count, KEY_VALUE_HEADS, HEAD_SIZE), gradient_value_rows.reshape(row_count, KEY_VALUE_HEADS, HEAD_SIZE), cosine_table, sine_table)
    delta_attn_in = jnp.dot(normed_first.T, gradient_projection_output, preferred_element_type=jnp.float32)
    grad_first = jnp.dot(gradient_projection_output, weights_in.T, preferred_element_type=jnp.float32)
    delta_gain_first = lax.optimization_barrier(jnp.sum(grad_first * residual * scale_first, axis=0))
    grad_enter = (grad_middle + norm_back(grad_first * gain_first, residual, scale_first)).astype(jnp.bfloat16)
    return (grad_enter, (delta_gain_first, delta_attn_in, delta_attn_out, delta_gain_second, delta_router, delta_in, delta_out))

def reference(layer_input, cotangent, positions, routes, gain_one, attn_in, attn_out, gain_two, router, experts_in, experts_out):
    layers = gain_one.shape[0]
    micros = layer_input.shape[0]

    def layer_params(layer_index):
        return (gain_one[layer_index], attn_in[layer_index], attn_out[layer_index], gain_two[layer_index], router[layer_index], experts_in[layer_index], experts_out[layer_index])
    entries = [[None] * micros for unused in range(layers)]
    hidden_list = [[None] * micros for unused in range(layers)]
    for micro_index in range(micros):
        current = layer_input[micro_index]
        for layer_index in range(layers):
            entries[layer_index][micro_index] = current
            current, unused = layer_forward(current, routes[layer_index, micro_index], positions[micro_index], layer_params(layer_index))
            hidden_list[layer_index][micro_index] = current
    grad_list = [[None] * micros for unused in range(layers)]
    totals = [None] * layers
    for micro_index in range(micros):
        upstream = cotangent[micro_index]
        for layer_index in reversed(range(layers)):
            params = layer_params(layer_index)
            unused, kept_state = layer_forward(entries[layer_index][micro_index], routes[layer_index, micro_index], positions[micro_index], params)
            upstream, deltas = layer_backward(kept_state, upstream, params)
            grad_list[layer_index][micro_index] = upstream
            if totals[layer_index] is None:
                totals[layer_index] = deltas
            else:
                totals[layer_index] = jax.tree.map(jnp.add, totals[layer_index], deltas)
    hidden = jnp.stack([jnp.stack(hidden_list[layer_index]) for layer_index in range(layers)])
    input_grad = jnp.stack([jnp.stack(grad_list[layer_index]) for layer_index in range(layers)])
    stacked = [jnp.stack([totals[layer_index][member] for layer_index in range(layers)]) for member in range(7)]
    return (hidden, input_grad, stacked[0], stacked[1], stacked[2], stacked[3], stacked[4], stacked[5], stacked[6])
```

```python
import functools

import jax
import jax.numpy as jnp
from jax import lax
from jax.experimental import pallas as pl
from jax.experimental.pallas import tpu as pltpu
from jax.sharding import PartitionSpec as P

MODEL_WIDTH = 1024
QUERY_HEADS = 16
KEY_VALUE_HEADS = 8
HEAD_SIZE = 64
FF = 512
EXPERTS = 32
TOPK = 8

QUERY_WIDTH = QUERY_HEADS * HEAD_SIZE
KEY_WIDTH = KEY_VALUE_HEADS * HEAD_SIZE
PROJECTED = QUERY_WIDTH + 2 * KEY_WIDTH
LANES = 128
HALF = HEAD_SIZE // 2

epsilon = 1e-06
rotary_base = 10000.0

F32 = jnp.float32
BF16 = jnp.bfloat16
MESH = pl.DeviceIdType.MESH
VMEM_LIMIT = 60 * 1024 * 1024


def dot_nn(a, b):
    return lax.dot_general(a, b, (((1,), (0,)), ((), ())), preferred_element_type=F32)


def dot_nt(a, b):
    return lax.dot_general(a, b, (((1,), (1,)), ((), ())), preferred_element_type=F32)


def dot_tn(a, b):
    return lax.dot_general(a, b, (((0,), (0,)), ((), ())), preferred_element_type=F32)


def row_scale(values):
    return lax.rsqrt(jnp.mean(values * values, axis=-1, keepdims=True) + epsilon)


def norm_back(grad_normed, inputs, scale):
    return scale * grad_normed - inputs * (scale * scale * scale) * jnp.mean(
        grad_normed * inputs, axis=-1, keepdims=True
    )


def lane_of(shape):
    return lax.broadcasted_iota(jnp.int32, shape, 1)


def turned(tile, low):
    return jnp.where(low, pltpu.roll(tile, LANES - HALF, 1), pltpu.roll(tile, HALF, 1))


def vmem_spec():
    return pl.BlockSpec(memory_space=pltpu.VMEM)


def any_spec():
    return pl.BlockSpec(memory_space=pl.ANY)


def gather_kernel(planes, owners, rows, in_ref, out_ref, win_ref, wout_ref, local_sem, z_send, z_recv, p_send, p_recv, c_send, c_recv):
    section = lax.axis_index("section")
    plane = lax.axis_index("dp")
    own = lax.axis_index("expert")
    part = rows // owners
    barrier = pltpu.get_barrier_semaphore()
    for step in range(1, planes):
        pl.semaphore_signal(barrier, inc=1, device_id={"dp": (plane + step) % planes}, device_id_type=MESH)
    for step in range(1, owners):
        pl.semaphore_signal(barrier, inc=1, device_id={"expert": (own + step) % owners}, device_id_type=MESH)
    pl.semaphore_signal(barrier, inc=1, device_id={"section": 1 - section}, device_id_type=MESH)
    pl.semaphore_wait(barrier, planes + owners - 1)

    pairs = ((in_ref, win_ref), (out_ref, wout_ref))
    locals_ = []
    for which, (source, full) in enumerate(pairs):
        copy = pltpu.make_async_copy(
            source.at[0], full.at[section, pl.ds(plane * rows, rows)], local_sem.at[which]
        )
        copy.start()
        locals_.append(copy)
    z_copies = {}
    for which, (source, full) in enumerate(pairs):
        for step in range(1, planes):
            copy = pltpu.make_async_remote_copy(
                src_ref=source.at[0, pl.ds(own * part, part)],
                dst_ref=full.at[section, pl.ds(plane * rows + own * part, part)],
                send_sem=z_send.at[step, which],
                recv_sem=z_recv.at[step, which],
                device_id={"dp": (plane + step) % planes},
                device_id_type=MESH,
            )
            copy.start()
            z_copies[which, step] = copy
    core_copies = []

    def push(which, slab, number):
        full = pairs[which][1]
        here = full.at[section, pl.ds(slab * rows, rows)]
        copy = pltpu.make_async_remote_copy(
            src_ref=here,
            dst_ref=here,
            send_sem=c_send.at[number, which],
            recv_sem=c_recv.at[number, which],
            device_id={"section": 1 - section},
            device_id_type=MESH,
        )
        copy.start()
        core_copies.append(copy)

    p_copies = {}
    for which, (source, full) in enumerate(pairs):
        locals_[which].wait()
        push(which, plane, 0)
        for step in range(1, planes):
            z_copies[which, step].wait_recv()
            origin = (plane + planes - step) % planes
            here = full.at[section, pl.ds(origin * rows + own * part, part)]
            for turn in range(1, owners):
                copy = pltpu.make_async_remote_copy(
                    src_ref=here,
                    dst_ref=here,
                    send_sem=p_send.at[step, turn, which],
                    recv_sem=p_recv.at[step, turn, which],
                    device_id={"expert": (own + turn) % owners},
                    device_id_type=MESH,
                )
                copy.start()
                p_copies[which, step, turn] = copy
    for which in range(2):
        for step in range(1, planes):
            for turn in range(1, owners):
                p_copies[which, step, turn].wait_recv()
            push(which, (plane + planes - step) % planes, step)
    for copy in z_copies.values():
        copy.wait_send()
    for copy in p_copies.values():
        copy.wait_send()
    for copy in core_copies:
        copy.wait()


def gather_weights(attn_in, attn_out):
    planes = lax.axis_size("dp")
    owners = lax.axis_size("expert")
    rows = attn_in.shape[1]
    sems = pltpu.SemaphoreType.DMA
    return pl.pallas_call(
        functools.partial(gather_kernel, planes, owners, rows),
        out_shape=(
            jax.ShapeDtypeStruct((2, planes * rows, attn_in.shape[2]), BF16),
            jax.ShapeDtypeStruct((2, planes * rows, attn_out.shape[2]), BF16),
        ),
        in_specs=[any_spec(), any_spec()],
        out_specs=(any_spec(), any_spec()),
        scratch_shapes=[
            sems((2,)),
            sems((planes, 2)),
            sems((planes, 2)),
            sems((planes, owners, 2)),
            sems((planes, owners, 2)),
            sems((planes, 2)),
            sems((planes, 2)),
        ],
        compiler_params=pltpu.CompilerParams(collective_id=0, has_side_effects=True, vmem_limit_bytes=VMEM_LIMIT),
        name="gather_weights",
    )(attn_in, attn_out)


def attention_forward_kernel(
    layer, x_ref, gain_one_ref, win_all, wout_all, gain_two_ref, router_ref, hot_ref, cos_ref, sin_ref,
    middle_ref, normed_ref, gate_ref, query_ref, key_ref, value_ref, attended_ref, log_ref,
    projected_ref, win_ref, wout_ref, sem,
):
    win_copy = pltpu.make_async_copy(win_all.at[layer], win_ref, sem.at[0])
    wout_copy = pltpu.make_async_copy(wout_all.at[layer], wout_ref, sem.at[1])
    win_copy.start()
    wout_copy.start()
    tokens = x_ref.shape[0]
    lane = lane_of((tokens, LANES))
    low = lane % HEAD_SIZE < HALF
    left = lane < HEAD_SIZE
    cosine, sine = cos_ref[...], sin_ref[...]
    residual = x_ref[...].astype(F32)
    normed_one = (residual * row_scale(residual) * gain_one_ref[...]).astype(BF16)
    win_copy.wait()
    projected_ref[...] = dot_nn(normed_one, win_ref[...])
    for tile in range(QUERY_WIDTH // LANES):
        columns = slice(tile * LANES, (tile + 1) * LANES)
        part = projected_ref[:, columns]
        query_ref[:, columns] = (part * cosine + turned(part, low) * sine).astype(BF16)
    for tile in range(KEY_WIDTH // LANES):
        first = slice(2 * tile * LANES, (2 * tile + 1) * LANES)
        second = slice((2 * tile + 1) * LANES, (2 * tile + 2) * LANES)
        part = projected_ref[:, QUERY_WIDTH + tile * LANES : QUERY_WIDTH + (tile + 1) * LANES]
        part = part * cosine + turned(part, low) * sine
        other = pltpu.roll(part, HEAD_SIZE, 1)
        key_ref[:, first] = jnp.where(left, part, other).astype(BF16)
        key_ref[:, second] = jnp.where(left, other, part).astype(BF16)
        start = QUERY_WIDTH + KEY_WIDTH + tile * LANES
        part = projected_ref[:, start : start + LANES]
        other = pltpu.roll(part, HEAD_SIZE, 1)
        value_ref[:, first] = jnp.where(left, part, other).astype(BF16)
        value_ref[:, second] = jnp.where(left, other, part).astype(BF16)
    pair_lane = lane_of((2 * tokens, LANES))
    row = lax.broadcasted_iota(jnp.int32, (2 * tokens, tokens), 0) % tokens
    allowed = row >= lax.broadcasted_iota(jnp.int32, (2 * tokens, tokens), 1)
    logs = jnp.zeros((2 * tokens, LANES), F32)
    for head in range(KEY_VALUE_HEADS):
        columns = slice(head * LANES, (head + 1) * LANES)
        query = query_ref[:, columns]
        nothing = jnp.zeros_like(query)
        stacked = jnp.concatenate([jnp.where(left, query, nothing), jnp.where(left, nothing, query)], axis=0)
        scores = dot_nt(stacked, key_ref[:, columns]) * HEAD_SIZE ** (-0.5)
        scores = jnp.where(allowed, scores, -1e30)
        top = jnp.max(scores, axis=-1, keepdims=True)
        log_total = top + jnp.log(jnp.sum(jnp.exp(scores - top), axis=-1, keepdims=True))
        logs = jnp.where(pair_lane == head, log_total, logs)
        weights = jnp.exp(scores - log_total).astype(BF16)
        mixed = dot_nn(weights, value_ref[:, columns])
        attended_ref[:, columns] = jnp.where(left, mixed[:tokens], mixed[tokens:]).astype(BF16)
    log_ref[...] = logs
    wout_copy.wait()
    middle = residual + dot_nn(attended_ref[...], wout_ref[...])
    middle_ref[...] = middle
    normed_two = (middle * row_scale(middle) * gain_two_ref[...]).astype(BF16)
    normed_ref[...] = normed_two
    logits = dot_nn(normed_two, router_ref[...])
    chosen = hot_ref[...] > 0.0
    top = jnp.max(jnp.where(chosen, logits, -1e30), axis=-1, keepdims=True)
    grown = jnp.where(chosen, jnp.exp(jnp.where(chosen, logits - top, 0.0)), 0.0)
    gate_ref[...] = grown / jnp.sum(grown, axis=-1, keepdims=True)


def weight_scratch():
    return [
        pltpu.VMEM((MODEL_WIDTH, PROJECTED), BF16),
        pltpu.VMEM((QUERY_WIDTH, MODEL_WIDTH), BF16),
        pltpu.SemaphoreType.DMA((2,)),
    ]


def attention_forward(layer, x, gain_one, win, wout, gain_two, router, hot, cosine, sine):
    tokens = x.shape[0]
    shape = jax.ShapeDtypeStruct
    return pl.pallas_call(
        functools.partial(attention_forward_kernel, layer),
        out_shape=(
            shape((tokens, MODEL_WIDTH), F32),
            shape((tokens, MODEL_WIDTH), BF16),
            shape((tokens, LANES), F32),
            shape((tokens, QUERY_WIDTH), BF16),
            shape((tokens, 2 * KEY_WIDTH), BF16),
            shape((tokens, 2 * KEY_WIDTH), BF16),
            shape((tokens, QUERY_WIDTH), BF16),
            shape((2 * tokens, LANES), F32),
        ),
        in_specs=[vmem_spec(), vmem_spec(), any_spec(), any_spec()] + [vmem_spec()] * 5,
        out_specs=tuple(vmem_spec() for _ in range(8)),
        scratch_shapes=[pltpu.VMEM((tokens, PROJECTED), F32)] + weight_scratch(),
        compiler_params=pltpu.CompilerParams(vmem_limit_bytes=VMEM_LIMIT),
        name="attention_forward",
    )(x, gain_one[layer], win, wout, gain_two[layer], router[layer], hot[layer], cosine, sine)


def attention_backward_kernel(
    layer, x_ref, gain_one_ref, win_all, wout_all, gain_two_ref, router_ref, cos_ref, sin_ref,
    middle_ref, gate_ref, query_ref, key_ref, value_ref, attended_ref, log_ref,
    up_ref, back_ref, gate_grad_ref,
    input_grad_ref, grad_projected_ref, low_ref, normed_ref, grad_logits_ref, gain_grad_ref,
    win_ref, wout_ref, sem,
):
    win_copy = pltpu.make_async_copy(win_all.at[layer], win_ref, sem.at[0])
    wout_copy = pltpu.make_async_copy(wout_all.at[layer], wout_ref, sem.at[1])
    wout_copy.start()
    win_copy.start()
    tokens = x_ref.shape[0]
    lane = lane_of((tokens, LANES))
    low_half = lane % HEAD_SIZE < HALF
    left = lane < HEAD_SIZE
    cosine, sine = cos_ref[...], sin_ref[...]
    gates, gate_grads = gate_ref[...], gate_grad_ref[...]
    grad_picked = gates * (gate_grads - jnp.sum(gates * gate_grads, axis=-1, keepdims=True))
    grad_logits = grad_picked.astype(BF16)
    grad_logits_ref[...] = grad_logits
    grad_second = back_ref[...] + dot_nt(grad_logits, router_ref[...])
    middle = middle_ref[...]
    scale_two = row_scale(middle)
    gain_two_grad = jnp.sum(grad_second * middle * scale_two, axis=0, keepdims=True)
    upstream = up_ref[...].astype(F32)
    grad_middle = upstream + norm_back(grad_second * gain_two_ref[...], middle, scale_two)
    low = grad_middle.astype(BF16)
    low_ref[...] = low
    wout_copy.wait()
    grad_attended = dot_nt(low, wout_ref[...]).astype(BF16)
    row = lax.broadcasted_iota(jnp.int32, (2 * tokens, tokens), 0) % tokens
    allowed = row >= lax.broadcasted_iota(jnp.int32, (2 * tokens, tokens), 1)
    root = HEAD_SIZE ** (-0.5)
    pair_lane = lane_of((2 * tokens, LANES))
    logs = log_ref[...]

    def stack(tile):
        nothing = jnp.zeros_like(tile)
        return jnp.concatenate([jnp.where(left, tile, nothing), jnp.where(left, nothing, tile)], axis=0)

    def fold(wide):
        return wide + pltpu.roll(wide, HEAD_SIZE, 1)

    key_grads, value_grads = [], []
    for head in range(KEY_VALUE_HEADS):
        columns = slice(head * LANES, (head + 1) * LANES)
        query = stack(query_ref[:, columns])
        key, value = key_ref[:, columns], value_ref[:, columns]
        scores = dot_nt(query, key) * root
        log_total = jnp.sum(jnp.where(pair_lane == head, logs, 0.0), axis=-1, keepdims=True)
        probabilities = jnp.where(allowed, jnp.exp(jnp.where(allowed, scores - log_total, 0.0)), 0.0)
        grad_tile = stack(grad_attended[:, columns])
        delta = jnp.sum(
            grad_tile.astype(F32) * stack(attended_ref[:, columns]).astype(F32), axis=-1, keepdims=True
        )
        grad_scores = (probabilities * (dot_nt(grad_tile, value) - delta)).astype(BF16)
        wide = dot_nn(grad_scores, key) * root
        grad_query = jnp.where(left, wide[:tokens], wide[tokens:])
        grad_query = grad_query * cosine - turned(grad_query, low_half) * sine
        grad_projected_ref[:, columns] = grad_query.astype(BF16)
        key_grads.append(fold(dot_tn(grad_scores, query)) * root)
        value_grads.append(fold(dot_tn(probabilities.astype(BF16), grad_tile)))
    for tile in range(KEY_WIDTH // LANES):
        part = jnp.where(left, key_grads[2 * tile], key_grads[2 * tile + 1])
        part = part * cosine - turned(part, low_half) * sine
        start = QUERY_WIDTH + tile * LANES
        grad_projected_ref[:, start : start + LANES] = part.astype(BF16)
        start += KEY_WIDTH
        grad_projected_ref[:, start : start + LANES] = jnp.where(
            left, value_grads[2 * tile], value_grads[2 * tile + 1]
        ).astype(BF16)
    win_copy.wait()
    grad_first = dot_nt(grad_projected_ref[...], win_ref[...])
    residual = x_ref[...].astype(F32)
    scale_one = row_scale(residual)
    normed_ref[...] = (residual * scale_one * gain_one_ref[...]).astype(BF16)
    gain_one_grad = jnp.sum(grad_first * residual * scale_one, axis=0, keepdims=True)
    gain_grad_ref[...] = jnp.concatenate(
        [gain_one_grad, gain_two_grad, jnp.zeros((6, MODEL_WIDTH), F32)], axis=0
    )
    input_grad_ref[...] = (
        grad_middle + norm_back(grad_first * gain_one_ref[...], residual, scale_one)
    ).astype(BF16)


def attention_backward(layer, x, gain_one, win, wout, gain_two, router, cosine, sine, kept, up, back, gate_grads):
    middle, gates, query, key, value, attended, logs = kept
    tokens = x.shape[0]
    shape = jax.ShapeDtypeStruct
    return pl.pallas_call(
        functools.partial(attention_backward_kernel, layer),
        out_shape=(
            shape((tokens, MODEL_WIDTH), BF16),
            shape((tokens, PROJECTED), BF16),
            shape((tokens, MODEL_WIDTH), BF16),
            shape((tokens, MODEL_WIDTH), BF16),
            shape((tokens, LANES), BF16),
            shape((8, MODEL_WIDTH), F32),
        ),
        in_specs=[vmem_spec(), vmem_spec(), any_spec(), any_spec()] + [vmem_spec()] * 14,
        out_specs=tuple(vmem_spec() for _ in range(6)),
        scratch_shapes=weight_scratch(),
        compiler_params=pltpu.CompilerParams(vmem_limit_bytes=VMEM_LIMIT),
        name="attention_backward",
    )(x, gain_one[layer], win, wout, gain_two[layer], router[layer], cosine, sine, middle, gates, query, key, value, attended, logs,
      up, back, gate_grads)


def expert_kernel(mode, layer, owners, tokens, local, *refs):
    forward, backward = "f" in mode, "b" in mode
    refs = list(refs)
    take = refs.pop
    win_own, win_other, wout_own, wout_other = (take(0) for _ in range(4))
    middle_in = take(0) if forward else None
    gate_in = take(0)
    normed_in = take(0)
    up_in = take(0) if backward else None
    hidden_out = take(0) if forward else None
    if forward:
        plane_out, plane_gate_out = take(0), take(0)
    if backward:
        back_out, gate_grad_out = take(0), take(0)
    win, wout, win_sem, wout_sem = (take(0) for _ in range(4))
    if forward:
        normed, gates = take(0), take(0)
        x_send, x_recv, g_send, g_recv = (take(0) for _ in range(4))
        total, leaving, coming, y_send, y_recv = (take(0) for _ in range(5))
    else:
        normed, gates = normed_in, gate_in
    if backward:
        ups, u_send, u_recv = (take(0) for _ in range(3))
        back_total, back_leaving, back_coming, b_send, b_recv = (take(0) for _ in range(5))
        grads, grads_leaving, grads_coming, d_send, d_recv = (take(0) for _ in range(5))

    section = lax.axis_index("section")
    own = lax.axis_index("expert")
    rows = owners * tokens

    @pl.when(section == layer)
    def _():
        for expert in range(local):
            pltpu.make_async_copy(win_own.at[0, expert], win.at[expert], win_sem.at[expert]).start()
            pltpu.make_async_copy(wout_own.at[0, expert], wout.at[expert], wout_sem.at[expert]).start()

    @pl.when(section != layer)
    def _():
        for expert in range(local):
            pltpu.make_async_copy(win_other.at[0, expert], win.at[expert], win_sem.at[expert]).start()
            pltpu.make_async_copy(wout_other.at[0, expert], wout.at[expert], wout_sem.at[expert]).start()

    barrier = pltpu.get_barrier_semaphore()
    for step in range(1, owners):
        pl.semaphore_signal(barrier, inc=1, device_id={"expert": (own + step) % owners}, device_id_type=MESH)
    here = pl.ds(own * tokens, tokens)
    if forward:
        normed[here] = normed_in[...]
        gates[here] = gate_in[...]
    if backward:
        ups[here] = up_in[...]
    pl.semaphore_wait(barrier, owners - 1)
    moves = []

    def spread(source, buffer, send, recv):
        for step in range(1, owners):
            copy = pltpu.make_async_remote_copy(
                src_ref=source,
                dst_ref=buffer.at[here],
                send_sem=send.at[step],
                recv_sem=recv.at[step],
                device_id={"expert": (own + step) % owners},
                device_id_type=MESH,
            )
            copy.start()
            moves.append(copy)

    if forward:
        spread(normed_in, normed, x_send, x_recv)
        spread(gate_in, gates, g_send, g_recv)
    if backward:
        spread(up_in, ups, u_send, u_recv)
    for copy in moves:
        copy.wait()

    chunk = min(rows, 256)
    if backward:
        grads[...] = jnp.zeros_like(grads)

    def one_expert(expert, carry):
        pltpu.make_async_copy(win_own.at[0, 0], win.at[expert], win_sem.at[expert]).wait()
        pltpu.make_async_copy(wout_own.at[0, 0], wout.at[expert], wout_sem.at[expert]).wait()
        mine = own * local + expert

        def one_chunk(number, carry):
            span = pl.ds(number * chunk, chunk)
            x = normed[span]
            lane = lane_of((chunk, LANES))
            gate = jnp.sum(jnp.where(lane == mine, gates[span], 0.0), axis=-1, keepdims=True)
            pair = dot_nn(x, win[expert])
            gate_part, up_part = pair[:, :FF], pair[:, FF:]
            sigmoid = 1.0 / (1.0 + jnp.exp(-gate_part))
            silu = gate_part * sigmoid
            activated = silu * up_part
            if forward:
                term = dot_nn((activated * gate).astype(BF16), wout[expert])

                @pl.when(expert == 0)
                def _():
                    total[span] = term

                @pl.when(expert > 0)
                def _():
                    total[span] += term

            if backward:
                inner = dot_nt(ups[span], wout[expert])
                gate_grad = jnp.sum(activated * inner, axis=-1, keepdims=True)
                grads[span] = jnp.where(lane == mine, gate_grad, grads[span])
                grad_activated = inner * gate
                grad_gate = grad_activated * up_part * sigmoid * (1.0 + gate_part * (1.0 - sigmoid))
                grad_up = grad_activated * silu
                grad_pair = jnp.concatenate([grad_gate.astype(BF16), grad_up.astype(BF16)], axis=-1)
                term_back = dot_nt(grad_pair, win[expert])

                @pl.when(expert == 0)
                def _():
                    back_total[span] = term_back

                @pl.when(expert > 0)
                def _():
                    back_total[span] += term_back

            return carry

        return lax.fori_loop(0, rows // chunk, one_chunk, carry)

    lax.fori_loop(0, local, one_expert, 0)

    def send_back(source, out, arriving, send, recv):
        copies = []
        for step in range(1, owners):
            target = (own + step) % owners
            out[step] = source[pl.ds(target * tokens, tokens)].astype(out.dtype)
            copy = pltpu.make_async_remote_copy(
                src_ref=out.at[step],
                dst_ref=arriving.at[step],
                send_sem=send.at[step],
                recv_sem=recv.at[step],
                device_id={"expert": target},
                device_id_type=MESH,
            )
            copy.start()
            copies.append(copy)
        return copies

    if backward:
        back_copies = send_back(back_total, back_leaving, back_coming, b_send, b_recv)
        grad_copies = send_back(grads, grads_leaving, grads_coming, d_send, d_recv)
    if forward:
        mix_copies = send_back(total, leaving, coming, y_send, y_recv)
        plane_out[...] = normed[...]
        plane_gate_out[...] = gates[...]

    def finish(source, arriving, copies):
        result = source[here]
        for step in range(1, owners):
            copies[step - 1].wait()
            result = result + arriving[step].astype(F32)
        return result

    if backward:
        back_out[...] = finish(back_total, back_coming, back_copies)
        gate_grad_out[...] = finish(grads, grads_coming, grad_copies)
    if forward:
        hidden_out[...] = (middle_in[...] + finish(total, coming, mix_copies)).astype(BF16)


def expert_stage(mode, layer, number, weights, middle, gates, normed, up):
    owners = lax.axis_size("expert")
    local = weights[0].shape[1]
    forward, backward = "f" in mode, "b" in mode
    tokens = (normed if forward else up).shape[0]
    rows = owners * tokens
    shape = jax.ShapeDtypeStruct
    sems = pltpu.SemaphoreType.DMA
    arguments, specs = list(weights), [any_spec()] * 4
    if forward:
        arguments.append(middle)
    arguments += [gates, normed]
    if backward:
        arguments.append(up)
    specs += [vmem_spec()] * (len(arguments) - 4)
    outs = []
    scratch = [
        pltpu.VMEM((local, MODEL_WIDTH, 2 * FF), BF16),
        pltpu.VMEM((local, FF, MODEL_WIDTH), BF16),
        sems((local,)),
        sems((local,)),
    ]
    pair = [sems((owners,)), sems((owners,))]
    if forward:
        outs += [
            shape((tokens, MODEL_WIDTH), BF16),
            shape((rows, MODEL_WIDTH), BF16),
            shape((rows, LANES), F32),
        ]
        scratch += [pltpu.VMEM((rows, MODEL_WIDTH), BF16), pltpu.VMEM((rows, LANES), F32)] + pair + pair
        scratch += [
            pltpu.VMEM((rows, MODEL_WIDTH), F32),
            pltpu.VMEM((owners, tokens, MODEL_WIDTH), BF16),
            pltpu.VMEM((owners, tokens, MODEL_WIDTH), BF16),
        ] + pair
    if backward:
        outs += [shape((tokens, MODEL_WIDTH), F32), shape((tokens, LANES), F32)]
        scratch += [pltpu.VMEM((rows, MODEL_WIDTH), BF16)] + pair
        scratch += [
            pltpu.VMEM((rows, MODEL_WIDTH), F32),
            pltpu.VMEM((owners, tokens, MODEL_WIDTH), BF16),
            pltpu.VMEM((owners, tokens, MODEL_WIDTH), BF16),
        ] + pair
        scratch += [
            pltpu.VMEM((rows, LANES), F32),
            pltpu.VMEM((owners, tokens, LANES), F32),
            pltpu.VMEM((owners, tokens, LANES), F32),
        ] + pair
    return pl.pallas_call(
        functools.partial(expert_kernel, mode, layer, owners, tokens, local),
        out_shape=tuple(outs),
        in_specs=specs,
        out_specs=tuple(vmem_spec() for _ in outs),
        scratch_shapes=scratch,
        compiler_params=pltpu.CompilerParams(
            collective_id=number, has_side_effects=True, vmem_limit_bytes=VMEM_LIMIT
        ),
        name="experts_" + mode,
    )(*arguments)


def weight_grad_kernel(
    x_ref, up_ref, gate_ref, win_ref, wout_ref, grad_in_ref, grad_out_ref, activated_ref
):
    expert, block = pl.program_id(0), pl.program_id(1)
    plane = lax.axis_index("dp")
    local = pl.num_programs(0)
    mine = lax.axis_index("expert") * local + expert
    slice_in, slice_out = grad_in_ref.shape[0], grad_out_ref.shape[0]
    lane = lane_of(gate_ref.shape)
    gate = jnp.sum(jnp.where(lane == mine, gate_ref[...], 0.0), axis=-1, keepdims=True)
    pair = dot_nn(x_ref[...], win_ref[...])
    gate_part, up_part = pair[:, :FF], pair[:, FF:]
    sigmoid = 1.0 / (1.0 + jnp.exp(-gate_part))
    silu = gate_part * sigmoid
    activated_ref[...] = (silu * up_part * gate).astype(BF16)
    grad_activated = dot_nt(up_ref[...], wout_ref[...]) * gate
    grad_gate = grad_activated * up_part * sigmoid * (1.0 + gate_part * (1.0 - sigmoid))
    grad_up = grad_activated * silu
    grad_pair = jnp.concatenate([grad_gate.astype(BF16), grad_up.astype(BF16)], axis=-1)
    mine_in = x_ref[:, pl.ds(pl.multiple_of(plane * slice_in, LANES), slice_in)]
    mine_out = activated_ref[:, pl.ds(pl.multiple_of(plane * slice_out, LANES), slice_out)]
    term_in = dot_tn(mine_in, grad_pair)
    term_out = dot_tn(mine_out, up_ref[...])

    @pl.when(block == 0)
    def _():
        grad_in_ref[...] = term_in
        grad_out_ref[...] = term_out

    @pl.when(block > 0)
    def _():
        grad_in_ref[...] += term_in
        grad_out_ref[...] += term_out


def weight_grads(x, up, gates, experts_in, experts_out):
    planes = lax.axis_size("dp")
    local = experts_in.shape[1]
    rows = x.shape[0]
    block = 512
    shape = jax.ShapeDtypeStruct
    return pl.pallas_call(
        weight_grad_kernel,
        grid=(local, rows // block),
        out_shape=(
            shape((local, MODEL_WIDTH // planes, 2 * FF), F32),
            shape((local, FF // planes, MODEL_WIDTH), F32),
        ),
        in_specs=[
            pl.BlockSpec((block, MODEL_WIDTH), lambda e, b: (b, 0)),
            pl.BlockSpec((block, MODEL_WIDTH), lambda e, b: (b, 0)),
            pl.BlockSpec((block, LANES), lambda e, b: (b, 0)),
            pl.BlockSpec((None, None, MODEL_WIDTH, 2 * FF), lambda e, b: (0, e, 0, 0)),
            pl.BlockSpec((None, None, FF, MODEL_WIDTH), lambda e, b: (0, e, 0, 0)),
        ],
        out_specs=(
            pl.BlockSpec((None, MODEL_WIDTH // planes, 2 * FF), lambda e, b: (e, 0, 0)),
            pl.BlockSpec((None, FF // planes, MODEL_WIDTH), lambda e, b: (e, 0, 0)),
        ),
        scratch_shapes=[pltpu.VMEM((block, FF), BF16)],
        compiler_params=pltpu.CompilerParams(vmem_limit_bytes=VMEM_LIMIT),
        name="weight_grads",
    )(x, up, gates, experts_in, experts_out)


def rotated_blocks(block, axis):
    length = lax.axis_size(axis)
    blocks = [block]
    for step in range(1, length):
        blocks.append(lax.ppermute(block, axis, [(i, (i + step) % length) for i in range(length)]))
    return jnp.stack(blocks)


def shards(layer_input, cotangent, positions, routes, gain_one, attn_in, attn_out, gain_two, router,
           experts_in, experts_out):
    section = lax.axis_index("section")
    first = section == 0
    planes = lax.axis_size("dp")
    owners = lax.axis_size("expert")
    own = lax.axis_index("expert")
    tokens = layer_input.shape[1]

    def swap(values):
        return lax.ppermute(values, "section", [(0, 1), (1, 0)])

    def layered(mine, other):
        return jnp.stack([jnp.where(first, mine, other), jnp.where(first, other, mine)])

    def both(mine):
        return layered(mine, swap(mine))

    win_other, wout_other = swap(experts_in), swap(experts_out)
    weights = (experts_in, win_other, experts_out, wout_other)
    win, wout = gather_weights(attn_in, attn_out)
    gains = both(jnp.concatenate([gain_one, gain_two], axis=0))
    gains_one, gains_two = gains[:, 0:1], gains[:, 1:2]
    routers = both(jnp.pad(router[0], ((0, 0), (0, LANES - EXPERTS))))

    pick = functools.partial(lax.dynamic_index_in_dim, axis=0, keepdims=False)
    x = pick(layer_input, section)
    up = pick(cotangent, section)
    place = pick(positions, section)
    choices = layered(pick(routes[0], section), swap(pick(routes[0], 1 - section)))
    hot = jnp.sum(
        (choices[..., None] == jnp.arange(LANES, dtype=jnp.int32)).astype(F32), axis=2
    )
    lane = jnp.arange(LANES)
    frequency = jnp.power(rotary_base, -((lane % HALF).astype(F32) * (2.0 / HEAD_SIZE)))
    angles = place.astype(F32)[:, None] * frequency[None, :]
    cosine = jnp.cos(angles)
    sine = jnp.where(lane % HEAD_SIZE < HALF, -1.0, 1.0) * jnp.sin(angles)

    def ahead(layer, entering):
        return attention_forward(layer, entering, gains_one, win, wout, gains_two, routers, hot, cosine, sine)

    def behind(layer, entering, kept, upstream, back, gate_grads):
        return attention_backward(
            layer, entering, gains_one, win, wout, gains_two, routers, cosine, sine, kept, upstream, back, gate_grads
        )

    middle0, normed0, gates0, *kept0 = ahead(0, x)
    hidden0, plane0, plane_gates0 = expert_stage("f", 0, 1, weights, middle0, gates0, normed0, None)
    middle1, normed1, gates1, *kept1 = ahead(1, hidden0)
    hidden1, plane1, plane_gates1, back1, gate_grads1 = expert_stage(
        "fb", 1, 2, weights, middle1, gates1, normed1, up
    )
    grad1, projected1, low1, first1, logits1, gain_grads1 = behind(
        1, hidden0, (middle1, gates1, *kept1), up, back1, gate_grads1
    )
    back0, gate_grads0 = expert_stage("b", 0, 3, weights, None, plane_gates0, plane0, grad1)
    grad0, projected0, low0, first0, logits0, gain_grads0 = behind(
        0, x, (middle0, gates0, *kept0), grad1, back0, gate_grads0
    )

    def regroup(value0, value1):
        mine = jnp.where(first, value0, value1)
        return mine, swap(jnp.where(first, value1, value0))

    def ordered(pair):
        mine, other = pair
        return jnp.stack([jnp.where(first, mine, other), jnp.where(first, other, mine)])

    hidden = ordered(regroup(hidden0, hidden1))[None]
    input_grad = ordered(regroup(grad0, grad1))[None]

    high0, high1 = gates0.astype(BF16), gates1.astype(BF16)
    rest0, rest1 = (gates0 - high0.astype(F32)).astype(BF16), (gates1 - high1.astype(F32)).astype(BF16)
    pack0 = jnp.concatenate([normed0, grad1, logits0, high0, rest0], axis=-1)
    pack1 = jnp.concatenate([normed1, up, logits1, high1, rest1], axis=-1)
    pack = jnp.concatenate(regroup(pack0, pack1), axis=0)
    everything = rotated_blocks(rotated_blocks(pack, "dp"), "expert").reshape(-1, pack.shape[1])
    every_x = everything[:, :MODEL_WIDTH]
    every_up = everything[:, MODEL_WIDTH : 2 * MODEL_WIDTH]
    small = everything[:, 2 * MODEL_WIDTH :].reshape(-1, 3, LANES)
    every_gate = small[:, 1].astype(F32) + small[:, 2].astype(F32)
    grad_experts_in, grad_experts_out = weight_grads(every_x, every_up, every_gate, experts_in, experts_out)
    grad_router = dot_tn(every_x, small[:, 0])[:, :EXPERTS]

    factors0 = jnp.concatenate([projected0, low0, first0, kept0[3]], axis=-1)
    factors1 = jnp.concatenate([projected1, low1, first1, kept1[3]], axis=-1)
    factors = jnp.concatenate(regroup(factors0, factors1), axis=0)
    around = rotated_blocks(factors, "expert").reshape(-1, factors.shape[1])
    part = MODEL_WIDTH // (planes * owners)

    def mine_of(values):
        blocks = values.reshape(-1, planes, owners, part)
        return lax.dynamic_index_in_dim(blocks, own, 2, keepdims=False).reshape(-1, planes * part)

    start = PROJECTED + MODEL_WIDTH
    grad_in = dot_tn(mine_of(around[:, start : start + MODEL_WIDTH]), around[:, :PROJECTED])
    grad_out = dot_tn(mine_of(around[:, start + MODEL_WIDTH :]), around[:, PROJECTED:start])
    partial = jnp.concatenate([grad_in, grad_out], axis=-1).reshape(planes, part, -1)
    plane = lax.axis_index("dp")
    total = pick(partial, plane)
    for step in range(1, planes):
        leaving = pick(partial, (plane + step) % planes).astype(BF16)
        pairs = [(i, (i + step) % planes) for i in range(planes)]
        total = total + lax.ppermute(leaving, "dp", pairs).astype(F32)
    grad_attn_in, grad_attn_out = total[:, :PROJECTED], total[:, PROJECTED:]

    gain_mine, gain_other = regroup(gain_grads0[:2], gain_grads1[:2])
    gain_sums = lax.psum(gain_mine + gain_other, ("dp", "expert"))
    return (
        hidden,
        input_grad,
        gain_sums[0:1],
        grad_attn_in[None],
        grad_attn_out[None],
        gain_sums[1:2],
        grad_router[None],
        grad_experts_in[None],
        grad_experts_out[None],
    )


def solution(mesh):
    in_specs = (
        P(None, ("dp", "expert"), None),
        P(None, ("dp", "expert"), None),
        P(None, ("dp", "expert")),
        P("section", None, ("dp", "expert"), None),
        P("section", None),
        P("section", "dp", None),
        P("section", "dp", None),
        P("section", None),
        P("section", None, None),
        P("section", "expert", None, None),
        P("section", "expert", None, None),
    )
    out_specs = (
        P("section", None, ("dp", "expert"), None),
        P("section", None, ("dp", "expert"), None),
        P("section", None),
        P("section", ("dp", "expert"), None),
        P("section", ("dp", "expert"), None),
        P("section", None),
        P("section", None, None),
        P("section", "expert", "dp", None),
        P("section", "expert", "dp", None),
    )
    return jax.shard_map(shards, mesh=mesh, in_specs=in_specs, out_specs=out_specs, check_vma=False)
```

```python
import functools

import jax
import jax.numpy as jnp
from jax import lax
from jax.experimental import pallas as pl
from jax.experimental.pallas import tpu as pltpu
from jax.sharding import PartitionSpec as P

MODEL_WIDTH = 1024
QUERY_HEADS = 16
KEY_VALUE_HEADS = 8
HEAD_SIZE = 64
FF = 512
EXPERTS = 32
TOPK = 8

QUERY_WIDTH = QUERY_HEADS * HEAD_SIZE
KEY_WIDTH = KEY_VALUE_HEADS * HEAD_SIZE
PROJECTED = QUERY_WIDTH + 2 * KEY_WIDTH
LANES = 128
HALF = HEAD_SIZE // 2
PACKED = MODEL_WIDTH + LANES

epsilon = 1e-06
rotary_base = 10000.0

F32 = jnp.float32
BF16 = jnp.bfloat16
MESH = pl.DeviceIdType.MESH
VMEM_LIMIT = 62 * 1024 * 1024


def dot_nn(a, b):
    return lax.dot_general(a, b, (((1,), (0,)), ((), ())), preferred_element_type=F32)


def dot_nt(a, b):
    return lax.dot_general(a, b, (((1,), (1,)), ((), ())), preferred_element_type=F32)


def dot_tn(a, b):
    return lax.dot_general(a, b, (((0,), (0,)), ((), ())), preferred_element_type=F32)


def row_scale(values):
    return lax.rsqrt(jnp.mean(values * values, axis=-1, keepdims=True) + epsilon)


def norm_back(grad_normed, inputs, scale):
    return scale * grad_normed - inputs * (scale * scale * scale) * jnp.mean(
        grad_normed * inputs, axis=-1, keepdims=True
    )


def lane_of(shape):
    return lax.broadcasted_iota(jnp.int32, shape, 1)


def turned(tile, low):
    return jnp.where(low, pltpu.roll(tile, LANES - HALF, 1), pltpu.roll(tile, HALF, 1))


def two_parts(values):
    high = values.astype(BF16).astype(F32)
    return (high + pltpu.roll(values - high, EXPERTS, 1)).astype(BF16)


def column_of(parts, lane, column):
    wide = parts.astype(F32)
    return jnp.sum(jnp.where((lane == column) | (lane == column + EXPERTS), wide, 0.0), axis=-1, keepdims=True)


def remote(source, target, send, recv, device):
    return pltpu.make_async_remote_copy(
        src_ref=source, dst_ref=target, send_sem=send, recv_sem=recv, device_id=device, device_id_type=MESH
    )


def vmem_spec():
    return pl.BlockSpec(memory_space=pltpu.VMEM)


def any_spec():
    return pl.BlockSpec(memory_space=pl.ANY)


class Names:
    pass


def call(kernel, name, number, inputs, outputs, scratch):
    labels = list(inputs) + list(outputs) + list(scratch)

    def body(*refs):
        names = Names()
        for label, ref in zip(labels, refs):
            setattr(names, label, ref)
        kernel(names)

    results = pl.pallas_call(
        body,
        out_shape=tuple(jax.ShapeDtypeStruct(shape, dtype) for shape, dtype, _ in outputs.values()),
        in_specs=[spec for _, spec in inputs.values()],
        out_specs=tuple(spec for _, _, spec in outputs.values()),
        scratch_shapes=list(scratch.values()),
        compiler_params=pltpu.CompilerParams(
            collective_id=number, has_side_effects=True, vmem_limit_bytes=VMEM_LIMIT
        ),
        name=name,
    )(*[array for array, _ in inputs.values()])
    return dict(zip(outputs, results))


def layers_kernel(planes, owners, tokens, local, slab, r):
    section = lax.axis_index("section")
    plane = lax.axis_index("dp")
    own = lax.axis_index("expert")
    rows = owners * tokens
    part = slab // owners
    here = pl.ds(own * tokens, tokens)
    partner = {"section": 1 - section}

    def planes_to(step):
        return (plane + step) % planes

    def owner_to(step):
        return (own + step) % owners

    barrier = pltpu.get_barrier_semaphore()
    for step in range(1, owners):
        pl.semaphore_signal(barrier, inc=1, device_id={"expert": owner_to(step)}, device_id_type=MESH)
    for step in range(1, planes):
        for target in range(2):
            pl.semaphore_signal(
                barrier, inc=1, device_id={"section": target, "dp": planes_to(step)}, device_id_type=MESH
            )
    pl.semaphore_signal(barrier, inc=1, device_id=partner, device_id_type=MESH)
    pl.semaphore_wait(barrier, owners - 1 + 2 * (planes - 1) + 1)

    unsent = []

    weight_pairs = ((r.attn_in, r.win), (r.attn_out, r.wout))

    def slab_local(layer, which):
        source, full = weight_pairs[which]
        return pltpu.make_async_copy(
            source.at[0], full.at[layer, pl.ds(plane * slab, slab)], r.w_local.at[layer, which]
        )

    def slab_z(layer, which, step):
        source, full = weight_pairs[which]
        return remote(
            source.at[0, pl.ds(own * part, part)],
            full.at[layer, pl.ds(plane * slab + own * part, part)],
            r.wz_send.at[layer, which, step],
            r.wz_recv.at[layer, which, step],
            {"dp": planes_to(step)},
        )

    def slab_plane(layer, which, step, turn):
        full = weight_pairs[which][1]
        origin = planes_to(planes - step)
        block = full.at[layer, pl.ds(origin * slab + own * part, part)]
        return remote(
            block,
            block,
            r.wp_send.at[layer, which, step, turn],
            r.wp_recv.at[layer, which, step, turn],
            {"expert": owner_to(turn)},
        )

    def slab_core(layer, which, step):
        full = weight_pairs[which][1]
        block = full.at[layer, pl.ds(planes_to(planes - step) * slab, slab)]
        return remote(block, block, r.wc_send.at[layer, which, step], r.wc_recv.at[layer, which, step], partner)

    def weights_start(layer, which):
        @pl.when(section == layer)
        def _():
            for step in range(1, planes):
                slab_z(layer, which, step).start()
            slab_local(layer, which).start()

    def weights_spread(layer, which):
        @pl.when(section == layer)
        def _():
            slab_local(layer, which).wait()
            slab_core(layer, which, 0).start()
            for step in range(1, planes):
                slab_z(layer, which, step).wait_recv()
                for turn in range(1, owners):
                    slab_plane(layer, which, step, turn).start()

    def weights_push(layer, which):
        @pl.when(section == layer)
        def _():
            for step in range(1, planes):
                for turn in range(1, owners):
                    slab_plane(layer, which, step, turn).wait_recv()
                slab_core(layer, which, step).start()

    def weights_wait(layer, which):
        @pl.when(section != layer)
        def _():
            for step in range(planes):
                slab_core(layer, which, step).wait_recv()

    def weights_unsent(layer, which):
        @pl.when(section == layer)
        def _():
            for step in range(1, planes):
                slab_z(layer, which, step).wait_send()
                for turn in range(1, owners):
                    slab_plane(layer, which, step, turn).wait_send()
            for step in range(planes):
                slab_core(layer, which, step).wait_send()

    def swap_pair(expert):
        return (
            remote(r.experts_in.at[0, expert], r.other_in.at[expert], r.s_send.at[0, expert], r.s_recv.at[0, expert], partner),
            remote(r.experts_out.at[0, expert], r.other_out.at[expert], r.s_send.at[1, expert], r.s_recv.at[1, expert], partner),
        )

    def load_in(layer, expert):
        mine = pltpu.make_async_copy(r.experts_in.at[0, expert], r.ein.at[expert], r.l_sem.at[0, expert])
        other = pltpu.make_async_copy(r.other_in.at[expert], r.ein.at[expert], r.l_sem.at[0, expert])
        return mine, other

    def load_out(layer, expert):
        target = r.eout.at[pl.ds(expert * FF, FF)]
        mine = pltpu.make_async_copy(r.experts_out.at[0, expert], target, r.l_sem.at[1, expert])
        other = pltpu.make_async_copy(r.other_out.at[expert], target, r.l_sem.at[1, expert])
        return mine, other

    def start_load(make, layer, expert, which, first_use):
        @pl.when(section == layer)
        def _():
            make(layer, expert)[0].start()

        @pl.when(section != layer)
        def _():
            if first_use:
                swap_pair(expert)[which].wait_recv()
            make(layer, expert)[1].start()

    class Spread:
        def __init__(self, source, buffer, index):
            self.copies = [
                remote(source, buffer.at[own], r.a_send.at[index, step], r.a_recv.at[index, step],
                       {"expert": owner_to(step)})
                for step in range(1, owners)
            ]
            self.source, self.buffer = source, buffer

        def start(self):
            for copy in self.copies:
                copy.start()
            self.buffer[own] = self.source[...]

        def wait(self):
            for copy in self.copies:
                copy.wait_recv()
            unsent.extend(self.copies)

    class Reduce:
        def __init__(self, leaving, coming, index, cuts):
            self.leaving, self.coming, self.index, self.cuts = leaving, coming, index, cuts
            self.copies = {
                (cut, step): remote(
                    leaving.at[step - 1, :, pl.ds(*cuts[cut])],
                    coming.at[step - 1, :, pl.ds(*cuts[cut])],
                    r.r_send.at[index, cut, step],
                    r.r_recv.at[index, cut, step],
                    {"expert": owner_to(step)},
                )
                for cut in range(len(cuts))
                for step in range(1, owners)
            }

        def put(self, step, columns, values):
            self.leaving[step - 1, :, columns] = values

        def start(self, cut):
            for step in range(1, owners):
                self.copies[cut, step].start()

        def wait(self):
            for copy in self.copies.values():
                copy.wait()

    class Gather:
        def __init__(self, layer, block, around, target, index):
            self.layer, self.block, self.around, self.target, self.index = layer, block, around, target, index

        def across(self, step):
            return [
                remote(
                    self.block,
                    self.target.at[own, (planes - step) % planes, section],
                    r.g_send.at[self.index, step],
                    r.g_recv.at[self.index, step, section],
                    {"section": self.layer, "dp": planes_to(step)},
                )
            ][0]

        def arrival(self, step, micro):
            return remote(
                self.block,
                self.target.at[own, (planes - step) % planes, micro],
                r.g_send.at[self.index, step],
                r.g_recv.at[self.index, step, micro],
                {"section": self.layer, "dp": planes_to(step)},
            )

        def home_local(self):
            return pltpu.make_async_copy(self.around, self.target.at[:, 0, section], r.g_local.at[self.index])

        def home_remote(self, micro):
            return remote(self.around, self.target.at[:, 0, micro], r.g_send.at[self.index, 0],
                          r.g_recv.at[self.index, 0, 0], partner)

        def inside(self, turn):
            column = self.target.at[own, pl.ds(1, planes - 1)]
            return remote(column, column, r.gp_send.at[self.index, turn], r.gp_recv.at[self.index, turn],
                          {"expert": owner_to(turn)})

        def start(self):
            for step in range(1, planes):
                self.across(step).start()

        def start_home(self):
            @pl.when(section == self.layer)
            def _():
                self.home_local().start()

            @pl.when(section != self.layer)
            def _():
                self.home_remote(section).start()

        def middle(self):
            @pl.when(section == self.layer)
            def _():
                for step in range(1, planes):
                    for micro in range(2):
                        self.arrival(step, micro).wait_recv()
                for turn in range(1, owners):
                    self.inside(turn).start()

        def finish(self):
            for step in range(1, planes):
                self.across(step).wait_send()

            @pl.when(section == self.layer)
            def _():
                self.home_local().wait()
                self.home_remote(1 - section).wait_recv()
                for turn in range(1, owners):
                    self.inside(turn).wait_recv()
                    self.inside(turn).wait_send()

            @pl.when(section != self.layer)
            def _():
                self.home_remote(section).wait_send()

    class SmallGather:
        def __init__(self, layer, block, target, index):
            self.layer, self.block, self.target, self.index = layer, block, target, index

        def local(self):
            return pltpu.make_async_copy(self.block, self.target.at[own, 0, section], r.q_local.at[self.index])

        def across(self, step, micro):
            device = partner if step == 0 else {"section": self.layer, "dp": planes_to(step)}
            return remote(
                self.block,
                self.target.at[own, (planes - step) % planes, micro],
                r.q_send.at[self.index, step],
                r.q_recv.at[self.index, step, micro],
                device,
            )

        def inside(self, turn):
            column = self.target.at[own]
            return remote(column, column, r.qp_send.at[self.index, turn], r.qp_recv.at[self.index, turn],
                          {"expert": owner_to(turn)})

        def start(self):
            for step in range(1, planes):
                self.across(step, section).start()

            @pl.when(section == self.layer)
            def _():
                self.local().start()

            @pl.when(section != self.layer)
            def _():
                self.across(0, section).start()

        def middle(self):
            @pl.when(section == self.layer)
            def _():
                self.local().wait()
                self.across(0, 1 - section).wait_recv()
                for step in range(1, planes):
                    for micro in range(2):
                        self.across(step, micro).wait_recv()
                for turn in range(1, owners):
                    self.inside(turn).start()

        def finish(self):
            for step in range(1, planes):
                self.across(step, section).wait_send()

            @pl.when(section == self.layer)
            def _():
                for turn in range(1, owners):
                    self.inside(turn).wait()

            @pl.when(section != self.layer)
            def _():
                self.across(0, section).wait_send()

    lane = lane_of((tokens, LANES))
    low_half = lane % HEAD_SIZE < HALF
    left = lane < HEAD_SIZE
    pair_lane = lane_of((2 * tokens, LANES))
    causal = lax.broadcasted_iota(jnp.int32, (2 * tokens, tokens), 0) % tokens >= lax.broadcasted_iota(
        jnp.int32, (2 * tokens, tokens), 1
    )
    root = HEAD_SIZE ** (-0.5)

    def stack(tile):
        nothing = jnp.zeros_like(tile)
        return jnp.concatenate([jnp.where(left, tile, nothing), jnp.where(left, nothing, tile)], axis=0)

    def attention_forward(layer, source, early, late):
        cosine, sine = r.cosine[...], r.sine[...]
        residual = source[...].astype(F32)
        normed_one = (residual * row_scale(residual) * r.gains[layer, 0:1]).astype(BF16)
        weights_wait(layer, 0)
        early()
        r.projected[...] = dot_nn(normed_one, r.win[layer])
        for tile in range(QUERY_WIDTH // LANES):
            columns = slice(tile * LANES, (tile + 1) * LANES)
            piece = r.projected[:, columns]
            r.query[layer, :, columns] = (piece * cosine + turned(piece, low_half) * sine).astype(BF16)
        for tile in range(KEY_WIDTH // LANES):
            first = slice(2 * tile * LANES, (2 * tile + 1) * LANES)
            second = slice((2 * tile + 1) * LANES, (2 * tile + 2) * LANES)
            piece = r.projected[:, QUERY_WIDTH + tile * LANES : QUERY_WIDTH + (tile + 1) * LANES]
            piece = piece * cosine + turned(piece, low_half) * sine
            other = pltpu.roll(piece, HEAD_SIZE, 1)
            r.key[layer, :, first] = jnp.where(left, piece, other).astype(BF16)
            r.key[layer, :, second] = jnp.where(left, other, piece).astype(BF16)
            start = QUERY_WIDTH + KEY_WIDTH + tile * LANES
            piece = r.projected[:, start : start + LANES]
            other = pltpu.roll(piece, HEAD_SIZE, 1)
            r.value[layer, :, first] = jnp.where(left, piece, other).astype(BF16)
            r.value[layer, :, second] = jnp.where(left, other, piece).astype(BF16)
        logs = jnp.zeros((2 * tokens, LANES), F32)
        for head in range(KEY_VALUE_HEADS):
            columns = slice(head * LANES, (head + 1) * LANES)
            scores = dot_nt(stack(r.query[layer, :, columns]), r.key[layer, :, columns]) * root
            scores = jnp.where(causal, scores, -1e30)
            top = jnp.max(scores, axis=-1, keepdims=True)
            log_total = top + jnp.log(jnp.sum(jnp.exp(scores - top), axis=-1, keepdims=True))
            logs = jnp.where(pair_lane == head, log_total, logs)
            weights = jnp.exp(scores - log_total).astype(BF16)
            mixed = dot_nn(weights, r.value[layer, :, columns])
            r.attended[layer, :, columns] = jnp.where(left, mixed[:tokens], mixed[tokens:]).astype(BF16)
        r.logs[layer] = logs
        late()
        weights_wait(layer, 1)
        middle = residual + dot_nn(r.attended[layer], r.wout[layer])
        r.middle[layer] = middle
        normed_two = (middle * row_scale(middle) * r.gains[layer, 1:2]).astype(BF16)
        r.packed[layer, :, :MODEL_WIDTH] = normed_two
        logits = dot_nn(normed_two, r.router[layer])
        chosen = r.hot[layer] > 0.0
        top = jnp.max(jnp.where(chosen, logits, -1e30), axis=-1, keepdims=True)
        grown = jnp.where(chosen, jnp.exp(jnp.where(chosen, logits - top, 0.0)), 0.0)
        gates = grown / jnp.sum(grown, axis=-1, keepdims=True)
        r.gates[layer] = gates
        r.packed[layer, :, MODEL_WIDTH:] = two_parts(gates)

    def attention_backward(layer, source, up, back, gate_grads):
        cosine, sine = r.cosine[...], r.sine[...]
        gates = r.gates[layer]
        grad_picked = gates * (gate_grads - jnp.sum(gates * gate_grads, axis=-1, keepdims=True))
        grad_logits = grad_picked.astype(BF16)
        r.grad_logits[layer] = grad_logits
        grad_second = back + dot_nt(grad_logits, r.router[layer])
        middle = r.middle[layer]
        scale_two = row_scale(middle)
        r.gain_grads[layer, 1:2] = jnp.sum(grad_second * middle * scale_two, axis=0, keepdims=True)
        grad_middle = up[...].astype(F32) + norm_back(grad_second * r.gains[layer, 1:2], middle, scale_two)
        low = grad_middle.astype(BF16)
        r.factors[layer, :, PROJECTED : PROJECTED + MODEL_WIDTH] = low
        r.grad_middle[...] = grad_middle
        r.grad_attended[...] = dot_nt(low, r.wout[layer]).astype(BF16)
        logs = r.logs[layer]
        held = []
        for head in range(KEY_VALUE_HEADS):
            columns = slice(head * LANES, (head + 1) * LANES)
            query = stack(r.query[layer, :, columns])
            key, value = r.key[layer, :, columns], r.value[layer, :, columns]
            scores = dot_nt(query, key) * root
            log_total = jnp.sum(jnp.where(pair_lane == head, logs, 0.0), axis=-1, keepdims=True)
            probabilities = jnp.where(causal, jnp.exp(jnp.where(causal, scores - log_total, 0.0)), 0.0)
            grad_tile = stack(r.grad_attended[:, columns])
            delta = jnp.sum(
                grad_tile.astype(F32) * stack(r.attended[layer, :, columns]).astype(F32), axis=-1, keepdims=True
            )
            grad_scores = (probabilities * (dot_nt(grad_tile, value) - delta)).astype(BF16)
            wide = dot_nn(grad_scores, key) * root
            grad_query = jnp.where(left, wide[:tokens], wide[tokens:])
            grad_query = grad_query * cosine - turned(grad_query, low_half) * sine
            r.factors[layer, :, columns] = grad_query.astype(BF16)
            key_grad = dot_tn(grad_scores, query) * root
            value_grad = dot_tn(probabilities.astype(BF16), grad_tile)
            key_grad = key_grad + pltpu.roll(key_grad, HEAD_SIZE, 1)
            value_grad = value_grad + pltpu.roll(value_grad, HEAD_SIZE, 1)
            if head % 2 == 0:
                held = [key_grad, value_grad]
            else:
                piece = jnp.where(left, held[0], key_grad)
                piece = piece * cosine - turned(piece, low_half) * sine
                start = QUERY_WIDTH + head // 2 * LANES
                r.factors[layer, :, start : start + LANES] = piece.astype(BF16)
                start += KEY_WIDTH
                r.factors[layer, :, start : start + LANES] = jnp.where(left, held[1], value_grad).astype(BF16)
        grad_first = dot_nt(r.factors[layer, :, :PROJECTED], r.win[layer])
        residual = source[...].astype(F32)
        scale_one = row_scale(residual)
        normed_one = (residual * scale_one * r.gains[layer, 0:1]).astype(BF16)
        r.factors[layer, :, PROJECTED + MODEL_WIDTH : PROJECTED + 2 * MODEL_WIDTH] = normed_one
        r.factors[layer, :, PROJECTED + 2 * MODEL_WIDTH :] = r.attended[layer]
        r.gain_grads[layer, 0:1] = jnp.sum(grad_first * residual * scale_one, axis=0, keepdims=True)
        return (
            r.grad_middle[...] + norm_back(grad_first * r.gains[layer, 0:1], residual, scale_one)
        ).astype(BF16)

    def place_local(source, target, index):
        return pltpu.make_async_copy(source, target.at[section], r.o_local.at[index])

    def place_remote(source, target, index, micro):
        return remote(source, target.at[micro], r.o_send.at[index], r.o_recv.at[index], partner)

    def place(layer, source, target, index):
        @pl.when(section == layer)
        def _():
            place_local(source, target, index).start()

        @pl.when(section != layer)
        def _():
            place_remote(source, target, index, section).start()

    def placed(layer, source, target, index):
        @pl.when(section == layer)
        def _():
            place_local(source, target, index).wait()
            place_remote(source, target, index, 1 - section).wait_recv()

        @pl.when(section != layer)
        def _():
            place_remote(source, target, index, section).wait_send()

    chunk = min(rows, 256)
    chunks = rows // chunk
    half = MODEL_WIDTH // 2

    def each_chunk(work):
        def one(number, carry):
            work(pl.ds(pl.multiple_of(number * chunk, chunk), chunk), pl.ds(number * (chunk // tokens), chunk // tokens))
            return carry

        if chunks == 1:
            work(pl.ds(0, chunk), pl.ds(0, owners))
        else:
            lax.fori_loop(0, chunks, one, 0)

    def flat(buffer, group, columns):
        values = buffer[group, :, columns]
        return values.reshape(chunk, values.shape[-1])

    model, packing = slice(0, MODEL_WIDTH), slice(MODEL_WIDTH, PACKED)

    def expert_columns(expert):
        return pl.ds(pl.multiple_of(expert * FF, FF), FF)

    def wait_in(expert):
        load_in(0, expert)[0].wait()

    def wait_out(expert):
        load_out(0, expert)[0].wait()

    def gate_of(plane_buffer, group, expert):
        return column_of(flat(plane_buffer, group, packing), lane_of((chunk, LANES)), own * local + expert)

    def backward_terms(expert, span, gate, gate_part, up_part, inner):
        sigmoid = 1.0 / (1.0 + jnp.exp(-gate_part))
        silu = gate_part * sigmoid
        activated = silu * up_part
        gate_grad = jnp.sum(activated * inner, axis=-1, keepdims=True)
        lanes = lane_of((chunk, LANES))
        r.gate_total[span] = jnp.where(lanes == own * local + expert, gate_grad, r.gate_total[span])
        grad_activated = inner * gate
        grad_gate = grad_activated * up_part * sigmoid * (1.0 + gate_part * (1.0 - sigmoid))
        grad_up = grad_activated * silu
        grad_pair = jnp.concatenate([grad_gate.astype(BF16), grad_up.astype(BF16)], axis=-1)
        term = dot_nt(grad_pair, r.ein[expert])

        @pl.when(expert == 0)
        def _():
            r.total[span] = term

        @pl.when(expert > 0)
        def _():
            r.total[span] += term

        return activated

    def mix(reduction):
        for cut in range(2):
            columns = slice(cut * half, (cut + 1) * half)

            def work(span, group):
                r.total[span, columns] = dot_nn(r.activated[span], r.eout[:, columns])

            each_chunk(work)
            for step in range(1, owners):
                reduction.put(
                    step, columns, r.total[pl.ds(owner_to(step) * tokens, tokens), columns].astype(BF16)
                )
            reduction.start(cut)

    def mixed(reduction, result):
        for step in range(1, owners):
            result = result + reduction.coming[step - 1].astype(F32)
        return result

    def send_back(reduction):
        for step in range(1, owners):
            span = pl.ds(owner_to(step) * tokens, tokens)
            reduction.put(step, slice(0, MODEL_WIDTH), r.total[span].astype(BF16))
            reduction.put(step, slice(MODEL_WIDTH, PACKED), two_parts(r.gate_total[span]))
        reduction.start(0)

    def came_back(reduction):
        back = r.kept_total[...]
        for step in range(1, owners):
            back = back + reduction.coming[step - 1, :, :MODEL_WIDTH].astype(F32)
        terms = reduction.coming[0, :, MODEL_WIDTH:].astype(F32)
        for step in range(2, owners):
            terms = terms + reduction.coming[step - 1, :, MODEL_WIDTH:].astype(F32)
        return back, r.kept_gate[...] + terms + pltpu.roll(terms, LANES - EXPERTS, 1)

    both_cuts = ((0, half), (half, half))
    spread_x0 = Spread(r.packed.at[0], r.plane0, 0)
    spread_x1 = Spread(r.packed.at[1], r.plane1, 1)
    spread_u1 = Spread(r.up, r.ups1, 2)
    spread_u0 = Spread(r.up0, r.ups0, 3)
    mix0 = Reduce(r.leave_y, r.come_y, 0, both_cuts)
    mix1 = Reduce(r.leave_y, r.come_y, 1, both_cuts)
    back1 = Reduce(r.leave_b, r.come_b, 2, ((0, PACKED),))
    back0 = Reduce(r.leave_b, r.come_b, 3, ((0, PACKED),))
    gather_x0 = Gather(0, r.packed.at[0], r.plane0, r.every_x, 0)
    gather_x1 = Gather(1, r.packed.at[1], r.plane1, r.every_x, 1)
    gather_u0 = Gather(0, r.up0, r.ups0, r.every_u, 2)
    gather_u1 = Gather(1, r.up, r.ups1, r.every_u, 3)
    small = [
        SmallGather(layer, source.at[layer], target, 2 * layer + which)
        for layer in range(2)
        for which, (source, target) in enumerate(
            ((r.grad_logits, r.every_logits), (r.gain_grads, r.every_gain))
        )
    ]

    weights_start(0, 0)
    weights_start(0, 1)
    for expert in range(local):
        for copy in swap_pair(expert):
            copy.start()

    @pl.when(section == 0)
    def _():
        for expert in range(local):
            load_in(0, expert)[0].start()
            load_out(0, expert)[0].start()

    r.gain_grads[...] = jnp.zeros_like(r.gain_grads)
    weights_spread(0, 0)
    weights_spread(0, 1)
    weights_push(0, 0)

    def early0():
        weights_start(1, 0)
        weights_start(1, 1)

    def late0():
        weights_push(0, 1)

    attention_forward(0, r.x, early0, late0)
    spread_x0.start()
    spread_u1.start()
    weights_spread(1, 0)
    weights_spread(1, 1)
    spread_x0.wait()
    gather_x0.start()
    gather_x0.start_home()

    def forward_expert(expert, carry):
        @pl.when(section != 0)
        def _():
            for which, make in enumerate((load_in, load_out)):
                swap_pair(expert)[which].wait_recv()
                make(0, expert)[1].start()

        wait_in(expert)

        def work(span, group):
            gate = gate_of(r.plane0, group, expert)
            pair = dot_nn(flat(r.plane0, group, model), r.ein[expert])
            r.pairs[expert, span] = pair.astype(BF16)
            gate_part, up_part = pair[:, :FF], pair[:, FF:]
            silu = gate_part / (1.0 + jnp.exp(-gate_part))
            r.activated[span, expert_columns(expert)] = (silu * up_part * gate).astype(BF16)

        each_chunk(work)
        start_load(load_in, 1, expert, 0, True)
        wait_out(expert)
        return carry

    lax.fori_loop(0, local, forward_expert, 0)
    mix(mix0)
    weights_push(1, 0)
    for expert in range(local):
        start_load(load_out, 1, expert, 1, True)
    gather_u1.start()
    spread_u1.wait()
    gather_u1.start_home()
    mix0.wait()
    r.hidden0[...] = (r.middle[0] + mixed(mix0, r.total[here])).astype(BF16)
    place(0, r.hidden0, r.hidden, 0)

    def late1():
        weights_push(1, 1)

    attention_forward(1, r.hidden0, lambda: None, late1)
    spread_x1.start()
    gather_x0.middle()

    def inner_expert(expert, carry):
        wait_out(expert)

        def work(span, group):
            r.inner[span, expert_columns(expert)] = dot_nt(
                flat(r.ups1, group, model), r.eout[expert_columns(expert)]
            ).astype(r.inner.dtype)

        each_chunk(work)
        return carry

    lax.fori_loop(0, local, inner_expert, 0)
    spread_x1.wait()
    gather_x1.start()
    gather_x1.start_home()
    r.gate_total[...] = jnp.zeros_like(r.gate_total)

    def both_expert(expert, carry):
        wait_in(expert)

        def work(span, group):
            gate = gate_of(r.plane1, group, expert)
            pair = dot_nn(flat(r.plane1, group, model), r.ein[expert])
            inner = r.inner[span, expert_columns(expert)].astype(F32)
            activated = backward_terms(expert, span, gate, pair[:, :FF], pair[:, FF:], inner)
            r.activated[span, expert_columns(expert)] = (activated * gate).astype(BF16)

        each_chunk(work)
        start_load(load_in, 0, expert, 0, False)
        return carry

    lax.fori_loop(0, local, both_expert, 0)
    send_back(back1)
    r.kept_total[...] = r.total[here]
    r.kept_gate[...] = r.gate_total[here]
    gather_u1.middle()
    mix(mix1)
    for expert in range(local):
        start_load(load_out, 0, expert, 1, False)
    back1.wait()
    back, gate_grads = came_back(back1)
    r.up0[...] = attention_backward(1, r.hidden0, r.up, back, gate_grads)
    spread_u0.start()
    place(1, r.up0, r.input_grad, 1)
    small[2].start()
    small[3].start()
    gather_x1.middle()
    mix1.wait()
    r.hidden1[...] = (r.middle[1] + mixed(mix1, r.total[here])).astype(BF16)
    place(1, r.hidden1, r.hidden, 2)
    r.gate_total[...] = jnp.zeros_like(r.gate_total)
    spread_u0.wait()
    gather_u0.start()
    gather_u0.start_home()
    small[2].middle()
    small[3].middle()

    def behind_expert(expert, carry):
        wait_in(expert)
        wait_out(expert)

        def work(span, group):
            gate = gate_of(r.plane0, group, expert)
            pair = r.pairs[expert, span].astype(F32)
            inner = dot_nt(flat(r.ups0, group, model), r.eout[expert_columns(expert)])
            backward_terms(expert, span, gate, pair[:, :FF], pair[:, FF:], inner)

        each_chunk(work)
        return carry

    lax.fori_loop(0, local, behind_expert, 0)
    send_back(back0)
    r.kept_total[...] = r.total[here]
    r.kept_gate[...] = r.gate_total[here]
    gather_u0.middle()
    back0.wait()
    back, gate_grads = came_back(back0)
    r.grad0[...] = attention_backward(0, r.x, r.up0, back, gate_grads)
    place(0, r.grad0, r.input_grad, 3)
    small[0].start()
    small[1].start()
    small[0].middle()
    small[1].middle()

    for layer in range(2):
        for which in range(2):
            weights_unsent(layer, which)
    for expert in range(local):
        for copy in swap_pair(expert):
            copy.wait_send()
    for copy in unsent:
        copy.wait_send()
    for gather in small:
        gather.finish()
    r.gain_sum[...] = jnp.sum(r.every_gain[...].reshape(-1, 8, MODEL_WIDTH), axis=0)
    placed(0, r.hidden0, r.hidden, 0)
    placed(1, r.up0, r.input_grad, 1)
    placed(1, r.hidden1, r.hidden, 2)
    placed(0, r.grad0, r.input_grad, 3)
    for gather in (gather_x0, gather_u1, gather_x1, gather_u0):
        gather.finish()


def both_layers(x, up, attn_in, attn_out, gains, routers, hot, cosine, sine, experts_in, experts_out):
    planes, owners = lax.axis_size("dp"), lax.axis_size("expert")
    tokens = x.shape[0]
    local = experts_in.shape[1]
    slab = attn_in.shape[1]
    rows = owners * tokens
    dma = lambda *shape: pltpu.SemaphoreType.DMA(shape)
    vmem = lambda shape, dtype: pltpu.VMEM(shape, dtype)
    wide = (2, tokens, MODEL_WIDTH)
    everywhere = (owners, planes, 2, tokens)
    inputs = {
        "x": (x, vmem_spec()),
        "up": (up, vmem_spec()),
        "attn_in": (attn_in, any_spec()),
        "attn_out": (attn_out, any_spec()),
        "gains": (gains, vmem_spec()),
        "router": (routers, vmem_spec()),
        "hot": (hot, vmem_spec()),
        "cosine": (cosine, vmem_spec()),
        "sine": (sine, vmem_spec()),
        "experts_in": (experts_in, any_spec()),
        "experts_out": (experts_out, any_spec()),
    }
    outputs = {
        "hidden": (wide, BF16, any_spec()),
        "input_grad": (wide, BF16, any_spec()),
        "other_in": (experts_in.shape[1:], BF16, any_spec()),
        "other_out": (experts_out.shape[1:], BF16, any_spec()),
        "every_x": (everywhere + (PACKED,), BF16, any_spec()),
        "every_u": (everywhere + (MODEL_WIDTH,), BF16, any_spec()),
        "every_logits": (everywhere + (LANES,), BF16, any_spec()),
        "factors": ((2, tokens, PROJECTED + 3 * MODEL_WIDTH), BF16, vmem_spec()),
        "gain_sum": ((8, MODEL_WIDTH), F32, vmem_spec()),
    }
    scratch = {
        "win": vmem((2, MODEL_WIDTH, PROJECTED), BF16),
        "wout": vmem((2, QUERY_WIDTH, MODEL_WIDTH), BF16),
        "ein": vmem((local, MODEL_WIDTH, 2 * FF), BF16),
        "eout": vmem((local * FF, MODEL_WIDTH), BF16),
        "projected": vmem((tokens, PROJECTED), F32),
        "query": vmem(wide, BF16),
        "key": vmem(wide, BF16),
        "value": vmem(wide, BF16),
        "attended": vmem(wide, BF16),
        "logs": vmem((2, 2 * tokens, LANES), F32),
        "middle": vmem(wide, F32),
        "packed": vmem((2, tokens, PACKED), BF16),
        "gates": vmem((2, tokens, LANES), F32),
        "grad_logits": vmem((2, tokens, LANES), BF16),
        "gain_grads": vmem((2, 8, MODEL_WIDTH), F32),
        "every_gain": vmem((owners, planes, 2, 8, MODEL_WIDTH), F32),
        "up0": vmem(wide[1:], BF16),
        "hidden0": vmem(wide[1:], BF16),
        "hidden1": vmem(wide[1:], BF16),
        "grad0": vmem(wide[1:], BF16),
        "grad_middle": vmem(wide[1:], F32),
        "grad_attended": vmem(wide[1:], BF16),
        "plane0": vmem((owners, tokens, PACKED), BF16),
        "plane1": vmem((owners, tokens, PACKED), BF16),
        "ups0": vmem((owners, tokens, MODEL_WIDTH), BF16),
        "ups1": vmem((owners, tokens, MODEL_WIDTH), BF16),
        "pairs": vmem((local, rows, 2 * FF), BF16),
        "inner": vmem((rows, local * FF), BF16),
        "activated": vmem((rows, local * FF), BF16),
        "total": vmem((rows, MODEL_WIDTH), F32),
        "gate_total": vmem((rows, LANES), F32),
        "kept_total": vmem((tokens, MODEL_WIDTH), F32),
        "kept_gate": vmem((tokens, LANES), F32),
        "leave_y": vmem((owners - 1, tokens, MODEL_WIDTH), BF16),
        "come_y": vmem((owners - 1, tokens, MODEL_WIDTH), BF16),
        "leave_b": vmem((owners - 1, tokens, PACKED), BF16),
        "come_b": vmem((owners - 1, tokens, PACKED), BF16),
        "w_local": dma(2, 2),
        "wz_send": dma(2, 2, planes),
        "wz_recv": dma(2, 2, planes),
        "wp_send": dma(2, 2, planes, owners),
        "wp_recv": dma(2, 2, planes, owners),
        "wc_send": dma(2, 2, planes),
        "wc_recv": dma(2, 2, planes),
        "s_send": dma(2, local),
        "s_recv": dma(2, local),
        "l_sem": dma(2, local),
        "a_send": dma(4, owners),
        "a_recv": dma(4, owners),
        "r_send": dma(4, 2, owners),
        "r_recv": dma(4, 2, owners),
        "g_send": dma(4, planes),
        "g_recv": dma(4, planes, 2),
        "g_local": dma(4),
        "gp_send": dma(4, owners),
        "gp_recv": dma(4, owners),
        "q_send": dma(4, planes),
        "q_recv": dma(4, planes, 2),
        "q_local": dma(4),
        "qp_send": dma(4, owners),
        "qp_recv": dma(4, owners),
        "o_send": dma(4),
        "o_recv": dma(4),
        "o_local": dma(4),
    }
    return call(
        functools.partial(layers_kernel, planes, owners, tokens, local, slab),
        "both_layers", 0, inputs, outputs, scratch,
    )


def weight_grad_kernel(
    x_ref, up_ref, gate_ref, win_ref, wout_ref, grad_in_ref, grad_out_ref, activated_ref
):
    expert, block = pl.program_id(0), pl.program_id(1)
    plane = lax.axis_index("dp")
    local = pl.num_programs(0)
    mine = lax.axis_index("expert") * local + expert
    slice_in, slice_out = grad_in_ref.shape[0], grad_out_ref.shape[0]
    lane = lane_of(gate_ref.shape)
    gate = column_of(gate_ref[...], lane, mine)
    pair = dot_nn(x_ref[...], win_ref[...])
    gate_part, up_part = pair[:, :FF], pair[:, FF:]
    sigmoid = 1.0 / (1.0 + jnp.exp(-gate_part))
    silu = gate_part * sigmoid
    activated_ref[...] = (silu * up_part * gate).astype(BF16)
    grad_activated = dot_nt(up_ref[...], wout_ref[...]) * gate
    grad_gate = grad_activated * up_part * sigmoid * (1.0 + gate_part * (1.0 - sigmoid))
    grad_up = grad_activated * silu
    grad_pair = jnp.concatenate([grad_gate.astype(BF16), grad_up.astype(BF16)], axis=-1)
    mine_in = x_ref[:, pl.ds(pl.multiple_of(plane * slice_in, LANES), slice_in)]
    mine_out = activated_ref[:, pl.ds(pl.multiple_of(plane * slice_out, LANES), slice_out)]
    term_in = dot_tn(mine_in, grad_pair)
    term_out = dot_tn(mine_out, up_ref[...])

    @pl.when(block == 0)
    def _():
        grad_in_ref[...] = term_in
        grad_out_ref[...] = term_out

    @pl.when(block > 0)
    def _():
        grad_in_ref[...] += term_in
        grad_out_ref[...] += term_out


def weight_grads(x, up, experts_in, experts_out):
    planes = lax.axis_size("dp")
    local = experts_in.shape[1]
    rows = x.shape[0]
    block = 512
    shape = jax.ShapeDtypeStruct
    return pl.pallas_call(
        weight_grad_kernel,
        grid=(local, rows // block),
        out_shape=(
            shape((local, MODEL_WIDTH // planes, 2 * FF), F32),
            shape((local, FF // planes, MODEL_WIDTH), F32),
        ),
        in_specs=[
            pl.BlockSpec((block, MODEL_WIDTH), lambda e, b: (b, 0)),
            pl.BlockSpec((block, MODEL_WIDTH), lambda e, b: (b, 0)),
            pl.BlockSpec((block, LANES), lambda e, b: (b, MODEL_WIDTH // LANES)),
            pl.BlockSpec((None, None, MODEL_WIDTH, 2 * FF), lambda e, b: (0, e, 0, 0)),
            pl.BlockSpec((None, None, FF, MODEL_WIDTH), lambda e, b: (0, e, 0, 0)),
        ],
        out_specs=(
            pl.BlockSpec((None, MODEL_WIDTH // planes, 2 * FF), lambda e, b: (e, 0, 0)),
            pl.BlockSpec((None, FF // planes, MODEL_WIDTH), lambda e, b: (e, 0, 0)),
        ),
        scratch_shapes=[pltpu.VMEM((block, FF), BF16)],
        compiler_params=pltpu.CompilerParams(vmem_limit_bytes=VMEM_LIMIT),
        name="weight_grads",
    )(x, up, x, experts_in, experts_out)


def rotated_blocks(block, axis):
    length = lax.axis_size(axis)
    blocks = [block]
    for step in range(1, length):
        blocks.append(lax.ppermute(block, axis, [(i, (i + step) % length) for i in range(length)]))
    return jnp.stack(blocks)


def shards(layer_input, cotangent, positions, routes, gain_one, attn_in, attn_out, gain_two, router,
           experts_in, experts_out):
    section = lax.axis_index("section")
    first = section == 0
    planes = lax.axis_size("dp")
    owners = lax.axis_size("expert")
    own = lax.axis_index("expert")
    tokens = layer_input.shape[1]

    def swap(values):
        return lax.ppermute(values, "section", [(0, 1), (1, 0)])

    def layered(mine, other):
        return jnp.stack([jnp.where(first, mine, other), jnp.where(first, other, mine)])

    def both(mine):
        return layered(mine, swap(mine))

    gains = both(jnp.concatenate([gain_one, gain_two], axis=0))
    routers = both(jnp.pad(router[0], ((0, 0), (0, LANES - EXPERTS))))

    pick = functools.partial(lax.dynamic_index_in_dim, axis=0, keepdims=False)
    x = pick(layer_input, section)
    up = pick(cotangent, section)
    place = pick(positions, section)
    choices = layered(pick(routes[0], section), swap(pick(routes[0], 1 - section)))
    hot = jnp.sum(
        (choices[..., None] == jnp.arange(LANES, dtype=jnp.int32)).astype(F32), axis=2
    )
    lane = jnp.arange(LANES)
    frequency = jnp.power(rotary_base, -((lane % HALF).astype(F32) * (2.0 / HEAD_SIZE)))
    angles = place.astype(F32)[:, None] * frequency[None, :]
    cosine = jnp.cos(angles)
    sine = jnp.where(lane % HEAD_SIZE < HALF, -1.0, 1.0) * jnp.sin(angles)

    done = both_layers(
        x, up, attn_in, attn_out, gains, routers, hot, cosine, sine, experts_in, experts_out
    )
    every_x = done["every_x"].reshape(-1, PACKED)
    every_u = done["every_u"].reshape(-1, MODEL_WIDTH)
    every_logits = done["every_logits"].reshape(-1, LANES)
    grad_experts_in, grad_experts_out = weight_grads(every_x, every_u, experts_in, experts_out)
    grad_router = dot_tn(every_x[:, :MODEL_WIDTH], every_logits)[:, :EXPERTS]

    factors = jnp.concatenate(
        [pick(done["factors"], section), swap(pick(done["factors"], 1 - section))], axis=0
    )
    around = rotated_blocks(factors, "expert").reshape(-1, factors.shape[1])
    part = MODEL_WIDTH // (planes * owners)

    def mine_of(values):
        blocks = values.reshape(-1, planes, owners, part)
        return lax.dynamic_index_in_dim(blocks, own, 2, keepdims=False).reshape(-1, planes * part)

    start = PROJECTED + MODEL_WIDTH
    grad_in = dot_tn(mine_of(around[:, start : start + MODEL_WIDTH]), around[:, :PROJECTED])
    grad_out = dot_tn(mine_of(around[:, start + MODEL_WIDTH :]), around[:, PROJECTED:start])
    partial = jnp.concatenate([grad_in, grad_out], axis=-1).reshape(planes, part, -1)
    plane = lax.axis_index("dp")
    total = pick(partial, plane)
    for step in range(1, planes):
        leaving = pick(partial, (plane + step) % planes).astype(BF16)
        pairs = [(i, (i + step) % planes) for i in range(planes)]
        total = total + lax.ppermute(leaving, "dp", pairs).astype(F32)
    grad_attn_in, grad_attn_out = total[:, :PROJECTED], total[:, PROJECTED:]

    return (
        done["hidden"][None],
        done["input_grad"][None],
        done["gain_sum"][0:1],
        grad_attn_in[None],
        grad_attn_out[None],
        done["gain_sum"][1:2],
        grad_router[None],
        grad_experts_in[None],
        grad_experts_out[None],
    )


def solution(mesh):
    in_specs = (
        P(None, ("dp", "expert"), None),
        P(None, ("dp", "expert"), None),
        P(None, ("dp", "expert")),
        P("section", None, ("dp", "expert"), None),
        P("section", None),
        P("section", "dp", None),
        P("section", "dp", None),
        P("section", None),
        P("section", None, None),
        P("section", "expert", None, None),
        P("section", "expert", None, None),
    )
    out_specs = (
        P("section", None, ("dp", "expert"), None),
        P("section", None, ("dp", "expert"), None),
        P("section", None),
        P("section", ("dp", "expert"), None),
        P("section", ("dp", "expert"), None),
        P("section", None),
        P("section", None, None),
        P("section", "expert", "dp", None),
        P("section", "expert", "dp", None),
    )
    return jax.shard_map(shards, mesh=mesh, in_specs=in_specs, out_specs=out_specs, check_vma=False)
```

```python
import functools

import jax
import jax.numpy as jnp
from jax import lax
from jax.experimental import pallas as pl
from jax.experimental.pallas import tpu as pltpu
from jax.sharding import PartitionSpec as P

MODEL_WIDTH = 1024
QUERY_HEADS = 16
KEY_VALUE_HEADS = 8
HEAD_SIZE = 64
FF = 512
EXPERTS = 32
TOPK = 8

QUERY_WIDTH = QUERY_HEADS * HEAD_SIZE
KEY_WIDTH = KEY_VALUE_HEADS * HEAD_SIZE
PROJECTED = QUERY_WIDTH + 2 * KEY_WIDTH
LANES = 128
HALF = HEAD_SIZE // 2
PACKED = MODEL_WIDTH + LANES

epsilon = 1e-06
rotary_base = 10000.0

F32 = jnp.float32
BF16 = jnp.bfloat16
MESH = pl.DeviceIdType.MESH
VMEM_LIMIT = 62 * 1024 * 1024


def dot_nn(a, b):
    return lax.dot_general(a, b, (((1,), (0,)), ((), ())), preferred_element_type=F32)


def dot_nt(a, b):
    return lax.dot_general(a, b, (((1,), (1,)), ((), ())), preferred_element_type=F32)


def dot_tn(a, b):
    return lax.dot_general(a, b, (((0,), (0,)), ((), ())), preferred_element_type=F32)


def row_scale(values):
    return lax.rsqrt(jnp.mean(values * values, axis=-1, keepdims=True) + epsilon)


def norm_back(grad_normed, inputs, scale):
    return scale * grad_normed - inputs * (scale * scale * scale) * jnp.mean(
        grad_normed * inputs, axis=-1, keepdims=True
    )


def lane_of(shape):
    return lax.broadcasted_iota(jnp.int32, shape, 1)


def turned(tile, low):
    return jnp.where(low, pltpu.roll(tile, LANES - HALF, 1), pltpu.roll(tile, HALF, 1))


def two_parts(values):
    high = values.astype(BF16).astype(F32)
    return (high + pltpu.roll(values - high, EXPERTS, 1)).astype(BF16)


def column_of(parts, lane, column):
    wide = parts.astype(F32)
    return jnp.sum(jnp.where((lane == column) | (lane == column + EXPERTS), wide, 0.0), axis=-1, keepdims=True)


def remote(source, target, send, recv, device):
    return pltpu.make_async_remote_copy(
        src_ref=source, dst_ref=target, send_sem=send, recv_sem=recv, device_id=device, device_id_type=MESH
    )


def vmem_spec():
    return pl.BlockSpec(memory_space=pltpu.VMEM)


def any_spec():
    return pl.BlockSpec(memory_space=pl.ANY)


class Names:
    pass


def call(kernel, name, number, inputs, outputs, scratch):
    labels = list(inputs) + list(outputs) + list(scratch)

    def body(*refs):
        names = Names()
        for label, ref in zip(labels, refs):
            setattr(names, label, ref)
        kernel(names)

    results = pl.pallas_call(
        body,
        out_shape=tuple(jax.ShapeDtypeStruct(shape, dtype) for shape, dtype, _ in outputs.values()),
        in_specs=[spec for _, spec in inputs.values()],
        out_specs=tuple(spec for _, _, spec in outputs.values()),
        scratch_shapes=list(scratch.values()),
        compiler_params=pltpu.CompilerParams(
            collective_id=number, has_side_effects=True, vmem_limit_bytes=VMEM_LIMIT
        ),
        name=name,
    )(*[array for array, _ in inputs.values()])
    return dict(zip(outputs, results))


def layers_kernel(planes, owners, tokens, local, slab, r):
    section = lax.axis_index("section")
    plane = lax.axis_index("dp")
    own = lax.axis_index("expert")
    rows = owners * tokens
    part = slab // owners
    here = pl.ds(own * tokens, tokens)
    partner = {"section": 1 - section}

    def planes_to(step):
        return (plane + step) % planes

    def owner_to(step):
        return (own + step) % owners

    barrier = pltpu.get_barrier_semaphore()
    for step in range(1, owners):
        pl.semaphore_signal(barrier, inc=1, device_id={"expert": owner_to(step)}, device_id_type=MESH)
    for step in range(1, planes):
        for target in range(2):
            pl.semaphore_signal(
                barrier, inc=1, device_id={"section": target, "dp": planes_to(step)}, device_id_type=MESH
            )
    pl.semaphore_signal(barrier, inc=1, device_id=partner, device_id_type=MESH)
    pl.semaphore_wait(barrier, owners - 1 + 2 * (planes - 1) + 1)

    unsent = []

    weight_pairs = ((r.attn_in, r.win), (r.attn_out, r.wout))

    def slab_local(layer, which):
        source, full = weight_pairs[which]
        return pltpu.make_async_copy(
            source.at[0], full.at[layer, pl.ds(plane * slab, slab)], r.w_local.at[layer, which]
        )

    def slab_z(layer, which, step):
        source, full = weight_pairs[which]
        return remote(
            source.at[0, pl.ds(own * part, part)],
            full.at[layer, pl.ds(plane * slab + own * part, part)],
            r.wz_send.at[layer, which, step],
            r.wz_recv.at[layer, which, step],
            {"dp": planes_to(step)},
        )

    def slab_plane(layer, which, step, turn):
        full = weight_pairs[which][1]
        origin = planes_to(planes - step)
        block = full.at[layer, pl.ds(origin * slab + own * part, part)]
        return remote(
            block,
            block,
            r.wp_send.at[layer, which, step, turn],
            r.wp_recv.at[layer, which, step, turn],
            {"expert": owner_to(turn)},
        )

    def slab_core(layer, which, step):
        full = weight_pairs[which][1]
        block = full.at[layer, pl.ds(planes_to(planes - step) * slab, slab)]
        return remote(block, block, r.wc_send.at[layer, which, step], r.wc_recv.at[layer, which, step], partner)

    def weights_start(layer, which):
        @pl.when(section == layer)
        def _():
            for step in range(1, planes):
                slab_z(layer, which, step).start()
            slab_local(layer, which).start()

    def weights_spread(layer, which):
        @pl.when(section == layer)
        def _():
            slab_local(layer, which).wait()
            slab_core(layer, which, 0).start()
            for step in range(1, planes):
                slab_z(layer, which, step).wait_recv()
                for turn in range(1, owners):
                    slab_plane(layer, which, step, turn).start()

    def weights_push(layer, which):
        @pl.when(section == layer)
        def _():
            for step in range(1, planes):
                for turn in range(1, owners):
                    slab_plane(layer, which, step, turn).wait_recv()
                slab_core(layer, which, step).start()

    def weights_wait(layer, which):
        @pl.when(section != layer)
        def _():
            for step in range(planes):
                slab_core(layer, which, step).wait_recv()

    def weights_unsent(layer, which):
        @pl.when(section == layer)
        def _():
            for step in range(1, planes):
                slab_z(layer, which, step).wait_send()
                for turn in range(1, owners):
                    slab_plane(layer, which, step, turn).wait_send()
            for step in range(planes):
                slab_core(layer, which, step).wait_send()

    def swap_pair(expert):
        return (
            remote(r.experts_in.at[0, expert], r.other_in.at[expert], r.s_send.at[0, expert], r.s_recv.at[0, expert], partner),
            remote(r.experts_out.at[0, expert], r.other_out.at[expert], r.s_send.at[1, expert], r.s_recv.at[1, expert], partner),
        )

    def load_in(layer, expert):
        mine = pltpu.make_async_copy(r.experts_in.at[0, expert], r.ein.at[expert], r.l_sem.at[0, expert])
        other = pltpu.make_async_copy(r.other_in.at[expert], r.ein.at[expert], r.l_sem.at[0, expert])
        return mine, other

    def load_out(layer, expert):
        target = r.eout.at[pl.ds(expert * FF, FF)]
        mine = pltpu.make_async_copy(r.experts_out.at[0, expert], target, r.l_sem.at[1, expert])
        other = pltpu.make_async_copy(r.other_out.at[expert], target, r.l_sem.at[1, expert])
        return mine, other

    def start_load(make, layer, expert, which, first_use):
        @pl.when(section == layer)
        def _():
            make(layer, expert)[0].start()

        @pl.when(section != layer)
        def _():
            if first_use:
                swap_pair(expert)[which].wait_recv()
            make(layer, expert)[1].start()

    class Spread:
        def __init__(self, source, buffer, index):
            self.copies = [
                remote(source, buffer.at[own], r.a_send.at[index, step], r.a_recv.at[index, step],
                       {"expert": owner_to(step)})
                for step in range(1, owners)
            ]
            self.source, self.buffer = source, buffer

        def start(self):
            for copy in self.copies:
                copy.start()
            self.buffer[own] = self.source[...]

        def wait(self):
            for copy in self.copies:
                copy.wait_recv()
            unsent.extend(self.copies)

    class Reduce:
        def __init__(self, leaving, coming, index, cuts):
            self.leaving, self.coming, self.index, self.cuts = leaving, coming, index, cuts
            self.copies = {
                (cut, step): remote(
                    leaving.at[step - 1, :, pl.ds(*cuts[cut])],
                    coming.at[step - 1, :, pl.ds(*cuts[cut])],
                    r.r_send.at[index, cut, step],
                    r.r_recv.at[index, cut, step],
                    {"expert": owner_to(step)},
                )
                for cut in range(len(cuts))
                for step in range(1, owners)
            }

        def put(self, step, columns, values):
            self.leaving[step - 1, :, columns] = values

        def start(self, cut):
            for step in range(1, owners):
                self.copies[cut, step].start()

        def wait(self):
            for copy in self.copies.values():
                copy.wait()

    class Gather:
        def __init__(self, layer, block, around, target, index):
            self.layer, self.block, self.around, self.target, self.index = layer, block, around, target, index

        def across(self, step):
            return [
                remote(
                    self.block,
                    self.target.at[own, (planes - step) % planes, section],
                    r.g_send.at[self.index, step],
                    r.g_recv.at[self.index, step, section],
                    {"section": self.layer, "dp": planes_to(step)},
                )
            ][0]

        def arrival(self, step, micro):
            return remote(
                self.block,
                self.target.at[own, (planes - step) % planes, micro],
                r.g_send.at[self.index, step],
                r.g_recv.at[self.index, step, micro],
                {"section": self.layer, "dp": planes_to(step)},
            )

        def home_local(self):
            return pltpu.make_async_copy(self.around, self.target.at[:, 0, section], r.g_local.at[self.index])

        def home_remote(self, micro):
            return remote(self.around, self.target.at[:, 0, micro], r.g_send.at[self.index, 0],
                          r.g_recv.at[self.index, 0, 0], partner)

        def inside(self, turn):
            column = self.target.at[own, pl.ds(1, planes - 1)]
            return remote(column, column, r.gp_send.at[self.index, turn], r.gp_recv.at[self.index, turn],
                          {"expert": owner_to(turn)})

        def start(self):
            for step in range(1, planes):
                self.across(step).start()

        def start_home(self):
            @pl.when(section == self.layer)
            def _():
                self.home_local().start()

            @pl.when(section != self.layer)
            def _():
                self.home_remote(section).start()

        def middle(self):
            @pl.when(section == self.layer)
            def _():
                for step in range(1, planes):
                    for micro in range(2):
                        self.arrival(step, micro).wait_recv()
                for turn in range(1, owners):
                    self.inside(turn).start()

        def finish(self):
            for step in range(1, planes):
                self.across(step).wait_send()

            @pl.when(section == self.layer)
            def _():
                self.home_local().wait()
                self.home_remote(1 - section).wait_recv()
                for turn in range(1, owners):
                    self.inside(turn).wait_recv()
                    self.inside(turn).wait_send()

            @pl.when(section != self.layer)
            def _():
                self.home_remote(section).wait_send()

    class SmallGather:
        def __init__(self, layer, block, target, index):
            self.layer, self.block, self.target, self.index = layer, block, target, index

        def local(self):
            return pltpu.make_async_copy(self.block, self.target.at[own, 0, section], r.q_local.at[self.index])

        def across(self, step, micro):
            device = partner if step == 0 else {"section": self.layer, "dp": planes_to(step)}
            return remote(
                self.block,
                self.target.at[own, (planes - step) % planes, micro],
                r.q_send.at[self.index, step],
                r.q_recv.at[self.index, step, micro],
                device,
            )

        def inside(self, turn):
            column = self.target.at[own]
            return remote(column, column, r.qp_send.at[self.index, turn], r.qp_recv.at[self.index, turn],
                          {"expert": owner_to(turn)})

        def start(self):
            for step in range(1, planes):
                self.across(step, section).start()

            @pl.when(section == self.layer)
            def _():
                self.local().start()

            @pl.when(section != self.layer)
            def _():
                self.across(0, section).start()

        def middle(self):
            @pl.when(section == self.layer)
            def _():
                self.local().wait()
                self.across(0, 1 - section).wait_recv()
                for step in range(1, planes):
                    for micro in range(2):
                        self.across(step, micro).wait_recv()
                for turn in range(1, owners):
                    self.inside(turn).start()

        def finish(self):
            for step in range(1, planes):
                self.across(step, section).wait_send()

            @pl.when(section == self.layer)
            def _():
                for turn in range(1, owners):
                    self.inside(turn).wait()

            @pl.when(section != self.layer)
            def _():
                self.across(0, section).wait_send()

    lane = lane_of((tokens, LANES))
    low_half = lane % HEAD_SIZE < HALF
    left = lane < HEAD_SIZE
    pair_lane = lane_of((2 * tokens, LANES))
    causal = lax.broadcasted_iota(jnp.int32, (2 * tokens, tokens), 0) % tokens >= lax.broadcasted_iota(
        jnp.int32, (2 * tokens, tokens), 1
    )
    root = HEAD_SIZE ** (-0.5)

    def stack(tile):
        nothing = jnp.zeros_like(tile)
        return jnp.concatenate([jnp.where(left, tile, nothing), jnp.where(left, nothing, tile)], axis=0)

    def attention_forward(layer, source, early, late):
        cosine, sine = r.cosine[...], r.sine[...]
        residual = source[...].astype(F32)
        normed_one = (residual * row_scale(residual) * r.gains[layer, 0:1]).astype(BF16)
        weights_wait(layer, 0)
        early()
        r.projected[...] = dot_nn(normed_one, r.win[layer])
        for tile in range(QUERY_WIDTH // LANES):
            columns = slice(tile * LANES, (tile + 1) * LANES)
            piece = r.projected[:, columns]
            r.query[layer, :, columns] = (piece * cosine + turned(piece, low_half) * sine).astype(BF16)
        for tile in range(KEY_WIDTH // LANES):
            first = slice(2 * tile * LANES, (2 * tile + 1) * LANES)
            second = slice((2 * tile + 1) * LANES, (2 * tile + 2) * LANES)
            piece = r.projected[:, QUERY_WIDTH + tile * LANES : QUERY_WIDTH + (tile + 1) * LANES]
            piece = piece * cosine + turned(piece, low_half) * sine
            other = pltpu.roll(piece, HEAD_SIZE, 1)
            r.key[layer, :, first] = jnp.where(left, piece, other).astype(BF16)
            r.key[layer, :, second] = jnp.where(left, other, piece).astype(BF16)
            start = QUERY_WIDTH + KEY_WIDTH + tile * LANES
            piece = r.projected[:, start : start + LANES]
            other = pltpu.roll(piece, HEAD_SIZE, 1)
            r.value[layer, :, first] = jnp.where(left, piece, other).astype(BF16)
            r.value[layer, :, second] = jnp.where(left, other, piece).astype(BF16)
        logs = jnp.zeros((2 * tokens, LANES), F32)
        for head in range(KEY_VALUE_HEADS):
            columns = slice(head * LANES, (head + 1) * LANES)
            scores = dot_nt(stack(r.query[layer, :, columns]), r.key[layer, :, columns]) * root
            scores = jnp.where(causal, scores, -1e30)
            top = jnp.max(scores, axis=-1, keepdims=True)
            log_total = top + jnp.log(jnp.sum(jnp.exp(scores - top), axis=-1, keepdims=True))
            logs = jnp.where(pair_lane == head, log_total, logs)
            weights = jnp.exp(scores - log_total).astype(BF16)
            mixed = dot_nn(weights, r.value[layer, :, columns])
            r.attended[layer, :, columns] = jnp.where(left, mixed[:tokens], mixed[tokens:]).astype(BF16)
        r.logs[layer] = logs
        late()
        weights_wait(layer, 1)
        middle = residual + dot_nn(r.attended[layer], r.wout[layer])
        r.middle[layer] = middle
        normed_two = (middle * row_scale(middle) * r.gains[layer, 1:2]).astype(BF16)
        r.packed[layer, :, :MODEL_WIDTH] = normed_two
        logits = dot_nn(normed_two, r.router[layer])
        chosen = r.hot[layer] > 0.0
        top = jnp.max(jnp.where(chosen, logits, -1e30), axis=-1, keepdims=True)
        grown = jnp.where(chosen, jnp.exp(jnp.where(chosen, logits - top, 0.0)), 0.0)
        gates = grown / jnp.sum(grown, axis=-1, keepdims=True)
        r.gates[layer] = gates
        r.packed[layer, :, MODEL_WIDTH:] = two_parts(gates)

    def attention_backward(layer, source, up, back, gate_grads):
        cosine, sine = r.cosine[...], r.sine[...]
        gates = r.gates[layer]
        grad_picked = gates * (gate_grads - jnp.sum(gates * gate_grads, axis=-1, keepdims=True))
        grad_logits = grad_picked.astype(BF16)
        r.grad_logits[layer] = grad_logits
        grad_second = back + dot_nt(grad_logits, r.router[layer])
        middle = r.middle[layer]
        scale_two = row_scale(middle)
        r.gain_grads[layer, 1:2] = jnp.sum(grad_second * middle * scale_two, axis=0, keepdims=True)
        grad_middle = up[...].astype(F32) + norm_back(grad_second * r.gains[layer, 1:2], middle, scale_two)
        low = grad_middle.astype(BF16)
        r.factors[layer, :, PROJECTED : PROJECTED + MODEL_WIDTH] = low
        r.grad_middle[...] = grad_middle
        r.grad_attended[...] = dot_nt(low, r.wout[layer]).astype(BF16)
        logs = r.logs[layer]
        held = []
        for head in range(KEY_VALUE_HEADS):
            columns = slice(head * LANES, (head + 1) * LANES)
            query = stack(r.query[layer, :, columns])
            key, value = r.key[layer, :, columns], r.value[layer, :, columns]
            scores = dot_nt(query, key) * root
            log_total = jnp.sum(jnp.where(pair_lane == head, logs, 0.0), axis=-1, keepdims=True)
            probabilities = jnp.where(causal, jnp.exp(jnp.where(causal, scores - log_total, 0.0)), 0.0)
            grad_tile = stack(r.grad_attended[:, columns])
            delta = jnp.sum(
                grad_tile.astype(F32) * stack(r.attended[layer, :, columns]).astype(F32), axis=-1, keepdims=True
            )
            grad_scores = (probabilities * (dot_nt(grad_tile, value) - delta)).astype(BF16)
            wide = dot_nn(grad_scores, key) * root
            grad_query = jnp.where(left, wide[:tokens], wide[tokens:])
            grad_query = grad_query * cosine - turned(grad_query, low_half) * sine
            r.factors[layer, :, columns] = grad_query.astype(BF16)
            key_grad = dot_tn(grad_scores, query) * root
            value_grad = dot_tn(probabilities.astype(BF16), grad_tile)
            key_grad = key_grad + pltpu.roll(key_grad, HEAD_SIZE, 1)
            value_grad = value_grad + pltpu.roll(value_grad, HEAD_SIZE, 1)
            if head % 2 == 0:
                held = [key_grad, value_grad]
            else:
                piece = jnp.where(left, held[0], key_grad)
                piece = piece * cosine - turned(piece, low_half) * sine
                start = QUERY_WIDTH + head // 2 * LANES
                r.factors[layer, :, start : start + LANES] = piece.astype(BF16)
                start += KEY_WIDTH
                r.factors[layer, :, start : start + LANES] = jnp.where(left, held[1], value_grad).astype(BF16)
        grad_first = dot_nt(r.factors[layer, :, :PROJECTED], r.win[layer])
        residual = source[...].astype(F32)
        scale_one = row_scale(residual)
        normed_one = (residual * scale_one * r.gains[layer, 0:1]).astype(BF16)
        r.factors[layer, :, PROJECTED + MODEL_WIDTH : PROJECTED + 2 * MODEL_WIDTH] = normed_one
        r.factors[layer, :, PROJECTED + 2 * MODEL_WIDTH :] = r.attended[layer]
        r.gain_grads[layer, 0:1] = jnp.sum(grad_first * residual * scale_one, axis=0, keepdims=True)
        return (
            r.grad_middle[...] + norm_back(grad_first * r.gains[layer, 0:1], residual, scale_one)
        ).astype(BF16)

    def place_local(source, target, index):
        return pltpu.make_async_copy(source, target.at[section], r.o_local.at[index])

    def place_remote(source, target, index, micro):
        return remote(source, target.at[micro], r.o_send.at[index], r.o_recv.at[index], partner)

    def place(layer, source, target, index):
        @pl.when(section == layer)
        def _():
            place_local(source, target, index).start()

        @pl.when(section != layer)
        def _():
            place_remote(source, target, index, section).start()

    def placed(layer, source, target, index):
        @pl.when(section == layer)
        def _():
            place_local(source, target, index).wait()
            place_remote(source, target, index, 1 - section).wait_recv()

        @pl.when(section != layer)
        def _():
            place_remote(source, target, index, section).wait_send()

    chunk = min(rows, 256)
    chunks = rows // chunk
    half = MODEL_WIDTH // 2

    def each_chunk(work):
        def one(number, carry):
            work(pl.ds(pl.multiple_of(number * chunk, chunk), chunk), pl.ds(number * (chunk // tokens), chunk // tokens))
            return carry

        if chunks == 1:
            work(pl.ds(0, chunk), pl.ds(0, owners))
        else:
            lax.fori_loop(0, chunks, one, 0)

    def flat(buffer, group, columns):
        values = buffer[group, :, columns]
        return values.reshape(chunk, values.shape[-1])

    model, packing = slice(0, MODEL_WIDTH), slice(MODEL_WIDTH, PACKED)

    def expert_columns(expert):
        return pl.ds(pl.multiple_of(expert * FF, FF), FF)

    def wait_in(expert):
        load_in(0, expert)[0].wait()

    def wait_out(expert):
        load_out(0, expert)[0].wait()

    def gate_of(plane_buffer, group, expert):
        return column_of(flat(plane_buffer, group, packing), lane_of((chunk, LANES)), own * local + expert)

    def backward_terms(expert, span, gate, gate_part, up_part, inner):
        sigmoid = 1.0 / (1.0 + jnp.exp(-gate_part))
        silu = gate_part * sigmoid
        activated = silu * up_part
        gate_grad = jnp.sum(activated * inner, axis=-1, keepdims=True)
        lanes = lane_of((chunk, LANES))
        r.gate_total[span] = jnp.where(lanes == own * local + expert, gate_grad, r.gate_total[span])
        grad_activated = inner * gate
        grad_gate = grad_activated * up_part * sigmoid * (1.0 + gate_part * (1.0 - sigmoid))
        grad_up = grad_activated * silu
        grad_pair = jnp.concatenate([grad_gate.astype(BF16), grad_up.astype(BF16)], axis=-1)
        term = dot_nt(grad_pair, r.ein[expert])

        @pl.when(expert == 0)
        def _():
            r.total[span] = term

        @pl.when(expert > 0)
        def _():
            r.total[span] += term

        return activated

    def mix(reduction):
        for cut in range(2):
            columns = slice(cut * half, (cut + 1) * half)

            def work(span, group):
                r.total[span, columns] = dot_nn(r.activated[span], r.eout[:, columns])

            each_chunk(work)
            for step in range(1, owners):
                reduction.put(
                    step, columns, r.total[pl.ds(owner_to(step) * tokens, tokens), columns].astype(BF16)
                )
            reduction.start(cut)

    def mixed(reduction, result):
        for step in range(1, owners):
            result = result + reduction.coming[step - 1].astype(F32)
        return result

    def send_back(reduction):
        for step in range(1, owners):
            span = pl.ds(owner_to(step) * tokens, tokens)
            reduction.put(step, slice(0, MODEL_WIDTH), r.total[span].astype(BF16))
            reduction.put(step, slice(MODEL_WIDTH, PACKED), two_parts(r.gate_total[span]))
        reduction.start(0)

    def came_back(reduction):
        back = r.kept_total[...]
        for step in range(1, owners):
            back = back + reduction.coming[step - 1, :, :MODEL_WIDTH].astype(F32)
        terms = reduction.coming[0, :, MODEL_WIDTH:].astype(F32)
        for step in range(2, owners):
            terms = terms + reduction.coming[step - 1, :, MODEL_WIDTH:].astype(F32)
        return back, r.kept_gate[...] + terms + pltpu.roll(terms, LANES - EXPERTS, 1)

    both_cuts = ((0, half), (half, half))
    spread_x0 = Spread(r.packed.at[0], r.plane0, 0)
    spread_x1 = Spread(r.packed.at[1], r.plane1, 1)
    spread_u1 = Spread(r.up, r.ups1, 2)
    spread_u0 = Spread(r.up0, r.ups0, 3)
    mix0 = Reduce(r.leave_y, r.come_y, 0, both_cuts)
    mix1 = Reduce(r.leave_y, r.come_y, 1, both_cuts)
    back1 = Reduce(r.leave_b, r.come_b, 2, ((0, PACKED),))
    back0 = Reduce(r.leave_b, r.come_b, 3, ((0, PACKED),))
    gather_x0 = Gather(0, r.packed.at[0], r.plane0, r.every_x, 0)
    gather_x1 = Gather(1, r.packed.at[1], r.plane1, r.every_x, 1)
    gather_u0 = Gather(0, r.up0, r.ups0, r.every_u, 2)
    gather_u1 = Gather(1, r.up, r.ups1, r.every_u, 3)
    small = [
        SmallGather(layer, source.at[layer], target, 2 * layer + which)
        for layer in range(2)
        for which, (source, target) in enumerate(
            ((r.grad_logits, r.every_logits), (r.gain_grads, r.every_gain))
        )
    ]

    weights_start(0, 0)
    weights_start(0, 1)
    for expert in range(local):
        for copy in swap_pair(expert):
            copy.start()

    @pl.when(section == 0)
    def _():
        for expert in range(local):
            load_in(0, expert)[0].start()
            load_out(0, expert)[0].start()

    r.gain_grads[...] = jnp.zeros_like(r.gain_grads)
    weights_spread(0, 0)
    weights_spread(0, 1)
    weights_push(0, 0)

    def early0():
        weights_start(1, 0)
        weights_start(1, 1)

    def late0():
        weights_push(0, 1)

    attention_forward(0, r.x, early0, late0)
    spread_x0.start()
    spread_u1.start()
    weights_spread(1, 0)
    weights_spread(1, 1)
    spread_x0.wait()
    gather_x0.start()
    gather_x0.start_home()

    def forward_expert(expert, carry):
        @pl.when(section != 0)
        def _():
            for which, make in enumerate((load_in, load_out)):
                swap_pair(expert)[which].wait_recv()
                make(0, expert)[1].start()

        wait_in(expert)

        def work(span, group):
            gate = gate_of(r.plane0, group, expert)
            pair = dot_nn(flat(r.plane0, group, model), r.ein[expert])
            r.pairs[expert, span] = pair.astype(BF16)
            gate_part, up_part = pair[:, :FF], pair[:, FF:]
            silu = gate_part / (1.0 + jnp.exp(-gate_part))
            r.activated[span, expert_columns(expert)] = (silu * up_part * gate).astype(BF16)

        each_chunk(work)
        start_load(load_in, 1, expert, 0, True)
        wait_out(expert)
        return carry

    lax.fori_loop(0, local, forward_expert, 0)
    mix(mix0)
    weights_push(1, 0)
    for expert in range(local):
        start_load(load_out, 1, expert, 1, True)
    gather_u1.start()
    spread_u1.wait()
    gather_u1.start_home()
    mix0.wait()
    r.hidden0[...] = (r.middle[0] + mixed(mix0, r.total[here])).astype(BF16)
    place(0, r.hidden0, r.hidden, 0)

    def late1():
        weights_push(1, 1)

    attention_forward(1, r.hidden0, lambda: None, late1)
    spread_x1.start()
    gather_x0.middle()

    def inner_expert(expert, carry):
        wait_out(expert)

        def work(span, group):
            r.inner[span, expert_columns(expert)] = dot_nt(
                flat(r.ups1, group, model), r.eout[expert_columns(expert)]
            ).astype(r.inner.dtype)

        each_chunk(work)
        return carry

    lax.fori_loop(0, local, inner_expert, 0)
    spread_x1.wait()
    gather_x1.start()
    gather_x1.start_home()
    r.gate_total[...] = jnp.zeros_like(r.gate_total)

    def both_expert(expert, carry):
        wait_in(expert)

        def work(span, group):
            gate = gate_of(r.plane1, group, expert)
            pair = dot_nn(flat(r.plane1, group, model), r.ein[expert])
            inner = r.inner[span, expert_columns(expert)].astype(F32)
            activated = backward_terms(expert, span, gate, pair[:, :FF], pair[:, FF:], inner)
            r.activated[span, expert_columns(expert)] = (activated * gate).astype(BF16)

        each_chunk(work)
        start_load(load_in, 0, expert, 0, False)
        return carry

    lax.fori_loop(0, local, both_expert, 0)
    send_back(back1)
    r.kept_total[...] = r.total[here]
    r.kept_gate[...] = r.gate_total[here]
    gather_u1.middle()
    mix(mix1)
    for expert in range(local):
        start_load(load_out, 0, expert, 1, False)
    back1.wait()
    back, gate_grads = came_back(back1)
    r.up0[...] = attention_backward(1, r.hidden0, r.up, back, gate_grads)
    spread_u0.start()
    place(1, r.up0, r.input_grad, 1)
    small[2].start()
    small[3].start()
    gather_x1.middle()
    mix1.wait()
    r.hidden1[...] = (r.middle[1] + mixed(mix1, r.total[here])).astype(BF16)
    place(1, r.hidden1, r.hidden, 2)
    r.gate_total[...] = jnp.zeros_like(r.gate_total)
    spread_u0.wait()
    gather_u0.start()
    gather_u0.start_home()
    small[2].middle()
    small[3].middle()

    def behind_expert(expert, carry):
        wait_in(expert)
        wait_out(expert)

        def work(span, group):
            gate = gate_of(r.plane0, group, expert)
            pair = r.pairs[expert, span].astype(F32)
            inner = dot_nt(flat(r.ups0, group, model), r.eout[expert_columns(expert)])
            backward_terms(expert, span, gate, pair[:, :FF], pair[:, FF:], inner)

        each_chunk(work)
        return carry

    lax.fori_loop(0, local, behind_expert, 0)
    send_back(back0)
    r.kept_total[...] = r.total[here]
    r.kept_gate[...] = r.gate_total[here]
    gather_u0.middle()
    back0.wait()
    back, gate_grads = came_back(back0)
    r.grad0[...] = attention_backward(0, r.x, r.up0, back, gate_grads)
    place(0, r.grad0, r.input_grad, 3)
    small[0].start()
    small[1].start()
    small[0].middle()
    small[1].middle()

    for layer in range(2):
        for which in range(2):
            weights_unsent(layer, which)
    for expert in range(local):
        for copy in swap_pair(expert):
            copy.wait_send()
    for copy in unsent:
        copy.wait_send()
    for gather in small:
        gather.finish()
    r.gain_sum[...] = jnp.sum(r.every_gain[...].reshape(-1, 8, MODEL_WIDTH), axis=0)
    placed(0, r.hidden0, r.hidden, 0)
    placed(1, r.up0, r.input_grad, 1)
    placed(1, r.hidden1, r.hidden, 2)
    placed(0, r.grad0, r.input_grad, 3)
    for gather in (gather_x0, gather_u1, gather_x1, gather_u0):
        gather.finish()


def both_layers(x, up, attn_in, attn_out, gains, routers, hot, cosine, sine, experts_in, experts_out):
    planes, owners = lax.axis_size("dp"), lax.axis_size("expert")
    tokens = x.shape[0]
    local = experts_in.shape[1]
    slab = attn_in.shape[1]
    rows = owners * tokens
    dma = lambda *shape: pltpu.SemaphoreType.DMA(shape)
    vmem = lambda shape, dtype: pltpu.VMEM(shape, dtype)
    wide = (2, tokens, MODEL_WIDTH)
    everywhere = (owners, planes, 2, tokens)
    inputs = {
        "x": (x, vmem_spec()),
        "up": (up, vmem_spec()),
        "attn_in": (attn_in, any_spec()),
        "attn_out": (attn_out, any_spec()),
        "gains": (gains, vmem_spec()),
        "router": (routers, vmem_spec()),
        "hot": (hot, vmem_spec()),
        "cosine": (cosine, vmem_spec()),
        "sine": (sine, vmem_spec()),
        "experts_in": (experts_in, any_spec()),
        "experts_out": (experts_out, any_spec()),
    }
    outputs = {
        "hidden": (wide, BF16, any_spec()),
        "input_grad": (wide, BF16, any_spec()),
        "other_in": (experts_in.shape[1:], BF16, any_spec()),
        "other_out": (experts_out.shape[1:], BF16, any_spec()),
        "every_x": (everywhere + (PACKED,), BF16, any_spec()),
        "every_u": (everywhere + (MODEL_WIDTH,), BF16, any_spec()),
        "every_logits": (everywhere + (LANES,), BF16, any_spec()),
        "factors": ((2, tokens, PROJECTED + 3 * MODEL_WIDTH), BF16, vmem_spec()),
        "gain_sum": ((8, MODEL_WIDTH), F32, vmem_spec()),
    }
    scratch = {
        "win": vmem((2, MODEL_WIDTH, PROJECTED), BF16),
        "wout": vmem((2, QUERY_WIDTH, MODEL_WIDTH), BF16),
        "ein": vmem((local, MODEL_WIDTH, 2 * FF), BF16),
        "eout": vmem((local * FF, MODEL_WIDTH), BF16),
        "projected": vmem((tokens, PROJECTED), F32),
        "query": vmem(wide, BF16),
        "key": vmem(wide, BF16),
        "value": vmem(wide, BF16),
        "attended": vmem(wide, BF16),
        "logs": vmem((2, 2 * tokens, LANES), F32),
        "middle": vmem(wide, F32),
        "packed": vmem((2, tokens, PACKED), BF16),
        "gates": vmem((2, tokens, LANES), F32),
        "grad_logits": vmem((2, tokens, LANES), BF16),
        "gain_grads": vmem((2, 8, MODEL_WIDTH), F32),
        "every_gain": vmem((owners, planes, 2, 8, MODEL_WIDTH), F32),
        "up0": vmem(wide[1:], BF16),
        "hidden0": vmem(wide[1:], BF16),
        "hidden1": vmem(wide[1:], BF16),
        "grad0": vmem(wide[1:], BF16),
        "grad_middle": vmem(wide[1:], F32),
        "grad_attended": vmem(wide[1:], BF16),
        "plane0": vmem((owners, tokens, PACKED), BF16),
        "plane1": vmem((owners, tokens, PACKED), BF16),
        "ups0": vmem((owners, tokens, MODEL_WIDTH), BF16),
        "ups1": vmem((owners, tokens, MODEL_WIDTH), BF16),
        "pairs": vmem((local, rows, 2 * FF), BF16),
        "inner": vmem((rows, local * FF), BF16),
        "activated": vmem((rows, local * FF), BF16),
        "total": vmem((rows, MODEL_WIDTH), F32),
        "gate_total": vmem((rows, LANES), F32),
        "kept_total": vmem((tokens, MODEL_WIDTH), F32),
        "kept_gate": vmem((tokens, LANES), F32),
        "leave_y": vmem((owners - 1, tokens, MODEL_WIDTH), BF16),
        "come_y": vmem((owners - 1, tokens, MODEL_WIDTH), BF16),
        "leave_b": vmem((owners - 1, tokens, PACKED), BF16),
        "come_b": vmem((owners - 1, tokens, PACKED), BF16),
        "w_local": dma(2, 2),
        "wz_send": dma(2, 2, planes),
        "wz_recv": dma(2, 2, planes),
        "wp_send": dma(2, 2, planes, owners),
        "wp_recv": dma(2, 2, planes, owners),
        "wc_send": dma(2, 2, planes),
        "wc_recv": dma(2, 2, planes),
        "s_send": dma(2, local),
        "s_recv": dma(2, local),
        "l_sem": dma(2, local),
        "a_send": dma(4, owners),
        "a_recv": dma(4, owners),
        "r_send": dma(4, 2, owners),
        "r_recv": dma(4, 2, owners),
        "g_send": dma(4, planes),
        "g_recv": dma(4, planes, 2),
        "g_local": dma(4),
        "gp_send": dma(4, owners),
        "gp_recv": dma(4, owners),
        "q_send": dma(4, planes),
        "q_recv": dma(4, planes, 2),
        "q_local": dma(4),
        "qp_send": dma(4, owners),
        "qp_recv": dma(4, owners),
        "o_send": dma(4),
        "o_recv": dma(4),
        "o_local": dma(4),
    }
    return call(
        functools.partial(layers_kernel, planes, owners, tokens, local, slab),
        "both_layers", 0, inputs, outputs, scratch,
    )


def weight_grad_kernel(start, local, x_ref, up_ref, gate_ref, win_ref, wout_ref, *refs):
    grad_in_ref, grad_out_ref, activated_ref = refs[-3:]
    expert, block = start + pl.program_id(0), pl.program_id(1)
    plane = lax.axis_index("dp")
    mine = lax.axis_index("expert") * local + expert
    slice_in, slice_out = grad_in_ref.shape[0], grad_out_ref.shape[0]
    lane = lane_of(gate_ref.shape)
    gate = column_of(gate_ref[...], lane, mine)
    pair = dot_nn(x_ref[...], win_ref[...])
    gate_part, up_part = pair[:, :FF], pair[:, FF:]
    sigmoid = 1.0 / (1.0 + jnp.exp(-gate_part))
    silu = gate_part * sigmoid
    activated_ref[...] = (silu * up_part * gate).astype(BF16)
    grad_activated = dot_nt(up_ref[...], wout_ref[...]) * gate
    grad_gate = grad_activated * up_part * sigmoid * (1.0 + gate_part * (1.0 - sigmoid))
    grad_up = grad_activated * silu
    grad_pair = jnp.concatenate([grad_gate.astype(BF16), grad_up.astype(BF16)], axis=-1)
    mine_in = x_ref[:, pl.ds(pl.multiple_of(plane * slice_in, LANES), slice_in)]
    mine_out = activated_ref[:, pl.ds(pl.multiple_of(plane * slice_out, LANES), slice_out)]
    term_in = dot_tn(mine_in, grad_pair)
    term_out = dot_tn(mine_out, up_ref[...])

    @pl.when(block == 0)
    def _():
        grad_in_ref[...] = term_in
        grad_out_ref[...] = term_out

    @pl.when(block > 0)
    def _():
        grad_in_ref[...] += term_in
        grad_out_ref[...] += term_out


def weight_grads(x, up, experts_in, experts_out, start, count, before):
    planes = lax.axis_size("dp")
    local = experts_in.shape[1]
    rows = x.shape[0]
    block = 512
    shape = jax.ShapeDtypeStruct
    slice_in, slice_out = MODEL_WIDTH // planes, FF // planes
    multiplies = rows * count * (3 * MODEL_WIDTH * FF + 2 * FF * slice_in + MODEL_WIDTH * slice_out)
    return pl.pallas_call(
        functools.partial(weight_grad_kernel, start, local),
        grid=(count, rows // block),
        out_shape=(shape((local, slice_in, 2 * FF), F32), shape((local, slice_out, MODEL_WIDTH), F32)),
        in_specs=[
            pl.BlockSpec((block, MODEL_WIDTH), lambda e, b: (b, 0)),
            pl.BlockSpec((block, MODEL_WIDTH), lambda e, b: (b, 0)),
            pl.BlockSpec((block, LANES), lambda e, b: (b, MODEL_WIDTH // LANES)),
            pl.BlockSpec((None, None, MODEL_WIDTH, 2 * FF), lambda e, b: (0, start + e, 0, 0)),
            pl.BlockSpec((None, None, FF, MODEL_WIDTH), lambda e, b: (0, start + e, 0, 0)),
        ] + [any_spec()] * len(before),
        out_specs=(
            pl.BlockSpec((None, slice_in, 2 * FF), lambda e, b: (start + e, 0, 0)),
            pl.BlockSpec((None, slice_out, MODEL_WIDTH), lambda e, b: (start + e, 0, 0)),
        ),
        scratch_shapes=[pltpu.VMEM((block, FF), BF16)],
        input_output_aliases={5 + i: i for i in range(len(before))},
        compiler_params=pltpu.CompilerParams(vmem_limit_bytes=VMEM_LIMIT),
        cost_estimate=pl.CostEstimate(
            flops=3 * multiplies, bytes_accessed=count * rows * 4 * MODEL_WIDTH, transcendentals=0
        ),
        name="weight_grads",
    )(x, up, x, experts_in, experts_out, *before)


def shards(layer_input, cotangent, positions, routes, gain_one, attn_in, attn_out, gain_two, router,
           experts_in, experts_out):
    section = lax.axis_index("section")
    first = section == 0
    planes = lax.axis_size("dp")
    owners = lax.axis_size("expert")
    own = lax.axis_index("expert")
    tokens = layer_input.shape[1]

    def swap(values):
        return lax.ppermute(values, "section", [(0, 1), (1, 0)])

    def layered(mine, other):
        return jnp.stack([jnp.where(first, mine, other), jnp.where(first, other, mine)])

    def both(mine):
        return layered(mine, swap(mine))

    gains = both(jnp.concatenate([gain_one, gain_two], axis=0))
    routers = both(jnp.pad(router[0], ((0, 0), (0, LANES - EXPERTS))))

    pick = functools.partial(lax.dynamic_index_in_dim, axis=0, keepdims=False)
    x = pick(layer_input, section)
    up = pick(cotangent, section)
    place = pick(positions, section)
    choices = layered(pick(routes[0], section), swap(pick(routes[0], 1 - section)))
    hot = jnp.sum(
        (choices[..., None] == jnp.arange(LANES, dtype=jnp.int32)).astype(F32), axis=2
    )
    lane = jnp.arange(LANES)
    frequency = jnp.power(rotary_base, -((lane % HALF).astype(F32) * (2.0 / HEAD_SIZE)))
    angles = place.astype(F32)[:, None] * frequency[None, :]
    cosine = jnp.cos(angles)
    sine = jnp.where(lane % HEAD_SIZE < HALF, -1.0, 1.0) * jnp.sin(angles)

    done = both_layers(
        x, up, attn_in, attn_out, gains, routers, hot, cosine, sine, experts_in, experts_out
    )
    every_x = done["every_x"].reshape(-1, PACKED)
    every_u = done["every_u"].reshape(-1, MODEL_WIDTH)
    every_logits = done["every_logits"].reshape(-1, LANES)

    factors = jnp.concatenate(
        [pick(done["factors"], section), swap(pick(done["factors"], 1 - section))], axis=0
    )
    blocks = [factors]
    for step in range(1, owners):
        pairs = [(i, (i + step) % owners) for i in range(owners)]
        blocks.append(lax.ppermute(factors, "expert", pairs))
    local = experts_in.shape[1]
    early = weight_grads(every_x, every_u, experts_in, experts_out, 0, local // 2, ())
    blocks, early = lax.optimization_barrier((blocks, early))
    around = jnp.concatenate(blocks, axis=0)
    part = MODEL_WIDTH // (planes * owners)

    def mine_of(values):
        blocks = values.reshape(-1, planes, owners, part)
        return lax.dynamic_index_in_dim(blocks, own, 2, keepdims=False).reshape(-1, planes * part)

    start = PROJECTED + MODEL_WIDTH
    grad_in = dot_tn(mine_of(around[:, start : start + MODEL_WIDTH]), around[:, :PROJECTED])
    grad_out = dot_tn(mine_of(around[:, start + MODEL_WIDTH :]), around[:, PROJECTED:start])
    partial = jnp.concatenate([grad_in, grad_out], axis=-1).reshape(planes, part, -1)
    plane = lax.axis_index("dp")
    total = pick(partial, plane)
    leaving = [pick(partial, (plane + step) % planes).astype(BF16) for step in range(1, planes)]
    early, leaving = lax.optimization_barrier((early, leaving))
    arriving = []
    for step in range(1, planes):
        pairs = [(i, (i + step) % planes) for i in range(planes)]
        arriving.append(lax.ppermute(leaving[step - 1], "dp", pairs))
    grad_experts_in, grad_experts_out = weight_grads(
        every_x, every_u, experts_in, experts_out, local // 2, local - local // 2, early
    )
    grad_router = dot_tn(every_x[:, :MODEL_WIDTH], every_logits)[:, :EXPERTS]
    arriving, grad_experts_in, grad_experts_out, grad_router = lax.optimization_barrier(
        (arriving, grad_experts_in, grad_experts_out, grad_router)
    )
    for piece in arriving:
        total = total + piece.astype(F32)
    grad_attn_in, grad_attn_out = total[:, :PROJECTED], total[:, PROJECTED:]

    return (
        done["hidden"][None],
        done["input_grad"][None],
        done["gain_sum"][0:1],
        grad_attn_in[None],
        grad_attn_out[None],
        done["gain_sum"][1:2],
        grad_router[None],
        grad_experts_in[None],
        grad_experts_out[None],
    )


def solution(mesh):
    in_specs = (
        P(None, ("dp", "expert"), None),
        P(None, ("dp", "expert"), None),
        P(None, ("dp", "expert")),
        P("section", None, ("dp", "expert"), None),
        P("section", None),
        P("section", "dp", None),
        P("section", "dp", None),
        P("section", None),
        P("section", None, None),
        P("section", "expert", None, None),
        P("section", "expert", None, None),
    )
    out_specs = (
        P("section", None, ("dp", "expert"), None),
        P("section", None, ("dp", "expert"), None),
        P("section", None),
        P("section", ("dp", "expert"), None),
        P("section", ("dp", "expert"), None),
        P("section", None),
        P("section", None, None),
        P("section", "expert", "dp", None),
        P("section", "expert", "dp", None),
    )
    return jax.shard_map(shards, mesh=mesh, in_specs=in_specs, out_specs=out_specs, check_vma=False)
```

```python
import functools

import jax
import jax.numpy as jnp
from jax import lax
from jax.experimental import pallas as pl
from jax.experimental.pallas import tpu as pltpu
from jax.sharding import PartitionSpec as P

MODEL_WIDTH = 1024
QUERY_HEADS = 16
KEY_VALUE_HEADS = 8
HEAD_SIZE = 64
FF = 512
EXPERTS = 32
TOPK = 8

QUERY_WIDTH = QUERY_HEADS * HEAD_SIZE
KEY_WIDTH = KEY_VALUE_HEADS * HEAD_SIZE
PROJECTED = QUERY_WIDTH + 2 * KEY_WIDTH
LANES = 128
HALF = HEAD_SIZE // 2
PACKED = MODEL_WIDTH + LANES

epsilon = 1e-06
rotary_base = 10000.0

F32 = jnp.float32
BF16 = jnp.bfloat16
MESH = pl.DeviceIdType.MESH
VMEM_LIMIT = 62 * 1024 * 1024


def dot_nn(a, b):
    return lax.dot_general(a, b, (((1,), (0,)), ((), ())), preferred_element_type=F32)


def dot_nt(a, b):
    return lax.dot_general(a, b, (((1,), (1,)), ((), ())), preferred_element_type=F32)


def dot_tn(a, b):
    return lax.dot_general(a, b, (((0,), (0,)), ((), ())), preferred_element_type=F32)


def row_scale(values):
    return lax.rsqrt(jnp.mean(values * values, axis=-1, keepdims=True) + epsilon)


def norm_back(grad_normed, inputs, scale):
    return scale * grad_normed - inputs * (scale * scale * scale) * jnp.mean(
        grad_normed * inputs, axis=-1, keepdims=True
    )


def lane_of(shape):
    return lax.broadcasted_iota(jnp.int32, shape, 1)


def turned(tile, low):
    return jnp.where(low, pltpu.roll(tile, LANES - HALF, 1), pltpu.roll(tile, HALF, 1))


def two_parts(values):
    high = values.astype(BF16).astype(F32)
    return (high + pltpu.roll(values - high, EXPERTS, 1)).astype(BF16)


def column_of(parts, lane, column):
    wide = parts.astype(F32)
    return jnp.sum(jnp.where((lane == column) | (lane == column + EXPERTS), wide, 0.0), axis=-1, keepdims=True)


def remote(source, target, send, recv, device):
    return pltpu.make_async_remote_copy(
        src_ref=source, dst_ref=target, send_sem=send, recv_sem=recv, device_id=device, device_id_type=MESH
    )


def vmem_spec():
    return pl.BlockSpec(memory_space=pltpu.VMEM)


def any_spec():
    return pl.BlockSpec(memory_space=pl.ANY)


class Names:
    pass


def call(kernel, name, number, inputs, outputs, scratch, cost=None):
    labels = list(inputs) + list(outputs) + list(scratch)

    def body(*refs):
        names = Names()
        for label, ref in zip(labels, refs):
            setattr(names, label, ref)
        kernel(names)

    if number is None:
        params = pltpu.CompilerParams(vmem_limit_bytes=VMEM_LIMIT)
    else:
        params = pltpu.CompilerParams(
            collective_id=number, has_side_effects=True, vmem_limit_bytes=VMEM_LIMIT
        )
    results = pl.pallas_call(
        body,
        out_shape=tuple(jax.ShapeDtypeStruct(shape, dtype) for shape, dtype, _ in outputs.values()),
        in_specs=[spec for _, spec in inputs.values()],
        out_specs=tuple(spec for _, _, spec in outputs.values()),
        scratch_shapes=list(scratch.values()),
        compiler_params=params,
        cost_estimate=cost,
        name=name,
    )(*[array for array, _ in inputs.values()])
    names = Names()
    for label, result in zip(outputs, results):
        setattr(names, label, result)
    return names


class PlaneBroadcast:
    def __init__(self, owners, own, piece, send, recv):
        self.owners, self.own = owners, own
        self.square = owners == 4
        self.piece, self.send, self.recv = piece, send, recv

    def hop(self, owner, half, index, device):
        block = self.piece(owner, half)
        return remote(block, block, self.send.at[index], self.recv.at[index], dict(expert=device))

    def hops(self):
        owners, own = self.owners, self.own

        def owner_to(step):
            return (own + step) % owners

        if not self.square:
            return [self.hop(own, None, turn, owner_to(turn)) for turn in range(1, owners)]
        beside = own + 1 - 2 * (own % 2)
        above = owner_to(2)
        return [
            self.hop(own, None, 0, beside),
            self.hop(own, None, 1, above),
            self.hop(beside, 0, 2, above),
            self.hop(above, 1, 3, beside),
        ]

    def start(self):
        hops = self.hops()
        for hop in hops[:2] if self.square else hops:
            hop.start()

    def forward(self):
        if self.square:
            hops = self.hops()
            for hop in range(2):
                hops[hop].wait_recv()
                hops[2 + hop].start()

    def wait(self):
        hops = self.hops()
        for hop in hops[2:] if self.square else hops:
            hop.wait_recv()

    def sent(self):
        for hop in self.hops():
            hop.wait_send()


def layers_kernel(planes, owners, tokens, local, slab, r):
    section = lax.axis_index("section")
    plane = lax.axis_index("dp")
    own = lax.axis_index("expert")
    rows = owners * tokens
    part = slab // owners
    here = pl.ds(own * tokens, tokens)
    partner = dict(section=1 - section)

    def planes_to(step):
        return (plane + step) % planes

    def owner_to(step):
        return (own + step) % owners

    barrier = pltpu.get_barrier_semaphore()
    for step in range(1, owners):
        pl.semaphore_signal(barrier, inc=1, device_id=dict(expert=owner_to(step)), device_id_type=MESH)
    for step in range(1, planes):
        for target in range(2):
            pl.semaphore_signal(
                barrier, inc=1, device_id=dict(section=target, dp=planes_to(step)), device_id_type=MESH
            )
    pl.semaphore_signal(barrier, inc=1, device_id=partner, device_id_type=MESH)
    pl.semaphore_wait(barrier, owners - 1 + 2 * (planes - 1) + 1)

    unsent = []

    own_rows = [
        pltpu.make_async_copy(r.layer_input.at[section], r.x, r.i_sem.at[0]),
        pltpu.make_async_copy(r.cotangent.at[section], r.up, r.i_sem.at[1]),
    ]
    for copy in own_rows:
        copy.start()

    def hot_of(choices):
        lanes = lane_of((tokens, LANES))
        found = jnp.zeros((tokens, LANES), F32)
        for choice in range(TOPK):
            found = jnp.where(lanes == choices[:, choice : choice + 1], 1.0, found)
        return found

    r.gains[section, 0:1] = r.gain_one[...]
    r.gains[section, 1:2] = r.gain_two[...]
    r.router[section] = r.router_in[0]
    r.hot[section] = hot_of(r.routes[0, section])
    r.hot_out[...] = hot_of(r.routes[0, 1 - section])
    shared = [
        remote(source, target, r.h_send.at[index], r.h_recv.at[index], partner)
        for index, (source, target) in enumerate(
            (
                (r.gains.at[section], r.gains.at[section]),
                (r.router.at[section], r.router.at[section]),
                (r.hot_out, r.hot.at[section]),
            )
        )
    ]
    for copy in shared:
        copy.start()

    def Broadcast(piece, send, recv):
        return PlaneBroadcast(owners, own, piece, send, recv)

    weight_pieces = ((r.attn_in, r.win, 0), (r.attn_in, r.win, QUERY_WIDTH), (r.attn_out, r.wout, 0))
    pieces = range(len(weight_pieces))

    def slab_local(layer, which):
        source, full, column = weight_pieces[which]
        columns = pl.ds(column, MODEL_WIDTH)
        return pltpu.make_async_copy(
            source.at[0, :, columns], full.at[layer, pl.ds(plane * slab, slab), columns], r.w_local.at[layer, which]
        )

    def slab_z(layer, which, step):
        source, full, column = weight_pieces[which]
        columns = pl.ds(column, MODEL_WIDTH)
        return remote(
            source.at[0, pl.ds(own * part, part), columns],
            full.at[layer, pl.ds(plane * slab + own * part, part), columns],
            r.wz_send.at[layer, which, step],
            r.wz_recv.at[layer, which, step],
            dict(dp=planes_to(step)),
        )

    def slab_plane(layer, which, step):
        full, column = weight_pieces[which][1:]
        origin = planes_to(planes - step)

        def piece(owner, half):
            start, length = origin * slab + owner * part, part
            if half is not None:
                length = part // 2
                start = start + half * length
            return full.at[layer, pl.ds(start, length), pl.ds(column, MODEL_WIDTH)]

        return Broadcast(piece, r.wp_send.at[layer, which, step], r.wp_recv.at[layer, which, step])

    def slab_core(layer, which, step):
        full, column = weight_pieces[which][1:]
        block = full.at[layer, pl.ds(planes_to(planes - step) * slab, slab), pl.ds(column, MODEL_WIDTH)]
        return remote(block, block, r.wc_send.at[layer, which, step], r.wc_recv.at[layer, which, step], partner)

    def weights_start(layer, which):
        @pl.when(section == layer)
        def _():
            for step in range(1, planes):
                slab_z(layer, which, step).start()
            slab_local(layer, which).start()

    def weights_spread(layer, which):
        @pl.when(section == layer)
        def _():
            slab_local(layer, which).wait()
            slab_core(layer, which, 0).start()
            for step in range(1, planes):
                slab_z(layer, which, step).wait_recv()
                slab_plane(layer, which, step).start()

    def weights_forward(layer, which):
        @pl.when(section == layer)
        def _():
            for step in range(1, planes):
                slab_plane(layer, which, step).forward()

    def weights_push(layer, which):
        @pl.when(section == layer)
        def _():
            for step in range(1, planes):
                slab_plane(layer, which, step).wait()
                slab_core(layer, which, step).start()

    def weights_wait(layer, which):
        @pl.when(section != layer)
        def _():
            for step in range(planes):
                slab_core(layer, which, step).wait_recv()

    def weights_unsent(layer, which):
        @pl.when(section == layer)
        def _():
            for step in range(1, planes):
                slab_z(layer, which, step).wait_send()
                slab_plane(layer, which, step).sent()
            for step in range(planes):
                slab_core(layer, which, step).wait_send()

    def swap_pair(expert):
        return (
            remote(r.experts_in.at[0, expert], r.other_in.at[expert], r.s_send.at[0, expert], r.s_recv.at[0, expert], partner),
            remote(r.experts_out.at[0, expert], r.other_out.at[expert], r.s_send.at[1, expert], r.s_recv.at[1, expert], partner),
        )

    def load_in(layer, expert):
        mine = pltpu.make_async_copy(r.experts_in.at[0, expert], r.ein.at[expert], r.l_sem.at[0, expert])
        other = pltpu.make_async_copy(r.other_in.at[expert], r.ein.at[expert], r.l_sem.at[0, expert])
        return mine, other

    def load_out(layer, expert):
        target = r.eout.at[pl.ds(expert * FF, FF)]
        mine = pltpu.make_async_copy(r.experts_out.at[0, expert], target, r.l_sem.at[1, expert])
        other = pltpu.make_async_copy(r.other_out.at[expert], target, r.l_sem.at[1, expert])
        return mine, other

    def start_load(make, layer, expert, which, first_use):
        @pl.when(section == layer)
        def _():
            make(layer, expert)[0].start()

        @pl.when(section != layer)
        def _():
            if first_use:
                swap_pair(expert)[which].wait_recv()
            make(layer, expert)[1].start()

    class Spread:
        def __init__(self, source, buffer, index):
            self.copies = [
                remote(source, buffer.at[own], r.a_send.at[index, step], r.a_recv.at[index, step],
                       dict(expert=owner_to(step)))
                for step in range(1, owners)
            ]
            self.source, self.buffer = source, buffer

        def start(self):
            for copy in self.copies:
                copy.start()
            self.buffer[own] = self.source[...]

        def wait(self):
            for copy in self.copies:
                copy.wait_recv()
            unsent.extend(self.copies)

    class Reduce:
        def __init__(self, leaving, coming, index, cuts):
            self.leaving, self.coming, self.index, self.cuts = leaving, coming, index, cuts
            self.copies = {
                (cut, step): remote(
                    leaving.at[step - 1, :, pl.ds(*cuts[cut])],
                    coming.at[step - 1, :, pl.ds(*cuts[cut])],
                    r.r_send.at[index, cut, step],
                    r.r_recv.at[index, cut, step],
                    dict(expert=owner_to(step)),
                )
                for cut in range(len(cuts))
                for step in range(1, owners)
            }

        def put(self, step, columns, values):
            self.leaving[step - 1, :, columns] = values

        def start(self, cut):
            for step in range(1, owners):
                self.copies[cut, step].start()

        def wait(self):
            for copy in self.copies.values():
                copy.wait()

    class Gather:
        def __init__(self, layer, block, around, target, index):
            self.layer, self.block, self.around, self.target, self.index = layer, block, around, target, index

        def across(self, step):
            return [
                remote(
                    self.block,
                    self.target.at[own, (planes - step) % planes, section],
                    r.g_send.at[self.index, step],
                    r.g_recv.at[self.index, step, section],
                    dict(section=self.layer, dp=planes_to(step)),
                )
            ][0]

        def arrival(self, step, micro):
            return remote(
                self.block,
                self.target.at[own, (planes - step) % planes, micro],
                r.g_send.at[self.index, step],
                r.g_recv.at[self.index, step, micro],
                dict(section=self.layer, dp=planes_to(step)),
            )

        def home_local(self):
            return pltpu.make_async_copy(self.around, self.target.at[:, 0, section], r.g_local.at[self.index])

        def home_remote(self, micro):
            return remote(self.around, self.target.at[:, 0, micro], r.g_send.at[self.index, 0],
                          r.g_recv.at[self.index, 0, 0], partner)

        def inside(self):
            def piece(owner, half):
                if half is None:
                    return self.target.at[owner, pl.ds(1, planes - 1)]
                return self.target.at[owner, pl.ds(1, planes - 1), half]

            return Broadcast(piece, r.gp_send.at[self.index], r.gp_recv.at[self.index])

        def whole_to(self, step, micro):
            return remote(
                self.around,
                self.target.at[:, (planes - step) % planes, micro],
                r.g_send.at[self.index, step],
                r.g_recv.at[self.index, step, micro],
                dict(section=self.layer, dp=planes_to(step)),
            )

        def start_whole(self):
            for step in range(1, planes):
                self.whole_to(step, section).start()

        def finish_whole(self):
            for step in range(1, planes):
                self.whole_to(step, section).wait_send()

            @pl.when(section == self.layer)
            def _():
                for step in range(1, planes):
                    for micro in range(2):
                        self.whole_to(step, micro).wait_recv()

            self.finish_home()

        def start(self):
            for step in range(1, planes):
                self.across(step).start()

        def start_home(self):
            @pl.when(section == self.layer)
            def _():
                self.home_local().start()

            @pl.when(section != self.layer)
            def _():
                self.home_remote(section).start()

        def middle(self):
            @pl.when(section == self.layer)
            def _():
                for step in range(1, planes):
                    for micro in range(2):
                        self.arrival(step, micro).wait_recv()
                self.inside().start()

        def forward(self):
            @pl.when(section == self.layer)
            def _():
                self.inside().forward()

        def finish(self):
            for step in range(1, planes):
                self.across(step).wait_send()

            @pl.when(section == self.layer)
            def _():
                self.inside().wait()
                self.inside().sent()

            self.finish_home()

        def finish_home(self):
            @pl.when(section == self.layer)
            def _():
                self.home_local().wait()
                self.home_remote(1 - section).wait_recv()

            @pl.when(section != self.layer)
            def _():
                self.home_remote(section).wait_send()

    lane = lane_of((tokens, LANES))
    low_half = lane % HEAD_SIZE < HALF
    left = lane < HEAD_SIZE
    pair_lane = lane_of((2 * tokens, LANES))
    causal = lax.broadcasted_iota(jnp.int32, (2 * tokens, tokens), 0) % tokens >= lax.broadcasted_iota(
        jnp.int32, (2 * tokens, tokens), 1
    )
    root = HEAD_SIZE ** (-0.5)

    def stack(tile):
        nothing = jnp.zeros_like(tile)
        return jnp.concatenate([jnp.where(left, tile, nothing), jnp.where(left, nothing, tile)], axis=0)

    def attention_forward(layer, source, early, late):
        cosine, sine = r.cosine[...], r.sine[...]
        residual = source[...].astype(F32)
        normed_one = (residual * row_scale(residual) * r.gains[layer, 0:1]).astype(BF16)
        weights_wait(layer, 0)
        early()
        r.projected[:, :QUERY_WIDTH] = dot_nn(normed_one, r.win[layer, :, :QUERY_WIDTH])
        weights_wait(layer, 1)
        r.projected[:, QUERY_WIDTH:] = dot_nn(normed_one, r.win[layer, :, QUERY_WIDTH:])
        for tile in range(QUERY_WIDTH // LANES):
            columns = slice(tile * LANES, (tile + 1) * LANES)
            piece = r.projected[:, columns]
            r.query[layer, :, columns] = (piece * cosine + turned(piece, low_half) * sine).astype(BF16)
        for tile in range(KEY_WIDTH // LANES):
            first = slice(2 * tile * LANES, (2 * tile + 1) * LANES)
            second = slice((2 * tile + 1) * LANES, (2 * tile + 2) * LANES)
            piece = r.projected[:, QUERY_WIDTH + tile * LANES : QUERY_WIDTH + (tile + 1) * LANES]
            piece = piece * cosine + turned(piece, low_half) * sine
            other = pltpu.roll(piece, HEAD_SIZE, 1)
            r.key[layer, :, first] = jnp.where(left, piece, other).astype(BF16)
            r.key[layer, :, second] = jnp.where(left, other, piece).astype(BF16)
            start = QUERY_WIDTH + KEY_WIDTH + tile * LANES
            piece = r.projected[:, start : start + LANES]
            other = pltpu.roll(piece, HEAD_SIZE, 1)
            r.value[layer, :, first] = jnp.where(left, piece, other).astype(BF16)
            r.value[layer, :, second] = jnp.where(left, other, piece).astype(BF16)
        logs = jnp.zeros((2 * tokens, LANES), F32)
        for head in range(KEY_VALUE_HEADS):
            columns = slice(head * LANES, (head + 1) * LANES)
            scores = dot_nt(stack(r.query[layer, :, columns]), r.key[layer, :, columns]) * root
            scores = jnp.where(causal, scores, -1e30)
            top = jnp.max(scores, axis=-1, keepdims=True)
            log_total = top + jnp.log(jnp.sum(jnp.exp(scores - top), axis=-1, keepdims=True))
            logs = jnp.where(pair_lane == head, log_total, logs)
            weights = jnp.exp(scores - log_total).astype(BF16)
            mixed = dot_nn(weights, r.value[layer, :, columns])
            r.attended[layer, :, columns] = jnp.where(left, mixed[:tokens], mixed[tokens:]).astype(BF16)
        r.logs[layer] = logs
        late()
        weights_wait(layer, 2)
        middle = residual + dot_nn(r.attended[layer], r.wout[layer])
        r.middle[layer] = middle
        normed_two = (middle * row_scale(middle) * r.gains[layer, 1:2]).astype(BF16)
        r.packed[layer, :, :MODEL_WIDTH] = normed_two
        logits = jnp.concatenate(
            [dot_nn(normed_two, r.router[layer]), jnp.zeros((tokens, LANES - EXPERTS), F32)], axis=-1
        )
        chosen = r.hot[layer] > 0.0
        top = jnp.max(jnp.where(chosen, logits, -1e30), axis=-1, keepdims=True)
        grown = jnp.where(chosen, jnp.exp(jnp.where(chosen, logits - top, 0.0)), 0.0)
        gates = grown / jnp.sum(grown, axis=-1, keepdims=True)
        r.gates[layer] = gates
        r.packed[layer, :, MODEL_WIDTH:] = two_parts(gates)

    def attention_backward(layer, source, up, back, gate_grads):
        cosine, sine = r.cosine[...], r.sine[...]
        gates = r.gates[layer]
        grad_picked = gates * (gate_grads - jnp.sum(gates * gate_grads, axis=-1, keepdims=True))
        grad_logits = grad_picked.astype(BF16)
        r.small[layer, 16:] = dot_tn(grad_logits, r.packed[layer, :, :MODEL_WIDTH])[:EXPERTS]
        grad_second = back + dot_nt(grad_logits[:, :EXPERTS], r.router[layer])
        middle = r.middle[layer]
        scale_two = row_scale(middle)
        r.small[layer, 1:2] = jnp.sum(grad_second * middle * scale_two, axis=0, keepdims=True)
        grad_middle = up[...].astype(F32) + norm_back(grad_second * r.gains[layer, 1:2], middle, scale_two)
        low = grad_middle.astype(BF16)
        r.low[layer] = low
        r.grad_middle[...] = grad_middle
        r.grad_attended[...] = dot_nt(low, r.wout[layer]).astype(BF16)
        logs = r.logs[layer]
        held = []
        for head in range(KEY_VALUE_HEADS):
            columns = slice(head * LANES, (head + 1) * LANES)
            query = stack(r.query[layer, :, columns])
            key, value = r.key[layer, :, columns], r.value[layer, :, columns]
            scores = dot_nt(query, key) * root
            log_total = jnp.sum(jnp.where(pair_lane == head, logs, 0.0), axis=-1, keepdims=True)
            probabilities = jnp.where(causal, jnp.exp(jnp.where(causal, scores - log_total, 0.0)), 0.0)
            grad_tile = stack(r.grad_attended[:, columns])
            delta = jnp.sum(
                grad_tile.astype(F32) * stack(r.attended[layer, :, columns]).astype(F32), axis=-1, keepdims=True
            )
            grad_scores = (probabilities * (dot_nt(grad_tile, value) - delta)).astype(BF16)
            wide = dot_nn(grad_scores, key) * root
            grad_query = jnp.where(left, wide[:tokens], wide[tokens:])
            grad_query = grad_query * cosine - turned(grad_query, low_half) * sine
            r.projected_grad[layer, :, columns] = grad_query.astype(BF16)
            key_grad = dot_tn(grad_scores, query) * root
            value_grad = dot_tn(probabilities.astype(BF16), grad_tile)
            key_grad = key_grad + pltpu.roll(key_grad, HEAD_SIZE, 1)
            value_grad = value_grad + pltpu.roll(value_grad, HEAD_SIZE, 1)
            if head % 2 == 0:
                held = [key_grad, value_grad]
            else:
                piece = jnp.where(left, held[0], key_grad)
                piece = piece * cosine - turned(piece, low_half) * sine
                start = QUERY_WIDTH + head // 2 * LANES
                r.projected_grad[layer, :, start : start + LANES] = piece.astype(BF16)
                start += KEY_WIDTH
                r.projected_grad[layer, :, start : start + LANES] = jnp.where(left, held[1], value_grad).astype(BF16)
        grad_first = dot_nt(r.projected_grad[layer], r.win[layer])
        residual = source[...].astype(F32)
        scale_one = row_scale(residual)
        normed_one = (residual * scale_one * r.gains[layer, 0:1]).astype(BF16)
        group = MODEL_WIDTH // planes
        for variant in range(group // LANES):
            for step in range(planes):
                start = step * group + variant * LANES
                r.chosen[layer, variant, :, step * LANES : (step + 1) * LANES] = normed_one[:, start : start + LANES]
                r.chosen[layer, variant, :, (planes + step) * LANES : (planes + step + 1) * LANES] = r.attended[
                    layer, :, start : start + LANES
                ]
        r.small[layer, 0:1] = jnp.sum(grad_first * residual * scale_one, axis=0, keepdims=True)
        return (
            r.grad_middle[...] + norm_back(grad_first * r.gains[layer, 0:1], residual, scale_one)
        ).astype(BF16)

    def place_local(source, target, index):
        return pltpu.make_async_copy(source, target.at[section], r.o_local.at[index])

    def place_remote(source, target, index, micro):
        return remote(source, target.at[micro], r.o_send.at[index], r.o_recv.at[index], partner)

    def place(layer, source, target, index):
        @pl.when(section == layer)
        def _():
            place_local(source, target, index).start()

        @pl.when(section != layer)
        def _():
            place_remote(source, target, index, section).start()

    def placed(layer, source, target, index):
        @pl.when(section == layer)
        def _():
            place_local(source, target, index).wait()
            place_remote(source, target, index, 1 - section).wait_recv()

        @pl.when(section != layer)
        def _():
            place_remote(source, target, index, section).wait_send()

    chunk = min(rows, 256)
    chunks = rows // chunk
    half = MODEL_WIDTH // 2

    def each_chunk(work):
        def one(number, carry):
            work(pl.ds(pl.multiple_of(number * chunk, chunk), chunk), pl.ds(number * (chunk // tokens), chunk // tokens))
            return carry

        if chunks == 1:
            work(pl.ds(0, chunk), pl.ds(0, owners))
        else:
            lax.fori_loop(0, chunks, one, 0)

    def flat(buffer, group, columns):
        values = buffer[group, :, columns]
        return values.reshape(chunk, values.shape[-1])

    model, packing = slice(0, MODEL_WIDTH), slice(MODEL_WIDTH, PACKED)

    def expert_columns(expert):
        return pl.ds(pl.multiple_of(expert * FF, FF), FF)

    def wait_in(expert):
        load_in(0, expert)[0].wait()

    def wait_out(expert):
        load_out(0, expert)[0].wait()

    def gate_of(plane_buffer, group, expert):
        return column_of(flat(plane_buffer, group, packing), lane_of((chunk, LANES)), own * local + expert)

    def backward_terms(expert, span, gate, gate_part, up_part, inner):
        sigmoid = 1.0 / (1.0 + jnp.exp(-gate_part))
        silu = gate_part * sigmoid
        activated = silu * up_part
        gate_grad = jnp.sum(activated * inner, axis=-1, keepdims=True)
        lanes = lane_of((chunk, LANES))
        r.gate_total[span] = jnp.where(lanes == own * local + expert, gate_grad, r.gate_total[span])
        grad_activated = inner * gate
        grad_gate = grad_activated * up_part * sigmoid * (1.0 + gate_part * (1.0 - sigmoid))
        grad_up = grad_activated * silu
        grad_pair = jnp.concatenate([grad_gate.astype(BF16), grad_up.astype(BF16)], axis=-1)
        term = dot_nt(grad_pair, r.ein[expert])

        @pl.when(expert == 0)
        def _():
            r.total[span] = term

        @pl.when(expert > 0)
        def _():
            r.total[span] += term

        return activated

    def mix(reduction):
        for cut in range(2):
            columns = slice(cut * half, (cut + 1) * half)

            def work(span, group):
                r.total[span, columns] = dot_nn(r.activated[span], r.eout[:, columns])

            each_chunk(work)
            for step in range(1, owners):
                reduction.put(
                    step, columns, r.total[pl.ds(owner_to(step) * tokens, tokens), columns].astype(BF16)
                )
            reduction.start(cut)

    def mixed(reduction, result):
        for step in range(1, owners):
            result = result + reduction.coming[step - 1].astype(F32)
        return result

    def send_back(reduction):
        for step in range(1, owners):
            span = pl.ds(owner_to(step) * tokens, tokens)
            reduction.put(step, slice(0, MODEL_WIDTH), r.total[span].astype(BF16))
            reduction.put(step, slice(MODEL_WIDTH, PACKED), two_parts(r.gate_total[span]))
        reduction.start(0)

    def came_back(reduction):
        back = r.kept_total[...]
        for step in range(1, owners):
            back = back + reduction.coming[step - 1, :, :MODEL_WIDTH].astype(F32)
        terms = reduction.coming[0, :, MODEL_WIDTH:].astype(F32)
        for step in range(2, owners):
            terms = terms + reduction.coming[step - 1, :, MODEL_WIDTH:].astype(F32)
        return back, r.kept_gate[...] + terms + pltpu.roll(terms, LANES - EXPERTS, 1)

    both_cuts = ((0, half), (half, half))
    spread_x0 = Spread(r.packed.at[0], r.plane0, 0)
    spread_x1 = Spread(r.packed.at[1], r.plane1, 1)
    spread_u1 = Spread(r.up, r.ups1, 2)
    spread_u0 = Spread(r.up0, r.ups0, 3)
    mix0 = Reduce(r.leave_y, r.come_y, 0, both_cuts)
    mix1 = Reduce(r.leave_y, r.come_y, 1, both_cuts)
    back1 = Reduce(r.leave_b, r.come_b, 2, ((0, PACKED),))
    back0 = Reduce(r.leave_b, r.come_b, 3, ((0, PACKED),))
    gather_x0 = Gather(0, r.packed.at[0], r.plane0, r.every_x, 0)
    gather_x1 = Gather(1, r.packed.at[1], r.plane1, r.every_x, 1)
    gather_u0 = Gather(0, r.up0, r.ups0, r.every_u, 2)
    gather_u1 = Gather(1, r.up, r.ups1, r.every_u, 3)
    for which in pieces:
        weights_start(0, which)
    for expert in range(local):
        for copy in swap_pair(expert):
            copy.start()

    @pl.when(section == 0)
    def _():
        for expert in range(local):
            load_in(0, expert)[0].start()
            load_out(0, expert)[0].start()

    r.small[...] = jnp.zeros_like(r.small)
    weights_spread(0, 0)
    weights_spread(0, 1)
    weights_forward(0, 0)
    weights_push(0, 0)
    weights_spread(0, 2)
    weights_forward(0, 1)
    weights_push(0, 1)

    def early0():
        for which in pieces:
            weights_start(1, which)

    def late0():
        weights_forward(0, 2)
        weights_push(0, 2)

    for copy in shared:
        copy.wait()
    for copy in own_rows:
        copy.wait()
    attention_forward(0, r.x, early0, late0)
    spread_x0.start()
    spread_x0.wait()
    for which in pieces:
        weights_spread(1, which)
    spread_u1.start()
    gather_u1.start()
    gather_x0.start_whole()
    gather_x0.start_home()

    def forward_expert(expert, carry):
        @pl.when(section != 0)
        def _():
            for which, make in enumerate((load_in, load_out)):
                swap_pair(expert)[which].wait_recv()
                make(0, expert)[1].start()

        wait_in(expert)

        def work(span, group):
            gate = gate_of(r.plane0, group, expert)
            pair = dot_nn(flat(r.plane0, group, model), r.ein[expert])
            r.pairs[expert, span] = pair.astype(BF16)
            gate_part, up_part = pair[:, :FF], pair[:, FF:]
            silu = gate_part / (1.0 + jnp.exp(-gate_part))
            r.activated[span, expert_columns(expert)] = (silu * up_part * gate).astype(BF16)

        each_chunk(work)
        start_load(load_in, 1, expert, 0, True)
        wait_out(expert)
        return carry

    lax.fori_loop(0, local // 2, forward_expert, 0)
    weights_forward(1, 0)
    weights_forward(1, 1)
    lax.fori_loop(local // 2, local, forward_expert, 0)
    mix(mix0)
    weights_forward(1, 2)
    weights_push(1, 0)
    weights_push(1, 1)
    for expert in range(local):
        start_load(load_out, 1, expert, 1, True)
    spread_u1.wait()
    gather_u1.start_home()
    mix0.wait()
    r.hidden0[...] = (r.middle[0] + mixed(mix0, r.total[here])).astype(BF16)
    place(0, r.hidden0, r.hidden, 0)

    def late1():
        weights_push(1, 2)

    attention_forward(1, r.hidden0, lambda: None, late1)
    spread_x1.start()

    def inner_expert(expert, carry):
        wait_out(expert)

        def work(span, group):
            r.inner[span, expert_columns(expert)] = dot_nt(
                flat(r.ups1, group, model), r.eout[expert_columns(expert)]
            ).astype(r.inner.dtype)

        each_chunk(work)
        return carry

    lax.fori_loop(0, local, inner_expert, 0)
    spread_x1.wait()
    gather_u1.middle()
    gather_x1.start()
    gather_x1.start_home()
    r.gate_total[...] = jnp.zeros_like(r.gate_total)

    def both_expert(expert, carry):
        wait_in(expert)

        def work(span, group):
            gate = gate_of(r.plane1, group, expert)
            pair = dot_nn(flat(r.plane1, group, model), r.ein[expert])
            inner = r.inner[span, expert_columns(expert)].astype(F32)
            activated = backward_terms(expert, span, gate, pair[:, :FF], pair[:, FF:], inner)
            r.activated[span, expert_columns(expert)] = (activated * gate).astype(BF16)

        each_chunk(work)
        start_load(load_in, 0, expert, 0, False)
        return carry

    lax.fori_loop(0, local // 2, both_expert, 0)
    gather_u1.forward()
    lax.fori_loop(local // 2, local, both_expert, 0)
    send_back(back1)
    r.kept_total[...] = r.total[here]
    r.kept_gate[...] = r.gate_total[here]
    mix(mix1)
    for expert in range(local):
        start_load(load_out, 0, expert, 1, False)
    back1.wait()
    back, gate_grads = came_back(back1)
    r.up0[...] = attention_backward(1, r.hidden0, r.up, back, gate_grads)
    spread_u0.start()
    place(1, r.up0, r.input_grad, 1)
    mix1.wait()
    r.hidden1[...] = (r.middle[1] + mixed(mix1, r.total[here])).astype(BF16)
    place(1, r.hidden1, r.hidden, 2)
    r.gate_total[...] = jnp.zeros_like(r.gate_total)
    spread_u0.wait()
    gather_x1.middle()
    gather_u0.start()
    gather_u0.start_home()

    def behind_expert(expert, carry):
        wait_in(expert)
        wait_out(expert)

        def work(span, group):
            gate = gate_of(r.plane0, group, expert)
            pair = r.pairs[expert, span].astype(F32)
            inner = dot_nt(flat(r.ups0, group, model), r.eout[expert_columns(expert)])
            backward_terms(expert, span, gate, pair[:, :FF], pair[:, FF:], inner)

        each_chunk(work)
        return carry

    lax.fori_loop(0, local // 2, behind_expert, 0)
    gather_x1.forward()
    lax.fori_loop(local // 2, local, behind_expert, 0)
    send_back(back0)
    r.kept_total[...] = r.total[here]
    r.kept_gate[...] = r.gate_total[here]
    back0.wait()
    gather_u0.middle()
    back, gate_grads = came_back(back0)
    r.grad0[...] = attention_backward(0, r.x, r.up0, back, gate_grads)
    place(0, r.grad0, r.input_grad, 3)
    gather_u0.forward()

    for layer in range(2):
        for which in pieces:
            weights_unsent(layer, which)
    for expert in range(local):
        for copy in swap_pair(expert):
            copy.wait_send()
    for copy in unsent:
        copy.wait_send()
    placed(0, r.hidden0, r.hidden, 0)
    placed(1, r.up0, r.input_grad, 1)
    placed(1, r.hidden1, r.hidden, 2)
    placed(0, r.grad0, r.input_grad, 3)
    gather_x0.finish_whole()
    for gather in (gather_u1, gather_x1, gather_u0):
        gather.finish()


def both_layers(layer_input, cotangent, routes, gain_one, attn_in, attn_out, gain_two, router, cosine, sine,
                experts_in, experts_out):
    planes, owners = lax.axis_size("dp"), lax.axis_size("expert")
    tokens = layer_input.shape[1]
    local = experts_in.shape[1]
    slab = attn_in.shape[1]
    rows = owners * tokens
    dma = lambda *shape: pltpu.SemaphoreType.DMA(shape)
    vmem = lambda shape, dtype: pltpu.VMEM(shape, dtype)
    wide = (2, tokens, MODEL_WIDTH)
    everywhere = (owners, planes, 2, tokens)
    inputs = dict(
        layer_input=(layer_input, any_spec()),
        cotangent=(cotangent, any_spec()),
        routes=(routes, vmem_spec()),
        gain_one=(gain_one, vmem_spec()),
        gain_two=(gain_two, vmem_spec()),
        router_in=(router, vmem_spec()),
        attn_in=(attn_in, any_spec()),
        attn_out=(attn_out, any_spec()),
        cosine=(cosine, vmem_spec()),
        sine=(sine, vmem_spec()),
        experts_in=(experts_in, any_spec()),
        experts_out=(experts_out, any_spec()),
    )
    outputs = dict(
        hidden=(wide, BF16, any_spec()),
        input_grad=(wide, BF16, any_spec()),
        other_in=(experts_in.shape[1:], BF16, any_spec()),
        other_out=(experts_out.shape[1:], BF16, any_spec()),
        every_x=(everywhere + (PACKED,), BF16, any_spec()),
        every_u=(everywhere + (MODEL_WIDTH,), BF16, any_spec()),
        projected_grad=((2, tokens, PROJECTED), BF16, vmem_spec()),
        low=(wide, BF16, vmem_spec()),
        chosen=(
            (2, MODEL_WIDTH // planes // LANES, tokens, 2 * planes * LANES), BF16, vmem_spec()
        ),
        small=((2, 16 + EXPERTS, MODEL_WIDTH), F32, vmem_spec()),
    )
    scratch = dict(
        win=vmem((2, MODEL_WIDTH, PROJECTED), BF16),
        wout=vmem((2, QUERY_WIDTH, MODEL_WIDTH), BF16),
        ein=vmem((local, MODEL_WIDTH, 2 * FF), BF16),
        eout=vmem((local * FF, MODEL_WIDTH), BF16),
        x=vmem(wide[1:], BF16),
        up=vmem(wide[1:], BF16),
        gains=vmem((2, 8, MODEL_WIDTH), F32),
        router=vmem((2, MODEL_WIDTH, EXPERTS), BF16),
        hot=vmem((2, tokens, LANES), F32),
        hot_out=vmem((tokens, LANES), F32),
        i_sem=dma(2),
        h_send=dma(3),
        h_recv=dma(3),
        projected=vmem((tokens, PROJECTED), F32),
        query=vmem(wide, BF16),
        key=vmem(wide, BF16),
        value=vmem(wide, BF16),
        attended=vmem(wide, BF16),
        logs=vmem((2, 2 * tokens, LANES), F32),
        middle=vmem(wide, F32),
        packed=vmem((2, tokens, PACKED), BF16),
        gates=vmem((2, tokens, LANES), F32),
        up0=vmem(wide[1:], BF16),
        hidden0=vmem(wide[1:], BF16),
        hidden1=vmem(wide[1:], BF16),
        grad0=vmem(wide[1:], BF16),
        grad_middle=vmem(wide[1:], F32),
        grad_attended=vmem(wide[1:], BF16),
        plane0=vmem((owners, tokens, PACKED), BF16),
        plane1=vmem((owners, tokens, PACKED), BF16),
        ups0=vmem((owners, tokens, MODEL_WIDTH), BF16),
        ups1=vmem((owners, tokens, MODEL_WIDTH), BF16),
        pairs=vmem((local, rows, 2 * FF), BF16),
        inner=vmem((rows, local * FF), BF16),
        activated=vmem((rows, local * FF), BF16),
        total=vmem((rows, MODEL_WIDTH), F32),
        gate_total=vmem((rows, LANES), F32),
        kept_total=vmem((tokens, MODEL_WIDTH), F32),
        kept_gate=vmem((tokens, LANES), F32),
        leave_y=vmem((owners - 1, tokens, MODEL_WIDTH), BF16),
        come_y=vmem((owners - 1, tokens, MODEL_WIDTH), BF16),
        leave_b=vmem((owners - 1, tokens, PACKED), BF16),
        come_b=vmem((owners - 1, tokens, PACKED), BF16),
        w_local=dma(2, 3),
        wz_send=dma(2, 3, planes),
        wz_recv=dma(2, 3, planes),
        wp_send=dma(2, 3, planes, owners),
        wp_recv=dma(2, 3, planes, owners),
        wc_send=dma(2, 3, planes),
        wc_recv=dma(2, 3, planes),
        s_send=dma(2, local),
        s_recv=dma(2, local),
        l_sem=dma(2, local),
        a_send=dma(4, owners),
        a_recv=dma(4, owners),
        r_send=dma(4, 2, owners),
        r_recv=dma(4, 2, owners),
        g_send=dma(4, planes),
        g_recv=dma(4, planes, 2),
        g_local=dma(4),
        gp_send=dma(4, owners),
        gp_recv=dma(4, owners),
        o_send=dma(4),
        o_recv=dma(4),
        o_local=dma(4),
    )
    return call(
        functools.partial(layers_kernel, planes, owners, tokens, local, slab),
        "both_layers", 0, inputs, outputs, scratch,
    )


def ExpertGrads(planes, owners, tokens, local, first, r):
    plane = lax.axis_index("dp")
    own = lax.axis_index("expert")
    group = 4 * tokens
    slots = group // 2
    groups = 2 * planes * owners * tokens // group
    slice_in, slice_out = MODEL_WIDTH // planes, FF // planes
    chunk = min(groups * slots, 1024)
    chunks = groups * slots // chunk
    tile = 512
    shift = first if r.grad_in.shape[0] < local else 0

    def weights_of(expert):
        slot = expert % 2
        return (
            pltpu.make_async_copy(r.experts_in.at[0, expert], r.ein.at[slot], r.e_sem.at[0, slot]),
            pltpu.make_async_copy(r.experts_out.at[0, expert], r.eout.at[slot], r.e_sem.at[1, slot]),
        )

    def rows_of(number):
        slot = number % 2
        span = pl.ds(pl.multiple_of(number * group, group), group)
        return (
            pltpu.make_async_copy(r.every_x.at[span], r.x_rows.at[slot], r.t_sem.at[0, slot]),
            pltpu.make_async_copy(r.every_u.at[span], r.u_rows.at[slot], r.t_sem.at[1, slot]),
        )

    pack = r.compact_x.shape[0]
    bunch = r.picks.shape[0] // slots
    before = (
        lax.broadcasted_iota(jnp.int32, (group, group), 0) < lax.broadcasted_iota(jnp.int32, (group, group), 1)
    ).astype(BF16)
    same = (
        lax.broadcasted_iota(jnp.int32, (group, group), 0) == lax.broadcasted_iota(jnp.int32, (group, group), 1)
    ).astype(BF16)
    numbers = lax.broadcasted_iota(jnp.int32, (slots, group), 0).astype(F32)

    def gather():
        def one(number, carry):
            slot = number % 2
            for copy in rows_of(number):
                copy.wait()

            @pl.when(number + 1 < groups)
            def _():
                for copy in rows_of(number + 1):
                    copy.start()

            parts = r.x_rows[slot, :, MODEL_WIDTH:].astype(F32)
            chosen = (parts != 0.0).astype(BF16)
            rank = dot_tn(chosen, before)
            r.ranks[...] = jnp.where(dot_tn(chosen, same) > 0.0, rank, -1.0)
            span = pl.ds(pl.multiple_of(number * slots, slots), slots)
            for low in range(0, pack, bunch):
                few = min(bunch, pack - low)
                for index in range(few):
                    rank_row = r.ranks[pl.ds(own * local + first + low + index, 1), :]
                    r.picks[index * slots : (index + 1) * slots, :] = (numbers == rank_row).astype(BF16)
                for source, target in ((r.x_rows, r.compact_x), (r.u_rows, r.compact_u)):
                    found = dot_nn(r.picks[: few * slots], source[slot]).astype(BF16)
                    for index in range(few):
                        target[low + index, span] = found[index * slots : (index + 1) * slots]
            return carry

        lax.fori_loop(0, groups, one, 0)

    def out_of(expert):
        slot = expert % 2
        return (
            pltpu.make_async_copy(r.din.at[slot], r.grad_in.at[expert - shift], r.d_sem.at[0, slot]),
            pltpu.make_async_copy(r.dout.at[slot], r.grad_out.at[expert - shift], r.d_sem.at[1, slot]),
        )

    def one_expert(expert, index):
        slot = expert % 2
        for copy in weights_of(expert):
            copy.wait()

        @pl.when(expert + 1 < first + pack)
        def _():
            for copy in weights_of(expert + 1):
                copy.start()

        @pl.when(expert >= first + 2)
        def _():
            for copy in out_of(expert - 2):
                copy.wait()

        for number in range(chunks):

            def one_tile(step, carry):
                span = pl.ds(pl.multiple_of(number * chunk + step * tile, tile), tile)
                here = pl.ds(pl.multiple_of(step * tile, tile), tile)
                gate = column_of(
                    r.compact_x[index, span, MODEL_WIDTH:], lane_of((tile, LANES)), own * local + expert
                )
                pair = dot_nn(r.compact_x[index, span, :MODEL_WIDTH], r.ein[slot])
                gate_part, up_part = pair[:, :FF], pair[:, FF:]
                sigmoid = 1.0 / (1.0 + jnp.exp(-gate_part))
                silu = gate_part * sigmoid
                r.activated[here] = (silu * up_part * gate).astype(BF16)
                grad_activated = dot_nt(r.compact_u[index, span], r.eout[slot]) * gate
                r.grad_pair[here, :FF] = (
                    grad_activated * up_part * sigmoid * (1.0 + gate_part * (1.0 - sigmoid))
                ).astype(BF16)
                r.grad_pair[here, FF:] = (grad_activated * silu).astype(BF16)
                return carry

            lax.fori_loop(0, chunk // tile, one_tile, 0)
            rows = slice(number * chunk, (number + 1) * chunk)
            left_in = r.compact_x[index, rows, pl.ds(pl.multiple_of(plane * slice_in, LANES), slice_in)]
            left_out = r.activated[:, pl.ds(pl.multiple_of(plane * slice_out, LANES), slice_out)]
            term_in = dot_tn(left_in, r.grad_pair[...])
            term_out = dot_tn(left_out, r.compact_u[index, rows])
            if number == 0:
                r.din[slot] = term_in
                r.dout[slot] = term_out
            else:
                r.din[slot] += term_in
                r.dout[slot] += term_out
        for copy in out_of(expert):
            copy.start()

    def run(low, high):
        def body(index, carry):
            one_expert(first + index, index)
            return carry

        if high > low:
            lax.fori_loop(low, high, body, 0)

    def start():
        for copy in weights_of(first) + rows_of(0):
            copy.start()

    def finish():
        for expert in range(max(first, first + pack - 2), first + pack):
            for copy in out_of(expert):
                copy.wait()

    names = Names()
    names.load, names.gather, names.run, names.finish, names.pack = start, gather, run, finish, pack
    return names


def gradients_kernel(planes, owners, tokens, local, r):
    section = lax.axis_index("section")
    plane = lax.axis_index("dp")
    own = lax.axis_index("expert")
    partner = dict(section=1 - section)
    part = MODEL_WIDTH // (planes * owners)
    barrier = pltpu.get_barrier_semaphore()
    for step in range(1, owners):
        pl.semaphore_signal(barrier, inc=1, device_id=dict(expert=(own + step) % owners), device_id_type=MESH)
    for step in range(1, planes):
        pl.semaphore_signal(barrier, inc=1, device_id=dict(dp=(plane + step) % planes), device_id_type=MESH)
    pl.semaphore_signal(barrier, inc=1, device_id=partner, device_id_type=MESH)

    experts = ExpertGrads(planes, owners, tokens, local, 0, r)
    experts.load()

    def meet(source, target, index):
        here = pltpu.make_async_copy(source.at[section], target.at[section], r.m_local.at[index])
        there = remote(source.at[1 - section], target.at[section], r.m_send.at[index], r.m_recv.at[index], partner)
        return here, there

    meets = [
        meet(r.low, r.all_low.at[own], 0),
        meet(r.chosen, r.both_chosen, 1),
        meet(r.small, r.both_small, 2),
        meet(r.projected_grad, r.all_projected.at[own], 3),
    ]
    pl.semaphore_wait(barrier, owners - 1 + planes - 1 + 1)
    for here, there in meets:
        here.start()
        there.start()

    def piece_of(buffer):
        return lambda owner, half: buffer.at[owner] if half is None else buffer.at[owner, half]

    spreads = (
        PlaneBroadcast(owners, own, piece_of(r.all_low), r.f_send.at[0], r.f_recv.at[0]),
        PlaneBroadcast(owners, own, piece_of(r.all_projected), r.f_send.at[1], r.f_recv.at[1]),
    )
    width = planes * LANES

    def variant_of(owner):
        return owner * part // LANES

    def chosen_to(step, which):
        target = (own + step) % owners
        columns = pl.ds((1 - which) * width, width)
        return remote(
            r.both_chosen.at[:, variant_of(target), :, columns], r.all_chosen.at[own, :, :, columns],
            r.c_send.at[which, step], r.c_recv.at[which, step], dict(expert=target),
        )

    def small_to(step):
        return remote(
            r.small_out, r.small_in.at[step - 1], r.v_send.at[step], r.v_recv.at[step],
            dict(expert=(own + step) % owners),
        )

    halves = (
        (r.all_low, r.product_out, r.sums, r.leaving_out),
        (r.all_projected, r.product_in, r.partial, r.leaving),
    )

    def sums_over(step):
        return remote(
            r.leaving_out.at[step - 1], r.arriving_out.at[step - 1], r.z_send.at[step], r.z_recv.at[step],
            dict(dp=(plane + step) % planes),
        )

    def attention_start():
        for here, there in meets:
            here.wait()
            there.wait_recv()
        r.small_kept[...] = r.both_small[0] + r.both_small[1]
        r.small_out[...] = r.small_kept[...].astype(BF16)
        for step in range(1, owners):
            small_to(step).start()
        for which in range(2):
            spreads[which].start()
            for step in range(1, owners):
                chosen_to(step, which).start()
        r.all_chosen[own] = r.both_chosen[:, variant_of(own)]

    def attention_small():
        total = r.small_kept[...]
        for step in range(1, owners):
            small_to(step).wait_recv()
            total = total + r.small_in[step - 1].astype(F32)
        r.sums[part:] = total
        for step in range(1, planes):
            r.leaving_out[step - 1, part:] = total.astype(BF16)

    def attention_partial(which):
        factors, product, partial, leaving = halves[which]
        spreads[which].wait()
        for step in range(1, owners):
            chosen_to(step, which).wait_recv()
        within = own * part % LANES
        some = min(owners, 4)
        pile = some * 2 * tokens
        for step in list(range(1, planes)) + [0]:
            target = (plane + step) % planes
            columns = pl.ds(pl.multiple_of(((1 - which) * planes + target) * LANES, LANES), LANES)
            for first in range(0, owners, some):
                left = r.all_chosen[first : first + some, :, :, columns].reshape(pile, LANES)
                term = dot_tn(left, factors[first : first + some].reshape(pile, factors.shape[-1]))
                if first == 0:
                    product[...] = term
                else:
                    product[...] += term
            mine = product[pl.ds(pl.multiple_of(within, 16), part)]
            if step == 0:
                partial[:part] = mine
            else:
                leaving[step - 1, :part] = mine.astype(BF16)
                if which == 0:
                    sums_over(step).start()

    def attention_last():
        total = r.sums[...]
        for step in range(1, planes):
            sums_over(step).wait()
            total = total + r.arriving_out[step - 1].astype(F32)
        r.sums[...] = total
        for here, there in meets:
            there.wait_send()
        for which in range(2):
            spreads[which].sent()
            for step in range(1, owners):
                chosen_to(step, which).wait_send()
        for step in range(1, owners):
            small_to(step).wait_send()

    attention_start()
    experts.gather()
    attention_small()
    spreads[0].forward()
    pack = experts.pack
    experts.run(0, pack // 5)
    spreads[1].forward()
    experts.run(pack // 5, 3 * pack // 5)
    attention_partial(0)
    experts.run(3 * pack // 5, pack)
    experts.finish()
    attention_partial(1)
    attention_last()


def rest_kernel(planes, owners, tokens, local, first, r):
    experts = ExpertGrads(planes, owners, tokens, local, first, r)
    experts.load()
    held = ((r.first_in, r.held_in, r.grad_in), (r.first_out, r.held_out, r.grad_out))
    entering = [
        pltpu.make_async_copy(source, here, r.move_sem.at[0, index]) for index, (source, here, _) in enumerate(held)
    ]
    moving = [
        pltpu.make_async_copy(here, target.at[pl.ds(0, first)], r.move_sem.at[1, index])
        for index, (_, here, target) in enumerate(held)
    ]
    for copy in entering:
        copy.start()
    experts.gather()
    for number in range(2):
        entering[number].wait()
        moving[number].start()
    experts.run(0, experts.pack)
    experts.finish()
    for copy in moving:
        copy.wait()


def grads_scratch(planes, owners, tokens, pack):
    group = 4 * tokens
    groups = 2 * planes * owners * tokens // group
    slots = group // 2
    chunk = min(groups * slots, 1024)
    dma = lambda *shape: pltpu.SemaphoreType.DMA(shape)
    vmem = lambda shape, dtype: pltpu.VMEM(shape, dtype)
    return dict(
        ein=vmem((2, MODEL_WIDTH, 2 * FF), BF16),
        eout=vmem((2, FF, MODEL_WIDTH), BF16),
        x_rows=vmem((2, group, PACKED), BF16),
        u_rows=vmem((2, group, MODEL_WIDTH), BF16),
        ranks=vmem((LANES, group), F32),
        picks=vmem((min(pack, 5) * slots, group), BF16),
        compact_x=vmem((pack, groups * slots, PACKED), BF16),
        compact_u=vmem((pack, groups * slots, MODEL_WIDTH), BF16),
        activated=vmem((chunk, FF), BF16),
        grad_pair=vmem((chunk, 2 * FF), BF16),
        din=vmem((2, MODEL_WIDTH // planes, 2 * FF), F32),
        dout=vmem((2, FF // planes, MODEL_WIDTH), F32),
        e_sem=dma(2, 2),
        t_sem=dma(2, 2),
        d_sem=dma(2, 2),
    )


def weight_gradients(done, experts_in, experts_out):
    planes, owners = lax.axis_size("dp"), lax.axis_size("expert")
    local = experts_in.shape[1]
    tokens = done.low.shape[1]
    part = MODEL_WIDTH // (planes * owners)
    first = max(1, 5 * local // 8)
    wide = 2 * planes * LANES
    variants = done.chosen.shape[1]
    small = done.small.shape[1:]
    dma = lambda *shape: pltpu.SemaphoreType.DMA(shape)
    vmem = lambda shape, dtype: pltpu.VMEM(shape, dtype)
    shape_in, shape_out = (MODEL_WIDTH // planes, 2 * FF), (FF // planes, MODEL_WIDTH)
    tables = dict(
        every_x=(done.every_x.reshape(-1, PACKED), any_spec()),
        every_u=(done.every_u.reshape(-1, MODEL_WIDTH), any_spec()),
        experts_in=(experts_in, any_spec()),
        experts_out=(experts_out, any_spec()),
    )
    exchanged = call(
        functools.partial(gradients_kernel, planes, owners, tokens, local),
        "weight_gradients",
        1,
        dict(
            projected_grad=(done.projected_grad, vmem_spec()),
            low=(done.low, vmem_spec()),
            chosen=(done.chosen, vmem_spec()),
            small=(done.small, vmem_spec()),
            **tables,
        ),
        dict(
            grad_in=((first,) + shape_in, F32, any_spec()),
            grad_out=((first,) + shape_out, F32, any_spec()),
            partial=((part, PROJECTED), F32, vmem_spec()),
            leaving=((planes - 1, part, PROJECTED), BF16, vmem_spec()),
            sums=((part + small[0], MODEL_WIDTH), F32, vmem_spec()),
        ),
        dict(
            all_low=vmem((owners, 2, tokens, MODEL_WIDTH), BF16),
            all_projected=vmem((owners, 2, tokens, PROJECTED), BF16),
            both_chosen=vmem((2, variants, tokens, wide), BF16),
            all_chosen=vmem((owners, 2, tokens, wide), BF16),
            both_small=vmem((2,) + small, F32),
            small_kept=vmem(small, F32),
            small_out=vmem(small, BF16),
            small_in=vmem((owners - 1,) + small, BF16),
            product_in=vmem((LANES, PROJECTED), F32),
            product_out=vmem((LANES, MODEL_WIDTH), F32),
            leaving_out=vmem((planes - 1, part + small[0], MODEL_WIDTH), BF16),
            arriving_out=vmem((planes - 1, part + small[0], MODEL_WIDTH), BF16),
            z_send=dma(planes),
            z_recv=dma(planes),
            m_local=dma(4),
            m_send=dma(4),
            m_recv=dma(4),
            f_send=dma(2, owners),
            f_recv=dma(2, owners),
            c_send=dma(2, owners),
            c_recv=dma(2, owners),
            v_send=dma(owners),
            v_recv=dma(owners),
            **grads_scratch(planes, owners, tokens, first),
        ),
    )
    total = exchanged.partial
    arriving = [
        lax.ppermute(exchanged.leaving[step - 1], "dp", [(i, (i + step) % planes) for i in range(planes)])
        for step in range(1, planes)
    ]
    count = local - first
    rows = 2 * planes * owners * tokens
    rest = call(
        functools.partial(rest_kernel, planes, owners, tokens, local, first),
        "other_experts",
        None,
        dict(first_in=(exchanged.grad_in, any_spec()), first_out=(exchanged.grad_out, any_spec()), **tables),
        dict(
            grad_in=((local,) + shape_in, F32, any_spec()),
            grad_out=((local,) + shape_out, F32, any_spec()),
        ),
        dict(
            held_in=vmem((first,) + shape_in, F32),
            held_out=vmem((first,) + shape_out, F32),
            move_sem=dma(2, 2),
            **grads_scratch(planes, owners, tokens, count),
        ),
        pl.CostEstimate(flops=count * rows * 6 * MODEL_WIDTH * FF, bytes_accessed=rows * 4 * MODEL_WIDTH, transcendentals=0),
    )
    arriving, grad_in, grad_out = lax.optimization_barrier((arriving, rest.grad_in, rest.grad_out))
    for piece in arriving:
        total = total + piece.astype(F32)
    sums = exchanged.sums
    return sums[part : part + 2], total, sums[:part], sums[part + 16 :].T, grad_in, grad_out


def shards(layer_input, cotangent, positions, routes, gain_one, attn_in, attn_out, gain_two, router,
           experts_in, experts_out):
    place = lax.dynamic_index_in_dim(positions, lax.axis_index("section"), 0, keepdims=False)
    lane = jnp.arange(LANES)
    frequency = jnp.power(rotary_base, -((lane % HALF).astype(F32) * (2.0 / HEAD_SIZE)))
    angles = place.astype(F32)[:, None] * frequency[None, :]
    cosine = jnp.cos(angles)
    sine = jnp.where(lane % HEAD_SIZE < HALF, -1.0, 1.0) * jnp.sin(angles)

    done = both_layers(
        layer_input, cotangent, routes, gain_one, attn_in, attn_out, gain_two, router, cosine, sine,
        experts_in, experts_out,
    )
    gains, grad_attn_in, grad_attn_out, grad_router, grad_in, grad_out = weight_gradients(
        done, experts_in, experts_out
    )
    return (
        done.hidden[None],
        done.input_grad[None],
        gains[0:1],
        grad_attn_in[None],
        grad_attn_out[None],
        gains[1:2],
        grad_router[None],
        grad_in[None],
        grad_out[None],
    )


def solution(mesh):
    in_specs = (
        P(None, ("dp", "expert"), None),
        P(None, ("dp", "expert"), None),
        P(None, ("dp", "expert")),
        P("section", None, ("dp", "expert"), None),
        P("section", None),
        P("section", "dp", None),
        P("section", "dp", None),
        P("section", None),
        P("section", None, None),
        P("section", "expert", None, None),
        P("section", "expert", None, None),
    )
    out_specs = (
        P("section", None, ("dp", "expert"), None),
        P("section", None, ("dp", "expert"), None),
        P("section", None),
        P("section", ("dp", "expert"), None),
        P("section", ("dp", "expert"), None),
        P("section", None),
        P("section", None, None),
        P("section", "expert", "dp", None),
        P("section", "expert", "dp", None),
    )
    return jax.shard_map(shards, mesh=mesh, in_specs=in_specs, out_specs=out_specs, check_vma=False)
```

```python
import functools

import jax
import jax.numpy as jnp
from jax import lax
from jax.experimental import pallas as pl
from jax.experimental.pallas import tpu as pltpu
from jax.sharding import PartitionSpec as P

MODEL_WIDTH = 1024
QUERY_HEADS = 16
KEY_VALUE_HEADS = 8
HEAD_SIZE = 64
FF = 512
EXPERTS = 32
TOPK = 8

QUERY_WIDTH = QUERY_HEADS * HEAD_SIZE
KEY_WIDTH = KEY_VALUE_HEADS * HEAD_SIZE
PROJECTED = QUERY_WIDTH + 2 * KEY_WIDTH
LANES = 128
HALF = HEAD_SIZE // 2
PACKED = MODEL_WIDTH + LANES

epsilon = 1e-06
rotary_base = 10000.0

F32 = jnp.float32
BF16 = jnp.bfloat16
MESH = pl.DeviceIdType.MESH
VMEM_LIMIT = 62 * 1024 * 1024


def dot_nn(a, b):
    return lax.dot_general(a, b, (((1,), (0,)), ((), ())), preferred_element_type=F32)


def dot_nt(a, b):
    return lax.dot_general(a, b, (((1,), (1,)), ((), ())), preferred_element_type=F32)


def dot_tn(a, b):
    return lax.dot_general(a, b, (((0,), (0,)), ((), ())), preferred_element_type=F32)


def row_scale(values):
    return lax.rsqrt(jnp.mean(values * values, axis=-1, keepdims=True) + epsilon)


def norm_back(grad_normed, inputs, scale):
    return scale * grad_normed - inputs * (scale * scale * scale) * jnp.mean(
        grad_normed * inputs, axis=-1, keepdims=True
    )


def lane_of(shape):
    return lax.broadcasted_iota(jnp.int32, shape, 1)


def turned(tile, low):
    return jnp.where(low, pltpu.roll(tile, LANES - HALF, 1), pltpu.roll(tile, HALF, 1))


def two_parts(values):
    high = values.astype(BF16).astype(F32)
    return (high + pltpu.roll(values - high, EXPERTS, 1)).astype(BF16)


def column_of(parts, lane, column):
    wide = parts.astype(F32)
    return jnp.sum(jnp.where((lane == column) | (lane == column + EXPERTS), wide, 0.0), axis=-1, keepdims=True)


def remote(source, target, send, recv, device):
    return pltpu.make_async_remote_copy(
        src_ref=source, dst_ref=target, send_sem=send, recv_sem=recv, device_id=device, device_id_type=MESH
    )


def vmem_spec():
    return pl.BlockSpec(memory_space=pltpu.VMEM)


def any_spec():
    return pl.BlockSpec(memory_space=pl.ANY)


class Names:
    pass


def call(kernel, name, number, inputs, outputs, scratch, cost=None):
    labels = list(inputs) + list(outputs) + list(scratch)

    def body(*refs):
        names = Names()
        for label, ref in zip(labels, refs):
            setattr(names, label, ref)
        kernel(names)

    if number is None:
        params = pltpu.CompilerParams(vmem_limit_bytes=VMEM_LIMIT)
    else:
        params = pltpu.CompilerParams(
            collective_id=number, has_side_effects=True, vmem_limit_bytes=VMEM_LIMIT
        )
    results = pl.pallas_call(
        body,
        out_shape=tuple(jax.ShapeDtypeStruct(shape, dtype) for shape, dtype, _ in outputs.values()),
        in_specs=[spec for _, spec in inputs.values()],
        out_specs=tuple(spec for _, _, spec in outputs.values()),
        scratch_shapes=list(scratch.values()),
        compiler_params=params,
        cost_estimate=cost,
        name=name,
    )(*[array for array, _ in inputs.values()])
    names = Names()
    for label, result in zip(outputs, results):
        setattr(names, label, result)
    return names


class PlaneBroadcast:
    def __init__(self, owners, own, piece, send, recv):
        self.owners, self.own = owners, own
        self.square = owners == 4
        self.piece, self.send, self.recv = piece, send, recv

    def hop(self, owner, half, index, device):
        block = self.piece(owner, half)
        return remote(block, block, self.send.at[index], self.recv.at[index], dict(expert=device))

    def hops(self):
        owners, own = self.owners, self.own

        def owner_to(step):
            return (own + step) % owners

        if not self.square:
            return [self.hop(own, None, turn, owner_to(turn)) for turn in range(1, owners)]
        beside = own + 1 - 2 * (own % 2)
        above = owner_to(2)
        return [
            self.hop(own, None, 0, beside),
            self.hop(own, None, 1, above),
            self.hop(beside, 0, 2, above),
            self.hop(above, 1, 3, beside),
        ]

    def start(self):
        hops = self.hops()
        for hop in hops[:2] if self.square else hops:
            hop.start()

    def forward(self):
        if self.square:
            hops = self.hops()
            for hop in range(2):
                hops[hop].wait_recv()
                hops[2 + hop].start()

    def wait(self):
        hops = self.hops()
        for hop in hops[2:] if self.square else hops:
            hop.wait_recv()

    def sent(self):
        for hop in self.hops():
            hop.wait_send()


def layers_kernel(planes, owners, tokens, local, slab, r):
    section = lax.axis_index("section")
    plane = lax.axis_index("dp")
    own = lax.axis_index("expert")
    rows = owners * tokens
    part = slab // owners
    here = pl.ds(own * tokens, tokens)
    partner = dict(section=1 - section)

    def planes_to(step):
        return (plane + step) % planes

    def owner_to(step):
        return (own + step) % owners

    barrier = pltpu.get_barrier_semaphore()
    for step in range(1, owners):
        pl.semaphore_signal(barrier, inc=1, device_id=dict(expert=owner_to(step)), device_id_type=MESH)
    for step in range(1, planes):
        for target in range(2):
            pl.semaphore_signal(
                barrier, inc=1, device_id=dict(section=target, dp=planes_to(step)), device_id_type=MESH
            )
    pl.semaphore_signal(barrier, inc=1, device_id=partner, device_id_type=MESH)
    pl.semaphore_wait(barrier, owners - 1 + 2 * (planes - 1) + 1)

    unsent = []

    own_rows = [
        pltpu.make_async_copy(r.layer_input.at[section], r.x, r.i_sem.at[0]),
        pltpu.make_async_copy(r.cotangent.at[section], r.up, r.i_sem.at[1]),
    ]
    for copy in own_rows:
        copy.start()

    unit = (
        lax.broadcasted_iota(jnp.int32, (EXPERTS, LANES), 0) == lax.broadcasted_iota(jnp.int32, (EXPERTS, LANES), 1)
    ).astype(BF16)

    def hot_of(choices):
        number = lax.broadcasted_iota(jnp.int32, (EXPERTS, tokens), 0)
        found = jnp.zeros((EXPERTS, tokens), F32)
        for choice in range(TOPK):
            found = jnp.where(number == choices[choice : choice + 1], 1.0, found)
        return dot_tn(found.astype(BF16), unit)

    r.gains[section, 0:1] = r.gain_one[...]
    r.gains[section, 1:2] = r.gain_two[...]
    r.router[section] = r.router_in[0]
    r.hot[section] = hot_of(r.routes[0, section])
    r.hot_out[...] = hot_of(r.routes[0, 1 - section])
    shared = [
        remote(source, target, r.h_send.at[index], r.h_recv.at[index], partner)
        for index, (source, target) in enumerate(
            (
                (r.gains.at[section], r.gains.at[section]),
                (r.router.at[section], r.router.at[section]),
                (r.hot_out, r.hot.at[section]),
            )
        )
    ]
    for copy in shared:
        copy.start()

    def Broadcast(piece, send, recv):
        return PlaneBroadcast(owners, own, piece, send, recv)

    weight_pieces = ((r.attn_in, r.win, 0), (r.attn_in, r.win, QUERY_WIDTH), (r.attn_out, r.wout, 0))
    pieces = range(len(weight_pieces))

    def slab_local(layer, which):
        source, full, column = weight_pieces[which]
        columns = pl.ds(column, MODEL_WIDTH)
        return pltpu.make_async_copy(
            source.at[0, :, columns], full.at[layer, pl.ds(plane * slab, slab), columns], r.w_local.at[layer, which]
        )

    def slab_z(layer, which, step):
        source, full, column = weight_pieces[which]
        columns = pl.ds(column, MODEL_WIDTH)
        return remote(
            source.at[0, pl.ds(own * part, part), columns],
            full.at[layer, pl.ds(plane * slab + own * part, part), columns],
            r.wz_send.at[layer, which, step],
            r.wz_recv.at[layer, which, step],
            dict(dp=planes_to(step)),
        )

    def slab_plane(layer, which, step):
        full, column = weight_pieces[which][1:]
        origin = planes_to(planes - step)

        def piece(owner, half):
            start, length = origin * slab + owner * part, part
            if half is not None:
                length = part // 2
                start = start + half * length
            return full.at[layer, pl.ds(start, length), pl.ds(column, MODEL_WIDTH)]

        return Broadcast(piece, r.wp_send.at[layer, which, step], r.wp_recv.at[layer, which, step])

    def slab_core(layer, which, step):
        full, column = weight_pieces[which][1:]
        block = full.at[layer, pl.ds(planes_to(planes - step) * slab, slab), pl.ds(column, MODEL_WIDTH)]
        return remote(block, block, r.wc_send.at[layer, which, step], r.wc_recv.at[layer, which, step], partner)

    def weights_start(layer, which):
        @pl.when(section == layer)
        def _():
            for step in range(1, planes):
                slab_z(layer, which, step).start()
            slab_local(layer, which).start()

    def weights_spread(layer, which):
        @pl.when(section == layer)
        def _():
            slab_local(layer, which).wait()
            slab_core(layer, which, 0).start()
            for step in range(1, planes):
                slab_z(layer, which, step).wait_recv()
                slab_plane(layer, which, step).start()

    def weights_forward(layer, which):
        @pl.when(section == layer)
        def _():
            for step in range(1, planes):
                slab_plane(layer, which, step).forward()

    def weights_push(layer, which):
        @pl.when(section == layer)
        def _():
            for step in range(1, planes):
                slab_plane(layer, which, step).wait()
                slab_core(layer, which, step).start()

    def weights_wait(layer, which):
        @pl.when(section != layer)
        def _():
            for step in range(planes):
                slab_core(layer, which, step).wait_recv()

    def weights_unsent(layer, which):
        @pl.when(section == layer)
        def _():
            for step in range(1, planes):
                slab_z(layer, which, step).wait_send()
                slab_plane(layer, which, step).sent()
            for step in range(planes):
                slab_core(layer, which, step).wait_send()

    def swap_pair(expert):
        return (
            remote(r.experts_in.at[0, expert], r.other_in.at[expert], r.s_send.at[0, expert], r.s_recv.at[0, expert], partner),
            remote(r.experts_out.at[0, expert], r.other_out.at[expert], r.s_send.at[1, expert], r.s_recv.at[1, expert], partner),
        )

    def load_in(layer, expert):
        mine = pltpu.make_async_copy(r.experts_in.at[0, expert], r.ein.at[expert], r.l_sem.at[0, expert])
        other = pltpu.make_async_copy(r.other_in.at[expert], r.ein.at[expert], r.l_sem.at[0, expert])
        return mine, other

    def load_out(layer, expert):
        target = r.eout.at[pl.ds(expert * FF, FF)]
        mine = pltpu.make_async_copy(r.experts_out.at[0, expert], target, r.l_sem.at[1, expert])
        other = pltpu.make_async_copy(r.other_out.at[expert], target, r.l_sem.at[1, expert])
        return mine, other

    def start_load(make, layer, expert, which, first_use):
        @pl.when(section == layer)
        def _():
            make(layer, expert)[0].start()

        @pl.when(section != layer)
        def _():
            if first_use:
                swap_pair(expert)[which].wait_recv()
            make(layer, expert)[1].start()

    class Spread:
        def __init__(self, source, buffer, index):
            self.copies = [
                remote(source, buffer.at[own], r.a_send.at[index, step], r.a_recv.at[index, step],
                       dict(expert=owner_to(step)))
                for step in range(1, owners)
            ]
            self.source, self.buffer = source, buffer

        def start(self):
            for copy in self.copies:
                copy.start()
            self.buffer[own] = self.source[...]

        def wait(self):
            for copy in self.copies:
                copy.wait_recv()
            unsent.extend(self.copies)

    class Reduce:
        def __init__(self, leaving, coming, index, cuts):
            self.leaving, self.coming, self.index, self.cuts = leaving, coming, index, cuts
            self.copies = {
                (cut, step): remote(
                    leaving.at[step - 1, :, pl.ds(*cuts[cut])],
                    coming.at[step - 1, :, pl.ds(*cuts[cut])],
                    r.r_send.at[index, cut, step],
                    r.r_recv.at[index, cut, step],
                    dict(expert=owner_to(step)),
                )
                for cut in range(len(cuts))
                for step in range(1, owners)
            }

        def put(self, step, columns, values):
            self.leaving[step - 1, :, columns] = values

        def start(self, cut):
            for step in range(1, owners):
                self.copies[cut, step].start()

        def wait(self):
            for copy in self.copies.values():
                copy.wait()

    class Gather:
        def __init__(self, layer, block, around, target, index):
            self.layer, self.block, self.around, self.target, self.index = layer, block, around, target, index

        def across(self, step):
            return [
                remote(
                    self.block,
                    self.target.at[own, (planes - step) % planes, section],
                    r.g_send.at[self.index, step],
                    r.g_recv.at[self.index, step, section],
                    dict(section=self.layer, dp=planes_to(step)),
                )
            ][0]

        def arrival(self, step, micro):
            return remote(
                self.block,
                self.target.at[own, (planes - step) % planes, micro],
                r.g_send.at[self.index, step],
                r.g_recv.at[self.index, step, micro],
                dict(section=self.layer, dp=planes_to(step)),
            )

        def home_local(self):
            return pltpu.make_async_copy(self.around, self.target.at[:, 0, section], r.g_local.at[self.index])

        def home_remote(self, micro):
            return remote(self.around, self.target.at[:, 0, micro], r.g_send.at[self.index, 0],
                          r.g_recv.at[self.index, 0, 0], partner)

        def inside(self):
            def piece(owner, half):
                if half is None:
                    return self.target.at[owner, pl.ds(1, planes - 1)]
                return self.target.at[owner, pl.ds(1, planes - 1), half]

            return Broadcast(piece, r.gp_send.at[self.index], r.gp_recv.at[self.index])

        def whole_to(self, step, micro):
            return remote(
                self.around,
                self.target.at[:, (planes - step) % planes, micro],
                r.g_send.at[self.index, step],
                r.g_recv.at[self.index, step, micro],
                dict(section=self.layer, dp=planes_to(step)),
            )

        def start_whole(self):
            for step in range(1, planes):
                self.whole_to(step, section).start()

        def finish_whole(self):
            for step in range(1, planes):
                self.whole_to(step, section).wait_send()

            @pl.when(section == self.layer)
            def _():
                for step in range(1, planes):
                    for micro in range(2):
                        self.whole_to(step, micro).wait_recv()

            self.finish_home()

        def start(self):
            for step in range(1, planes):
                self.across(step).start()

        def start_home(self):
            @pl.when(section == self.layer)
            def _():
                self.home_local().start()

            @pl.when(section != self.layer)
            def _():
                self.home_remote(section).start()

        def middle(self):
            @pl.when(section == self.layer)
            def _():
                for step in range(1, planes):
                    for micro in range(2):
                        self.arrival(step, micro).wait_recv()
                self.inside().start()

        def forward(self):
            @pl.when(section == self.layer)
            def _():
                self.inside().forward()

        def finish(self):
            for step in range(1, planes):
                self.across(step).wait_send()

            @pl.when(section == self.layer)
            def _():
                self.inside().wait()
                self.inside().sent()

            self.finish_home()

        def finish_home(self):
            @pl.when(section == self.layer)
            def _():
                self.home_local().wait()
                self.home_remote(1 - section).wait_recv()

            @pl.when(section != self.layer)
            def _():
                self.home_remote(section).wait_send()

    lane = lane_of((tokens, LANES))
    low_half = lane % HEAD_SIZE < HALF
    left = lane < HEAD_SIZE
    pair_lane = lane_of((2 * tokens, LANES))
    causal = lax.broadcasted_iota(jnp.int32, (2 * tokens, tokens), 0) % tokens >= lax.broadcasted_iota(
        jnp.int32, (2 * tokens, tokens), 1
    )
    root = HEAD_SIZE ** (-0.5)

    def stack(tile):
        nothing = jnp.zeros_like(tile)
        return jnp.concatenate([jnp.where(left, tile, nothing), jnp.where(left, nothing, tile)], axis=0)

    def attention_forward(layer, source, early, late):
        cosine, sine = r.cosine[...], r.sine[...]
        residual = source[...].astype(F32)
        normed_one = (residual * row_scale(residual) * r.gains[layer, 0:1]).astype(BF16)
        weights_wait(layer, 0)
        early()
        r.projected[:, :QUERY_WIDTH] = dot_nn(normed_one, r.win[layer, :, :QUERY_WIDTH])
        weights_wait(layer, 1)
        r.projected[:, QUERY_WIDTH:] = dot_nn(normed_one, r.win[layer, :, QUERY_WIDTH:])
        for tile in range(QUERY_WIDTH // LANES):
            columns = slice(tile * LANES, (tile + 1) * LANES)
            piece = r.projected[:, columns]
            r.query[layer, :, columns] = (piece * cosine + turned(piece, low_half) * sine).astype(BF16)
        for tile in range(KEY_WIDTH // LANES):
            first = slice(2 * tile * LANES, (2 * tile + 1) * LANES)
            second = slice((2 * tile + 1) * LANES, (2 * tile + 2) * LANES)
            piece = r.projected[:, QUERY_WIDTH + tile * LANES : QUERY_WIDTH + (tile + 1) * LANES]
            piece = piece * cosine + turned(piece, low_half) * sine
            other = pltpu.roll(piece, HEAD_SIZE, 1)
            r.key[layer, :, first] = jnp.where(left, piece, other).astype(BF16)
            r.key[layer, :, second] = jnp.where(left, other, piece).astype(BF16)
            start = QUERY_WIDTH + KEY_WIDTH + tile * LANES
            piece = r.projected[:, start : start + LANES]
            other = pltpu.roll(piece, HEAD_SIZE, 1)
            r.value[layer, :, first] = jnp.where(left, piece, other).astype(BF16)
            r.value[layer, :, second] = jnp.where(left, other, piece).astype(BF16)
        logs = jnp.zeros((2 * tokens, LANES), F32)
        for head in range(KEY_VALUE_HEADS):
            columns = slice(head * LANES, (head + 1) * LANES)
            scores = dot_nt(stack(r.query[layer, :, columns]), r.key[layer, :, columns]) * root
            scores = jnp.where(causal, scores, -1e30)
            top = jnp.max(scores, axis=-1, keepdims=True)
            log_total = top + jnp.log(jnp.sum(jnp.exp(scores - top), axis=-1, keepdims=True))
            logs = jnp.where(pair_lane == head, log_total, logs)
            weights = jnp.exp(scores - log_total).astype(BF16)
            mixed = dot_nn(weights, r.value[layer, :, columns])
            r.attended[layer, :, columns] = jnp.where(left, mixed[:tokens], mixed[tokens:]).astype(BF16)
        r.logs[layer] = logs
        late()
        weights_wait(layer, 2)
        middle = residual + dot_nn(r.attended[layer], r.wout[layer])
        r.middle[layer] = middle
        normed_two = (middle * row_scale(middle) * r.gains[layer, 1:2]).astype(BF16)
        r.packed[layer, :, :MODEL_WIDTH] = normed_two
        logits = jnp.concatenate(
            [dot_nt(normed_two, r.router[layer]), jnp.zeros((tokens, LANES - EXPERTS), F32)], axis=-1
        )
        chosen = r.hot[layer] > 0.0
        top = jnp.max(jnp.where(chosen, logits, -1e30), axis=-1, keepdims=True)
        grown = jnp.where(chosen, jnp.exp(jnp.where(chosen, logits - top, 0.0)), 0.0)
        gates = grown / jnp.sum(grown, axis=-1, keepdims=True)
        r.gates[layer] = gates
        r.packed[layer, :, MODEL_WIDTH:] = two_parts(gates)

    def attention_backward(layer, source, up, back, gate_grads):
        cosine, sine = r.cosine[...], r.sine[...]
        gates = r.gates[layer]
        grad_picked = gates * (gate_grads - jnp.sum(gates * gate_grads, axis=-1, keepdims=True))
        grad_logits = grad_picked.astype(BF16)
        r.small[layer, 16:] = dot_tn(grad_logits, r.packed[layer, :, :MODEL_WIDTH])[:EXPERTS]
        grad_second = back + dot_nn(grad_logits[:, :EXPERTS], r.router[layer])
        middle = r.middle[layer]
        scale_two = row_scale(middle)
        r.small[layer, 1:2] = jnp.sum(grad_second * middle * scale_two, axis=0, keepdims=True)
        grad_middle = up[...].astype(F32) + norm_back(grad_second * r.gains[layer, 1:2], middle, scale_two)
        low = grad_middle.astype(BF16)
        r.low[layer] = low
        r.grad_middle[...] = grad_middle
        r.grad_attended[...] = dot_nt(low, r.wout[layer]).astype(BF16)
        logs = r.logs[layer]
        held = []
        for head in range(KEY_VALUE_HEADS):
            columns = slice(head * LANES, (head + 1) * LANES)
            query = stack(r.query[layer, :, columns])
            key, value = r.key[layer, :, columns], r.value[layer, :, columns]
            scores = dot_nt(query, key) * root
            log_total = jnp.sum(jnp.where(pair_lane == head, logs, 0.0), axis=-1, keepdims=True)
            probabilities = jnp.where(causal, jnp.exp(jnp.where(causal, scores - log_total, 0.0)), 0.0)
            grad_tile = stack(r.grad_attended[:, columns])
            delta = jnp.sum(
                grad_tile.astype(F32) * stack(r.attended[layer, :, columns]).astype(F32), axis=-1, keepdims=True
            )
            grad_scores = (probabilities * (dot_nt(grad_tile, value) - delta)).astype(BF16)
            wide = dot_nn(grad_scores, key) * root
            grad_query = jnp.where(left, wide[:tokens], wide[tokens:])
            grad_query = grad_query * cosine - turned(grad_query, low_half) * sine
            r.projected_grad[layer, :, columns] = grad_query.astype(BF16)
            key_grad = dot_tn(grad_scores, query) * root
            value_grad = dot_tn(probabilities.astype(BF16), grad_tile)
            key_grad = key_grad + pltpu.roll(key_grad, HEAD_SIZE, 1)
            value_grad = value_grad + pltpu.roll(value_grad, HEAD_SIZE, 1)
            if head % 2 == 0:
                held = [key_grad, value_grad]
            else:
                piece = jnp.where(left, held[0], key_grad)
                piece = piece * cosine - turned(piece, low_half) * sine
                start = QUERY_WIDTH + head // 2 * LANES
                r.projected_grad[layer, :, start : start + LANES] = piece.astype(BF16)
                start += KEY_WIDTH
                r.projected_grad[layer, :, start : start + LANES] = jnp.where(left, held[1], value_grad).astype(BF16)
        grad_first = dot_nt(r.projected_grad[layer], r.win[layer])
        residual = source[...].astype(F32)
        scale_one = row_scale(residual)
        normed_one = (residual * scale_one * r.gains[layer, 0:1]).astype(BF16)
        group = MODEL_WIDTH // planes
        for variant in range(group // LANES):
            for step in range(planes):
                start = step * group + variant * LANES
                r.chosen[layer, variant, :, step * LANES : (step + 1) * LANES] = normed_one[:, start : start + LANES]
                r.chosen[layer, variant, :, (planes + step) * LANES : (planes + step + 1) * LANES] = r.attended[
                    layer, :, start : start + LANES
                ]
        r.small[layer, 0:1] = jnp.sum(grad_first * residual * scale_one, axis=0, keepdims=True)
        return (
            r.grad_middle[...] + norm_back(grad_first * r.gains[layer, 0:1], residual, scale_one)
        ).astype(BF16)

    def place_local(source, target, index):
        return pltpu.make_async_copy(source, target.at[section], r.o_local.at[index])

    def place_remote(source, target, index, micro):
        return remote(source, target.at[micro], r.o_send.at[index], r.o_recv.at[index], partner)

    def place(layer, source, target, index):
        @pl.when(section == layer)
        def _():
            place_local(source, target, index).start()

        @pl.when(section != layer)
        def _():
            place_remote(source, target, index, section).start()

    def placed(layer, source, target, index):
        @pl.when(section == layer)
        def _():
            place_local(source, target, index).wait()
            place_remote(source, target, index, 1 - section).wait_recv()

        @pl.when(section != layer)
        def _():
            place_remote(source, target, index, section).wait_send()

    chunk = min(rows, 256)
    chunks = rows // chunk
    half = MODEL_WIDTH // 2

    def each_chunk(work):
        def one(number, carry):
            work(pl.ds(pl.multiple_of(number * chunk, chunk), chunk), pl.ds(number * (chunk // tokens), chunk // tokens))
            return carry

        if chunks == 1:
            work(pl.ds(0, chunk), pl.ds(0, owners))
        else:
            lax.fori_loop(0, chunks, one, 0)

    def flat(buffer, group, columns):
        values = buffer[group, :, columns]
        return values.reshape(chunk, values.shape[-1])

    model, packing = slice(0, MODEL_WIDTH), slice(MODEL_WIDTH, PACKED)

    def expert_columns(expert):
        return pl.ds(pl.multiple_of(expert * FF, FF), FF)

    def wait_in(expert):
        load_in(0, expert)[0].wait()

    def wait_out(expert):
        load_out(0, expert)[0].wait()

    def gate_of(plane_buffer, group, expert):
        return column_of(flat(plane_buffer, group, packing), lane_of((chunk, LANES)), own * local + expert)

    def backward_terms(expert, span, gate, gate_part, up_part, inner):
        sigmoid = 1.0 / (1.0 + jnp.exp(-gate_part))
        silu = gate_part * sigmoid
        activated = silu * up_part
        gate_grad = jnp.sum(activated * inner, axis=-1, keepdims=True)
        lanes = lane_of((chunk, LANES))
        r.gate_total[span] = jnp.where(lanes == own * local + expert, gate_grad, r.gate_total[span])
        grad_activated = inner * gate
        grad_gate = grad_activated * up_part * sigmoid * (1.0 + gate_part * (1.0 - sigmoid))
        grad_up = grad_activated * silu
        grad_pair = jnp.concatenate([grad_gate.astype(BF16), grad_up.astype(BF16)], axis=-1)
        term = dot_nt(grad_pair, r.ein[expert])

        @pl.when(expert == 0)
        def _():
            r.total[span] = term

        @pl.when(expert > 0)
        def _():
            r.total[span] += term

        return activated

    def mix(reduction):
        for cut in range(2):
            columns = slice(cut * half, (cut + 1) * half)

            def work(span, group):
                r.total[span, columns] = dot_nn(r.activated[span], r.eout[:, columns])

            each_chunk(work)
            for step in range(1, owners):
                reduction.put(
                    step, columns, r.total[pl.ds(owner_to(step) * tokens, tokens), columns].astype(BF16)
                )
            reduction.start(cut)

    def mixed(reduction, result):
        for step in range(1, owners):
            result = result + reduction.coming[step - 1].astype(F32)
        return result

    def send_back(reduction):
        for step in range(1, owners):
            span = pl.ds(owner_to(step) * tokens, tokens)
            reduction.put(step, slice(0, MODEL_WIDTH), r.total[span].astype(BF16))
            reduction.put(step, slice(MODEL_WIDTH, PACKED), two_parts(r.gate_total[span]))
        reduction.start(0)

    def came_back(reduction):
        back = r.kept_total[...]
        for step in range(1, owners):
            back = back + reduction.coming[step - 1, :, :MODEL_WIDTH].astype(F32)
        terms = reduction.coming[0, :, MODEL_WIDTH:].astype(F32)
        for step in range(2, owners):
            terms = terms + reduction.coming[step - 1, :, MODEL_WIDTH:].astype(F32)
        return back, r.kept_gate[...] + terms + pltpu.roll(terms, LANES - EXPERTS, 1)

    both_cuts = ((0, half), (half, half))
    spread_x0 = Spread(r.packed.at[0], r.plane0, 0)
    spread_x1 = Spread(r.packed.at[1], r.plane1, 1)
    spread_u1 = Spread(r.up, r.ups1, 2)
    spread_u0 = Spread(r.up0, r.ups0, 3)
    mix0 = Reduce(r.leave_y, r.come_y, 0, both_cuts)
    mix1 = Reduce(r.leave_y, r.come_y, 1, both_cuts)
    back1 = Reduce(r.leave_b, r.come_b, 2, ((0, PACKED),))
    back0 = Reduce(r.leave_b, r.come_b, 3, ((0, PACKED),))
    gather_x0 = Gather(0, r.packed.at[0], r.plane0, r.every_x, 0)
    gather_x1 = Gather(1, r.packed.at[1], r.plane1, r.every_x, 1)
    gather_u0 = Gather(0, r.up0, r.ups0, r.every_u, 2)
    gather_u1 = Gather(1, r.up, r.ups1, r.every_u, 3)
    for which in pieces:
        weights_start(0, which)
    for expert in range(local):
        for copy in swap_pair(expert):
            copy.start()

    @pl.when(section == 0)
    def _():
        for expert in range(local):
            load_in(0, expert)[0].start()
            load_out(0, expert)[0].start()

    r.small[...] = jnp.zeros_like(r.small)
    weights_spread(0, 0)
    weights_spread(0, 1)
    weights_forward(0, 0)
    weights_push(0, 0)
    weights_spread(0, 2)
    weights_forward(0, 1)
    weights_push(0, 1)

    def early0():
        for which in pieces:
            weights_start(1, which)

    def late0():
        weights_forward(0, 2)
        weights_push(0, 2)

    for copy in shared:
        copy.wait()
    for copy in own_rows:
        copy.wait()
    attention_forward(0, r.x, early0, late0)
    spread_x0.start()
    spread_x0.wait()
    for which in pieces:
        weights_spread(1, which)
    spread_u1.start()
    gather_u1.start()
    gather_x0.start_whole()
    gather_x0.start_home()

    def forward_expert(expert, carry):
        @pl.when(section != 0)
        def _():
            for which, make in enumerate((load_in, load_out)):
                swap_pair(expert)[which].wait_recv()
                make(0, expert)[1].start()

        wait_in(expert)

        def work(span, group):
            gate = gate_of(r.plane0, group, expert)
            pair = dot_nn(flat(r.plane0, group, model), r.ein[expert])
            r.pairs[expert, span] = pair.astype(BF16)
            gate_part, up_part = pair[:, :FF], pair[:, FF:]
            silu = gate_part / (1.0 + jnp.exp(-gate_part))
            r.activated[span, expert_columns(expert)] = (silu * up_part * gate).astype(BF16)

        each_chunk(work)
        start_load(load_in, 1, expert, 0, True)
        wait_out(expert)
        return carry

    lax.fori_loop(0, local // 2, forward_expert, 0)
    weights_forward(1, 0)
    weights_forward(1, 1)
    lax.fori_loop(local // 2, local, forward_expert, 0)
    mix(mix0)
    weights_forward(1, 2)
    weights_push(1, 0)
    weights_push(1, 1)
    for expert in range(local):
        start_load(load_out, 1, expert, 1, True)
    spread_u1.wait()
    gather_u1.start_home()
    mix0.wait()
    r.hidden0[...] = (r.middle[0] + mixed(mix0, r.total[here])).astype(BF16)
    place(0, r.hidden0, r.hidden, 0)

    def late1():
        weights_push(1, 2)

    attention_forward(1, r.hidden0, lambda: None, late1)
    spread_x1.start()

    def inner_expert(expert, carry):
        wait_out(expert)

        def work(span, group):
            r.inner[span, expert_columns(expert)] = dot_nt(
                flat(r.ups1, group, model), r.eout[expert_columns(expert)]
            ).astype(r.inner.dtype)

        each_chunk(work)
        return carry

    lax.fori_loop(0, local, inner_expert, 0)
    spread_x1.wait()
    gather_u1.middle()
    gather_x1.start()
    gather_x1.start_home()
    r.gate_total[...] = jnp.zeros_like(r.gate_total)

    def both_expert(expert, carry):
        wait_in(expert)

        def work(span, group):
            gate = gate_of(r.plane1, group, expert)
            pair = dot_nn(flat(r.plane1, group, model), r.ein[expert])
            inner = r.inner[span, expert_columns(expert)].astype(F32)
            activated = backward_terms(expert, span, gate, pair[:, :FF], pair[:, FF:], inner)
            r.activated[span, expert_columns(expert)] = (activated * gate).astype(BF16)

        each_chunk(work)
        start_load(load_in, 0, expert, 0, False)
        return carry

    lax.fori_loop(0, local // 2, both_expert, 0)
    gather_u1.forward()
    lax.fori_loop(local // 2, local, both_expert, 0)
    send_back(back1)
    r.kept_total[...] = r.total[here]
    r.kept_gate[...] = r.gate_total[here]
    mix(mix1)
    for expert in range(local):
        start_load(load_out, 0, expert, 1, False)
    back1.wait()
    back, gate_grads = came_back(back1)
    r.up0[...] = attention_backward(1, r.hidden0, r.up, back, gate_grads)
    spread_u0.start()
    place(1, r.up0, r.input_grad, 1)
    mix1.wait()
    r.hidden1[...] = (r.middle[1] + mixed(mix1, r.total[here])).astype(BF16)
    place(1, r.hidden1, r.hidden, 2)
    r.gate_total[...] = jnp.zeros_like(r.gate_total)
    spread_u0.wait()
    gather_x1.middle()
    gather_u0.start()
    gather_u0.start_home()

    def behind_expert(expert, carry):
        wait_in(expert)
        wait_out(expert)

        def work(span, group):
            gate = gate_of(r.plane0, group, expert)
            pair = r.pairs[expert, span].astype(F32)
            inner = dot_nt(flat(r.ups0, group, model), r.eout[expert_columns(expert)])
            backward_terms(expert, span, gate, pair[:, :FF], pair[:, FF:], inner)

        each_chunk(work)
        return carry

    lax.fori_loop(0, local // 2, behind_expert, 0)
    gather_x1.forward()
    lax.fori_loop(local // 2, local, behind_expert, 0)
    send_back(back0)
    r.kept_total[...] = r.total[here]
    r.kept_gate[...] = r.gate_total[here]
    back0.wait()
    gather_u0.middle()
    back, gate_grads = came_back(back0)
    r.grad0[...] = attention_backward(0, r.x, r.up0, back, gate_grads)
    place(0, r.grad0, r.input_grad, 3)
    gather_u0.forward()

    for layer in range(2):
        for which in pieces:
            weights_unsent(layer, which)
    for expert in range(local):
        for copy in swap_pair(expert):
            copy.wait_send()
    for copy in unsent:
        copy.wait_send()
    placed(0, r.hidden0, r.hidden, 0)
    placed(1, r.up0, r.input_grad, 1)
    placed(1, r.hidden1, r.hidden, 2)
    placed(0, r.grad0, r.input_grad, 3)
    gather_x0.finish_whole()
    for gather in (gather_u1, gather_x1, gather_u0):
        gather.finish()


def both_layers(layer_input, cotangent, routes, gain_one, attn_in, attn_out, gain_two, router, cosine, sine,
                experts_in, experts_out):
    planes, owners = lax.axis_size("dp"), lax.axis_size("expert")
    tokens = layer_input.shape[1]
    local = experts_in.shape[1]
    slab = attn_in.shape[1]
    rows = owners * tokens
    dma = lambda *shape: pltpu.SemaphoreType.DMA(shape)
    vmem = lambda shape, dtype: pltpu.VMEM(shape, dtype)
    wide = (2, tokens, MODEL_WIDTH)
    everywhere = (owners, planes, 2, tokens)
    inputs = dict(
        layer_input=(layer_input, any_spec()),
        cotangent=(cotangent, any_spec()),
        routes=(jnp.swapaxes(routes, 2, 3), vmem_spec()),
        gain_one=(gain_one, vmem_spec()),
        gain_two=(gain_two, vmem_spec()),
        router_in=(jnp.swapaxes(router, 1, 2), vmem_spec()),
        attn_in=(attn_in, any_spec()),
        attn_out=(attn_out, any_spec()),
        cosine=(cosine, vmem_spec()),
        sine=(sine, vmem_spec()),
        experts_in=(experts_in, any_spec()),
        experts_out=(experts_out, any_spec()),
    )
    outputs = dict(
        hidden=(wide, BF16, any_spec()),
        input_grad=(wide, BF16, any_spec()),
        other_in=(experts_in.shape[1:], BF16, any_spec()),
        other_out=(experts_out.shape[1:], BF16, any_spec()),
        every_x=(everywhere + (PACKED,), BF16, any_spec()),
        every_u=(everywhere + (MODEL_WIDTH,), BF16, any_spec()),
        projected_grad=((2, tokens, PROJECTED), BF16, vmem_spec()),
        low=(wide, BF16, vmem_spec()),
        chosen=(
            (2, MODEL_WIDTH // planes // LANES, tokens, 2 * planes * LANES), BF16, vmem_spec()
        ),
        small=((2, 16 + EXPERTS, MODEL_WIDTH), F32, vmem_spec()),
    )
    scratch = dict(
        win=vmem((2, MODEL_WIDTH, PROJECTED), BF16),
        wout=vmem((2, QUERY_WIDTH, MODEL_WIDTH), BF16),
        ein=vmem((local, MODEL_WIDTH, 2 * FF), BF16),
        eout=vmem((local * FF, MODEL_WIDTH), BF16),
        x=vmem(wide[1:], BF16),
        up=vmem(wide[1:], BF16),
        gains=vmem((2, 8, MODEL_WIDTH), F32),
        router=vmem((2, EXPERTS, MODEL_WIDTH), BF16),
        hot=vmem((2, tokens, LANES), F32),
        hot_out=vmem((tokens, LANES), F32),
        i_sem=dma(2),
        h_send=dma(3),
        h_recv=dma(3),
        projected=vmem((tokens, PROJECTED), F32),
        query=vmem(wide, BF16),
        key=vmem(wide, BF16),
        value=vmem(wide, BF16),
        attended=vmem(wide, BF16),
        logs=vmem((2, 2 * tokens, LANES), F32),
        middle=vmem(wide, F32),
        packed=vmem((2, tokens, PACKED), BF16),
        gates=vmem((2, tokens, LANES), F32),
        up0=vmem(wide[1:], BF16),
        hidden0=vmem(wide[1:], BF16),
        hidden1=vmem(wide[1:], BF16),
        grad0=vmem(wide[1:], BF16),
        grad_middle=vmem(wide[1:], F32),
        grad_attended=vmem(wide[1:], BF16),
        plane0=vmem((owners, tokens, PACKED), BF16),
        plane1=vmem((owners, tokens, PACKED), BF16),
        ups0=vmem((owners, tokens, MODEL_WIDTH), BF16),
        ups1=vmem((owners, tokens, MODEL_WIDTH), BF16),
        pairs=vmem((local, rows, 2 * FF), BF16),
        inner=vmem((rows, local * FF), BF16),
        activated=vmem((rows, local * FF), BF16),
        total=vmem((rows, MODEL_WIDTH), F32),
        gate_total=vmem((rows, LANES), F32),
        kept_total=vmem((tokens, MODEL_WIDTH), F32),
        kept_gate=vmem((tokens, LANES), F32),
        leave_y=vmem((owners - 1, tokens, MODEL_WIDTH), BF16),
        come_y=vmem((owners - 1, tokens, MODEL_WIDTH), BF16),
        leave_b=vmem((owners - 1, tokens, PACKED), BF16),
        come_b=vmem((owners - 1, tokens, PACKED), BF16),
        w_local=dma(2, 3),
        wz_send=dma(2, 3, planes),
        wz_recv=dma(2, 3, planes),
        wp_send=dma(2, 3, planes, owners),
        wp_recv=dma(2, 3, planes, owners),
        wc_send=dma(2, 3, planes),
        wc_recv=dma(2, 3, planes),
        s_send=dma(2, local),
        s_recv=dma(2, local),
        l_sem=dma(2, local),
        a_send=dma(4, owners),
        a_recv=dma(4, owners),
        r_send=dma(4, 2, owners),
        r_recv=dma(4, 2, owners),
        g_send=dma(4, planes),
        g_recv=dma(4, planes, 2),
        g_local=dma(4),
        gp_send=dma(4, owners),
        gp_recv=dma(4, owners),
        o_send=dma(4),
        o_recv=dma(4),
        o_local=dma(4),
    )
    return call(
        functools.partial(layers_kernel, planes, owners, tokens, local, slab),
        "both_layers", 0, inputs, outputs, scratch,
    )


def ExpertGrads(planes, owners, tokens, local, first, r):
    plane = lax.axis_index("dp")
    own = lax.axis_index("expert")
    group = 4 * tokens
    slots = group // 2
    groups = 2 * planes * owners * tokens // group
    slice_in, slice_out = MODEL_WIDTH // planes, FF // planes
    chunk = min(groups * slots, 1024)
    chunks = groups * slots // chunk
    tile = 512
    depth = r.x_rows.shape[0]
    shift = first if r.grad_in.shape[0] < local else 0

    def weights_of(expert):
        slot = expert % 2
        return (
            pltpu.make_async_copy(r.experts_in.at[0, expert], r.ein.at[slot], r.e_sem.at[0, slot]),
            pltpu.make_async_copy(r.experts_out.at[0, expert], r.eout.at[slot], r.e_sem.at[1, slot]),
        )

    def rows_of(number):
        slot = number % depth
        span = pl.ds(pl.multiple_of(number * group, group), group)
        return (
            pltpu.make_async_copy(r.every_x.at[span], r.x_rows.at[slot], r.t_sem.at[0, slot]),
            pltpu.make_async_copy(r.every_u.at[span], r.u_rows.at[slot], r.t_sem.at[1, slot]),
        )

    pack = r.compact_x.shape[0]
    bunch = r.picks.shape[0] // slots
    before = (
        lax.broadcasted_iota(jnp.int32, (group, group), 0) < lax.broadcasted_iota(jnp.int32, (group, group), 1)
    ).astype(BF16)
    same = (
        lax.broadcasted_iota(jnp.int32, (group, group), 0) == lax.broadcasted_iota(jnp.int32, (group, group), 1)
    ).astype(BF16)
    numbers = lax.broadcasted_iota(jnp.int32, (slots, group), 0).astype(F32)

    def gather():
        def one(number, carry):
            slot = number % depth
            for copy in rows_of(number):
                copy.wait()

            @pl.when(number + depth - 1 < groups)
            def _():
                for copy in rows_of(number + depth - 1):
                    copy.start()

            parts = r.x_rows[slot, :, MODEL_WIDTH:].astype(F32)
            chosen = (parts != 0.0).astype(BF16)
            rank = dot_tn(chosen, before)
            r.ranks[...] = jnp.where(dot_tn(chosen, same) > 0.0, rank, -1.0)
            span = pl.ds(pl.multiple_of(number * slots, slots), slots)
            for low in range(0, pack, bunch):
                few = min(bunch, pack - low)
                for index in range(few):
                    rank_row = r.ranks[pl.ds(own * local + first + low + index, 1), :]
                    r.picks[index * slots : (index + 1) * slots, :] = (numbers == rank_row).astype(BF16)
                for source, target in ((r.x_rows, r.compact_x), (r.u_rows, r.compact_u)):
                    found = dot_nn(r.picks[: few * slots], source[slot]).astype(BF16)
                    for index in range(few):
                        target[low + index, span] = found[index * slots : (index + 1) * slots]
            return carry

        lax.fori_loop(0, groups, one, 0)

    def out_of(expert):
        slot = expert % 2
        return (
            pltpu.make_async_copy(r.din.at[slot], r.grad_in.at[expert - shift], r.d_sem.at[0, slot]),
            pltpu.make_async_copy(r.dout.at[slot], r.grad_out.at[expert - shift], r.d_sem.at[1, slot]),
        )

    def one_expert(expert, index):
        slot = expert % 2
        for copy in weights_of(expert):
            copy.wait()

        @pl.when(expert + 1 < first + pack)
        def _():
            for copy in weights_of(expert + 1):
                copy.start()

        @pl.when(expert >= first + 2)
        def _():
            for copy in out_of(expert - 2):
                copy.wait()

        for number in range(chunks):

            def one_tile(step, carry):
                span = pl.ds(pl.multiple_of(number * chunk + step * tile, tile), tile)
                here = pl.ds(pl.multiple_of(step * tile, tile), tile)
                gate = column_of(
                    r.compact_x[index, span, MODEL_WIDTH:], lane_of((tile, LANES)), own * local + expert
                )
                pair = dot_nn(r.compact_x[index, span, :MODEL_WIDTH], r.ein[slot])
                gate_part, up_part = pair[:, :FF], pair[:, FF:]
                sigmoid = 1.0 / (1.0 + jnp.exp(-gate_part))
                silu = gate_part * sigmoid
                r.activated[here] = (silu * up_part * gate).astype(BF16)
                grad_activated = dot_nt(r.compact_u[index, span], r.eout[slot]) * gate
                r.grad_pair[here, :FF] = (
                    grad_activated * up_part * sigmoid * (1.0 + gate_part * (1.0 - sigmoid))
                ).astype(BF16)
                r.grad_pair[here, FF:] = (grad_activated * silu).astype(BF16)
                return carry

            lax.fori_loop(0, chunk // tile, one_tile, 0)
            rows = slice(number * chunk, (number + 1) * chunk)
            left_in = r.compact_x[index, rows, pl.ds(pl.multiple_of(plane * slice_in, LANES), slice_in)]
            left_out = r.activated[:, pl.ds(pl.multiple_of(plane * slice_out, LANES), slice_out)]
            term_in = dot_tn(left_in, r.grad_pair[...])
            term_out = dot_tn(left_out, r.compact_u[index, rows])
            if number == 0:
                r.din[slot] = term_in
                r.dout[slot] = term_out
            else:
                r.din[slot] += term_in
                r.dout[slot] += term_out
        for copy in out_of(expert):
            copy.start()

    def run(low, high):
        def body(index, carry):
            one_expert(first + index, index)
            return carry

        if high > low:
            lax.fori_loop(low, high, body, 0)

    def start():
        for number in range(min(depth - 1, groups)):
            for copy in rows_of(number):
                copy.start()
        for copy in weights_of(first):
            copy.start()

    def finish():
        for expert in range(max(first, first + pack - 2), first + pack):
            for copy in out_of(expert):
                copy.wait()

    names = Names()
    names.load, names.gather, names.run, names.finish, names.pack = start, gather, run, finish, pack
    return names


def gradients_kernel(planes, owners, tokens, local, r):
    section = lax.axis_index("section")
    plane = lax.axis_index("dp")
    own = lax.axis_index("expert")
    partner = dict(section=1 - section)
    part = MODEL_WIDTH // (planes * owners)
    barrier = pltpu.get_barrier_semaphore()
    for step in range(1, owners):
        pl.semaphore_signal(barrier, inc=1, device_id=dict(expert=(own + step) % owners), device_id_type=MESH)
    for step in range(1, planes):
        pl.semaphore_signal(barrier, inc=1, device_id=dict(dp=(plane + step) % planes), device_id_type=MESH)
    pl.semaphore_signal(barrier, inc=1, device_id=partner, device_id_type=MESH)

    experts = ExpertGrads(planes, owners, tokens, local, 0, r)
    experts.load()

    def meet(source, target, index):
        here = pltpu.make_async_copy(source.at[section], target.at[section], r.m_local.at[index])
        there = remote(source.at[1 - section], target.at[section], r.m_send.at[index], r.m_recv.at[index], partner)
        return here, there

    meets = [
        meet(r.low, r.all_low.at[own], 0),
        meet(r.chosen, r.both_chosen, 1),
        meet(r.small, r.both_small, 2),
        meet(r.projected_grad, r.all_projected.at[own], 3),
    ]
    pl.semaphore_wait(barrier, owners - 1 + planes - 1 + 1)
    for here, there in meets:
        here.start()
        there.start()

    def piece_of(buffer):
        return lambda owner, half: buffer.at[owner] if half is None else buffer.at[owner, half]

    spreads = (
        PlaneBroadcast(owners, own, piece_of(r.all_low), r.f_send.at[0], r.f_recv.at[0]),
        PlaneBroadcast(owners, own, piece_of(r.all_projected), r.f_send.at[1], r.f_recv.at[1]),
    )
    width = planes * LANES

    def variant_of(owner):
        return owner * part // LANES

    def chosen_to(step, which):
        target = (own + step) % owners
        columns = pl.ds((1 - which) * width, width)
        return remote(
            r.both_chosen.at[:, variant_of(target), :, columns], r.all_chosen.at[own, :, :, columns],
            r.c_send.at[which, step], r.c_recv.at[which, step], dict(expert=target),
        )

    def small_to(step):
        return remote(
            r.small_out, r.small_in.at[step - 1], r.v_send.at[step], r.v_recv.at[step],
            dict(expert=(own + step) % owners),
        )

    halves = (
        (r.all_low, r.product_out, r.sums, r.leaving_out),
        (r.all_projected, r.product_in, r.partial, None),
    )

    def sums_over(step):
        return remote(
            r.leaving_out.at[step - 1], r.arriving_out.at[step - 1], r.z_send.at[step], r.z_recv.at[step],
            dict(dp=(plane + step) % planes),
        )

    def attention_start():
        for here, there in meets:
            here.wait()
            there.wait_recv()
        r.small_kept[...] = r.both_small[0] + r.both_small[1]
        r.small_out[...] = r.small_kept[...].astype(BF16)
        for step in range(1, owners):
            small_to(step).start()
        for which in range(2):
            spreads[which].start()
            for step in range(1, owners):
                chosen_to(step, which).start()
        r.all_chosen[own] = r.both_chosen[:, variant_of(own)]

    def attention_small():
        total = r.small_kept[...]
        for step in range(1, owners):
            small_to(step).wait_recv()
            total = total + r.small_in[step - 1].astype(F32)
        r.sums[part:] = total
        for step in range(1, planes):
            r.leaving_out[step - 1, part:] = total.astype(BF16)

    def attention_partial(which):
        factors, product, partial, leaving = halves[which]
        spreads[which].wait()
        for step in range(1, owners):
            chosen_to(step, which).wait_recv()
        within = own * part % LANES
        some = min(owners, 4)
        pile = some * 2 * tokens
        for step in list(range(1, planes)) + [0]:
            target = (plane + step) % planes
            columns = pl.ds(pl.multiple_of(((1 - which) * planes + target) * LANES, LANES), LANES)
            for first in range(0, owners, some):
                left = r.all_chosen[first : first + some, :, :, columns].reshape(pile, LANES)
                term = dot_tn(left, factors[first : first + some].reshape(pile, factors.shape[-1]))
                if first == 0:
                    product[...] = term
                else:
                    product[...] += term
            mine = product[pl.ds(pl.multiple_of(within, 16), part)]
            if step == 0:
                partial[:part] = mine
            else:
                if which == 0:
                    leaving[step - 1, :part] = mine.astype(BF16)
                    sums_over(step).start()
                else:
                    getattr(r, f"to{step}")[...] = mine.astype(BF16)

    def attention_last():
        total = r.sums[...]
        for step in range(1, planes):
            sums_over(step).wait()
            total = total + r.arriving_out[step - 1].astype(F32)
        r.sums[...] = total
        for here, there in meets:
            there.wait_send()
        for which in range(2):
            spreads[which].sent()
            for step in range(1, owners):
                chosen_to(step, which).wait_send()
        for step in range(1, owners):
            small_to(step).wait_send()

    attention_start()
    experts.gather()
    pack = experts.pack
    experts.run(0, pack // 6)
    attention_small()
    spreads[0].forward()
    experts.run(pack // 6, 2 * pack // 6)
    spreads[1].forward()
    experts.run(2 * pack // 6, 4 * pack // 6)
    attention_partial(0)
    experts.run(4 * pack // 6, pack)
    experts.finish()
    attention_partial(1)
    attention_last()


def rest_kernel(planes, owners, tokens, local, first, r):
    experts = ExpertGrads(planes, owners, tokens, local, first, r)
    experts.load()
    held = ((r.first_in, r.held_in, r.grad_in), (r.first_out, r.held_out, r.grad_out))
    entering = [
        pltpu.make_async_copy(source, here, r.move_sem.at[0, index]) for index, (source, here, _) in enumerate(held)
    ]
    moving = [
        pltpu.make_async_copy(here, target.at[pl.ds(0, first)], r.move_sem.at[1, index])
        for index, (_, here, target) in enumerate(held)
    ]
    for copy in entering:
        copy.start()
    r.grad_attn_out[...] = r.sums[: r.grad_attn_out.shape[0]]
    r.hidden_out[...] = r.hidden[...]
    r.input_grad_out[...] = r.input_grad[...]
    experts.gather()
    for number in range(2):
        entering[number].wait()
        moving[number].start()
    experts.run(0, experts.pack)
    experts.finish()
    for copy in moving:
        copy.wait()


def grads_scratch(planes, owners, tokens, pack):
    group = 4 * tokens
    groups = 2 * planes * owners * tokens // group
    slots = group // 2
    chunk = min(groups * slots, 1024)
    dma = lambda *shape: pltpu.SemaphoreType.DMA(shape)
    vmem = lambda shape, dtype: pltpu.VMEM(shape, dtype)
    return dict(
        ein=vmem((2, MODEL_WIDTH, 2 * FF), BF16),
        eout=vmem((2, FF, MODEL_WIDTH), BF16),
        x_rows=vmem((4, group, PACKED), BF16),
        u_rows=vmem((4, group, MODEL_WIDTH), BF16),
        ranks=vmem((LANES, group), F32),
        picks=vmem((min(pack, 5) * slots, group), BF16),
        compact_x=vmem((pack, groups * slots, PACKED), BF16),
        compact_u=vmem((pack, groups * slots, MODEL_WIDTH), BF16),
        activated=vmem((chunk, FF), BF16),
        grad_pair=vmem((chunk, 2 * FF), BF16),
        din=vmem((2, MODEL_WIDTH // planes, 2 * FF), F32),
        dout=vmem((2, FF // planes, MODEL_WIDTH), F32),
        e_sem=dma(2, 2),
        t_sem=dma(2, 4),
        d_sem=dma(2, 2),
    )


def weight_gradients(done, experts_in, experts_out):
    planes, owners = lax.axis_size("dp"), lax.axis_size("expert")
    local = experts_in.shape[1]
    tokens = done.low.shape[1]
    part = MODEL_WIDTH // (planes * owners)
    first = max(1, 6 * local // 8)
    wide = 2 * planes * LANES
    variants = done.chosen.shape[1]
    small = done.small.shape[1:]
    dma = lambda *shape: pltpu.SemaphoreType.DMA(shape)
    vmem = lambda shape, dtype: pltpu.VMEM(shape, dtype)
    shape_in, shape_out = (MODEL_WIDTH // planes, 2 * FF), (FF // planes, MODEL_WIDTH)
    tables = dict(
        every_x=(done.every_x.reshape(-1, PACKED), any_spec()),
        every_u=(done.every_u.reshape(-1, MODEL_WIDTH), any_spec()),
        experts_in=(experts_in, any_spec()),
        experts_out=(experts_out, any_spec()),
    )
    exchanged = call(
        functools.partial(gradients_kernel, planes, owners, tokens, local),
        "weight_gradients",
        1,
        dict(
            projected_grad=(done.projected_grad, vmem_spec()),
            low=(done.low, vmem_spec()),
            chosen=(done.chosen, vmem_spec()),
            small=(done.small, vmem_spec()),
            **tables,
        ),
        dict(
            grad_in=((first,) + shape_in, F32, any_spec()),
            grad_out=((first,) + shape_out, F32, any_spec()),
            partial=((part, PROJECTED), F32, vmem_spec()),
            sums=((part + small[0], MODEL_WIDTH), F32, vmem_spec()),
            **{f"to{step}": ((part, PROJECTED), BF16, vmem_spec()) for step in range(1, planes)},
        ),
        dict(
            all_low=vmem((owners, 2, tokens, MODEL_WIDTH), BF16),
            all_projected=vmem((owners, 2, tokens, PROJECTED), BF16),
            both_chosen=vmem((2, variants, tokens, wide), BF16),
            all_chosen=vmem((owners, 2, tokens, wide), BF16),
            both_small=vmem((2,) + small, F32),
            small_kept=vmem(small, F32),
            small_out=vmem(small, BF16),
            small_in=vmem((owners - 1,) + small, BF16),
            product_in=vmem((LANES, PROJECTED), F32),
            product_out=vmem((LANES, MODEL_WIDTH), F32),
            leaving_out=vmem((planes - 1, part + small[0], MODEL_WIDTH), BF16),
            arriving_out=vmem((planes - 1, part + small[0], MODEL_WIDTH), BF16),
            z_send=dma(planes),
            z_recv=dma(planes),
            m_local=dma(4),
            m_send=dma(4),
            m_recv=dma(4),
            f_send=dma(2, owners),
            f_recv=dma(2, owners),
            c_send=dma(2, owners),
            c_recv=dma(2, owners),
            v_send=dma(owners),
            v_recv=dma(owners),
            **grads_scratch(planes, owners, tokens, first),
        ),
    )
    total = exchanged.partial
    arriving = [
        lax.ppermute(getattr(exchanged, f"to{step}"), "dp", [(i, (i + step) % planes) for i in range(planes)])
        for step in range(1, planes)
    ]
    count = local - first
    rows = 2 * planes * owners * tokens
    rest = call(
        functools.partial(rest_kernel, planes, owners, tokens, local, first),
        "other_experts",
        None,
        dict(
            first_in=(exchanged.grad_in, any_spec()),
            first_out=(exchanged.grad_out, any_spec()),
            sums=(exchanged.sums, vmem_spec()),
            hidden=(done.hidden, vmem_spec()),
            input_grad=(done.input_grad, vmem_spec()),
            **tables,
        ),
        dict(
            grad_in=((local,) + shape_in, F32, any_spec()),
            grad_out=((local,) + shape_out, F32, any_spec()),
            grad_attn_out=((part, MODEL_WIDTH), F32, vmem_spec()),
            hidden_out=(done.hidden.shape, BF16, vmem_spec()),
            input_grad_out=(done.hidden.shape, BF16, vmem_spec()),
        ),
        dict(
            held_in=vmem((first,) + shape_in, F32),
            held_out=vmem((first,) + shape_out, F32),
            move_sem=dma(2, 2),
            **grads_scratch(planes, owners, tokens, count),
        ),
        pl.CostEstimate(flops=count * rows * 6 * MODEL_WIDTH * FF, bytes_accessed=rows * 4 * MODEL_WIDTH, transcendentals=0),
    )
    arriving, rest.grad_in = lax.optimization_barrier((arriving, rest.grad_in))
    for piece in arriving:
        total = total + piece.astype(F32)
    sums = exchanged.sums
    return rest, total, sums[part : part + 1], sums[part + 1 : part + 2], sums[part + 16 :].T


def shards(layer_input, cotangent, positions, routes, gain_one, attn_in, attn_out, gain_two, router,
           experts_in, experts_out):
    place = lax.dynamic_index_in_dim(positions, lax.axis_index("section"), 0, keepdims=False)
    lane = jnp.arange(LANES)
    frequency = jnp.power(rotary_base, -((lane % HALF).astype(F32) * (2.0 / HEAD_SIZE)))
    angles = place.astype(F32)[:, None] * frequency[None, :]
    cosine = jnp.cos(angles)
    sine = jnp.where(lane % HEAD_SIZE < HALF, -1.0, 1.0) * jnp.sin(angles)

    done = both_layers(
        layer_input, cotangent, routes, gain_one, attn_in, attn_out, gain_two, router, cosine, sine,
        experts_in, experts_out,
    )
    rest, grad_attn_in, grad_gain_one, grad_gain_two, grad_router = weight_gradients(done, experts_in, experts_out)
    return (
        rest.hidden_out[None],
        rest.input_grad_out[None],
        grad_gain_one,
        grad_attn_in[None],
        rest.grad_attn_out[None],
        grad_gain_two,
        grad_router[None],
        rest.grad_in[None],
        rest.grad_out[None],
    )


def solution(mesh):
    in_specs = (
        P(None, ("dp", "expert"), None),
        P(None, ("dp", "expert"), None),
        P(None, ("dp", "expert")),
        P("section", None, ("dp", "expert"), None),
        P("section", None),
        P("section", "dp", None),
        P("section", "dp", None),
        P("section", None),
        P("section", None, None),
        P("section", "expert", None, None),
        P("section", "expert", None, None),
    )
    out_specs = (
        P("section", None, ("dp", "expert"), None),
        P("section", None, ("dp", "expert"), None),
        P("section", None),
        P("section", ("dp", "expert"), None),
        P("section", ("dp", "expert"), None),
        P("section", None),
        P("section", None, None),
        P("section", "expert", "dp", None),
        P("section", "expert", "dp", None),
    )
    return jax.shard_map(shards, mesh=mesh, in_specs=in_specs, out_specs=out_specs, check_vma=False)
```

```python
import functools

import jax
import jax.numpy as jnp
from jax import lax
from jax.experimental import pallas as pl
from jax.experimental.pallas import tpu as pltpu
from jax.sharding import PartitionSpec as P

MODEL_WIDTH = 1024
QUERY_HEADS = 16
KEY_VALUE_HEADS = 8
HEAD_SIZE = 64
FF = 512
EXPERTS = 32
TOPK = 8

QUERY_WIDTH = QUERY_HEADS * HEAD_SIZE
KEY_WIDTH = KEY_VALUE_HEADS * HEAD_SIZE
PROJECTED = QUERY_WIDTH + 2 * KEY_WIDTH
LANES = 128
HALF = HEAD_SIZE // 2
PACKED = MODEL_WIDTH + LANES

epsilon = 1e-06
rotary_base = 10000.0

F32 = jnp.float32
BF16 = jnp.bfloat16
MESH = pl.DeviceIdType.MESH
VMEM_LIMIT = 62 * 1024 * 1024


def dot_nn(a, b):
    return lax.dot_general(a, b, (((1,), (0,)), ((), ())), preferred_element_type=F32)


def dot_nt(a, b):
    return lax.dot_general(a, b, (((1,), (1,)), ((), ())), preferred_element_type=F32)


def dot_tn(a, b):
    return lax.dot_general(a, b, (((0,), (0,)), ((), ())), preferred_element_type=F32)


def row_scale(values):
    return lax.rsqrt(jnp.mean(values * values, axis=-1, keepdims=True) + epsilon)


def norm_back(grad_normed, inputs, scale):
    return scale * grad_normed - inputs * (scale * scale * scale) * jnp.mean(
        grad_normed * inputs, axis=-1, keepdims=True
    )


def lane_of(shape):
    return lax.broadcasted_iota(jnp.int32, shape, 1)


def turned(tile, low):
    return jnp.where(low, pltpu.roll(tile, LANES - HALF, 1), pltpu.roll(tile, HALF, 1))


def two_parts(values):
    high = values.astype(BF16).astype(F32)
    return (high + pltpu.roll(values - high, EXPERTS, 1)).astype(BF16)


def column_of(parts, lane, column):
    wide = parts.astype(F32)
    return jnp.sum(jnp.where((lane == column) | (lane == column + EXPERTS), wide, 0.0), axis=-1, keepdims=True)


def remote(source, target, send, recv, device):
    return pltpu.make_async_remote_copy(
        src_ref=source, dst_ref=target, send_sem=send, recv_sem=recv, device_id=device, device_id_type=MESH
    )


def vmem_spec():
    return pl.BlockSpec(memory_space=pltpu.VMEM)


def any_spec():
    return pl.BlockSpec(memory_space=pl.ANY)


class Names:
    pass


def call(kernel, name, number, inputs, outputs, scratch, cost=None):
    labels = list(inputs) + list(outputs) + list(scratch)

    def body(*refs):
        names = Names()
        for label, ref in zip(labels, refs):
            setattr(names, label, ref)
        kernel(names)

    if number is None:
        params = pltpu.CompilerParams(vmem_limit_bytes=VMEM_LIMIT)
    else:
        params = pltpu.CompilerParams(
            collective_id=number, has_side_effects=True, vmem_limit_bytes=VMEM_LIMIT
        )
    results = pl.pallas_call(
        body,
        out_shape=tuple(jax.ShapeDtypeStruct(shape, dtype) for shape, dtype, _ in outputs.values()),
        in_specs=[spec for _, spec in inputs.values()],
        out_specs=tuple(spec for _, _, spec in outputs.values()),
        scratch_shapes=list(scratch.values()),
        compiler_params=params,
        cost_estimate=cost,
        name=name,
    )(*[array for array, _ in inputs.values()])
    names = Names()
    for label, result in zip(outputs, results):
        setattr(names, label, result)
    return names


class PlaneBroadcast:
    def __init__(self, owners, own, piece, send, recv):
        self.owners, self.own = owners, own
        self.square = owners == 4
        self.piece, self.send, self.recv = piece, send, recv

    def hop(self, owner, half, index, device):
        block = self.piece(owner, half)
        return remote(block, block, self.send.at[index], self.recv.at[index], dict(expert=device))

    def hops(self):
        owners, own = self.owners, self.own

        def owner_to(step):
            return (own + step) % owners

        if not self.square:
            return [self.hop(own, None, turn, owner_to(turn)) for turn in range(1, owners)]
        beside = own + 1 - 2 * (own % 2)
        above = owner_to(2)
        return [
            self.hop(own, None, 0, beside),
            self.hop(own, None, 1, above),
            self.hop(beside, 0, 2, above),
            self.hop(above, 1, 3, beside),
        ]

    def start(self):
        hops = self.hops()
        for hop in hops[:2] if self.square else hops:
            hop.start()

    def forward(self):
        if self.square:
            hops = self.hops()
            for hop in range(2):
                hops[hop].wait_recv()
                hops[2 + hop].start()

    def wait(self):
        hops = self.hops()
        for hop in hops[2:] if self.square else hops:
            hop.wait_recv()

    def sent(self):
        for hop in self.hops():
            hop.wait_send()


def layers_kernel(planes, owners, tokens, local, slab, r):
    section = lax.axis_index("section")
    plane = lax.axis_index("dp")
    own = lax.axis_index("expert")
    rows = owners * tokens
    part = slab // owners
    here = pl.ds(own * tokens, tokens)
    partner = dict(section=1 - section)

    def planes_to(step):
        return (plane + step) % planes

    def owner_to(step):
        return (own + step) % owners

    barrier = pltpu.get_barrier_semaphore()
    for step in range(1, owners):
        pl.semaphore_signal(barrier, inc=1, device_id=dict(expert=owner_to(step)), device_id_type=MESH)
    for step in range(1, planes):
        for target in range(2):
            pl.semaphore_signal(
                barrier, inc=1, device_id=dict(section=target, dp=planes_to(step)), device_id_type=MESH
            )
    pl.semaphore_signal(barrier, inc=1, device_id=partner, device_id_type=MESH)
    pl.semaphore_wait(barrier, owners - 1 + 2 * (planes - 1) + 1)

    unsent = []

    own_rows = [
        pltpu.make_async_copy(r.layer_input.at[section], r.x, r.i_sem.at[0]),
        pltpu.make_async_copy(r.cotangent.at[section], r.up, r.i_sem.at[1]),
    ]
    for copy in own_rows:
        copy.start()

    unit = (
        lax.broadcasted_iota(jnp.int32, (EXPERTS, LANES), 0) == lax.broadcasted_iota(jnp.int32, (EXPERTS, LANES), 1)
    ).astype(BF16)

    def hot_of(choices):
        number = lax.broadcasted_iota(jnp.int32, (EXPERTS, tokens), 0)
        found = jnp.zeros((EXPERTS, tokens), F32)
        for choice in range(TOPK):
            found = jnp.where(number == choices[choice : choice + 1], 1.0, found)
        return dot_tn(found.astype(BF16), unit)

    r.gains[section, 0:1] = r.gain_one[...]
    r.gains[section, 1:2] = r.gain_two[...]
    r.router[section] = r.router_in[0]
    r.hot[section] = hot_of(r.routes[0, section])
    r.hot_out[...] = hot_of(r.routes[0, 1 - section])
    shared = [
        remote(source, target, r.h_send.at[index], r.h_recv.at[index], partner)
        for index, (source, target) in enumerate(
            (
                (r.gains.at[section], r.gains.at[section]),
                (r.router.at[section], r.router.at[section]),
                (r.hot_out, r.hot.at[section]),
            )
        )
    ]
    for copy in shared:
        copy.start()

    def Broadcast(piece, send, recv):
        return PlaneBroadcast(owners, own, piece, send, recv)

    weight_pieces = ((r.attn_in, r.win, 0), (r.attn_in, r.win, QUERY_WIDTH), (r.attn_out, r.wout, 0))
    pieces = range(len(weight_pieces))

    def slab_local(layer, which):
        source, full, column = weight_pieces[which]
        columns = pl.ds(column, MODEL_WIDTH)
        return pltpu.make_async_copy(
            source.at[0, :, columns], full.at[layer, pl.ds(plane * slab, slab), columns], r.w_local.at[layer, which]
        )

    def slab_z(layer, which, step):
        source, full, column = weight_pieces[which]
        columns = pl.ds(column, MODEL_WIDTH)
        return remote(
            source.at[0, pl.ds(own * part, part), columns],
            full.at[layer, pl.ds(plane * slab + own * part, part), columns],
            r.wz_send.at[layer, which, step],
            r.wz_recv.at[layer, which, step],
            dict(dp=planes_to(step)),
        )

    def slab_plane(layer, which, step):
        full, column = weight_pieces[which][1:]
        origin = planes_to(planes - step)

        def piece(owner, half):
            start, length = origin * slab + owner * part, part
            if half is not None:
                length = part // 2
                start = start + half * length
            return full.at[layer, pl.ds(start, length), pl.ds(column, MODEL_WIDTH)]

        return Broadcast(piece, r.wp_send.at[layer, which, step], r.wp_recv.at[layer, which, step])

    def slab_core(layer, which, step):
        full, column = weight_pieces[which][1:]
        block = full.at[layer, pl.ds(planes_to(planes - step) * slab, slab), pl.ds(column, MODEL_WIDTH)]
        return remote(block, block, r.wc_send.at[layer, which, step], r.wc_recv.at[layer, which, step], partner)

    def weights_start(layer, which):
        @pl.when(section == layer)
        def _():
            for step in range(1, planes):
                slab_z(layer, which, step).start()
            slab_local(layer, which).start()

    def weights_spread(layer, which):
        @pl.when(section == layer)
        def _():
            slab_local(layer, which).wait()
            slab_core(layer, which, 0).start()
            for step in range(1, planes):
                slab_z(layer, which, step).wait_recv()
                slab_plane(layer, which, step).start()

    def weights_forward(layer, which):
        @pl.when(section == layer)
        def _():
            for step in range(1, planes):
                slab_plane(layer, which, step).forward()

    def weights_push(layer, which):
        @pl.when(section == layer)
        def _():
            for step in range(1, planes):
                slab_plane(layer, which, step).wait()
                slab_core(layer, which, step).start()

    def weights_wait(layer, which):
        @pl.when(section != layer)
        def _():
            for step in range(planes):
                slab_core(layer, which, step).wait_recv()

    def weights_unsent(layer, which):
        @pl.when(section == layer)
        def _():
            for step in range(1, planes):
                slab_z(layer, which, step).wait_send()
                slab_plane(layer, which, step).sent()
            for step in range(planes):
                slab_core(layer, which, step).wait_send()

    def swap_pair(expert):
        return (
            remote(r.experts_in.at[0, expert], r.other_in.at[expert], r.s_send.at[0, expert], r.s_recv.at[0, expert], partner),
            remote(r.experts_out.at[0, expert], r.other_out.at[expert], r.s_send.at[1, expert], r.s_recv.at[1, expert], partner),
        )

    def load_in(layer, expert):
        mine = pltpu.make_async_copy(r.experts_in.at[0, expert], r.ein.at[expert], r.l_sem.at[0, expert])
        other = pltpu.make_async_copy(r.other_in.at[expert], r.ein.at[expert], r.l_sem.at[0, expert])
        return mine, other

    def load_out(layer, expert):
        target = r.eout.at[pl.ds(expert * FF, FF)]
        mine = pltpu.make_async_copy(r.experts_out.at[0, expert], target, r.l_sem.at[1, expert])
        other = pltpu.make_async_copy(r.other_out.at[expert], target, r.l_sem.at[1, expert])
        return mine, other

    def start_load(make, layer, expert, which, first_use):
        @pl.when(section == layer)
        def _():
            make(layer, expert)[0].start()

        @pl.when(section != layer)
        def _():
            if first_use:
                swap_pair(expert)[which].wait_recv()
            make(layer, expert)[1].start()

    class Spread:
        def __init__(self, source, buffer, index):
            self.copies = [
                remote(source, buffer.at[own], r.a_send.at[index, step], r.a_recv.at[index, step],
                       dict(expert=owner_to(step)))
                for step in range(1, owners)
            ]
            self.source, self.buffer = source, buffer

        def start(self):
            for copy in self.copies:
                copy.start()
            self.buffer[own] = self.source[...]

        def wait(self):
            for copy in self.copies:
                copy.wait_recv()
            unsent.extend(self.copies)

    class Reduce:
        def __init__(self, leaving, coming, index, cuts):
            self.leaving, self.coming, self.index, self.cuts = leaving, coming, index, cuts
            self.copies = {
                (cut, step): remote(
                    leaving.at[step - 1, :, pl.ds(*cuts[cut])],
                    coming.at[step - 1, :, pl.ds(*cuts[cut])],
                    r.r_send.at[index, cut, step],
                    r.r_recv.at[index, cut, step],
                    dict(expert=owner_to(step)),
                )
                for cut in range(len(cuts))
                for step in range(1, owners)
            }

        def put(self, step, columns, values):
            self.leaving[step - 1, :, columns] = values

        def start(self, cut):
            for step in range(1, owners):
                self.copies[cut, step].start()

        def wait(self):
            for copy in self.copies.values():
                copy.wait()

    class Gather:
        def __init__(self, layer, block, around, target, index):
            self.layer, self.block, self.around, self.target, self.index = layer, block, around, target, index

        def across(self, step):
            return [
                remote(
                    self.block,
                    self.target.at[own, (planes - step) % planes, section],
                    r.g_send.at[self.index, step],
                    r.g_recv.at[self.index, step, section],
                    dict(section=self.layer, dp=planes_to(step)),
                )
            ][0]

        def arrival(self, step, micro):
            return remote(
                self.block,
                self.target.at[own, (planes - step) % planes, micro],
                r.g_send.at[self.index, step],
                r.g_recv.at[self.index, step, micro],
                dict(section=self.layer, dp=planes_to(step)),
            )

        def home_local(self):
            return pltpu.make_async_copy(self.around, self.target.at[:, 0, section], r.g_local.at[self.index])

        def home_remote(self, micro):
            return remote(self.around, self.target.at[:, 0, micro], r.g_send.at[self.index, 0],
                          r.g_recv.at[self.index, 0, 0], partner)

        def inside(self):
            def piece(owner, half):
                if half is None:
                    return self.target.at[owner, pl.ds(1, planes - 1)]
                return self.target.at[owner, pl.ds(1, planes - 1), half]

            return Broadcast(piece, r.gp_send.at[self.index], r.gp_recv.at[self.index])

        def whole_to(self, step, micro):
            return remote(
                self.around,
                self.target.at[:, (planes - step) % planes, micro],
                r.g_send.at[self.index, step],
                r.g_recv.at[self.index, step, micro],
                dict(section=self.layer, dp=planes_to(step)),
            )

        def start_whole(self):
            for step in range(1, planes):
                self.whole_to(step, section).start()

        def finish_whole(self):
            for step in range(1, planes):
                self.whole_to(step, section).wait_send()

            @pl.when(section == self.layer)
            def _():
                for step in range(1, planes):
                    for micro in range(2):
                        self.whole_to(step, micro).wait_recv()

            self.finish_home()

        def start(self):
            for step in range(1, planes):
                self.across(step).start()

        def start_home(self):
            @pl.when(section == self.layer)
            def _():
                self.home_local().start()

            @pl.when(section != self.layer)
            def _():
                self.home_remote(section).start()

        def middle(self):
            @pl.when(section == self.layer)
            def _():
                for step in range(1, planes):
                    for micro in range(2):
                        self.arrival(step, micro).wait_recv()
                self.inside().start()

        def forward(self):
            @pl.when(section == self.layer)
            def _():
                self.inside().forward()

        def finish(self):
            for step in range(1, planes):
                self.across(step).wait_send()

            @pl.when(section == self.layer)
            def _():
                self.inside().wait()
                self.inside().sent()

            self.finish_home()

        def finish_home(self):
            @pl.when(section == self.layer)
            def _():
                self.home_local().wait()
                self.home_remote(1 - section).wait_recv()

            @pl.when(section != self.layer)
            def _():
                self.home_remote(section).wait_send()

    lane = lane_of((tokens, LANES))
    low_half = lane % HEAD_SIZE < HALF
    left = lane < HEAD_SIZE
    pair_lane = lane_of((2 * tokens, LANES))
    causal = lax.broadcasted_iota(jnp.int32, (2 * tokens, tokens), 0) % tokens >= lax.broadcasted_iota(
        jnp.int32, (2 * tokens, tokens), 1
    )
    root = HEAD_SIZE ** (-0.5)

    def stack(tile):
        nothing = jnp.zeros_like(tile)
        return jnp.concatenate([jnp.where(left, tile, nothing), jnp.where(left, nothing, tile)], axis=0)

    def attention_forward(layer, source, early, late):
        cosine, sine = r.cosine[...], r.sine[...]
        residual = source[...].astype(F32)
        normed_one = (residual * row_scale(residual) * r.gains[layer, 0:1]).astype(BF16)
        weights_wait(layer, 0)
        early()
        r.projected[:, :QUERY_WIDTH] = dot_nn(normed_one, r.win[layer, :, :QUERY_WIDTH])
        weights_wait(layer, 1)
        r.projected[:, QUERY_WIDTH:] = dot_nn(normed_one, r.win[layer, :, QUERY_WIDTH:])
        for tile in range(QUERY_WIDTH // LANES):
            columns = slice(tile * LANES, (tile + 1) * LANES)
            piece = r.projected[:, columns]
            r.query[layer, :, columns] = (piece * cosine + turned(piece, low_half) * sine).astype(BF16)
        for tile in range(KEY_WIDTH // LANES):
            first = slice(2 * tile * LANES, (2 * tile + 1) * LANES)
            second = slice((2 * tile + 1) * LANES, (2 * tile + 2) * LANES)
            piece = r.projected[:, QUERY_WIDTH + tile * LANES : QUERY_WIDTH + (tile + 1) * LANES]
            piece = piece * cosine + turned(piece, low_half) * sine
            other = pltpu.roll(piece, HEAD_SIZE, 1)
            r.key[layer, :, first] = jnp.where(left, piece, other).astype(BF16)
            r.key[layer, :, second] = jnp.where(left, other, piece).astype(BF16)
            start = QUERY_WIDTH + KEY_WIDTH + tile * LANES
            piece = r.projected[:, start : start + LANES]
            other = pltpu.roll(piece, HEAD_SIZE, 1)
            r.value[layer, :, first] = jnp.where(left, piece, other).astype(BF16)
            r.value[layer, :, second] = jnp.where(left, other, piece).astype(BF16)
        logs = jnp.zeros((2 * tokens, LANES), F32)
        for head in range(KEY_VALUE_HEADS):
            columns = slice(head * LANES, (head + 1) * LANES)
            scores = dot_nt(stack(r.query[layer, :, columns]), r.key[layer, :, columns]) * root
            scores = jnp.where(causal, scores, -1e30)
            top = jnp.max(scores, axis=-1, keepdims=True)
            log_total = top + jnp.log(jnp.sum(jnp.exp(scores - top), axis=-1, keepdims=True))
            logs = jnp.where(pair_lane == head, log_total, logs)
            weights = jnp.exp(scores - log_total).astype(BF16)
            mixed = dot_nn(weights, r.value[layer, :, columns])
            r.attended[layer, :, columns] = jnp.where(left, mixed[:tokens], mixed[tokens:]).astype(BF16)
        r.logs[layer] = logs
        late()
        weights_wait(layer, 2)
        middle = residual + dot_nn(r.attended[layer], r.wout[layer])
        r.middle[layer] = middle
        normed_two = (middle * row_scale(middle) * r.gains[layer, 1:2]).astype(BF16)
        r.packed[layer, :, :MODEL_WIDTH] = normed_two
        logits = jnp.concatenate(
            [dot_nt(normed_two, r.router[layer]), jnp.zeros((tokens, LANES - EXPERTS), F32)], axis=-1
        )
        chosen = r.hot[layer] > 0.0
        top = jnp.max(jnp.where(chosen, logits, -1e30), axis=-1, keepdims=True)
        grown = jnp.where(chosen, jnp.exp(jnp.where(chosen, logits - top, 0.0)), 0.0)
        gates = grown / jnp.sum(grown, axis=-1, keepdims=True)
        r.gates[layer] = gates
        r.packed[layer, :, MODEL_WIDTH:] = two_parts(gates)

    def attention_backward(layer, source, up, back, gate_grads):
        cosine, sine = r.cosine[...], r.sine[...]
        gates = r.gates[layer]
        grad_picked = gates * (gate_grads - jnp.sum(gates * gate_grads, axis=-1, keepdims=True))
        grad_logits = grad_picked.astype(BF16)
        r.small[layer, 16:] = dot_tn(grad_logits, r.packed[layer, :, :MODEL_WIDTH])[:EXPERTS]
        grad_second = back + dot_nn(grad_logits[:, :EXPERTS], r.router[layer])
        middle = r.middle[layer]
        scale_two = row_scale(middle)
        r.small[layer, 1:2] = jnp.sum(grad_second * middle * scale_two, axis=0, keepdims=True)
        grad_middle = up[...].astype(F32) + norm_back(grad_second * r.gains[layer, 1:2], middle, scale_two)
        low = grad_middle.astype(BF16)
        r.low[layer] = low
        r.grad_middle[...] = grad_middle
        r.grad_attended[...] = dot_nt(low, r.wout[layer]).astype(BF16)
        logs = r.logs[layer]
        held = []
        for head in range(KEY_VALUE_HEADS):
            columns = slice(head * LANES, (head + 1) * LANES)
            query = stack(r.query[layer, :, columns])
            key, value = r.key[layer, :, columns], r.value[layer, :, columns]
            scores = dot_nt(query, key) * root
            log_total = jnp.sum(jnp.where(pair_lane == head, logs, 0.0), axis=-1, keepdims=True)
            probabilities = jnp.where(causal, jnp.exp(jnp.where(causal, scores - log_total, 0.0)), 0.0)
            grad_tile = stack(r.grad_attended[:, columns])
            delta = jnp.sum(
                grad_tile.astype(F32) * stack(r.attended[layer, :, columns]).astype(F32), axis=-1, keepdims=True
            )
            grad_scores = (probabilities * (dot_nt(grad_tile, value) - delta)).astype(BF16)
            wide = dot_nn(grad_scores, key) * root
            grad_query = jnp.where(left, wide[:tokens], wide[tokens:])
            grad_query = grad_query * cosine - turned(grad_query, low_half) * sine
            r.projected_grad[layer, :, columns] = grad_query.astype(BF16)
            key_grad = dot_tn(grad_scores, query) * root
            value_grad = dot_tn(probabilities.astype(BF16), grad_tile)
            key_grad = key_grad + pltpu.roll(key_grad, HEAD_SIZE, 1)
            value_grad = value_grad + pltpu.roll(value_grad, HEAD_SIZE, 1)
            if head % 2 == 0:
                held = [key_grad, value_grad]
            else:
                piece = jnp.where(left, held[0], key_grad)
                piece = piece * cosine - turned(piece, low_half) * sine
                start = QUERY_WIDTH + head // 2 * LANES
                r.projected_grad[layer, :, start : start + LANES] = piece.astype(BF16)
                start += KEY_WIDTH
                r.projected_grad[layer, :, start : start + LANES] = jnp.where(left, held[1], value_grad).astype(BF16)
        grad_first = dot_nt(r.projected_grad[layer], r.win[layer])
        residual = source[...].astype(F32)
        scale_one = row_scale(residual)
        normed_one = (residual * scale_one * r.gains[layer, 0:1]).astype(BF16)
        group = MODEL_WIDTH // planes
        for variant in range(group // LANES):
            for step in range(planes):
                start = step * group + variant * LANES
                r.chosen[layer, variant, :, step * LANES : (step + 1) * LANES] = normed_one[:, start : start + LANES]
                r.chosen[layer, variant, :, (planes + step) * LANES : (planes + step + 1) * LANES] = r.attended[
                    layer, :, start : start + LANES
                ]
        r.small[layer, 0:1] = jnp.sum(grad_first * residual * scale_one, axis=0, keepdims=True)
        return (
            r.grad_middle[...] + norm_back(grad_first * r.gains[layer, 0:1], residual, scale_one)
        ).astype(BF16)

    def place_local(source, target, index):
        return pltpu.make_async_copy(source, target.at[section], r.o_local.at[index])

    def place_remote(source, target, index, micro):
        return remote(source, target.at[micro], r.o_send.at[index], r.o_recv.at[index], partner)

    def place(layer, source, target, index):
        @pl.when(section == layer)
        def _():
            place_local(source, target, index).start()

        @pl.when(section != layer)
        def _():
            place_remote(source, target, index, section).start()

    def placed(layer, source, target, index):
        @pl.when(section == layer)
        def _():
            place_local(source, target, index).wait()
            place_remote(source, target, index, 1 - section).wait_recv()

        @pl.when(section != layer)
        def _():
            place_remote(source, target, index, section).wait_send()

    chunk = min(rows, 256)
    chunks = rows // chunk
    half = MODEL_WIDTH // 2

    def each_chunk(work):
        def one(number, carry):
            work(pl.ds(pl.multiple_of(number * chunk, chunk), chunk), pl.ds(number * (chunk // tokens), chunk // tokens))
            return carry

        if chunks == 1:
            work(pl.ds(0, chunk), pl.ds(0, owners))
        else:
            lax.fori_loop(0, chunks, one, 0)

    def flat(buffer, group, columns):
        values = buffer[group, :, columns]
        return values.reshape(chunk, values.shape[-1])

    model, packing = slice(0, MODEL_WIDTH), slice(MODEL_WIDTH, PACKED)

    def expert_columns(expert):
        return pl.ds(pl.multiple_of(expert * FF, FF), FF)

    def wait_in(expert):
        load_in(0, expert)[0].wait()

    def wait_out(expert):
        load_out(0, expert)[0].wait()

    def gate_of(plane_buffer, group, expert):
        return column_of(flat(plane_buffer, group, packing), lane_of((chunk, LANES)), own * local + expert)

    def backward_terms(expert, span, gate, gate_part, up_part, inner):
        sigmoid = 1.0 / (1.0 + jnp.exp(-gate_part))
        silu = gate_part * sigmoid
        activated = silu * up_part
        gate_grad = jnp.sum(activated * inner, axis=-1, keepdims=True)
        lanes = lane_of((chunk, LANES))
        r.gate_total[span] = jnp.where(lanes == own * local + expert, gate_grad, r.gate_total[span])
        grad_activated = inner * gate
        grad_gate = grad_activated * up_part * sigmoid * (1.0 + gate_part * (1.0 - sigmoid))
        grad_up = grad_activated * silu
        grad_pair = jnp.concatenate([grad_gate.astype(BF16), grad_up.astype(BF16)], axis=-1)
        term = dot_nt(grad_pair, r.ein[expert])

        @pl.when(expert == 0)
        def _():
            r.total[span] = term

        @pl.when(expert > 0)
        def _():
            r.total[span] += term

        return activated

    def mix(reduction):
        for cut in range(2):
            columns = slice(cut * half, (cut + 1) * half)

            def work(span, group):
                r.total[span, columns] = dot_nn(r.activated[span], r.eout[:, columns])

            each_chunk(work)
            for step in range(1, owners):
                reduction.put(
                    step, columns, r.total[pl.ds(owner_to(step) * tokens, tokens), columns].astype(BF16)
                )
            reduction.start(cut)

    def mixed(reduction, result):
        for step in range(1, owners):
            result = result + reduction.coming[step - 1].astype(F32)
        return result

    def send_back(reduction):
        for step in range(1, owners):
            span = pl.ds(owner_to(step) * tokens, tokens)
            reduction.put(step, slice(0, MODEL_WIDTH), r.total[span].astype(BF16))
            reduction.put(step, slice(MODEL_WIDTH, PACKED), two_parts(r.gate_total[span]))
        reduction.start(0)

    def came_back(reduction):
        back = r.kept_total[...]
        for step in range(1, owners):
            back = back + reduction.coming[step - 1, :, :MODEL_WIDTH].astype(F32)
        terms = reduction.coming[0, :, MODEL_WIDTH:].astype(F32)
        for step in range(2, owners):
            terms = terms + reduction.coming[step - 1, :, MODEL_WIDTH:].astype(F32)
        return back, r.kept_gate[...] + terms + pltpu.roll(terms, LANES - EXPERTS, 1)

    both_cuts = ((0, half), (half, half))
    spread_x0 = Spread(r.packed.at[0], r.plane0, 0)
    spread_x1 = Spread(r.packed.at[1], r.plane1, 1)
    spread_u1 = Spread(r.up, r.ups1, 2)
    spread_u0 = Spread(r.up0, r.ups0, 3)
    mix0 = Reduce(r.leave_y, r.come_y, 0, both_cuts)
    mix1 = Reduce(r.leave_y, r.come_y, 1, both_cuts)
    back1 = Reduce(r.leave_b, r.come_b, 2, ((0, PACKED),))
    back0 = Reduce(r.leave_b, r.come_b, 3, ((0, PACKED),))
    gather_x0 = Gather(0, r.packed.at[0], r.plane0, r.every_x, 0)
    gather_x1 = Gather(1, r.packed.at[1], r.plane1, r.every_x, 1)
    gather_u0 = Gather(0, r.up0, r.ups0, r.every_u, 2)
    gather_u1 = Gather(1, r.up, r.ups1, r.every_u, 3)
    for which in pieces:
        weights_start(0, which)
    for expert in range(local):
        for copy in swap_pair(expert):
            copy.start()

    @pl.when(section == 0)
    def _():
        for expert in range(local):
            load_in(0, expert)[0].start()
            load_out(0, expert)[0].start()

    r.small[...] = jnp.zeros_like(r.small)
    weights_spread(0, 0)
    weights_spread(0, 1)
    weights_forward(0, 0)
    weights_push(0, 0)
    weights_spread(0, 2)
    weights_forward(0, 1)
    weights_push(0, 1)

    def early0():
        for which in pieces:
            weights_start(1, which)

    def late0():
        weights_forward(0, 2)
        weights_push(0, 2)

    for copy in shared:
        copy.wait()
    for copy in own_rows:
        copy.wait()
    attention_forward(0, r.x, early0, late0)
    spread_x0.start()
    spread_x0.wait()
    for which in pieces:
        weights_spread(1, which)
    spread_u1.start()
    gather_u1.start()
    gather_x0.start_whole()
    gather_x0.start_home()

    def forward_expert(expert, carry):
        @pl.when(section != 0)
        def _():
            for which, make in enumerate((load_in, load_out)):
                swap_pair(expert)[which].wait_recv()
                make(0, expert)[1].start()

        wait_in(expert)

        def work(span, group):
            gate = gate_of(r.plane0, group, expert)
            pair = dot_nn(flat(r.plane0, group, model), r.ein[expert])
            r.pairs[expert, span] = pair.astype(BF16)
            gate_part, up_part = pair[:, :FF], pair[:, FF:]
            silu = gate_part / (1.0 + jnp.exp(-gate_part))
            r.activated[span, expert_columns(expert)] = (silu * up_part * gate).astype(BF16)

        each_chunk(work)
        start_load(load_in, 1, expert, 0, True)
        wait_out(expert)
        return carry

    lax.fori_loop(0, local // 2, forward_expert, 0)
    weights_forward(1, 0)
    weights_forward(1, 1)
    lax.fori_loop(local // 2, local, forward_expert, 0)
    mix(mix0)
    weights_forward(1, 2)
    weights_push(1, 0)
    weights_push(1, 1)
    for expert in range(local):
        start_load(load_out, 1, expert, 1, True)
    spread_u1.wait()
    gather_u1.start_home()
    mix0.wait()
    r.hidden0[...] = (r.middle[0] + mixed(mix0, r.total[here])).astype(BF16)
    place(0, r.hidden0, r.hidden, 0)

    def late1():
        weights_push(1, 2)

    attention_forward(1, r.hidden0, lambda: None, late1)
    spread_x1.start()
    gather_x1.start()

    def inner_expert(expert, carry):
        wait_out(expert)

        def work(span, group):
            r.inner[span, expert_columns(expert)] = dot_nt(
                flat(r.ups1, group, model), r.eout[expert_columns(expert)]
            ).astype(r.inner.dtype)

        each_chunk(work)
        return carry

    lax.fori_loop(0, local, inner_expert, 0)
    spread_x1.wait()
    gather_u1.middle()
    gather_x1.start_home()
    r.gate_total[...] = jnp.zeros_like(r.gate_total)

    def both_expert(expert, carry):
        wait_in(expert)

        def work(span, group):
            gate = gate_of(r.plane1, group, expert)
            pair = dot_nn(flat(r.plane1, group, model), r.ein[expert])
            inner = r.inner[span, expert_columns(expert)].astype(F32)
            activated = backward_terms(expert, span, gate, pair[:, :FF], pair[:, FF:], inner)
            r.activated[span, expert_columns(expert)] = (activated * gate).astype(BF16)

        each_chunk(work)
        start_load(load_in, 0, expert, 0, False)
        return carry

    lax.fori_loop(0, local // 2, both_expert, 0)
    gather_u1.forward()
    lax.fori_loop(local // 2, local, both_expert, 0)
    send_back(back1)
    r.kept_total[...] = r.total[here]
    r.kept_gate[...] = r.gate_total[here]
    mix(mix1)
    for expert in range(local):
        start_load(load_out, 0, expert, 1, False)
    back1.wait()
    back, gate_grads = came_back(back1)
    r.up0[...] = attention_backward(1, r.hidden0, r.up, back, gate_grads)
    spread_u0.start()
    gather_u0.start()
    place(1, r.up0, r.input_grad, 1)
    mix1.wait()
    r.hidden1[...] = (r.middle[1] + mixed(mix1, r.total[here])).astype(BF16)
    place(1, r.hidden1, r.hidden, 2)
    r.gate_total[...] = jnp.zeros_like(r.gate_total)
    spread_u0.wait()
    gather_x1.middle()
    gather_u0.start_home()

    def behind_expert(expert, carry):
        wait_in(expert)
        wait_out(expert)

        def work(span, group):
            gate = gate_of(r.plane0, group, expert)
            pair = r.pairs[expert, span].astype(F32)
            inner = dot_nt(flat(r.ups0, group, model), r.eout[expert_columns(expert)])
            backward_terms(expert, span, gate, pair[:, :FF], pair[:, FF:], inner)

        each_chunk(work)
        return carry

    lax.fori_loop(0, local // 2, behind_expert, 0)
    gather_x1.forward()
    gather_u0.middle()
    lax.fori_loop(local // 2, local, behind_expert, 0)
    send_back(back0)
    r.kept_total[...] = r.total[here]
    r.kept_gate[...] = r.gate_total[here]
    back0.wait()
    gather_u0.forward()
    back, gate_grads = came_back(back0)
    r.grad0[...] = attention_backward(0, r.x, r.up0, back, gate_grads)
    place(0, r.grad0, r.input_grad, 3)

    for layer in range(2):
        for which in pieces:
            weights_unsent(layer, which)
    for expert in range(local):
        for copy in swap_pair(expert):
            copy.wait_send()
    for copy in unsent:
        copy.wait_send()
    placed(0, r.hidden0, r.hidden, 0)
    placed(1, r.up0, r.input_grad, 1)
    placed(1, r.hidden1, r.hidden, 2)
    placed(0, r.grad0, r.input_grad, 3)
    gather_x0.finish_whole()
    for gather in (gather_u1, gather_x1, gather_u0):
        gather.finish()


def both_layers(layer_input, cotangent, routes, gain_one, attn_in, attn_out, gain_two, router, cosine, sine,
                experts_in, experts_out):
    planes, owners = lax.axis_size("dp"), lax.axis_size("expert")
    tokens = layer_input.shape[1]
    local = experts_in.shape[1]
    slab = attn_in.shape[1]
    rows = owners * tokens
    dma = lambda *shape: pltpu.SemaphoreType.DMA(shape)
    vmem = lambda shape, dtype: pltpu.VMEM(shape, dtype)
    wide = (2, tokens, MODEL_WIDTH)
    everywhere = (owners, planes, 2, tokens)
    inputs = dict(
        layer_input=(layer_input, any_spec()),
        cotangent=(cotangent, any_spec()),
        routes=(jnp.swapaxes(routes, 2, 3), vmem_spec()),
        gain_one=(gain_one, vmem_spec()),
        gain_two=(gain_two, vmem_spec()),
        router_in=(jnp.swapaxes(router, 1, 2), vmem_spec()),
        attn_in=(attn_in, any_spec()),
        attn_out=(attn_out, any_spec()),
        cosine=(cosine, vmem_spec()),
        sine=(sine, vmem_spec()),
        experts_in=(experts_in, any_spec()),
        experts_out=(experts_out, any_spec()),
    )
    outputs = dict(
        hidden=(wide, BF16, any_spec()),
        input_grad=(wide, BF16, any_spec()),
        other_in=(experts_in.shape[1:], BF16, any_spec()),
        other_out=(experts_out.shape[1:], BF16, any_spec()),
        every_x=(everywhere + (PACKED,), BF16, any_spec()),
        every_u=(everywhere + (MODEL_WIDTH,), BF16, any_spec()),
        projected_grad=((2, tokens, PROJECTED), BF16, vmem_spec()),
        low=(wide, BF16, vmem_spec()),
        chosen=(
            (2, MODEL_WIDTH // planes // LANES, tokens, 2 * planes * LANES), BF16, vmem_spec()
        ),
        small=((2, 16 + EXPERTS, MODEL_WIDTH), F32, vmem_spec()),
    )
    scratch = dict(
        win=vmem((2, MODEL_WIDTH, PROJECTED), BF16),
        wout=vmem((2, QUERY_WIDTH, MODEL_WIDTH), BF16),
        ein=vmem((local, MODEL_WIDTH, 2 * FF), BF16),
        eout=vmem((local * FF, MODEL_WIDTH), BF16),
        x=vmem(wide[1:], BF16),
        up=vmem(wide[1:], BF16),
        gains=vmem((2, 8, MODEL_WIDTH), F32),
        router=vmem((2, EXPERTS, MODEL_WIDTH), BF16),
        hot=vmem((2, tokens, LANES), F32),
        hot_out=vmem((tokens, LANES), F32),
        i_sem=dma(2),
        h_send=dma(3),
        h_recv=dma(3),
        projected=vmem((tokens, PROJECTED), F32),
        query=vmem(wide, BF16),
        key=vmem(wide, BF16),
        value=vmem(wide, BF16),
        attended=vmem(wide, BF16),
        logs=vmem((2, 2 * tokens, LANES), F32),
        middle=vmem(wide, F32),
        packed=vmem((2, tokens, PACKED), BF16),
        gates=vmem((2, tokens, LANES), F32),
        up0=vmem(wide[1:], BF16),
        hidden0=vmem(wide[1:], BF16),
        hidden1=vmem(wide[1:], BF16),
        grad0=vmem(wide[1:], BF16),
        grad_middle=vmem(wide[1:], F32),
        grad_attended=vmem(wide[1:], BF16),
        plane0=vmem((owners, tokens, PACKED), BF16),
        plane1=vmem((owners, tokens, PACKED), BF16),
        ups0=vmem((owners, tokens, MODEL_WIDTH), BF16),
        ups1=vmem((owners, tokens, MODEL_WIDTH), BF16),
        pairs=vmem((local, rows, 2 * FF), BF16),
        inner=vmem((rows, local * FF), BF16),
        activated=vmem((rows, local * FF), BF16),
        total=vmem((rows, MODEL_WIDTH), F32),
        gate_total=vmem((rows, LANES), F32),
        kept_total=vmem((tokens, MODEL_WIDTH), F32),
        kept_gate=vmem((tokens, LANES), F32),
        leave_y=vmem((owners - 1, tokens, MODEL_WIDTH), BF16),
        come_y=vmem((owners - 1, tokens, MODEL_WIDTH), BF16),
        leave_b=vmem((owners - 1, tokens, PACKED), BF16),
        come_b=vmem((owners - 1, tokens, PACKED), BF16),
        w_local=dma(2, 3),
        wz_send=dma(2, 3, planes),
        wz_recv=dma(2, 3, planes),
        wp_send=dma(2, 3, planes, owners),
        wp_recv=dma(2, 3, planes, owners),
        wc_send=dma(2, 3, planes),
        wc_recv=dma(2, 3, planes),
        s_send=dma(2, local),
        s_recv=dma(2, local),
        l_sem=dma(2, local),
        a_send=dma(4, owners),
        a_recv=dma(4, owners),
        r_send=dma(4, 2, owners),
        r_recv=dma(4, 2, owners),
        g_send=dma(4, planes),
        g_recv=dma(4, planes, 2),
        g_local=dma(4),
        gp_send=dma(4, owners),
        gp_recv=dma(4, owners),
        o_send=dma(4),
        o_recv=dma(4),
        o_local=dma(4),
    )
    return call(
        functools.partial(layers_kernel, planes, owners, tokens, local, slab),
        "both_layers", 0, inputs, outputs, scratch,
    )


def ExpertGrads(planes, owners, tokens, local, first, r):
    plane = lax.axis_index("dp")
    own = lax.axis_index("expert")
    group = 4 * tokens
    slots = group // 2
    groups = 2 * planes * owners * tokens // group
    slice_in, slice_out = MODEL_WIDTH // planes, FF // planes
    chunk = min(groups * slots, 1024)
    chunks = groups * slots // chunk
    tile = 512
    depth = r.x_rows.shape[0]
    shift = first if r.grad_in.shape[0] < local else 0

    def weights_of(expert):
        slot = expert % 2
        return (
            pltpu.make_async_copy(r.experts_in.at[0, expert], r.ein.at[slot], r.e_sem.at[0, slot]),
            pltpu.make_async_copy(r.experts_out.at[0, expert], r.eout.at[slot], r.e_sem.at[1, slot]),
        )

    def rows_of(number):
        slot = number % depth
        span = pl.ds(pl.multiple_of(number * group, group), group)
        return (
            pltpu.make_async_copy(r.every_x.at[span], r.x_rows.at[slot], r.t_sem.at[0, slot]),
            pltpu.make_async_copy(r.every_u.at[span], r.u_rows.at[slot], r.t_sem.at[1, slot]),
        )

    pack = r.compact_x.shape[0]
    bunch = r.picks.shape[0] // slots
    before = (
        lax.broadcasted_iota(jnp.int32, (group, group), 0) < lax.broadcasted_iota(jnp.int32, (group, group), 1)
    ).astype(BF16)
    same = (
        lax.broadcasted_iota(jnp.int32, (group, group), 0) == lax.broadcasted_iota(jnp.int32, (group, group), 1)
    ).astype(BF16)
    numbers = lax.broadcasted_iota(jnp.int32, (slots, group), 0).astype(F32)

    def gather():
        def one(number, carry):
            slot = number % depth
            for copy in rows_of(number):
                copy.wait()

            @pl.when(number + depth - 1 < groups)
            def _():
                for copy in rows_of(number + depth - 1):
                    copy.start()

            parts = r.x_rows[slot, :, MODEL_WIDTH:].astype(F32)
            chosen = (parts != 0.0).astype(BF16)
            rank = dot_tn(chosen, before)
            r.ranks[...] = jnp.where(dot_tn(chosen, same) > 0.0, rank, -1.0)
            span = pl.ds(pl.multiple_of(number * slots, slots), slots)
            for low in range(0, pack, bunch):
                few = min(bunch, pack - low)
                for index in range(few):
                    rank_row = r.ranks[pl.ds(own * local + first + low + index, 1), :]
                    r.picks[index * slots : (index + 1) * slots, :] = (numbers == rank_row).astype(BF16)
                for source, target in ((r.x_rows, r.compact_x), (r.u_rows, r.compact_u)):
                    found = dot_nn(r.picks[: few * slots], source[slot]).astype(BF16)
                    for index in range(few):
                        target[low + index, span] = found[index * slots : (index + 1) * slots]
            return carry

        lax.fori_loop(0, groups, one, 0)

    def out_of(expert):
        slot = expert % 2
        return (
            pltpu.make_async_copy(r.din.at[slot], r.grad_in.at[expert - shift], r.d_sem.at[0, slot]),
            pltpu.make_async_copy(r.dout.at[slot], r.grad_out.at[expert - shift], r.d_sem.at[1, slot]),
        )

    def one_expert(expert, index):
        slot = expert % 2
        for copy in weights_of(expert):
            copy.wait()

        @pl.when(expert + 1 < first + pack)
        def _():
            for copy in weights_of(expert + 1):
                copy.start()

        @pl.when(expert >= first + 2)
        def _():
            for copy in out_of(expert - 2):
                copy.wait()

        for number in range(chunks):

            def one_tile(step, carry):
                span = pl.ds(pl.multiple_of(number * chunk + step * tile, tile), tile)
                here = pl.ds(pl.multiple_of(step * tile, tile), tile)
                gate = column_of(
                    r.compact_x[index, span, MODEL_WIDTH:], lane_of((tile, LANES)), own * local + expert
                )
                pair = dot_nn(r.compact_x[index, span, :MODEL_WIDTH], r.ein[slot])
                gate_part, up_part = pair[:, :FF], pair[:, FF:]
                sigmoid = 1.0 / (1.0 + jnp.exp(-gate_part))
                silu = gate_part * sigmoid
                r.activated[here] = (silu * up_part * gate).astype(BF16)
                grad_activated = dot_nt(r.compact_u[index, span], r.eout[slot]) * gate
                r.grad_pair[here, :FF] = (
                    grad_activated * up_part * sigmoid * (1.0 + gate_part * (1.0 - sigmoid))
                ).astype(BF16)
                r.grad_pair[here, FF:] = (grad_activated * silu).astype(BF16)
                return carry

            lax.fori_loop(0, chunk // tile, one_tile, 0)
            rows = slice(number * chunk, (number + 1) * chunk)
            left_in = r.compact_x[index, rows, pl.ds(pl.multiple_of(plane * slice_in, LANES), slice_in)]
            left_out = r.activated[:, pl.ds(pl.multiple_of(plane * slice_out, LANES), slice_out)]
            term_in = dot_tn(left_in, r.grad_pair[...])
            term_out = dot_tn(left_out, r.compact_u[index, rows])
            if number == 0:
                r.din[slot] = term_in
                r.dout[slot] = term_out
            else:
                r.din[slot] += term_in
                r.dout[slot] += term_out
        for copy in out_of(expert):
            copy.start()

    def run(low, high):
        def body(index, carry):
            one_expert(first + index, index)
            return carry

        if high > low:
            lax.fori_loop(low, high, body, 0)

    def start():
        for number in range(min(depth - 1, groups)):
            for copy in rows_of(number):
                copy.start()
        for copy in weights_of(first):
            copy.start()

    def finish():
        for expert in range(max(first, first + pack - 2), first + pack):
            for copy in out_of(expert):
                copy.wait()

    names = Names()
    names.load, names.gather, names.run, names.finish, names.pack = start, gather, run, finish, pack
    return names


def gradients_kernel(planes, owners, tokens, local, r):
    section = lax.axis_index("section")
    plane = lax.axis_index("dp")
    own = lax.axis_index("expert")
    partner = dict(section=1 - section)
    part = MODEL_WIDTH // (planes * owners)
    barrier = pltpu.get_barrier_semaphore()
    for step in range(1, owners):
        pl.semaphore_signal(barrier, inc=1, device_id=dict(expert=(own + step) % owners), device_id_type=MESH)
    for step in range(1, planes):
        pl.semaphore_signal(barrier, inc=1, device_id=dict(dp=(plane + step) % planes), device_id_type=MESH)
    pl.semaphore_signal(barrier, inc=1, device_id=partner, device_id_type=MESH)

    experts = ExpertGrads(planes, owners, tokens, local, 0, r)
    experts.load()

    def meet(source, target, index):
        here = pltpu.make_async_copy(source.at[section], target.at[section], r.m_local.at[index])
        there = remote(source.at[1 - section], target.at[section], r.m_send.at[index], r.m_recv.at[index], partner)
        return here, there

    meets = [
        meet(r.low, r.all_low.at[own], 0),
        meet(r.chosen, r.both_chosen, 1),
        meet(r.small, r.both_small, 2),
        meet(r.projected_grad, r.all_projected.at[own], 3),
    ]
    pl.semaphore_wait(barrier, owners - 1 + planes - 1 + 1)
    for here, there in meets:
        here.start()
        there.start()

    def piece_of(buffer):
        return lambda owner, half: buffer.at[owner] if half is None else buffer.at[owner, half]

    spreads = (
        PlaneBroadcast(owners, own, piece_of(r.all_low), r.f_send.at[0], r.f_recv.at[0]),
        PlaneBroadcast(owners, own, piece_of(r.all_projected), r.f_send.at[1], r.f_recv.at[1]),
    )
    width = planes * LANES

    def variant_of(owner):
        return owner * part // LANES

    def chosen_to(step, which):
        target = (own + step) % owners
        columns = pl.ds((1 - which) * width, width)
        return remote(
            r.both_chosen.at[:, variant_of(target), :, columns], r.all_chosen.at[own, :, :, columns],
            r.c_send.at[which, step], r.c_recv.at[which, step], dict(expert=target),
        )

    def small_to(step):
        return remote(
            r.small_out, r.small_in.at[step - 1], r.v_send.at[step], r.v_recv.at[step],
            dict(expert=(own + step) % owners),
        )

    halves = (
        (r.all_low, r.product_out, r.sums, r.leaving_out),
        (r.all_projected, r.product_in, r.partial, None),
    )

    def sums_over(step):
        return remote(
            r.leaving_out.at[step - 1], r.arriving_out.at[step - 1], r.z_send.at[step], r.z_recv.at[step],
            dict(dp=(plane + step) % planes),
        )

    def attention_start():
        for here, there in meets:
            here.wait()
            there.wait_recv()
        r.small_kept[...] = r.both_small[0] + r.both_small[1]
        r.small_out[...] = r.small_kept[...].astype(BF16)
        for step in range(1, owners):
            small_to(step).start()
        for which in range(2):
            spreads[which].start()
            for step in range(1, owners):
                chosen_to(step, which).start()
        r.all_chosen[own] = r.both_chosen[:, variant_of(own)]

    def attention_small():
        total = r.small_kept[...]
        for step in range(1, owners):
            small_to(step).wait_recv()
            total = total + r.small_in[step - 1].astype(F32)
        r.sums[part:] = total
        for step in range(1, planes):
            r.leaving_out[step - 1, part:] = total.astype(BF16)

    def attention_partial(which):
        factors, product, partial, leaving = halves[which]
        spreads[which].wait()
        for step in range(1, owners):
            chosen_to(step, which).wait_recv()
        within = own * part % LANES
        some = min(owners, 4)
        pile = some * 2 * tokens
        for step in list(range(1, planes)) + [0]:
            target = (plane + step) % planes
            columns = pl.ds(pl.multiple_of(((1 - which) * planes + target) * LANES, LANES), LANES)
            for first in range(0, owners, some):
                left = r.all_chosen[first : first + some, :, :, columns].reshape(pile, LANES)
                term = dot_tn(left, factors[first : first + some].reshape(pile, factors.shape[-1]))
                if first == 0:
                    product[...] = term
                else:
                    product[...] += term
            mine = product[pl.ds(pl.multiple_of(within, 16), part)]
            if step == 0:
                partial[:part] = mine
            else:
                if which == 0:
                    leaving[step - 1, :part] = mine.astype(BF16)
                    sums_over(step).start()
                else:
                    getattr(r, f"to{step}")[...] = mine.astype(BF16)

    def attention_last():
        total = r.sums[...]
        for step in range(1, planes):
            sums_over(step).wait()
            total = total + r.arriving_out[step - 1].astype(F32)
        r.sums[...] = total
        for here, there in meets:
            there.wait_send()
        for which in range(2):
            spreads[which].sent()
            for step in range(1, owners):
                chosen_to(step, which).wait_send()
        for step in range(1, owners):
            small_to(step).wait_send()

    attention_start()
    experts.gather()
    pack = experts.pack
    experts.run(0, pack // 6)
    attention_small()
    spreads[0].forward()
    experts.run(pack // 6, 2 * pack // 6)
    spreads[1].forward()
    experts.run(2 * pack // 6, 4 * pack // 6)
    attention_partial(0)
    experts.run(4 * pack // 6, pack)
    experts.finish()
    attention_partial(1)
    attention_last()


def rest_kernel(planes, owners, tokens, local, first, r):
    experts = ExpertGrads(planes, owners, tokens, local, first, r)
    experts.load()
    held = ((r.first_in, r.held_in, r.grad_in), (r.first_out, r.held_out, r.grad_out))
    entering = [
        pltpu.make_async_copy(source, here, r.move_sem.at[0, index]) for index, (source, here, _) in enumerate(held)
    ]
    moving = [
        pltpu.make_async_copy(here, target.at[pl.ds(0, first)], r.move_sem.at[1, index])
        for index, (_, here, target) in enumerate(held)
    ]
    for copy in entering:
        copy.start()
    part = r.grad_attn_out.shape[0]
    r.grad_attn_out[...] = r.sums[:part]
    r.grad_gain_one[...] = r.sums[part : part + 1]
    r.grad_gain_two[...] = r.sums[part + 1 : part + 2]
    r.grad_router[...] = r.sums[part + 16 :]
    r.hidden_out[...] = r.hidden[...]
    r.input_grad_out[...] = r.input_grad[...]
    experts.gather()
    for number in range(2):
        entering[number].wait()
        moving[number].start()
    experts.run(0, experts.pack)
    experts.finish()
    for copy in moving:
        copy.wait()


def grads_scratch(planes, owners, tokens, pack):
    group = 4 * tokens
    groups = 2 * planes * owners * tokens // group
    slots = group // 2
    chunk = min(groups * slots, 1024)
    dma = lambda *shape: pltpu.SemaphoreType.DMA(shape)
    vmem = lambda shape, dtype: pltpu.VMEM(shape, dtype)
    return dict(
        ein=vmem((2, MODEL_WIDTH, 2 * FF), BF16),
        eout=vmem((2, FF, MODEL_WIDTH), BF16),
        x_rows=vmem((4, group, PACKED), BF16),
        u_rows=vmem((4, group, MODEL_WIDTH), BF16),
        ranks=vmem((LANES, group), F32),
        picks=vmem((min(pack, 5) * slots, group), BF16),
        compact_x=vmem((pack, groups * slots, PACKED), BF16),
        compact_u=vmem((pack, groups * slots, MODEL_WIDTH), BF16),
        activated=vmem((chunk, FF), BF16),
        grad_pair=vmem((chunk, 2 * FF), BF16),
        din=vmem((2, MODEL_WIDTH // planes, 2 * FF), F32),
        dout=vmem((2, FF // planes, MODEL_WIDTH), F32),
        e_sem=dma(2, 2),
        t_sem=dma(2, 4),
        d_sem=dma(2, 2),
    )


def weight_gradients(done, experts_in, experts_out):
    planes, owners = lax.axis_size("dp"), lax.axis_size("expert")
    local = experts_in.shape[1]
    tokens = done.low.shape[1]
    part = MODEL_WIDTH // (planes * owners)
    first = max(1, 6 * local // 8)
    wide = 2 * planes * LANES
    variants = done.chosen.shape[1]
    small = done.small.shape[1:]
    dma = lambda *shape: pltpu.SemaphoreType.DMA(shape)
    vmem = lambda shape, dtype: pltpu.VMEM(shape, dtype)
    shape_in, shape_out = (MODEL_WIDTH // planes, 2 * FF), (FF // planes, MODEL_WIDTH)
    tables = dict(
        every_x=(done.every_x.reshape(-1, PACKED), any_spec()),
        every_u=(done.every_u.reshape(-1, MODEL_WIDTH), any_spec()),
        experts_in=(experts_in, any_spec()),
        experts_out=(experts_out, any_spec()),
    )
    exchanged = call(
        functools.partial(gradients_kernel, planes, owners, tokens, local),
        "weight_gradients",
        1,
        dict(
            projected_grad=(done.projected_grad, vmem_spec()),
            low=(done.low, vmem_spec()),
            chosen=(done.chosen, vmem_spec()),
            small=(done.small, vmem_spec()),
            **tables,
        ),
        dict(
            grad_in=((first,) + shape_in, F32, any_spec()),
            grad_out=((first,) + shape_out, F32, any_spec()),
            partial=((part, PROJECTED), F32, vmem_spec()),
            sums=((part + small[0], MODEL_WIDTH), F32, vmem_spec()),
            **{f"to{step}": ((part, PROJECTED), BF16, vmem_spec()) for step in range(1, planes)},
        ),
        dict(
            all_low=vmem((owners, 2, tokens, MODEL_WIDTH), BF16),
            all_projected=vmem((owners, 2, tokens, PROJECTED), BF16),
            both_chosen=vmem((2, variants, tokens, wide), BF16),
            all_chosen=vmem((owners, 2, tokens, wide), BF16),
            both_small=vmem((2,) + small, F32),
            small_kept=vmem(small, F32),
            small_out=vmem(small, BF16),
            small_in=vmem((owners - 1,) + small, BF16),
            product_in=vmem((LANES, PROJECTED), F32),
            product_out=vmem((LANES, MODEL_WIDTH), F32),
            leaving_out=vmem((planes - 1, part + small[0], MODEL_WIDTH), BF16),
            arriving_out=vmem((planes - 1, part + small[0], MODEL_WIDTH), BF16),
            z_send=dma(planes),
            z_recv=dma(planes),
            m_local=dma(4),
            m_send=dma(4),
            m_recv=dma(4),
            f_send=dma(2, owners),
            f_recv=dma(2, owners),
            c_send=dma(2, owners),
            c_recv=dma(2, owners),
            v_send=dma(owners),
            v_recv=dma(owners),
            **grads_scratch(planes, owners, tokens, first),
        ),
    )
    total = exchanged.partial
    arriving = [
        lax.ppermute(getattr(exchanged, f"to{step}"), "dp", [(i, (i + step) % planes) for i in range(planes)])
        for step in range(1, planes)
    ]
    count = local - first
    rows = 2 * planes * owners * tokens
    rest = call(
        functools.partial(rest_kernel, planes, owners, tokens, local, first),
        "other_experts",
        None,
        dict(
            first_in=(exchanged.grad_in, any_spec()),
            first_out=(exchanged.grad_out, any_spec()),
            sums=(exchanged.sums, vmem_spec()),
            hidden=(done.hidden, vmem_spec()),
            input_grad=(done.input_grad, vmem_spec()),
            **tables,
        ),
        dict(
            grad_in=((local,) + shape_in, F32, any_spec()),
            grad_out=((local,) + shape_out, F32, any_spec()),
            grad_attn_out=((part, MODEL_WIDTH), F32, vmem_spec()),
            grad_gain_one=((1, MODEL_WIDTH), F32, vmem_spec()),
            grad_gain_two=((1, MODEL_WIDTH), F32, vmem_spec()),
            grad_router=((EXPERTS, MODEL_WIDTH), F32, vmem_spec()),
            hidden_out=(done.hidden.shape, BF16, vmem_spec()),
            input_grad_out=(done.hidden.shape, BF16, vmem_spec()),
        ),
        dict(
            held_in=vmem((first,) + shape_in, F32),
            held_out=vmem((first,) + shape_out, F32),
            move_sem=dma(2, 2),
            **grads_scratch(planes, owners, tokens, count),
        ),
        pl.CostEstimate(flops=count * rows * 6 * MODEL_WIDTH * FF, bytes_accessed=rows * 4 * MODEL_WIDTH, transcendentals=0),
    )
    arriving, rest.grad_in = lax.optimization_barrier((arriving, rest.grad_in))
    for piece in arriving:
        total = total + piece.astype(F32)
    return rest, total


def shards(layer_input, cotangent, positions, routes, gain_one, attn_in, attn_out, gain_two, router,
           experts_in, experts_out):
    place = lax.dynamic_index_in_dim(positions, lax.axis_index("section"), 0, keepdims=False)
    lane = jnp.arange(LANES)
    frequency = jnp.power(rotary_base, -((lane % HALF).astype(F32) * (2.0 / HEAD_SIZE)))
    angles = place.astype(F32)[:, None] * frequency[None, :]
    cosine = jnp.cos(angles)
    sine = jnp.where(lane % HEAD_SIZE < HALF, -1.0, 1.0) * jnp.sin(angles)

    done = both_layers(
        layer_input, cotangent, routes, gain_one, attn_in, attn_out, gain_two, router, cosine, sine,
        experts_in, experts_out,
    )
    rest, grad_attn_in = weight_gradients(done, experts_in, experts_out)
    return (
        rest.hidden_out[None],
        rest.input_grad_out[None],
        rest.grad_gain_one,
        grad_attn_in[None],
        rest.grad_attn_out[None],
        rest.grad_gain_two,
        rest.grad_router.T[None],
        rest.grad_in[None],
        rest.grad_out[None],
    )


def solution(mesh):
    in_specs = (
        P(None, ("dp", "expert"), None),
        P(None, ("dp", "expert"), None),
        P(None, ("dp", "expert")),
        P("section", None, ("dp", "expert"), None),
        P("section", None),
        P("section", "dp", None),
        P("section", "dp", None),
        P("section", None),
        P("section", None, None),
        P("section", "expert", None, None),
        P("section", "expert", None, None),
    )
    out_specs = (
        P("section", None, ("dp", "expert"), None),
        P("section", None, ("dp", "expert"), None),
        P("section", None),
        P("section", ("dp", "expert"), None),
        P("section", ("dp", "expert"), None),
        P("section", None),
        P("section", None, None),
        P("section", "expert", "dp", None),
        P("section", "expert", "dp", None),
    )
    return jax.shard_map(shards, mesh=mesh, in_specs=in_specs, out_specs=out_specs, check_vma=False)
```

```python
import functools

import jax
import jax.numpy as jnp
from jax import lax
from jax.experimental import pallas as pl
from jax.experimental.pallas import tpu as pltpu
from jax.sharding import PartitionSpec as P

MODEL_WIDTH = 1024
QUERY_HEADS = 16
KEY_VALUE_HEADS = 8
HEAD_SIZE = 64
FF = 512
EXPERTS = 32
TOPK = 8

QUERY_WIDTH = QUERY_HEADS * HEAD_SIZE
KEY_WIDTH = KEY_VALUE_HEADS * HEAD_SIZE
PROJECTED = QUERY_WIDTH + 2 * KEY_WIDTH
LANES = 128
HALF = HEAD_SIZE // 2
PACKED = MODEL_WIDTH + LANES

epsilon = 1e-06
rotary_base = 10000.0

F32 = jnp.float32
BF16 = jnp.bfloat16
MESH = pl.DeviceIdType.MESH
VMEM_LIMIT = 62 * 1024 * 1024


def dot_nn(a, b):
    return lax.dot_general(a, b, (((1,), (0,)), ((), ())), preferred_element_type=F32)


def dot_nt(a, b):
    return lax.dot_general(a, b, (((1,), (1,)), ((), ())), preferred_element_type=F32)


def dot_tn(a, b):
    return lax.dot_general(a, b, (((0,), (0,)), ((), ())), preferred_element_type=F32)


def row_scale(values):
    return lax.rsqrt(jnp.mean(values * values, axis=-1, keepdims=True) + epsilon)


def norm_back(grad_normed, inputs, scale):
    return scale * grad_normed - inputs * (scale * scale * scale) * jnp.mean(
        grad_normed * inputs, axis=-1, keepdims=True
    )


def lane_of(shape):
    return lax.broadcasted_iota(jnp.int32, shape, 1)


def turned(tile, low):
    return jnp.where(low, pltpu.roll(tile, LANES - HALF, 1), pltpu.roll(tile, HALF, 1))


def two_parts(values):
    high = values.astype(BF16).astype(F32)
    return (high + pltpu.roll(values - high, EXPERTS, 1)).astype(BF16)


def column_of(parts, lane, column):
    wide = parts.astype(F32)
    return jnp.sum(jnp.where((lane == column) | (lane == column + EXPERTS), wide, 0.0), axis=-1, keepdims=True)


def remote(source, target, send, recv, device):
    return pltpu.make_async_remote_copy(
        src_ref=source, dst_ref=target, send_sem=send, recv_sem=recv, device_id=device, device_id_type=MESH
    )


def vmem_spec():
    return pl.BlockSpec(memory_space=pltpu.VMEM)


def any_spec():
    return pl.BlockSpec(memory_space=pl.ANY)


class Names:
    pass


def call(kernel, name, number, inputs, outputs, scratch, cost=None):
    labels = list(inputs) + list(outputs) + list(scratch)

    def body(*refs):
        names = Names()
        for label, ref in zip(labels, refs):
            setattr(names, label, ref)
        kernel(names)

    if number is None:
        params = pltpu.CompilerParams(vmem_limit_bytes=VMEM_LIMIT)
    else:
        params = pltpu.CompilerParams(
            collective_id=number, has_side_effects=True, vmem_limit_bytes=VMEM_LIMIT
        )
    results = pl.pallas_call(
        body,
        out_shape=tuple(jax.ShapeDtypeStruct(shape, dtype) for shape, dtype, _ in outputs.values()),
        in_specs=[spec for _, spec in inputs.values()],
        out_specs=tuple(spec for _, _, spec in outputs.values()),
        scratch_shapes=list(scratch.values()),
        compiler_params=params,
        cost_estimate=cost,
        name=name,
    )(*[array for array, _ in inputs.values()])
    names = Names()
    for label, result in zip(outputs, results):
        setattr(names, label, result)
    return names


class PlaneBroadcast:
    def __init__(self, owners, own, piece, send, recv):
        self.owners, self.own = owners, own
        self.square = owners == 4
        self.piece, self.send, self.recv = piece, send, recv

    def hop(self, owner, half, index, device):
        block = self.piece(owner, half)
        return remote(block, block, self.send.at[index], self.recv.at[index], dict(expert=device))

    def hops(self):
        owners, own = self.owners, self.own

        def owner_to(step):
            return (own + step) % owners

        if not self.square:
            return [self.hop(own, None, turn, owner_to(turn)) for turn in range(1, owners)]
        beside = own + 1 - 2 * (own % 2)
        above = owner_to(2)
        return [
            self.hop(own, None, 0, beside),
            self.hop(own, None, 1, above),
            self.hop(beside, 0, 2, above),
            self.hop(above, 1, 3, beside),
        ]

    def start(self):
        hops = self.hops()
        for hop in hops[:2] if self.square else hops:
            hop.start()

    def forward(self):
        if self.square:
            hops = self.hops()
            for hop in range(2):
                hops[hop].wait_recv()
                hops[2 + hop].start()

    def wait(self):
        hops = self.hops()
        for hop in hops[2:] if self.square else hops:
            hop.wait_recv()

    def sent(self):
        for hop in self.hops():
            hop.wait_send()


def layers_kernel(planes, owners, tokens, local, slab, r):
    section = lax.axis_index("section")
    plane = lax.axis_index("dp")
    own = lax.axis_index("expert")
    rows = owners * tokens
    part = slab // owners
    here = pl.ds(own * tokens, tokens)
    partner = dict(section=1 - section)

    def planes_to(step):
        return (plane + step) % planes

    def owner_to(step):
        return (own + step) % owners

    barrier = pltpu.get_barrier_semaphore()
    for step in range(1, owners):
        pl.semaphore_signal(barrier, inc=1, device_id=dict(expert=owner_to(step)), device_id_type=MESH)
    for step in range(1, planes):
        for target in range(2):
            pl.semaphore_signal(
                barrier, inc=1, device_id=dict(section=target, dp=planes_to(step)), device_id_type=MESH
            )
    pl.semaphore_signal(barrier, inc=1, device_id=partner, device_id_type=MESH)
    pl.semaphore_wait(barrier, owners - 1 + 2 * (planes - 1) + 1)

    unsent = []

    own_rows = [
        pltpu.make_async_copy(r.layer_input.at[section], r.x, r.i_sem.at[0]),
        pltpu.make_async_copy(r.cotangent.at[section], r.up, r.i_sem.at[1]),
    ]
    for copy in own_rows:
        copy.start()

    unit = (
        lax.broadcasted_iota(jnp.int32, (EXPERTS, LANES), 0) == lax.broadcasted_iota(jnp.int32, (EXPERTS, LANES), 1)
    ).astype(BF16)

    def hot_of(choices):
        number = lax.broadcasted_iota(jnp.int32, (EXPERTS, tokens), 0)
        found = jnp.zeros((EXPERTS, tokens), F32)
        for choice in range(TOPK):
            found = jnp.where(number == choices[choice : choice + 1], 1.0, found)
        return dot_tn(found.astype(BF16), unit)

    r.gains[section, 0:1] = r.gain_one[...]
    r.gains[section, 1:2] = r.gain_two[...]
    r.router[section] = r.router_in[0]
    r.hot[section] = hot_of(r.routes[0, section])
    r.hot_out[...] = hot_of(r.routes[0, 1 - section])
    shared = [
        remote(source, target, r.h_send.at[index], r.h_recv.at[index], partner)
        for index, (source, target) in enumerate(
            (
                (r.gains.at[section], r.gains.at[section]),
                (r.router.at[section], r.router.at[section]),
                (r.hot_out, r.hot.at[section]),
            )
        )
    ]
    for copy in shared:
        copy.start()

    def Broadcast(piece, send, recv):
        return PlaneBroadcast(owners, own, piece, send, recv)

    weight_pieces = ((r.attn_in, r.win, 0), (r.attn_in, r.win, QUERY_WIDTH), (r.attn_out, r.wout, 0))
    pieces = range(len(weight_pieces))

    def slab_local(layer, which):
        source, full, column = weight_pieces[which]
        columns = pl.ds(column, MODEL_WIDTH)
        return pltpu.make_async_copy(
            source.at[0, :, columns], full.at[layer, pl.ds(plane * slab, slab), columns], r.w_local.at[layer, which]
        )

    def slab_z(layer, which, step):
        source, full, column = weight_pieces[which]
        columns = pl.ds(column, MODEL_WIDTH)
        return remote(
            source.at[0, pl.ds(own * part, part), columns],
            full.at[layer, pl.ds(plane * slab + own * part, part), columns],
            r.wz_send.at[layer, which, step],
            r.wz_recv.at[layer, which, step],
            dict(dp=planes_to(step)),
        )

    def slab_plane(layer, which, step):
        full, column = weight_pieces[which][1:]
        origin = planes_to(planes - step)

        def piece(owner, half):
            start, length = origin * slab + owner * part, part
            if half is not None:
                length = part // 2
                start = start + half * length
            return full.at[layer, pl.ds(start, length), pl.ds(column, MODEL_WIDTH)]

        return Broadcast(piece, r.wp_send.at[layer, which, step], r.wp_recv.at[layer, which, step])

    def slab_core(layer, which, step):
        full, column = weight_pieces[which][1:]
        block = full.at[layer, pl.ds(planes_to(planes - step) * slab, slab), pl.ds(column, MODEL_WIDTH)]
        return remote(block, block, r.wc_send.at[layer, which, step], r.wc_recv.at[layer, which, step], partner)

    def weights_start(layer, which):
        @pl.when(section == layer)
        def _():
            for step in range(1, planes):
                slab_z(layer, which, step).start()
            slab_local(layer, which).start()

    def weights_spread(layer, which):
        @pl.when(section == layer)
        def _():
            slab_local(layer, which).wait()
            slab_core(layer, which, 0).start()
            for step in range(1, planes):
                slab_z(layer, which, step).wait_recv()
                slab_plane(layer, which, step).start()

    def weights_forward(layer, which):
        @pl.when(section == layer)
        def _():
            for step in range(1, planes):
                slab_plane(layer, which, step).forward()

    def weights_push(layer, which):
        @pl.when(section == layer)
        def _():
            for step in range(1, planes):
                slab_plane(layer, which, step).wait()
                slab_core(layer, which, step).start()

    def weights_wait(layer, which):
        @pl.when(section != layer)
        def _():
            for step in range(planes):
                slab_core(layer, which, step).wait_recv()

    def weights_unsent(layer, which):
        @pl.when(section == layer)
        def _():
            for step in range(1, planes):
                slab_z(layer, which, step).wait_send()
                slab_plane(layer, which, step).sent()
            for step in range(planes):
                slab_core(layer, which, step).wait_send()

    def swap_pair(expert):
        return (
            remote(r.experts_in.at[0, expert], r.other_in.at[expert], r.s_send.at[0, expert], r.s_recv.at[0, expert], partner),
            remote(r.experts_out.at[0, expert], r.other_out.at[expert], r.s_send.at[1, expert], r.s_recv.at[1, expert], partner),
        )

    def load_in(layer, expert):
        mine = pltpu.make_async_copy(r.experts_in.at[0, expert], r.ein.at[expert], r.l_sem.at[0, expert])
        other = pltpu.make_async_copy(r.other_in.at[expert], r.ein.at[expert], r.l_sem.at[0, expert])
        return mine, other

    def load_out(layer, expert):
        target = r.eout.at[pl.ds(expert * FF, FF)]
        mine = pltpu.make_async_copy(r.experts_out.at[0, expert], target, r.l_sem.at[1, expert])
        other = pltpu.make_async_copy(r.other_out.at[expert], target, r.l_sem.at[1, expert])
        return mine, other

    def start_load(make, layer, expert, which, first_use):
        @pl.when(section == layer)
        def _():
            make(layer, expert)[0].start()

        @pl.when(section != layer)
        def _():
            if first_use:
                swap_pair(expert)[which].wait_recv()
            make(layer, expert)[1].start()

    class Spread:
        def __init__(self, source, buffer, index):
            self.copies = [
                remote(source, buffer.at[own], r.a_send.at[index, step], r.a_recv.at[index, step],
                       dict(expert=owner_to(step)))
                for step in range(1, owners)
            ]
            self.source, self.buffer = source, buffer

        def start(self):
            for copy in self.copies:
                copy.start()
            self.buffer[own] = self.source[...]

        def wait(self):
            for copy in self.copies:
                copy.wait_recv()
            unsent.extend(self.copies)

    class Reduce:
        def __init__(self, leaving, coming, index, cuts):
            self.leaving, self.coming, self.index, self.cuts = leaving, coming, index, cuts
            self.copies = {
                (cut, step): remote(
                    leaving.at[step - 1, :, pl.ds(*cuts[cut])],
                    coming.at[step - 1, :, pl.ds(*cuts[cut])],
                    r.r_send.at[index, cut, step],
                    r.r_recv.at[index, cut, step],
                    dict(expert=owner_to(step)),
                )
                for cut in range(len(cuts))
                for step in range(1, owners)
            }

        def put(self, step, columns, values):
            self.leaving[step - 1, :, columns] = values

        def start(self, cut):
            for step in range(1, owners):
                self.copies[cut, step].start()

        def wait(self):
            for copy in self.copies.values():
                copy.wait()

    class Gather:
        def __init__(self, layer, block, around, target, index):
            self.layer, self.block, self.around, self.target, self.index = layer, block, around, target, index

        def across(self, step):
            return [
                remote(
                    self.block,
                    self.target.at[own, (planes - step) % planes, section],
                    r.g_send.at[self.index, step],
                    r.g_recv.at[self.index, step, section],
                    dict(section=self.layer, dp=planes_to(step)),
                )
            ][0]

        def arrival(self, step, micro):
            return remote(
                self.block,
                self.target.at[own, (planes - step) % planes, micro],
                r.g_send.at[self.index, step],
                r.g_recv.at[self.index, step, micro],
                dict(section=self.layer, dp=planes_to(step)),
            )

        def home_local(self):
            return pltpu.make_async_copy(self.around, self.target.at[:, 0, section], r.g_local.at[self.index])

        def home_remote(self, micro):
            return remote(self.around, self.target.at[:, 0, micro], r.g_send.at[self.index, 0],
                          r.g_recv.at[self.index, 0, 0], partner)

        def inside(self):
            def piece(owner, half):
                if half is None:
                    return self.target.at[owner, pl.ds(1, planes - 1)]
                return self.target.at[owner, pl.ds(1, planes - 1), half]

            return Broadcast(piece, r.gp_send.at[self.index], r.gp_recv.at[self.index])

        def whole_to(self, step, micro):
            return remote(
                self.around,
                self.target.at[:, (planes - step) % planes, micro],
                r.g_send.at[self.index, step],
                r.g_recv.at[self.index, step, micro],
                dict(section=self.layer, dp=planes_to(step)),
            )

        def start_whole(self):
            for step in range(1, planes):
                self.whole_to(step, section).start()

        def finish_whole(self):
            for step in range(1, planes):
                self.whole_to(step, section).wait_send()

            @pl.when(section == self.layer)
            def _():
                for step in range(1, planes):
                    for micro in range(2):
                        self.whole_to(step, micro).wait_recv()

            self.finish_home()

        def start(self):
            for step in range(1, planes):
                self.across(step).start()

        def start_home(self):
            @pl.when(section == self.layer)
            def _():
                self.home_local().start()

            @pl.when(section != self.layer)
            def _():
                self.home_remote(section).start()

        def middle(self):
            @pl.when(section == self.layer)
            def _():
                for step in range(1, planes):
                    for micro in range(2):
                        self.arrival(step, micro).wait_recv()
                self.inside().start()

        def forward(self):
            @pl.when(section == self.layer)
            def _():
                self.inside().forward()

        def finish(self):
            for step in range(1, planes):
                self.across(step).wait_send()

            @pl.when(section == self.layer)
            def _():
                self.inside().wait()
                self.inside().sent()

            self.finish_home()

        def finish_home(self):
            @pl.when(section == self.layer)
            def _():
                self.home_local().wait()
                self.home_remote(1 - section).wait_recv()

            @pl.when(section != self.layer)
            def _():
                self.home_remote(section).wait_send()

    lane = lane_of((tokens, LANES))
    low_half = lane % HEAD_SIZE < HALF
    left = lane < HEAD_SIZE
    pair_lane = lane_of((2 * tokens, LANES))
    causal = lax.broadcasted_iota(jnp.int32, (2 * tokens, tokens), 0) % tokens >= lax.broadcasted_iota(
        jnp.int32, (2 * tokens, tokens), 1
    )
    root = HEAD_SIZE ** (-0.5)

    def stack(tile):
        nothing = jnp.zeros_like(tile)
        return jnp.concatenate([jnp.where(left, tile, nothing), jnp.where(left, nothing, tile)], axis=0)

    def attention_forward(layer, source, early, late):
        cosine, sine = r.cosine[...], r.sine[...]
        residual = source[...].astype(F32)
        normed_one = (residual * row_scale(residual) * r.gains[layer, 0:1]).astype(BF16)
        weights_wait(layer, 0)
        early()
        r.projected[:, :QUERY_WIDTH] = dot_nn(normed_one, r.win[layer, :, :QUERY_WIDTH])
        weights_wait(layer, 1)
        r.projected[:, QUERY_WIDTH:] = dot_nn(normed_one, r.win[layer, :, QUERY_WIDTH:])
        for tile in range(QUERY_WIDTH // LANES):
            columns = slice(tile * LANES, (tile + 1) * LANES)
            piece = r.projected[:, columns]
            r.query[layer, :, columns] = (piece * cosine + turned(piece, low_half) * sine).astype(BF16)
        for tile in range(KEY_WIDTH // LANES):
            first = slice(2 * tile * LANES, (2 * tile + 1) * LANES)
            second = slice((2 * tile + 1) * LANES, (2 * tile + 2) * LANES)
            piece = r.projected[:, QUERY_WIDTH + tile * LANES : QUERY_WIDTH + (tile + 1) * LANES]
            piece = piece * cosine + turned(piece, low_half) * sine
            other = pltpu.roll(piece, HEAD_SIZE, 1)
            r.key[layer, :, first] = jnp.where(left, piece, other).astype(BF16)
            r.key[layer, :, second] = jnp.where(left, other, piece).astype(BF16)
            start = QUERY_WIDTH + KEY_WIDTH + tile * LANES
            piece = r.projected[:, start : start + LANES]
            other = pltpu.roll(piece, HEAD_SIZE, 1)
            r.value[layer, :, first] = jnp.where(left, piece, other).astype(BF16)
            r.value[layer, :, second] = jnp.where(left, other, piece).astype(BF16)
        logs = jnp.zeros((2 * tokens, LANES), F32)
        for head in range(KEY_VALUE_HEADS):
            columns = slice(head * LANES, (head + 1) * LANES)
            scores = dot_nt(stack(r.query[layer, :, columns]), r.key[layer, :, columns]) * root
            scores = jnp.where(causal, scores, -1e30)
            top = jnp.max(scores, axis=-1, keepdims=True)
            log_total = top + jnp.log(jnp.sum(jnp.exp(scores - top), axis=-1, keepdims=True))
            logs = jnp.where(pair_lane == head, log_total, logs)
            weights = jnp.exp(scores - log_total).astype(BF16)
            mixed = dot_nn(weights, r.value[layer, :, columns])
            r.attended[layer, :, columns] = jnp.where(left, mixed[:tokens], mixed[tokens:]).astype(BF16)
        r.logs[layer] = logs
        late()
        weights_wait(layer, 2)
        middle = residual + dot_nn(r.attended[layer], r.wout[layer])
        r.middle[layer] = middle
        normed_two = (middle * row_scale(middle) * r.gains[layer, 1:2]).astype(BF16)
        r.packed[layer, :, :MODEL_WIDTH] = normed_two
        logits = jnp.concatenate(
            [dot_nt(normed_two, r.router[layer]), jnp.zeros((tokens, LANES - EXPERTS), F32)], axis=-1
        )
        chosen = r.hot[layer] > 0.0
        top = jnp.max(jnp.where(chosen, logits, -1e30), axis=-1, keepdims=True)
        grown = jnp.where(chosen, jnp.exp(jnp.where(chosen, logits - top, 0.0)), 0.0)
        gates = grown / jnp.sum(grown, axis=-1, keepdims=True)
        r.gates[layer] = gates
        r.packed[layer, :, MODEL_WIDTH:] = two_parts(gates)

    def attention_backward(layer, source, up, back, gate_grads):
        cosine, sine = r.cosine[...], r.sine[...]
        gates = r.gates[layer]
        grad_picked = gates * (gate_grads - jnp.sum(gates * gate_grads, axis=-1, keepdims=True))
        grad_logits = grad_picked.astype(BF16)
        r.small[layer, 16:] = dot_tn(grad_logits, r.packed[layer, :, :MODEL_WIDTH])[:EXPERTS]
        grad_second = back + dot_nn(grad_logits[:, :EXPERTS], r.router[layer])
        middle = r.middle[layer]
        scale_two = row_scale(middle)
        r.small[layer, 1:2] = jnp.sum(grad_second * middle * scale_two, axis=0, keepdims=True)
        grad_middle = up[...].astype(F32) + norm_back(grad_second * r.gains[layer, 1:2], middle, scale_two)
        low = grad_middle.astype(BF16)
        r.low[layer] = low
        r.grad_middle[...] = grad_middle
        r.grad_attended[...] = dot_nt(low, r.wout[layer]).astype(BF16)
        logs = r.logs[layer]
        held = []
        for head in range(KEY_VALUE_HEADS):
            columns = slice(head * LANES, (head + 1) * LANES)
            query = stack(r.query[layer, :, columns])
            key, value = r.key[layer, :, columns], r.value[layer, :, columns]
            scores = dot_nt(query, key) * root
            log_total = jnp.sum(jnp.where(pair_lane == head, logs, 0.0), axis=-1, keepdims=True)
            probabilities = jnp.where(causal, jnp.exp(jnp.where(causal, scores - log_total, 0.0)), 0.0)
            grad_tile = stack(r.grad_attended[:, columns])
            delta = jnp.sum(
                grad_tile.astype(F32) * stack(r.attended[layer, :, columns]).astype(F32), axis=-1, keepdims=True
            )
            grad_scores = (probabilities * (dot_nt(grad_tile, value) - delta)).astype(BF16)
            wide = dot_nn(grad_scores, key) * root
            grad_query = jnp.where(left, wide[:tokens], wide[tokens:])
            grad_query = grad_query * cosine - turned(grad_query, low_half) * sine
            r.projected_grad[layer, :, columns] = grad_query.astype(BF16)
            key_grad = dot_tn(grad_scores, query) * root
            value_grad = dot_tn(probabilities.astype(BF16), grad_tile)
            key_grad = key_grad + pltpu.roll(key_grad, HEAD_SIZE, 1)
            value_grad = value_grad + pltpu.roll(value_grad, HEAD_SIZE, 1)
            if head % 2 == 0:
                held = [key_grad, value_grad]
            else:
                piece = jnp.where(left, held[0], key_grad)
                piece = piece * cosine - turned(piece, low_half) * sine
                start = QUERY_WIDTH + head // 2 * LANES
                r.projected_grad[layer, :, start : start + LANES] = piece.astype(BF16)
                start += KEY_WIDTH
                r.projected_grad[layer, :, start : start + LANES] = jnp.where(left, held[1], value_grad).astype(BF16)
        grad_first = dot_nt(r.projected_grad[layer], r.win[layer])
        residual = source[...].astype(F32)
        scale_one = row_scale(residual)
        normed_one = (residual * scale_one * r.gains[layer, 0:1]).astype(BF16)
        group = MODEL_WIDTH // planes
        for variant in range(group // LANES):
            for step in range(planes):
                start = step * group + variant * LANES
                r.chosen[layer, variant, :, step * LANES : (step + 1) * LANES] = normed_one[:, start : start + LANES]
                r.chosen[layer, variant, :, (planes + step) * LANES : (planes + step + 1) * LANES] = r.attended[
                    layer, :, start : start + LANES
                ]
        r.small[layer, 0:1] = jnp.sum(grad_first * residual * scale_one, axis=0, keepdims=True)
        return (
            r.grad_middle[...] + norm_back(grad_first * r.gains[layer, 0:1], residual, scale_one)
        ).astype(BF16)

    def place_local(source, target, index):
        return pltpu.make_async_copy(source, target.at[section], r.o_local.at[index])

    def place_remote(source, target, index, micro):
        return remote(source, target.at[micro], r.o_send.at[index], r.o_recv.at[index], partner)

    def place(layer, source, target, index):
        @pl.when(section == layer)
        def _():
            place_local(source, target, index).start()

        @pl.when(section != layer)
        def _():
            place_remote(source, target, index, section).start()

    def placed(layer, source, target, index):
        @pl.when(section == layer)
        def _():
            place_local(source, target, index).wait()
            place_remote(source, target, index, 1 - section).wait_recv()

        @pl.when(section != layer)
        def _():
            place_remote(source, target, index, section).wait_send()

    chunk = min(rows, 256)
    chunks = rows // chunk
    half = MODEL_WIDTH // 2

    def each_chunk(work):
        def one(number, carry):
            work(pl.ds(pl.multiple_of(number * chunk, chunk), chunk), pl.ds(number * (chunk // tokens), chunk // tokens))
            return carry

        if chunks == 1:
            work(pl.ds(0, chunk), pl.ds(0, owners))
        else:
            lax.fori_loop(0, chunks, one, 0)

    def flat(buffer, group, columns):
        values = buffer[group, :, columns]
        return values.reshape(chunk, values.shape[-1])

    model, packing = slice(0, MODEL_WIDTH), slice(MODEL_WIDTH, PACKED)

    def expert_columns(expert):
        return pl.ds(pl.multiple_of(expert * FF, FF), FF)

    def wait_in(expert):
        load_in(0, expert)[0].wait()

    def wait_out(expert):
        load_out(0, expert)[0].wait()

    def gate_of(plane_buffer, group, expert):
        return column_of(flat(plane_buffer, group, packing), lane_of((chunk, LANES)), own * local + expert)

    def backward_terms(expert, span, gate, gate_part, up_part, inner):
        sigmoid = 1.0 / (1.0 + jnp.exp(-gate_part))
        silu = gate_part * sigmoid
        activated = silu * up_part
        gate_grad = jnp.sum(activated * inner, axis=-1, keepdims=True)
        lanes = lane_of((chunk, LANES))
        r.gate_total[span] = jnp.where(lanes == own * local + expert, gate_grad, r.gate_total[span])
        grad_activated = inner * gate
        grad_gate = grad_activated * up_part * sigmoid * (1.0 + gate_part * (1.0 - sigmoid))
        grad_up = grad_activated * silu
        grad_pair = jnp.concatenate([grad_gate.astype(BF16), grad_up.astype(BF16)], axis=-1)
        term = dot_nt(grad_pair, r.ein[expert])

        @pl.when(expert == 0)
        def _():
            r.total[span] = term

        @pl.when(expert > 0)
        def _():
            r.total[span] += term

        return activated

    def mix(reduction):
        for cut in range(2):
            columns = slice(cut * half, (cut + 1) * half)

            def work(span, group):
                r.total[span, columns] = dot_nn(r.activated[span], r.eout[:, columns])

            each_chunk(work)
            for step in range(1, owners):
                reduction.put(
                    step, columns, r.total[pl.ds(owner_to(step) * tokens, tokens), columns].astype(BF16)
                )
            reduction.start(cut)

    def mixed(reduction, result):
        for step in range(1, owners):
            result = result + reduction.coming[step - 1].astype(F32)
        return result

    def send_back(reduction):
        for step in range(1, owners):
            span = pl.ds(owner_to(step) * tokens, tokens)
            reduction.put(step, slice(0, MODEL_WIDTH), r.total[span].astype(BF16))
            reduction.put(step, slice(MODEL_WIDTH, PACKED), two_parts(r.gate_total[span]))
        reduction.start(0)

    def came_back(reduction):
        back = r.kept_total[...]
        for step in range(1, owners):
            back = back + reduction.coming[step - 1, :, :MODEL_WIDTH].astype(F32)
        terms = reduction.coming[0, :, MODEL_WIDTH:].astype(F32)
        for step in range(2, owners):
            terms = terms + reduction.coming[step - 1, :, MODEL_WIDTH:].astype(F32)
        return back, r.kept_gate[...] + terms + pltpu.roll(terms, LANES - EXPERTS, 1)

    both_cuts = ((0, half), (half, half))
    spread_x0 = Spread(r.packed.at[0], r.plane0, 0)
    spread_x1 = Spread(r.packed.at[1], r.plane1, 1)
    spread_u1 = Spread(r.up, r.ups1, 2)
    spread_u0 = Spread(r.up0, r.ups0, 3)
    mix0 = Reduce(r.leave_y, r.come_y, 0, both_cuts)
    mix1 = Reduce(r.leave_y, r.come_y, 1, both_cuts)
    back1 = Reduce(r.leave_b, r.come_b, 2, ((0, PACKED),))
    back0 = Reduce(r.leave_b, r.come_b, 3, ((0, PACKED),))
    gather_x0 = Gather(0, r.packed.at[0], r.plane0, r.every_x, 0)
    gather_x1 = Gather(1, r.packed.at[1], r.plane1, r.every_x, 1)
    gather_u0 = Gather(0, r.up0, r.ups0, r.every_u, 2)
    gather_u1 = Gather(1, r.up, r.ups1, r.every_u, 3)
    for which in pieces:
        weights_start(0, which)
    for expert in range(local):
        for copy in swap_pair(expert):
            copy.start()

    @pl.when(section == 0)
    def _():
        for expert in range(local):
            load_in(0, expert)[0].start()
            load_out(0, expert)[0].start()

    r.small[...] = jnp.zeros_like(r.small)
    weights_spread(0, 0)
    weights_spread(0, 1)
    weights_forward(0, 0)
    weights_push(0, 0)
    weights_spread(0, 2)
    weights_forward(0, 1)
    weights_push(0, 1)

    def early0():
        for which in pieces:
            weights_start(1, which)

    def late0():
        weights_forward(0, 2)
        weights_push(0, 2)

    for copy in shared:
        copy.wait()
    for copy in own_rows:
        copy.wait()
    attention_forward(0, r.x, early0, late0)
    spread_x0.start()
    spread_x0.wait()
    for which in pieces:
        weights_spread(1, which)
    spread_u1.start()
    gather_u1.start()
    gather_x0.start_whole()
    gather_x0.start_home()

    def forward_expert(expert, carry):
        @pl.when(section != 0)
        def _():
            for which, make in enumerate((load_in, load_out)):
                swap_pair(expert)[which].wait_recv()
                make(0, expert)[1].start()

        wait_in(expert)

        def work(span, group):
            gate = gate_of(r.plane0, group, expert)
            pair = dot_nn(flat(r.plane0, group, model), r.ein[expert])
            r.pairs[expert, span] = pair.astype(BF16)
            gate_part, up_part = pair[:, :FF], pair[:, FF:]
            silu = gate_part / (1.0 + jnp.exp(-gate_part))
            r.activated[span, expert_columns(expert)] = (silu * up_part * gate).astype(BF16)

        each_chunk(work)
        start_load(load_in, 1, expert, 0, True)
        wait_out(expert)
        return carry

    lax.fori_loop(0, local // 2, forward_expert, 0)
    weights_forward(1, 0)
    weights_forward(1, 1)
    lax.fori_loop(local // 2, local, forward_expert, 0)
    mix(mix0)
    weights_forward(1, 2)
    weights_push(1, 0)
    weights_push(1, 1)
    for expert in range(local):
        start_load(load_out, 1, expert, 1, True)
    spread_u1.wait()
    gather_u1.start_home()
    mix0.wait()
    r.hidden0[...] = (r.middle[0] + mixed(mix0, r.total[here])).astype(BF16)
    place(0, r.hidden0, r.hidden, 0)

    def late1():
        weights_push(1, 2)

    attention_forward(1, r.hidden0, lambda: None, late1)
    spread_x1.start()
    gather_x1.start()

    def inner_expert(expert, carry):
        wait_out(expert)

        def work(span, group):
            r.inner[span, expert_columns(expert)] = dot_nt(
                flat(r.ups1, group, model), r.eout[expert_columns(expert)]
            ).astype(r.inner.dtype)

        each_chunk(work)
        return carry

    lax.fori_loop(0, local, inner_expert, 0)
    spread_x1.wait()
    gather_u1.middle()
    gather_x1.start_home()
    r.gate_total[...] = jnp.zeros_like(r.gate_total)

    def both_expert(expert, carry):
        wait_in(expert)

        def work(span, group):
            gate = gate_of(r.plane1, group, expert)
            pair = dot_nn(flat(r.plane1, group, model), r.ein[expert])
            inner = r.inner[span, expert_columns(expert)].astype(F32)
            activated = backward_terms(expert, span, gate, pair[:, :FF], pair[:, FF:], inner)
            r.activated[span, expert_columns(expert)] = (activated * gate).astype(BF16)

        each_chunk(work)
        start_load(load_in, 0, expert, 0, False)
        return carry

    lax.fori_loop(0, local // 2, both_expert, 0)
    gather_u1.forward()
    lax.fori_loop(local // 2, local, both_expert, 0)
    send_back(back1)
    r.kept_total[...] = r.total[here]
    r.kept_gate[...] = r.gate_total[here]
    mix(mix1)
    for expert in range(local):
        start_load(load_out, 0, expert, 1, False)
    back1.wait()
    back, gate_grads = came_back(back1)
    r.up0[...] = attention_backward(1, r.hidden0, r.up, back, gate_grads)
    spread_u0.start()
    gather_u0.start()
    place(1, r.up0, r.input_grad, 1)
    mix1.wait()
    r.hidden1[...] = (r.middle[1] + mixed(mix1, r.total[here])).astype(BF16)
    place(1, r.hidden1, r.hidden, 2)
    r.gate_total[...] = jnp.zeros_like(r.gate_total)
    spread_u0.wait()
    gather_x1.middle()
    gather_u0.start_home()

    def behind_expert(expert, carry):
        wait_in(expert)
        wait_out(expert)

        def work(span, group):
            gate = gate_of(r.plane0, group, expert)
            pair = r.pairs[expert, span].astype(F32)
            inner = dot_nt(flat(r.ups0, group, model), r.eout[expert_columns(expert)])
            backward_terms(expert, span, gate, pair[:, :FF], pair[:, FF:], inner)

        each_chunk(work)
        return carry

    lax.fori_loop(0, local // 2, behind_expert, 0)
    gather_x1.forward()
    gather_u0.middle()
    lax.fori_loop(local // 2, local, behind_expert, 0)
    send_back(back0)
    r.kept_total[...] = r.total[here]
    r.kept_gate[...] = r.gate_total[here]
    back0.wait()
    gather_u0.forward()
    back, gate_grads = came_back(back0)
    r.grad0[...] = attention_backward(0, r.x, r.up0, back, gate_grads)
    place(0, r.grad0, r.input_grad, 3)

    for layer in range(2):
        for which in pieces:
            weights_unsent(layer, which)
    for expert in range(local):
        for copy in swap_pair(expert):
            copy.wait_send()
    for copy in unsent:
        copy.wait_send()
    placed(0, r.hidden0, r.hidden, 0)
    placed(1, r.up0, r.input_grad, 1)
    placed(1, r.hidden1, r.hidden, 2)
    placed(0, r.grad0, r.input_grad, 3)
    gather_x0.finish_whole()
    for gather in (gather_u1, gather_x1, gather_u0):
        gather.finish()


def both_layers(layer_input, cotangent, routes, gain_one, attn_in, attn_out, gain_two, router, cosine, sine,
                experts_in, experts_out):
    planes, owners = lax.axis_size("dp"), lax.axis_size("expert")
    tokens = layer_input.shape[1]
    local = experts_in.shape[1]
    slab = attn_in.shape[1]
    rows = owners * tokens
    dma = lambda *shape: pltpu.SemaphoreType.DMA(shape)
    vmem = lambda shape, dtype: pltpu.VMEM(shape, dtype)
    wide = (2, tokens, MODEL_WIDTH)
    everywhere = (owners, planes, 2, tokens)
    inputs = dict(
        layer_input=(layer_input, any_spec()),
        cotangent=(cotangent, any_spec()),
        routes=(jnp.swapaxes(routes, 2, 3), vmem_spec()),
        gain_one=(gain_one, vmem_spec()),
        gain_two=(gain_two, vmem_spec()),
        router_in=(jnp.swapaxes(router, 1, 2), vmem_spec()),
        attn_in=(attn_in, any_spec()),
        attn_out=(attn_out, any_spec()),
        cosine=(cosine, vmem_spec()),
        sine=(sine, vmem_spec()),
        experts_in=(experts_in, any_spec()),
        experts_out=(experts_out, any_spec()),
    )
    outputs = dict(
        hidden=(wide, BF16, any_spec()),
        input_grad=(wide, BF16, any_spec()),
        other_in=(experts_in.shape[1:], BF16, any_spec()),
        other_out=(experts_out.shape[1:], BF16, any_spec()),
        every_x=(everywhere + (PACKED,), BF16, any_spec()),
        every_u=(everywhere + (MODEL_WIDTH,), BF16, any_spec()),
        projected_grad=((2, tokens, PROJECTED), BF16, vmem_spec()),
        low=(wide, BF16, vmem_spec()),
        chosen=(
            (2, MODEL_WIDTH // planes // LANES, tokens, 2 * planes * LANES), BF16, vmem_spec()
        ),
        small=((2, 16 + EXPERTS, MODEL_WIDTH), F32, vmem_spec()),
    )
    scratch = dict(
        win=vmem((2, MODEL_WIDTH, PROJECTED), BF16),
        wout=vmem((2, QUERY_WIDTH, MODEL_WIDTH), BF16),
        ein=vmem((local, MODEL_WIDTH, 2 * FF), BF16),
        eout=vmem((local * FF, MODEL_WIDTH), BF16),
        x=vmem(wide[1:], BF16),
        up=vmem(wide[1:], BF16),
        gains=vmem((2, 8, MODEL_WIDTH), F32),
        router=vmem((2, EXPERTS, MODEL_WIDTH), BF16),
        hot=vmem((2, tokens, LANES), F32),
        hot_out=vmem((tokens, LANES), F32),
        i_sem=dma(2),
        h_send=dma(3),
        h_recv=dma(3),
        projected=vmem((tokens, PROJECTED), F32),
        query=vmem(wide, BF16),
        key=vmem(wide, BF16),
        value=vmem(wide, BF16),
        attended=vmem(wide, BF16),
        logs=vmem((2, 2 * tokens, LANES), F32),
        middle=vmem(wide, F32),
        packed=vmem((2, tokens, PACKED), BF16),
        gates=vmem((2, tokens, LANES), F32),
        up0=vmem(wide[1:], BF16),
        hidden0=vmem(wide[1:], BF16),
        hidden1=vmem(wide[1:], BF16),
        grad0=vmem(wide[1:], BF16),
        grad_middle=vmem(wide[1:], F32),
        grad_attended=vmem(wide[1:], BF16),
        plane0=vmem((owners, tokens, PACKED), BF16),
        plane1=vmem((owners, tokens, PACKED), BF16),
        ups0=vmem((owners, tokens, MODEL_WIDTH), BF16),
        ups1=vmem((owners, tokens, MODEL_WIDTH), BF16),
        pairs=vmem((local, rows, 2 * FF), BF16),
        inner=vmem((rows, local * FF), BF16),
        activated=vmem((rows, local * FF), BF16),
        total=vmem((rows, MODEL_WIDTH), F32),
        gate_total=vmem((rows, LANES), F32),
        kept_total=vmem((tokens, MODEL_WIDTH), F32),
        kept_gate=vmem((tokens, LANES), F32),
        leave_y=vmem((owners - 1, tokens, MODEL_WIDTH), BF16),
        come_y=vmem((owners - 1, tokens, MODEL_WIDTH), BF16),
        leave_b=vmem((owners - 1, tokens, PACKED), BF16),
        come_b=vmem((owners - 1, tokens, PACKED), BF16),
        w_local=dma(2, 3),
        wz_send=dma(2, 3, planes),
        wz_recv=dma(2, 3, planes),
        wp_send=dma(2, 3, planes, owners),
        wp_recv=dma(2, 3, planes, owners),
        wc_send=dma(2, 3, planes),
        wc_recv=dma(2, 3, planes),
        s_send=dma(2, local),
        s_recv=dma(2, local),
        l_sem=dma(2, local),
        a_send=dma(4, owners),
        a_recv=dma(4, owners),
        r_send=dma(4, 2, owners),
        r_recv=dma(4, 2, owners),
        g_send=dma(4, planes),
        g_recv=dma(4, planes, 2),
        g_local=dma(4),
        gp_send=dma(4, owners),
        gp_recv=dma(4, owners),
        o_send=dma(4),
        o_recv=dma(4),
        o_local=dma(4),
    )
    return call(
        functools.partial(layers_kernel, planes, owners, tokens, local, slab),
        "both_layers", 0, inputs, outputs, scratch,
    )


def ExpertGrads(planes, owners, tokens, local, first, r):
    plane = lax.axis_index("dp")
    own = lax.axis_index("expert")
    group = 4 * tokens
    slots = group // 2
    groups = 2 * planes * owners * tokens // group
    slice_in, slice_out = MODEL_WIDTH // planes, FF // planes
    chunk = min(groups * slots, 1024)
    chunks = groups * slots // chunk
    tile = 512
    depth = r.x_rows.shape[0]
    shift = first if r.grad_in.shape[0] < local else 0

    def weights_of(expert):
        slot = expert % 2
        return (
            pltpu.make_async_copy(r.experts_in.at[0, expert], r.ein.at[slot], r.e_sem.at[0, slot]),
            pltpu.make_async_copy(r.experts_out.at[0, expert], r.eout.at[slot], r.e_sem.at[1, slot]),
        )

    def rows_of(number):
        slot = number % depth
        span = pl.ds(pl.multiple_of(number * group, group), group)
        return (
            pltpu.make_async_copy(r.every_x.at[span], r.x_rows.at[slot], r.t_sem.at[0, slot]),
            pltpu.make_async_copy(r.every_u.at[span], r.u_rows.at[slot], r.t_sem.at[1, slot]),
        )

    pack = r.compact_x.shape[0]
    bunch = r.picks.shape[0] // slots
    before = (
        lax.broadcasted_iota(jnp.int32, (group, group), 0) < lax.broadcasted_iota(jnp.int32, (group, group), 1)
    ).astype(BF16)
    same = (
        lax.broadcasted_iota(jnp.int32, (group, group), 0) == lax.broadcasted_iota(jnp.int32, (group, group), 1)
    ).astype(BF16)
    numbers = lax.broadcasted_iota(jnp.int32, (slots, group), 0).astype(F32)

    def gather():
        def one(number, carry):
            slot = number % depth
            for copy in rows_of(number):
                copy.wait()

            @pl.when(number + depth - 1 < groups)
            def _():
                for copy in rows_of(number + depth - 1):
                    copy.start()

            parts = r.x_rows[slot, :, MODEL_WIDTH:].astype(F32)
            chosen = (parts != 0.0).astype(BF16)
            rank = dot_tn(chosen, before)
            r.ranks[...] = jnp.where(dot_tn(chosen, same) > 0.0, rank, -1.0)
            span = pl.ds(pl.multiple_of(number * slots, slots), slots)
            for low in range(0, pack, bunch):
                few = min(bunch, pack - low)
                for index in range(few):
                    rank_row = r.ranks[pl.ds(own * local + first + low + index, 1), :]
                    r.picks[index * slots : (index + 1) * slots, :] = (numbers == rank_row).astype(BF16)
                for source, target in ((r.x_rows, r.compact_x), (r.u_rows, r.compact_u)):
                    found = dot_nn(r.picks[: few * slots], source[slot]).astype(BF16)
                    for index in range(few):
                        target[low + index, span] = found[index * slots : (index + 1) * slots]
            return carry

        lax.fori_loop(0, groups, one, 0)

    def out_of(expert):
        slot = expert % 2
        return (
            pltpu.make_async_copy(r.din.at[slot], r.grad_in.at[expert - shift], r.d_sem.at[0, slot]),
            pltpu.make_async_copy(r.dout.at[slot], r.grad_out.at[expert - shift], r.d_sem.at[1, slot]),
        )

    def one_expert(expert, index):
        slot = expert % 2
        for copy in weights_of(expert):
            copy.wait()

        @pl.when(expert + 1 < first + pack)
        def _():
            for copy in weights_of(expert + 1):
                copy.start()

        @pl.when(expert >= first + 2)
        def _():
            for copy in out_of(expert - 2):
                copy.wait()

        for number in range(chunks):

            def one_tile(step, carry):
                span = pl.ds(pl.multiple_of(number * chunk + step * tile, tile), tile)
                here = pl.ds(pl.multiple_of(step * tile, tile), tile)
                gate = column_of(
                    r.compact_x[index, span, MODEL_WIDTH:], lane_of((tile, LANES)), own * local + expert
                )
                pair = dot_nn(r.compact_x[index, span, :MODEL_WIDTH], r.ein[slot])
                gate_part, up_part = pair[:, :FF], pair[:, FF:]
                sigmoid = 1.0 / (1.0 + jnp.exp(-gate_part))
                silu = gate_part * sigmoid
                r.activated[here] = (silu * up_part * gate).astype(BF16)
                grad_activated = dot_nt(r.compact_u[index, span], r.eout[slot]) * gate
                r.grad_pair[here, :FF] = (
                    grad_activated * up_part * sigmoid * (1.0 + gate_part * (1.0 - sigmoid))
                ).astype(BF16)
                r.grad_pair[here, FF:] = (grad_activated * silu).astype(BF16)
                return carry

            lax.fori_loop(0, chunk // tile, one_tile, 0)
            rows = slice(number * chunk, (number + 1) * chunk)
            left_in = r.compact_x[index, rows, pl.ds(pl.multiple_of(plane * slice_in, LANES), slice_in)]
            left_out = r.activated[:, pl.ds(pl.multiple_of(plane * slice_out, LANES), slice_out)]
            term_in = dot_tn(left_in, r.grad_pair[...])
            term_out = dot_tn(left_out, r.compact_u[index, rows])
            if number == 0:
                r.din[slot] = term_in
                r.dout[slot] = term_out
            else:
                r.din[slot] += term_in
                r.dout[slot] += term_out
        for copy in out_of(expert):
            copy.start()

    def run(low, high):
        def body(index, carry):
            one_expert(first + index, index)
            return carry

        if high > low:
            lax.fori_loop(low, high, body, 0)

    def start():
        for number in range(min(depth - 1, groups)):
            for copy in rows_of(number):
                copy.start()
        for copy in weights_of(first):
            copy.start()

    def finish():
        for expert in range(max(first, first + pack - 2), first + pack):
            for copy in out_of(expert):
                copy.wait()

    names = Names()
    names.load, names.gather, names.run, names.finish, names.pack = start, gather, run, finish, pack
    return names


def gradients_kernel(planes, owners, tokens, local, r):
    section = lax.axis_index("section")
    plane = lax.axis_index("dp")
    own = lax.axis_index("expert")
    partner = dict(section=1 - section)
    part = MODEL_WIDTH // (planes * owners)
    barrier = pltpu.get_barrier_semaphore()
    for step in range(1, owners):
        pl.semaphore_signal(barrier, inc=1, device_id=dict(expert=(own + step) % owners), device_id_type=MESH)
    for step in range(1, planes):
        pl.semaphore_signal(barrier, inc=1, device_id=dict(dp=(plane + step) % planes), device_id_type=MESH)
    pl.semaphore_signal(barrier, inc=1, device_id=partner, device_id_type=MESH)

    experts = ExpertGrads(planes, owners, tokens, local, 0, r)
    experts.load()

    def meet(source, target, index):
        here = pltpu.make_async_copy(source.at[section], target.at[section], r.m_local.at[index])
        there = remote(source.at[1 - section], target.at[section], r.m_send.at[index], r.m_recv.at[index], partner)
        return here, there

    meets = [
        meet(r.low, r.all_low.at[own], 0),
        meet(r.chosen, r.both_chosen, 1),
        meet(r.small, r.both_small, 2),
        meet(r.projected_grad, r.all_projected.at[own], 3),
    ]
    pl.semaphore_wait(barrier, owners - 1 + planes - 1 + 1)
    for here, there in meets:
        here.start()
        there.start()

    def piece_of(buffer):
        return lambda owner, half: buffer.at[owner] if half is None else buffer.at[owner, half]

    spreads = (
        PlaneBroadcast(owners, own, piece_of(r.all_low), r.f_send.at[0], r.f_recv.at[0]),
        PlaneBroadcast(owners, own, piece_of(r.all_projected), r.f_send.at[1], r.f_recv.at[1]),
    )
    width = planes * LANES

    def variant_of(owner):
        return owner * part // LANES

    def chosen_to(step, which):
        target = (own + step) % owners
        columns = pl.ds((1 - which) * width, width)
        return remote(
            r.both_chosen.at[:, variant_of(target), :, columns], r.all_chosen.at[own, :, :, columns],
            r.c_send.at[which, step], r.c_recv.at[which, step], dict(expert=target),
        )

    def small_to(step):
        return remote(
            r.small_out, r.small_in.at[step - 1], r.v_send.at[step], r.v_recv.at[step],
            dict(expert=(own + step) % owners),
        )

    halves = (
        (r.all_low, r.product_out, r.sums, r.leaving_out),
        (r.all_projected, r.product_in, r.partial, None),
    )

    def sums_over(step):
        return remote(
            r.leaving_out.at[step - 1], r.arriving_out.at[step - 1], r.z_send.at[step], r.z_recv.at[step],
            dict(dp=(plane + step) % planes),
        )

    def attention_start():
        for here, there in meets:
            here.wait()
            there.wait_recv()
        r.small_kept[...] = r.both_small[0] + r.both_small[1]
        r.small_out[...] = r.small_kept[...].astype(BF16)
        for step in range(1, owners):
            small_to(step).start()
        for which in range(2):
            spreads[which].start()
            for step in range(1, owners):
                chosen_to(step, which).start()
        r.all_chosen[own] = r.both_chosen[:, variant_of(own)]

    def attention_small():
        total = r.small_kept[...]
        for step in range(1, owners):
            small_to(step).wait_recv()
            total = total + r.small_in[step - 1].astype(F32)
        r.sums[part:] = total
        for step in range(1, planes):
            r.leaving_out[step - 1, part:] = total.astype(BF16)

    def attention_partial(which):
        factors, product, partial, leaving = halves[which]
        spreads[which].wait()
        for step in range(1, owners):
            chosen_to(step, which).wait_recv()
        within = own * part % LANES
        some = min(owners, 4)
        pile = some * 2 * tokens
        for step in list(range(1, planes)) + [0]:
            target = (plane + step) % planes
            columns = pl.ds(pl.multiple_of(((1 - which) * planes + target) * LANES, LANES), LANES)
            for first in range(0, owners, some):
                left = r.all_chosen[first : first + some, :, :, columns].reshape(pile, LANES)
                term = dot_tn(left, factors[first : first + some].reshape(pile, factors.shape[-1]))
                if first == 0:
                    product[...] = term
                else:
                    product[...] += term
            mine = product[pl.ds(pl.multiple_of(within, 16), part)]
            if step == 0:
                partial[:part] = mine
            else:
                if which == 0:
                    leaving[step - 1, :part] = mine.astype(BF16)
                    sums_over(step).start()
                else:
                    getattr(r, f"to{step}")[...] = mine.astype(BF16)

    def attention_last():
        total = r.sums[...]
        for step in range(1, planes):
            sums_over(step).wait()
            total = total + r.arriving_out[step - 1].astype(F32)
        r.sums[...] = total
        for here, there in meets:
            there.wait_send()
        for which in range(2):
            spreads[which].sent()
            for step in range(1, owners):
                chosen_to(step, which).wait_send()
        for step in range(1, owners):
            small_to(step).wait_send()

    attention_start()
    experts.gather()
    pack = experts.pack
    experts.run(0, pack // 6)
    attention_small()
    spreads[0].forward()
    experts.run(pack // 6, 2 * pack // 6)
    spreads[1].forward()
    experts.run(2 * pack // 6, 3 * pack // 6)
    attention_partial(0)
    experts.run(3 * pack // 6, pack)
    experts.finish()
    attention_partial(1)
    attention_last()


def rest_kernel(planes, owners, tokens, local, first, r):
    experts = ExpertGrads(planes, owners, tokens, local, first, r)
    experts.load()
    held = ((r.first_in, r.held_in, r.grad_in), (r.first_out, r.held_out, r.grad_out))
    entering = [
        pltpu.make_async_copy(source, here, r.move_sem.at[0, index]) for index, (source, here, _) in enumerate(held)
    ]
    moving = [
        pltpu.make_async_copy(here, target.at[pl.ds(0, first)], r.move_sem.at[1, index])
        for index, (_, here, target) in enumerate(held)
    ]
    for copy in entering:
        copy.start()
    part = r.grad_attn_out.shape[0]
    r.grad_attn_out[...] = r.sums[:part]
    r.grad_gain_one[...] = r.sums[part : part + 1]
    r.grad_gain_two[...] = r.sums[part + 1 : part + 2]
    r.grad_router[...] = r.sums[part + 16 :]
    r.hidden_out[...] = r.hidden[...]
    r.input_grad_out[...] = r.input_grad[...]
    experts.gather()
    for number in range(2):
        entering[number].wait()
        moving[number].start()
    experts.run(0, experts.pack)
    experts.finish()
    for copy in moving:
        copy.wait()


def grads_scratch(planes, owners, tokens, pack):
    group = 4 * tokens
    groups = 2 * planes * owners * tokens // group
    slots = group // 2
    chunk = min(groups * slots, 1024)
    dma = lambda *shape: pltpu.SemaphoreType.DMA(shape)
    vmem = lambda shape, dtype: pltpu.VMEM(shape, dtype)
    return dict(
        ein=vmem((2, MODEL_WIDTH, 2 * FF), BF16),
        eout=vmem((2, FF, MODEL_WIDTH), BF16),
        x_rows=vmem((4, group, PACKED), BF16),
        u_rows=vmem((4, group, MODEL_WIDTH), BF16),
        ranks=vmem((LANES, group), F32),
        picks=vmem((min(pack, 5) * slots, group), BF16),
        compact_x=vmem((pack, groups * slots, PACKED), BF16),
        compact_u=vmem((pack, groups * slots, MODEL_WIDTH), BF16),
        activated=vmem((chunk, FF), BF16),
        grad_pair=vmem((chunk, 2 * FF), BF16),
        din=vmem((2, MODEL_WIDTH // planes, 2 * FF), F32),
        dout=vmem((2, FF // planes, MODEL_WIDTH), F32),
        e_sem=dma(2, 2),
        t_sem=dma(2, 4),
        d_sem=dma(2, 2),
    )


def weight_gradients(done, experts_in, experts_out):
    planes, owners = lax.axis_size("dp"), lax.axis_size("expert")
    local = experts_in.shape[1]
    tokens = done.low.shape[1]
    part = MODEL_WIDTH // (planes * owners)
    first = max(1, 6 * local // 8)
    wide = 2 * planes * LANES
    variants = done.chosen.shape[1]
    small = done.small.shape[1:]
    dma = lambda *shape: pltpu.SemaphoreType.DMA(shape)
    vmem = lambda shape, dtype: pltpu.VMEM(shape, dtype)
    shape_in, shape_out = (MODEL_WIDTH // planes, 2 * FF), (FF // planes, MODEL_WIDTH)
    tables = dict(
        every_x=(done.every_x.reshape(-1, PACKED), any_spec()),
        every_u=(done.every_u.reshape(-1, MODEL_WIDTH), any_spec()),
        experts_in=(experts_in, any_spec()),
        experts_out=(experts_out, any_spec()),
    )
    exchanged = call(
        functools.partial(gradients_kernel, planes, owners, tokens, local),
        "weight_gradients",
        1,
        dict(
            projected_grad=(done.projected_grad, vmem_spec()),
            low=(done.low, vmem_spec()),
            chosen=(done.chosen, vmem_spec()),
            small=(done.small, vmem_spec()),
            **tables,
        ),
        dict(
            grad_in=((first,) + shape_in, F32, any_spec()),
            grad_out=((first,) + shape_out, F32, any_spec()),
            partial=((part, PROJECTED), F32, vmem_spec()),
            sums=((part + small[0], MODEL_WIDTH), F32, vmem_spec()),
            **{f"to{step}": ((part, PROJECTED), BF16, vmem_spec()) for step in range(1, planes)},
        ),
        dict(
            all_low=vmem((owners, 2, tokens, MODEL_WIDTH), BF16),
            all_projected=vmem((owners, 2, tokens, PROJECTED), BF16),
            both_chosen=vmem((2, variants, tokens, wide), BF16),
            all_chosen=vmem((owners, 2, tokens, wide), BF16),
            both_small=vmem((2,) + small, F32),
            small_kept=vmem(small, F32),
            small_out=vmem(small, BF16),
            small_in=vmem((owners - 1,) + small, BF16),
            product_in=vmem((LANES, PROJECTED), F32),
            product_out=vmem((LANES, MODEL_WIDTH), F32),
            leaving_out=vmem((planes - 1, part + small[0], MODEL_WIDTH), BF16),
            arriving_out=vmem((planes - 1, part + small[0], MODEL_WIDTH), BF16),
            z_send=dma(planes),
            z_recv=dma(planes),
            m_local=dma(4),
            m_send=dma(4),
            m_recv=dma(4),
            f_send=dma(2, owners),
            f_recv=dma(2, owners),
            c_send=dma(2, owners),
            c_recv=dma(2, owners),
            v_send=dma(owners),
            v_recv=dma(owners),
            **grads_scratch(planes, owners, tokens, first),
        ),
    )
    total = exchanged.partial
    arriving = [
        lax.ppermute(getattr(exchanged, f"to{step}"), "dp", [(i, (i + step) % planes) for i in range(planes)])
        for step in range(1, planes)
    ]
    count = local - first
    rows = 2 * planes * owners * tokens
    rest = call(
        functools.partial(rest_kernel, planes, owners, tokens, local, first),
        "other_experts",
        None,
        dict(
            first_in=(exchanged.grad_in, any_spec()),
            first_out=(exchanged.grad_out, any_spec()),
            sums=(exchanged.sums, vmem_spec()),
            hidden=(done.hidden, vmem_spec()),
            input_grad=(done.input_grad, vmem_spec()),
            **tables,
        ),
        dict(
            grad_in=((local,) + shape_in, F32, any_spec()),
            grad_out=((local,) + shape_out, F32, any_spec()),
            grad_attn_out=((part, MODEL_WIDTH), F32, vmem_spec()),
            grad_gain_one=((1, MODEL_WIDTH), F32, vmem_spec()),
            grad_gain_two=((1, MODEL_WIDTH), F32, vmem_spec()),
            grad_router=((EXPERTS, MODEL_WIDTH), F32, vmem_spec()),
            hidden_out=(done.hidden.shape, BF16, vmem_spec()),
            input_grad_out=(done.hidden.shape, BF16, vmem_spec()),
        ),
        dict(
            held_in=vmem((first,) + shape_in, F32),
            held_out=vmem((first,) + shape_out, F32),
            move_sem=dma(2, 2),
            **grads_scratch(planes, owners, tokens, count),
        ),
        pl.CostEstimate(flops=count * rows * 6 * MODEL_WIDTH * FF, bytes_accessed=rows * 4 * MODEL_WIDTH, transcendentals=0),
    )
    arriving, rest.grad_in = lax.optimization_barrier((arriving, rest.grad_in))
    for piece in arriving:
        total = total + piece.astype(F32)
    return rest, total


def shards(layer_input, cotangent, positions, routes, gain_one, attn_in, attn_out, gain_two, router,
           experts_in, experts_out):
    place = lax.dynamic_index_in_dim(positions, lax.axis_index("section"), 0, keepdims=False)
    lane = jnp.arange(LANES)
    frequency = jnp.power(rotary_base, -((lane % HALF).astype(F32) * (2.0 / HEAD_SIZE)))
    angles = place.astype(F32)[:, None] * frequency[None, :]
    cosine = jnp.cos(angles)
    sine = jnp.where(lane % HEAD_SIZE < HALF, -1.0, 1.0) * jnp.sin(angles)

    done = both_layers(
        layer_input, cotangent, routes, gain_one, attn_in, attn_out, gain_two, router, cosine, sine,
        experts_in, experts_out,
    )
    rest, grad_attn_in = weight_gradients(done, experts_in, experts_out)
    return (
        rest.hidden_out[None],
        rest.input_grad_out[None],
        rest.grad_gain_one,
        grad_attn_in[None],
        rest.grad_attn_out[None],
        rest.grad_gain_two,
        rest.grad_router.T[None],
        rest.grad_in[None],
        rest.grad_out[None],
    )


def solution(mesh):
    in_specs = (
        P(None, ("dp", "expert"), None),
        P(None, ("dp", "expert"), None),
        P(None, ("dp", "expert")),
        P("section", None, ("dp", "expert"), None),
        P("section", None),
        P("section", "dp", None),
        P("section", "dp", None),
        P("section", None),
        P("section", None, None),
        P("section", "expert", None, None),
        P("section", "expert", None, None),
    )
    out_specs = (
        P("section", None, ("dp", "expert"), None),
        P("section", None, ("dp", "expert"), None),
        P("section", None),
        P("section", ("dp", "expert"), None),
        P("section", ("dp", "expert"), None),
        P("section", None),
        P("section", None, None),
        P("section", "expert", "dp", None),
        P("section", "expert", "dp", None),
    )
    return jax.shard_map(shards, mesh=mesh, in_specs=in_specs, out_specs=out_specs, check_vma=False)
```

```python
import functools

import jax
import jax.numpy as jnp
from jax import lax
from jax.experimental import pallas as pl
from jax.experimental.pallas import tpu as pltpu
from jax.sharding import PartitionSpec as P

MODEL_WIDTH = 1024
QUERY_HEADS = 16
KEY_VALUE_HEADS = 8
HEAD_SIZE = 64
FF = 512
EXPERTS = 32
TOPK = 8

QUERY_WIDTH = QUERY_HEADS * HEAD_SIZE
KEY_WIDTH = KEY_VALUE_HEADS * HEAD_SIZE
PROJECTED = QUERY_WIDTH + 2 * KEY_WIDTH
LANES = 128
HALF = HEAD_SIZE // 2
PACKED = MODEL_WIDTH + LANES

epsilon = 1e-06
rotary_base = 10000.0

F32 = jnp.float32
BF16 = jnp.bfloat16
MESH = pl.DeviceIdType.MESH
VMEM_LIMIT = 62 * 1024 * 1024


def dot_nn(a, b):
    return lax.dot_general(a, b, (((1,), (0,)), ((), ())), preferred_element_type=F32)


def dot_nt(a, b):
    return lax.dot_general(a, b, (((1,), (1,)), ((), ())), preferred_element_type=F32)


def dot_tn(a, b):
    return lax.dot_general(a, b, (((0,), (0,)), ((), ())), preferred_element_type=F32)


def row_scale(values):
    return lax.rsqrt(jnp.mean(values * values, axis=-1, keepdims=True) + epsilon)


def norm_back(grad_normed, inputs, scale):
    return scale * grad_normed - inputs * (scale * scale * scale) * jnp.mean(
        grad_normed * inputs, axis=-1, keepdims=True
    )


def lane_of(shape):
    return lax.broadcasted_iota(jnp.int32, shape, 1)


def turned(tile, low):
    return jnp.where(low, pltpu.roll(tile, LANES - HALF, 1), pltpu.roll(tile, HALF, 1))


def two_parts(values):
    high = values.astype(BF16).astype(F32)
    return (high + pltpu.roll(values - high, EXPERTS, 1)).astype(BF16)


def column_of(parts, lane, column):
    wide = parts.astype(F32)
    return jnp.sum(jnp.where((lane == column) | (lane == column + EXPERTS), wide, 0.0), axis=-1, keepdims=True)


def remote(source, target, send, recv, device):
    return pltpu.make_async_remote_copy(
        src_ref=source, dst_ref=target, send_sem=send, recv_sem=recv, device_id=device, device_id_type=MESH
    )


def vmem_spec():
    return pl.BlockSpec(memory_space=pltpu.VMEM)


def any_spec():
    return pl.BlockSpec(memory_space=pl.ANY)


class Names:
    pass


def call(kernel, name, number, inputs, outputs, scratch, cost=None):
    labels = list(inputs) + list(outputs) + list(scratch)

    def body(*refs):
        names = Names()
        for label, ref in zip(labels, refs):
            setattr(names, label, ref)
        kernel(names)

    if number is None:
        params = pltpu.CompilerParams(vmem_limit_bytes=VMEM_LIMIT)
    else:
        params = pltpu.CompilerParams(
            collective_id=number, has_side_effects=True, vmem_limit_bytes=VMEM_LIMIT
        )
    results = pl.pallas_call(
        body,
        out_shape=tuple(jax.ShapeDtypeStruct(shape, dtype) for shape, dtype, _ in outputs.values()),
        in_specs=[spec for _, spec in inputs.values()],
        out_specs=tuple(spec for _, _, spec in outputs.values()),
        scratch_shapes=list(scratch.values()),
        compiler_params=params,
        cost_estimate=cost,
        name=name,
    )(*[array for array, _ in inputs.values()])
    names = Names()
    for label, result in zip(outputs, results):
        setattr(names, label, result)
    return names


class PlaneBroadcast:
    def __init__(self, owners, own, piece, send, recv):
        self.owners, self.own = owners, own
        self.square = owners == 4
        self.piece, self.send, self.recv = piece, send, recv

    def hop(self, owner, half, index, device):
        block = self.piece(owner, half)
        return remote(block, block, self.send.at[index], self.recv.at[index], dict(expert=device))

    def hops(self):
        owners, own = self.owners, self.own

        def owner_to(step):
            return (own + step) % owners

        if not self.square:
            return [self.hop(own, None, turn, owner_to(turn)) for turn in range(1, owners)]
        beside = own + 1 - 2 * (own % 2)
        above = owner_to(2)
        return [
            self.hop(own, None, 0, beside),
            self.hop(own, None, 1, above),
            self.hop(beside, 0, 2, above),
            self.hop(above, 1, 3, beside),
        ]

    def start(self):
        hops = self.hops()
        for hop in hops[:2] if self.square else hops:
            hop.start()

    def forward(self):
        if self.square:
            hops = self.hops()
            for hop in range(2):
                hops[hop].wait_recv()
                hops[2 + hop].start()

    def wait(self):
        hops = self.hops()
        for hop in hops[2:] if self.square else hops:
            hop.wait_recv()

    def sent(self):
        for hop in self.hops():
            hop.wait_send()


def layers_kernel(planes, owners, tokens, local, slab, r):
    section = lax.axis_index("section")
    plane = lax.axis_index("dp")
    own = lax.axis_index("expert")
    rows = owners * tokens
    part = slab // owners
    here = pl.ds(own * tokens, tokens)
    partner = dict(section=1 - section)

    def planes_to(step):
        return (plane + step) % planes

    def owner_to(step):
        return (own + step) % owners

    barrier = pltpu.get_barrier_semaphore()
    for step in range(1, owners):
        pl.semaphore_signal(barrier, inc=1, device_id=dict(expert=owner_to(step)), device_id_type=MESH)
    for step in range(1, planes):
        for target in range(2):
            pl.semaphore_signal(
                barrier, inc=1, device_id=dict(section=target, dp=planes_to(step)), device_id_type=MESH
            )
    pl.semaphore_signal(barrier, inc=1, device_id=partner, device_id_type=MESH)
    pl.semaphore_wait(barrier, owners - 1 + 2 * (planes - 1) + 1)

    unsent = []

    own_rows = [
        pltpu.make_async_copy(r.layer_input.at[section], r.x, r.i_sem.at[0]),
        pltpu.make_async_copy(r.cotangent.at[section], r.up, r.i_sem.at[1]),
    ]
    for copy in own_rows:
        copy.start()

    unit = (
        lax.broadcasted_iota(jnp.int32, (EXPERTS, LANES), 0) == lax.broadcasted_iota(jnp.int32, (EXPERTS, LANES), 1)
    ).astype(BF16)

    def hot_of(choices):
        number = lax.broadcasted_iota(jnp.int32, (EXPERTS, tokens), 0)
        found = jnp.zeros((EXPERTS, tokens), F32)
        for choice in range(TOPK):
            found = jnp.where(number == choices[choice : choice + 1], 1.0, found)
        return dot_tn(found.astype(BF16), unit)

    r.gains[section, 0:1] = r.gain_one[...]
    r.gains[section, 1:2] = r.gain_two[...]
    r.router[section] = r.router_in[0]
    r.hot[section] = hot_of(r.routes[0, section])
    r.hot_out[...] = hot_of(r.routes[0, 1 - section])
    shared = [
        remote(source, target, r.h_send.at[index], r.h_recv.at[index], partner)
        for index, (source, target) in enumerate(
            (
                (r.gains.at[section], r.gains.at[section]),
                (r.router.at[section], r.router.at[section]),
                (r.hot_out, r.hot.at[section]),
            )
        )
    ]
    for copy in shared:
        copy.start()

    def Broadcast(piece, send, recv):
        return PlaneBroadcast(owners, own, piece, send, recv)

    weight_pieces = ((r.attn_in, r.win, 0), (r.attn_in, r.win, QUERY_WIDTH), (r.attn_out, r.wout, 0))
    pieces = range(len(weight_pieces))

    def slab_local(layer, which):
        source, full, column = weight_pieces[which]
        columns = pl.ds(column, MODEL_WIDTH)
        return pltpu.make_async_copy(
            source.at[0, :, columns], full.at[layer, pl.ds(plane * slab, slab), columns], r.w_local.at[layer, which]
        )

    def slab_z(layer, which, step):
        source, full, column = weight_pieces[which]
        columns = pl.ds(column, MODEL_WIDTH)
        return remote(
            source.at[0, pl.ds(own * part, part), columns],
            full.at[layer, pl.ds(plane * slab + own * part, part), columns],
            r.wz_send.at[layer, which, step],
            r.wz_recv.at[layer, which, step],
            dict(dp=planes_to(step)),
        )

    def slab_plane(layer, which, step):
        full, column = weight_pieces[which][1:]
        origin = planes_to(planes - step)

        def piece(owner, half):
            start, length = origin * slab + owner * part, part
            if half is not None:
                length = part // 2
                start = start + half * length
            return full.at[layer, pl.ds(start, length), pl.ds(column, MODEL_WIDTH)]

        return Broadcast(piece, r.wp_send.at[layer, which, step], r.wp_recv.at[layer, which, step])

    def slab_core(layer, which, step):
        full, column = weight_pieces[which][1:]
        block = full.at[layer, pl.ds(planes_to(planes - step) * slab, slab), pl.ds(column, MODEL_WIDTH)]
        return remote(block, block, r.wc_send.at[layer, which, step], r.wc_recv.at[layer, which, step], partner)

    def weights_start(layer, which):
        @pl.when(section == layer)
        def _():
            for step in range(1, planes):
                slab_z(layer, which, step).start()
            slab_local(layer, which).start()

    def weights_spread(layer, which):
        @pl.when(section == layer)
        def _():
            slab_local(layer, which).wait()
            slab_core(layer, which, 0).start()
            for step in range(1, planes):
                slab_z(layer, which, step).wait_recv()
                slab_plane(layer, which, step).start()

    def weights_forward(layer, which):
        @pl.when(section == layer)
        def _():
            for step in range(1, planes):
                slab_plane(layer, which, step).forward()

    def weights_push(layer, which):
        @pl.when(section == layer)
        def _():
            for step in range(1, planes):
                slab_plane(layer, which, step).wait()
                slab_core(layer, which, step).start()

    def weights_wait(layer, which):
        @pl.when(section != layer)
        def _():
            for step in range(planes):
                slab_core(layer, which, step).wait_recv()

    def weights_unsent(layer, which):
        @pl.when(section == layer)
        def _():
            for step in range(1, planes):
                slab_z(layer, which, step).wait_send()
                slab_plane(layer, which, step).sent()
            for step in range(planes):
                slab_core(layer, which, step).wait_send()

    def swap_pair(expert):
        return (
            remote(r.experts_in.at[0, expert], r.other_in.at[expert], r.s_send.at[0, expert], r.s_recv.at[0, expert], partner),
            remote(r.experts_out.at[0, expert], r.other_out.at[expert], r.s_send.at[1, expert], r.s_recv.at[1, expert], partner),
        )

    def load_in(layer, expert):
        mine = pltpu.make_async_copy(r.experts_in.at[0, expert], r.ein.at[expert], r.l_sem.at[0, expert])
        other = pltpu.make_async_copy(r.other_in.at[expert], r.ein.at[expert], r.l_sem.at[0, expert])
        return mine, other

    def load_out(layer, expert):
        target = r.eout.at[pl.ds(expert * FF, FF)]
        mine = pltpu.make_async_copy(r.experts_out.at[0, expert], target, r.l_sem.at[1, expert])
        other = pltpu.make_async_copy(r.other_out.at[expert], target, r.l_sem.at[1, expert])
        return mine, other

    def start_load(make, layer, expert, which, first_use):
        @pl.when(section == layer)
        def _():
            make(layer, expert)[0].start()

        @pl.when(section != layer)
        def _():
            if first_use:
                swap_pair(expert)[which].wait_recv()
            make(layer, expert)[1].start()

    class Spread:
        def __init__(self, source, buffer, index):
            self.copies = [
                remote(source, buffer.at[own], r.a_send.at[index, step], r.a_recv.at[index, step],
                       dict(expert=owner_to(step)))
                for step in range(1, owners)
            ]
            self.source, self.buffer = source, buffer

        def start(self):
            for copy in self.copies:
                copy.start()
            self.buffer[own] = self.source[...]

        def wait(self):
            for copy in self.copies:
                copy.wait_recv()
            unsent.extend(self.copies)

    class Reduce:
        def __init__(self, leaving, coming, index, cuts):
            self.leaving, self.coming, self.index, self.cuts = leaving, coming, index, cuts
            self.copies = {
                (cut, step): remote(
                    leaving.at[step - 1, :, pl.ds(*cuts[cut])],
                    coming.at[step - 1, :, pl.ds(*cuts[cut])],
                    r.r_send.at[index, cut, step],
                    r.r_recv.at[index, cut, step],
                    dict(expert=owner_to(step)),
                )
                for cut in range(len(cuts))
                for step in range(1, owners)
            }

        def put(self, step, columns, values):
            self.leaving[step - 1, :, columns] = values

        def start(self, cut):
            for step in range(1, owners):
                self.copies[cut, step].start()

        def wait(self):
            for copy in self.copies.values():
                copy.wait()

    class Gather:
        def __init__(self, layer, block, around, target, index):
            self.layer, self.block, self.around, self.target, self.index = layer, block, around, target, index

        def across(self, step):
            return [
                remote(
                    self.block,
                    self.target.at[own, (planes - step) % planes, section],
                    r.g_send.at[self.index, step],
                    r.g_recv.at[self.index, step, section],
                    dict(section=self.layer, dp=planes_to(step)),
                )
            ][0]

        def arrival(self, step, micro):
            return remote(
                self.block,
                self.target.at[own, (planes - step) % planes, micro],
                r.g_send.at[self.index, step],
                r.g_recv.at[self.index, step, micro],
                dict(section=self.layer, dp=planes_to(step)),
            )

        def home_local(self):
            return pltpu.make_async_copy(self.around, self.target.at[:, 0, section], r.g_local.at[self.index])

        def home_remote(self, micro):
            return remote(self.around, self.target.at[:, 0, micro], r.g_send.at[self.index, 0],
                          r.g_recv.at[self.index, 0, 0], partner)

        def inside(self):
            def piece(owner, half):
                if half is None:
                    return self.target.at[owner, pl.ds(1, planes - 1)]
                return self.target.at[owner, pl.ds(1, planes - 1), half]

            return Broadcast(piece, r.gp_send.at[self.index], r.gp_recv.at[self.index])

        def whole_to(self, step, micro):
            return remote(
                self.around,
                self.target.at[:, (planes - step) % planes, micro],
                r.g_send.at[self.index, step],
                r.g_recv.at[self.index, step, micro],
                dict(section=self.layer, dp=planes_to(step)),
            )

        def start_whole(self):
            for step in range(1, planes):
                self.whole_to(step, section).start()

        def finish_whole(self):
            for step in range(1, planes):
                self.whole_to(step, section).wait_send()

            @pl.when(section == self.layer)
            def _():
                for step in range(1, planes):
                    for micro in range(2):
                        self.whole_to(step, micro).wait_recv()

            self.finish_home()

        def start(self):
            for step in range(1, planes):
                self.across(step).start()

        def start_home(self):
            @pl.when(section == self.layer)
            def _():
                self.home_local().start()

            @pl.when(section != self.layer)
            def _():
                self.home_remote(section).start()

        def middle(self):
            @pl.when(section == self.layer)
            def _():
                for step in range(1, planes):
                    for micro in range(2):
                        self.arrival(step, micro).wait_recv()
                self.inside().start()

        def forward(self):
            @pl.when(section == self.layer)
            def _():
                self.inside().forward()

        def finish(self):
            for step in range(1, planes):
                self.across(step).wait_send()

            @pl.when(section == self.layer)
            def _():
                self.inside().wait()
                self.inside().sent()

            self.finish_home()

        def finish_home(self):
            @pl.when(section == self.layer)
            def _():
                self.home_local().wait()
                self.home_remote(1 - section).wait_recv()

            @pl.when(section != self.layer)
            def _():
                self.home_remote(section).wait_send()

    lane = lane_of((tokens, LANES))
    low_half = lane % HEAD_SIZE < HALF
    left = lane < HEAD_SIZE
    pair_lane = lane_of((2 * tokens, LANES))
    causal = lax.broadcasted_iota(jnp.int32, (2 * tokens, tokens), 0) % tokens >= lax.broadcasted_iota(
        jnp.int32, (2 * tokens, tokens), 1
    )
    root = HEAD_SIZE ** (-0.5)

    def stack(tile):
        nothing = jnp.zeros_like(tile)
        return jnp.concatenate([jnp.where(left, tile, nothing), jnp.where(left, nothing, tile)], axis=0)

    def attention_forward(layer, source, early, late):
        cosine, sine = r.cosine[...], r.sine[...]
        residual = source[...].astype(F32)
        normed_one = (residual * row_scale(residual) * r.gains[layer, 0:1]).astype(BF16)
        weights_wait(layer, 0)
        early()
        r.projected[:, :QUERY_WIDTH] = dot_nn(normed_one, r.win[layer, :, :QUERY_WIDTH])
        weights_wait(layer, 1)
        r.projected[:, QUERY_WIDTH:] = dot_nn(normed_one, r.win[layer, :, QUERY_WIDTH:])
        for tile in range(QUERY_WIDTH // LANES):
            columns = slice(tile * LANES, (tile + 1) * LANES)
            piece = r.projected[:, columns]
            r.query[layer, :, columns] = (piece * cosine + turned(piece, low_half) * sine).astype(BF16)
        for tile in range(KEY_WIDTH // LANES):
            first = slice(2 * tile * LANES, (2 * tile + 1) * LANES)
            second = slice((2 * tile + 1) * LANES, (2 * tile + 2) * LANES)
            piece = r.projected[:, QUERY_WIDTH + tile * LANES : QUERY_WIDTH + (tile + 1) * LANES]
            piece = piece * cosine + turned(piece, low_half) * sine
            other = pltpu.roll(piece, HEAD_SIZE, 1)
            r.key[layer, :, first] = jnp.where(left, piece, other).astype(BF16)
            r.key[layer, :, second] = jnp.where(left, other, piece).astype(BF16)
            start = QUERY_WIDTH + KEY_WIDTH + tile * LANES
            piece = r.projected[:, start : start + LANES]
            other = pltpu.roll(piece, HEAD_SIZE, 1)
            r.value[layer, :, first] = jnp.where(left, piece, other).astype(BF16)
            r.value[layer, :, second] = jnp.where(left, other, piece).astype(BF16)
        logs = jnp.zeros((2 * tokens, LANES), F32)
        for head in range(KEY_VALUE_HEADS):
            columns = slice(head * LANES, (head + 1) * LANES)
            scores = dot_nt(stack(r.query[layer, :, columns]), r.key[layer, :, columns]) * root
            scores = jnp.where(causal, scores, -1e30)
            top = jnp.max(scores, axis=-1, keepdims=True)
            log_total = top + jnp.log(jnp.sum(jnp.exp(scores - top), axis=-1, keepdims=True))
            logs = jnp.where(pair_lane == head, log_total, logs)
            weights = jnp.exp(scores - log_total).astype(BF16)
            mixed = dot_nn(weights, r.value[layer, :, columns])
            r.attended[layer, :, columns] = jnp.where(left, mixed[:tokens], mixed[tokens:]).astype(BF16)
        r.logs[layer] = logs
        late()
        weights_wait(layer, 2)
        middle = residual + dot_nn(r.attended[layer], r.wout[layer])
        r.middle[layer] = middle
        normed_two = (middle * row_scale(middle) * r.gains[layer, 1:2]).astype(BF16)
        r.packed[layer, :, :MODEL_WIDTH] = normed_two
        logits = jnp.concatenate(
            [dot_nt(normed_two, r.router[layer]), jnp.zeros((tokens, LANES - EXPERTS), F32)], axis=-1
        )
        chosen = r.hot[layer] > 0.0
        top = jnp.max(jnp.where(chosen, logits, -1e30), axis=-1, keepdims=True)
        grown = jnp.where(chosen, jnp.exp(jnp.where(chosen, logits - top, 0.0)), 0.0)
        gates = grown / jnp.sum(grown, axis=-1, keepdims=True)
        r.gates[layer] = gates
        r.packed[layer, :, MODEL_WIDTH:] = two_parts(gates)

    def attention_backward(layer, source, up, back, gate_grads):
        cosine, sine = r.cosine[...], r.sine[...]
        gates = r.gates[layer]
        grad_picked = gates * (gate_grads - jnp.sum(gates * gate_grads, axis=-1, keepdims=True))
        grad_logits = grad_picked.astype(BF16)
        r.small[layer, 16:] = dot_tn(grad_logits, r.packed[layer, :, :MODEL_WIDTH])[:EXPERTS]
        grad_second = back + dot_nn(grad_logits[:, :EXPERTS], r.router[layer])
        middle = r.middle[layer]
        scale_two = row_scale(middle)
        r.small[layer, 1:2] = jnp.sum(grad_second * middle * scale_two, axis=0, keepdims=True)
        grad_middle = up[...].astype(F32) + norm_back(grad_second * r.gains[layer, 1:2], middle, scale_two)
        low = grad_middle.astype(BF16)
        r.low[layer] = low
        r.grad_middle[...] = grad_middle
        r.grad_attended[...] = dot_nt(low, r.wout[layer]).astype(BF16)
        logs = r.logs[layer]
        held = []
        for head in range(KEY_VALUE_HEADS):
            columns = slice(head * LANES, (head + 1) * LANES)
            query = stack(r.query[layer, :, columns])
            key, value = r.key[layer, :, columns], r.value[layer, :, columns]
            scores = dot_nt(query, key) * root
            log_total = jnp.sum(jnp.where(pair_lane == head, logs, 0.0), axis=-1, keepdims=True)
            probabilities = jnp.where(causal, jnp.exp(jnp.where(causal, scores - log_total, 0.0)), 0.0)
            grad_tile = stack(r.grad_attended[:, columns])
            delta = jnp.sum(
                grad_tile.astype(F32) * stack(r.attended[layer, :, columns]).astype(F32), axis=-1, keepdims=True
            )
            grad_scores = (probabilities * (dot_nt(grad_tile, value) - delta)).astype(BF16)
            wide = dot_nn(grad_scores, key) * root
            grad_query = jnp.where(left, wide[:tokens], wide[tokens:])
            grad_query = grad_query * cosine - turned(grad_query, low_half) * sine
            r.projected_grad[layer, :, columns] = grad_query.astype(BF16)
            key_grad = dot_tn(grad_scores, query) * root
            value_grad = dot_tn(probabilities.astype(BF16), grad_tile)
            key_grad = key_grad + pltpu.roll(key_grad, HEAD_SIZE, 1)
            value_grad = value_grad + pltpu.roll(value_grad, HEAD_SIZE, 1)
            if head % 2 == 0:
                held = [key_grad, value_grad]
            else:
                piece = jnp.where(left, held[0], key_grad)
                piece = piece * cosine - turned(piece, low_half) * sine
                start = QUERY_WIDTH + head // 2 * LANES
                r.projected_grad[layer, :, start : start + LANES] = piece.astype(BF16)
                start += KEY_WIDTH
                r.projected_grad[layer, :, start : start + LANES] = jnp.where(left, held[1], value_grad).astype(BF16)
        grad_first = dot_nt(r.projected_grad[layer], r.win[layer])
        residual = source[...].astype(F32)
        scale_one = row_scale(residual)
        normed_one = (residual * scale_one * r.gains[layer, 0:1]).astype(BF16)
        group = MODEL_WIDTH // planes
        for variant in range(group // LANES):
            for step in range(planes):
                start = step * group + variant * LANES
                r.chosen[layer, variant, :, step * LANES : (step + 1) * LANES] = normed_one[:, start : start + LANES]
                r.chosen[layer, variant, :, (planes + step) * LANES : (planes + step + 1) * LANES] = r.attended[
                    layer, :, start : start + LANES
                ]
        r.small[layer, 0:1] = jnp.sum(grad_first * residual * scale_one, axis=0, keepdims=True)
        return (
            r.grad_middle[...] + norm_back(grad_first * r.gains[layer, 0:1], residual, scale_one)
        ).astype(BF16)

    def place_local(source, target, index):
        return pltpu.make_async_copy(source, target.at[section], r.o_local.at[index])

    def place_remote(source, target, index, micro):
        return remote(source, target.at[micro], r.o_send.at[index], r.o_recv.at[index], partner)

    def place(layer, source, target, index):
        @pl.when(section == layer)
        def _():
            place_local(source, target, index).start()

        @pl.when(section != layer)
        def _():
            place_remote(source, target, index, section).start()

    def placed(layer, source, target, index):
        @pl.when(section == layer)
        def _():
            place_local(source, target, index).wait()
            place_remote(source, target, index, 1 - section).wait_recv()

        @pl.when(section != layer)
        def _():
            place_remote(source, target, index, section).wait_send()

    chunk = min(rows, 256)
    chunks = rows // chunk
    half = MODEL_WIDTH // 2

    def each_chunk(work):
        def one(number, carry):
            work(pl.ds(pl.multiple_of(number * chunk, chunk), chunk), pl.ds(number * (chunk // tokens), chunk // tokens))
            return carry

        if chunks == 1:
            work(pl.ds(0, chunk), pl.ds(0, owners))
        else:
            lax.fori_loop(0, chunks, one, 0)

    def flat(buffer, group, columns):
        values = buffer[group, :, columns]
        return values.reshape(chunk, values.shape[-1])

    model, packing = slice(0, MODEL_WIDTH), slice(MODEL_WIDTH, PACKED)

    def expert_columns(expert):
        return pl.ds(pl.multiple_of(expert * FF, FF), FF)

    def wait_in(expert):
        load_in(0, expert)[0].wait()

    def wait_out(expert):
        load_out(0, expert)[0].wait()

    def gate_of(plane_buffer, group, expert):
        return column_of(flat(plane_buffer, group, packing), lane_of((chunk, LANES)), own * local + expert)

    def backward_terms(expert, span, gate, gate_part, up_part, inner):
        sigmoid = 1.0 / (1.0 + jnp.exp(-gate_part))
        silu = gate_part * sigmoid
        activated = silu * up_part
        gate_grad = jnp.sum(activated * inner, axis=-1, keepdims=True)
        lanes = lane_of((chunk, LANES))
        r.gate_total[span] = jnp.where(lanes == own * local + expert, gate_grad, r.gate_total[span])
        grad_activated = inner * gate
        grad_gate = grad_activated * up_part * sigmoid * (1.0 + gate_part * (1.0 - sigmoid))
        grad_up = grad_activated * silu
        grad_pair = jnp.concatenate([grad_gate.astype(BF16), grad_up.astype(BF16)], axis=-1)
        term = dot_nt(grad_pair, r.ein[expert])

        @pl.when(expert == 0)
        def _():
            r.total[span] = term

        @pl.when(expert > 0)
        def _():
            r.total[span] += term

        return activated

    def mix(reduction):
        for cut in range(2):
            columns = slice(cut * half, (cut + 1) * half)

            def work(span, group):
                r.total[span, columns] = dot_nn(r.activated[span], r.eout[:, columns])

            each_chunk(work)
            for step in range(1, owners):
                reduction.put(
                    step, columns, r.total[pl.ds(owner_to(step) * tokens, tokens), columns].astype(BF16)
                )
            reduction.start(cut)

    def mixed(reduction, result):
        for step in range(1, owners):
            result = result + reduction.coming[step - 1].astype(F32)
        return result

    def send_back(reduction):
        for step in range(1, owners):
            span = pl.ds(owner_to(step) * tokens, tokens)
            reduction.put(step, slice(0, MODEL_WIDTH), r.total[span].astype(BF16))
            reduction.put(step, slice(MODEL_WIDTH, PACKED), two_parts(r.gate_total[span]))
        reduction.start(0)

    def came_back(reduction):
        back = r.kept_total[...]
        for step in range(1, owners):
            back = back + reduction.coming[step - 1, :, :MODEL_WIDTH].astype(F32)
        terms = reduction.coming[0, :, MODEL_WIDTH:].astype(F32)
        for step in range(2, owners):
            terms = terms + reduction.coming[step - 1, :, MODEL_WIDTH:].astype(F32)
        return back, r.kept_gate[...] + terms + pltpu.roll(terms, LANES - EXPERTS, 1)

    both_cuts = ((0, half), (half, half))
    spread_x0 = Spread(r.packed.at[0], r.plane0, 0)
    spread_x1 = Spread(r.packed.at[1], r.plane1, 1)
    spread_u1 = Spread(r.up, r.ups1, 2)
    spread_u0 = Spread(r.up0, r.ups0, 3)
    mix0 = Reduce(r.leave_y, r.come_y, 0, both_cuts)
    mix1 = Reduce(r.leave_y, r.come_y, 1, both_cuts)
    back1 = Reduce(r.leave_b, r.come_b, 2, ((0, PACKED),))
    back0 = Reduce(r.leave_b, r.come_b, 3, ((0, PACKED),))
    gather_x0 = Gather(0, r.packed.at[0], r.plane0, r.every_x, 0)
    gather_x1 = Gather(1, r.packed.at[1], r.plane1, r.every_x, 1)
    gather_u0 = Gather(0, r.up0, r.ups0, r.every_u, 2)
    gather_u1 = Gather(1, r.up, r.ups1, r.every_u, 3)
    for which in pieces:
        weights_start(0, which)
    for expert in range(local):
        for copy in swap_pair(expert):
            copy.start()

    @pl.when(section == 0)
    def _():
        for expert in range(local):
            load_in(0, expert)[0].start()
            load_out(0, expert)[0].start()

    r.small[...] = jnp.zeros_like(r.small)
    weights_spread(0, 0)
    weights_spread(0, 1)
    weights_forward(0, 0)
    weights_push(0, 0)
    weights_spread(0, 2)
    weights_forward(0, 1)
    weights_push(0, 1)

    def early0():
        for which in pieces:
            weights_start(1, which)

    def late0():
        weights_forward(0, 2)
        weights_push(0, 2)

    for copy in shared:
        copy.wait()
    for copy in own_rows:
        copy.wait()
    attention_forward(0, r.x, early0, late0)
    spread_x0.start()
    spread_x0.wait()
    for which in pieces:
        weights_spread(1, which)
    spread_u1.start()
    gather_u1.start()
    gather_x0.start_whole()
    gather_x0.start_home()

    def forward_expert(expert, carry):
        @pl.when(section != 0)
        def _():
            for which, make in enumerate((load_in, load_out)):
                swap_pair(expert)[which].wait_recv()
                make(0, expert)[1].start()

        wait_in(expert)

        def work(span, group):
            gate = gate_of(r.plane0, group, expert)
            pair = dot_nn(flat(r.plane0, group, model), r.ein[expert])
            r.pairs[expert, span] = pair.astype(BF16)
            gate_part, up_part = pair[:, :FF], pair[:, FF:]
            silu = gate_part / (1.0 + jnp.exp(-gate_part))
            r.activated[span, expert_columns(expert)] = (silu * up_part * gate).astype(BF16)

        each_chunk(work)
        start_load(load_in, 1, expert, 0, True)
        wait_out(expert)
        return carry

    lax.fori_loop(0, local // 2, forward_expert, 0)
    weights_forward(1, 0)
    weights_forward(1, 1)
    lax.fori_loop(local // 2, local, forward_expert, 0)
    mix(mix0)
    weights_forward(1, 2)
    weights_push(1, 0)
    weights_push(1, 1)
    for expert in range(local):
        start_load(load_out, 1, expert, 1, True)
    spread_u1.wait()
    gather_u1.start_home()
    mix0.wait()
    r.hidden0[...] = (r.middle[0] + mixed(mix0, r.total[here])).astype(BF16)
    place(0, r.hidden0, r.hidden, 0)

    def late1():
        weights_push(1, 2)

    attention_forward(1, r.hidden0, lambda: None, late1)
    spread_x1.start()
    gather_x1.start()

    def inner_expert(expert, carry):
        wait_out(expert)

        def work(span, group):
            r.inner[span, expert_columns(expert)] = dot_nt(
                flat(r.ups1, group, model), r.eout[expert_columns(expert)]
            ).astype(r.inner.dtype)

        each_chunk(work)
        return carry

    lax.fori_loop(0, local, inner_expert, 0)
    spread_x1.wait()
    gather_u1.middle()
    gather_x1.start_home()
    r.gate_total[...] = jnp.zeros_like(r.gate_total)

    def both_expert(expert, carry):
        wait_in(expert)

        def work(span, group):
            gate = gate_of(r.plane1, group, expert)
            pair = dot_nn(flat(r.plane1, group, model), r.ein[expert])
            inner = r.inner[span, expert_columns(expert)].astype(F32)
            activated = backward_terms(expert, span, gate, pair[:, :FF], pair[:, FF:], inner)
            r.activated[span, expert_columns(expert)] = (activated * gate).astype(BF16)

        each_chunk(work)
        start_load(load_in, 0, expert, 0, False)
        return carry

    lax.fori_loop(0, local // 2, both_expert, 0)
    gather_u1.forward()
    lax.fori_loop(local // 2, local, both_expert, 0)
    send_back(back1)
    r.kept_total[...] = r.total[here]
    r.kept_gate[...] = r.gate_total[here]
    mix(mix1)
    for expert in range(local):
        start_load(load_out, 0, expert, 1, False)
    back1.wait()
    back, gate_grads = came_back(back1)
    r.up0[...] = attention_backward(1, r.hidden0, r.up, back, gate_grads)
    spread_u0.start()
    gather_u0.start()
    place(1, r.up0, r.input_grad, 1)
    mix1.wait()
    r.hidden1[...] = (r.middle[1] + mixed(mix1, r.total[here])).astype(BF16)
    place(1, r.hidden1, r.hidden, 2)
    r.gate_total[...] = jnp.zeros_like(r.gate_total)
    spread_u0.wait()
    gather_x1.middle()
    gather_u0.start_home()

    def behind_expert(expert, carry):
        wait_in(expert)
        wait_out(expert)

        def work(span, group):
            gate = gate_of(r.plane0, group, expert)
            pair = r.pairs[expert, span].astype(F32)
            inner = dot_nt(flat(r.ups0, group, model), r.eout[expert_columns(expert)])
            backward_terms(expert, span, gate, pair[:, :FF], pair[:, FF:], inner)

        each_chunk(work)
        return carry

    lax.fori_loop(0, local // 2, behind_expert, 0)
    gather_x1.forward()
    gather_u0.middle()
    lax.fori_loop(local // 2, local, behind_expert, 0)
    send_back(back0)
    r.kept_total[...] = r.total[here]
    r.kept_gate[...] = r.gate_total[here]
    back0.wait()
    gather_u0.forward()
    back, gate_grads = came_back(back0)
    r.grad0[...] = attention_backward(0, r.x, r.up0, back, gate_grads)
    place(0, r.grad0, r.input_grad, 3)

    for layer in range(2):
        for which in pieces:
            weights_unsent(layer, which)
    for expert in range(local):
        for copy in swap_pair(expert):
            copy.wait_send()
    for copy in unsent:
        copy.wait_send()
    placed(0, r.hidden0, r.hidden, 0)
    placed(1, r.up0, r.input_grad, 1)
    placed(1, r.hidden1, r.hidden, 2)
    placed(0, r.grad0, r.input_grad, 3)
    gather_x0.finish_whole()
    for gather in (gather_u1, gather_x1, gather_u0):
        gather.finish()


def both_layers(layer_input, cotangent, routes, gain_one, attn_in, attn_out, gain_two, router, cosine, sine,
                experts_in, experts_out):
    planes, owners = lax.axis_size("dp"), lax.axis_size("expert")
    tokens = layer_input.shape[1]
    local = experts_in.shape[1]
    slab = attn_in.shape[1]
    rows = owners * tokens
    dma = lambda *shape: pltpu.SemaphoreType.DMA(shape)
    vmem = lambda shape, dtype: pltpu.VMEM(shape, dtype)
    wide = (2, tokens, MODEL_WIDTH)
    everywhere = (owners, planes, 2, tokens)
    inputs = dict(
        layer_input=(layer_input, any_spec()),
        cotangent=(cotangent, any_spec()),
        routes=(jnp.swapaxes(routes, 2, 3), vmem_spec()),
        gain_one=(gain_one, vmem_spec()),
        gain_two=(gain_two, vmem_spec()),
        router_in=(jnp.swapaxes(router, 1, 2), vmem_spec()),
        attn_in=(attn_in, any_spec()),
        attn_out=(attn_out, any_spec()),
        cosine=(cosine, vmem_spec()),
        sine=(sine, vmem_spec()),
        experts_in=(experts_in, any_spec()),
        experts_out=(experts_out, any_spec()),
    )
    outputs = dict(
        hidden=(wide, BF16, any_spec()),
        input_grad=(wide, BF16, any_spec()),
        other_in=(experts_in.shape[1:], BF16, any_spec()),
        other_out=(experts_out.shape[1:], BF16, any_spec()),
        every_x=(everywhere + (PACKED,), BF16, any_spec()),
        every_u=(everywhere + (MODEL_WIDTH,), BF16, any_spec()),
        projected_grad=((2, tokens, PROJECTED), BF16, vmem_spec()),
        low=(wide, BF16, vmem_spec()),
        chosen=(
            (2, MODEL_WIDTH // planes // LANES, tokens, 2 * planes * LANES), BF16, vmem_spec()
        ),
        small=((2, 16 + EXPERTS, MODEL_WIDTH), F32, vmem_spec()),
    )
    scratch = dict(
        win=vmem((2, MODEL_WIDTH, PROJECTED), BF16),
        wout=vmem((2, QUERY_WIDTH, MODEL_WIDTH), BF16),
        ein=vmem((local, MODEL_WIDTH, 2 * FF), BF16),
        eout=vmem((local * FF, MODEL_WIDTH), BF16),
        x=vmem(wide[1:], BF16),
        up=vmem(wide[1:], BF16),
        gains=vmem((2, 8, MODEL_WIDTH), F32),
        router=vmem((2, EXPERTS, MODEL_WIDTH), BF16),
        hot=vmem((2, tokens, LANES), F32),
        hot_out=vmem((tokens, LANES), F32),
        i_sem=dma(2),
        h_send=dma(3),
        h_recv=dma(3),
        projected=vmem((tokens, PROJECTED), F32),
        query=vmem(wide, BF16),
        key=vmem(wide, BF16),
        value=vmem(wide, BF16),
        attended=vmem(wide, BF16),
        logs=vmem((2, 2 * tokens, LANES), F32),
        middle=vmem(wide, F32),
        packed=vmem((2, tokens, PACKED), BF16),
        gates=vmem((2, tokens, LANES), F32),
        up0=vmem(wide[1:], BF16),
        hidden0=vmem(wide[1:], BF16),
        hidden1=vmem(wide[1:], BF16),
        grad0=vmem(wide[1:], BF16),
        grad_middle=vmem(wide[1:], F32),
        grad_attended=vmem(wide[1:], BF16),
        plane0=vmem((owners, tokens, PACKED), BF16),
        plane1=vmem((owners, tokens, PACKED), BF16),
        ups0=vmem((owners, tokens, MODEL_WIDTH), BF16),
        ups1=vmem((owners, tokens, MODEL_WIDTH), BF16),
        pairs=vmem((local, rows, 2 * FF), BF16),
        inner=vmem((rows, local * FF), BF16),
        activated=vmem((rows, local * FF), BF16),
        total=vmem((rows, MODEL_WIDTH), F32),
        gate_total=vmem((rows, LANES), F32),
        kept_total=vmem((tokens, MODEL_WIDTH), F32),
        kept_gate=vmem((tokens, LANES), F32),
        leave_y=vmem((owners - 1, tokens, MODEL_WIDTH), BF16),
        come_y=vmem((owners - 1, tokens, MODEL_WIDTH), BF16),
        leave_b=vmem((owners - 1, tokens, PACKED), BF16),
        come_b=vmem((owners - 1, tokens, PACKED), BF16),
        w_local=dma(2, 3),
        wz_send=dma(2, 3, planes),
        wz_recv=dma(2, 3, planes),
        wp_send=dma(2, 3, planes, owners),
        wp_recv=dma(2, 3, planes, owners),
        wc_send=dma(2, 3, planes),
        wc_recv=dma(2, 3, planes),
        s_send=dma(2, local),
        s_recv=dma(2, local),
        l_sem=dma(2, local),
        a_send=dma(4, owners),
        a_recv=dma(4, owners),
        r_send=dma(4, 2, owners),
        r_recv=dma(4, 2, owners),
        g_send=dma(4, planes),
        g_recv=dma(4, planes, 2),
        g_local=dma(4),
        gp_send=dma(4, owners),
        gp_recv=dma(4, owners),
        o_send=dma(4),
        o_recv=dma(4),
        o_local=dma(4),
    )
    return call(
        functools.partial(layers_kernel, planes, owners, tokens, local, slab),
        "both_layers", 0, inputs, outputs, scratch,
    )


def ExpertGrads(planes, owners, tokens, local, first, r):
    plane = lax.axis_index("dp")
    own = lax.axis_index("expert")
    group = 4 * tokens
    slots = group // 2
    groups = 2 * planes * owners * tokens // group
    slice_in, slice_out = MODEL_WIDTH // planes, FF // planes
    chunk = min(groups * slots, 1024)
    chunks = groups * slots // chunk
    tile = 512
    depth = r.x_rows.shape[0]
    shift = first if r.grad_in.shape[0] < local else 0

    def weights_of(expert):
        slot = expert % 2
        return (
            pltpu.make_async_copy(r.experts_in.at[0, expert], r.ein.at[slot], r.e_sem.at[0, slot]),
            pltpu.make_async_copy(r.experts_out.at[0, expert], r.eout.at[slot], r.e_sem.at[1, slot]),
        )

    def rows_of(number):
        slot = number % depth
        span = pl.ds(pl.multiple_of(number * group, group), group)
        return (
            pltpu.make_async_copy(r.every_x.at[span], r.x_rows.at[slot], r.t_sem.at[0, slot]),
            pltpu.make_async_copy(r.every_u.at[span], r.u_rows.at[slot], r.t_sem.at[1, slot]),
        )

    pack = r.compact_x.shape[0]
    bunch = r.picks.shape[0] // slots
    before = (
        lax.broadcasted_iota(jnp.int32, (group, group), 0) < lax.broadcasted_iota(jnp.int32, (group, group), 1)
    ).astype(BF16)
    same = (
        lax.broadcasted_iota(jnp.int32, (group, group), 0) == lax.broadcasted_iota(jnp.int32, (group, group), 1)
    ).astype(BF16)
    numbers = lax.broadcasted_iota(jnp.int32, (slots, group), 0).astype(F32)

    def gather():
        def one(number, carry):
            slot = number % depth
            for copy in rows_of(number):
                copy.wait()

            @pl.when(number + depth - 1 < groups)
            def _():
                for copy in rows_of(number + depth - 1):
                    copy.start()

            parts = r.x_rows[slot, :, MODEL_WIDTH:].astype(F32)
            chosen = (parts != 0.0).astype(BF16)
            rank = dot_tn(chosen, before)
            r.ranks[...] = jnp.where(dot_tn(chosen, same) > 0.0, rank, -1.0)
            span = pl.ds(pl.multiple_of(number * slots, slots), slots)
            for low in range(0, pack, bunch):
                few = min(bunch, pack - low)
                for index in range(few):
                    rank_row = r.ranks[pl.ds(own * local + first + low + index, 1), :]
                    r.picks[index * slots : (index + 1) * slots, :] = (numbers == rank_row).astype(BF16)
                for source, target in ((r.x_rows, r.compact_x), (r.u_rows, r.compact_u)):
                    found = dot_nn(r.picks[: few * slots], source[slot]).astype(BF16)
                    for index in range(few):
                        target[low + index, span] = found[index * slots : (index + 1) * slots]
            return carry

        lax.fori_loop(0, groups, one, 0)

    def out_of(expert):
        slot = expert % 2
        return (
            pltpu.make_async_copy(r.din.at[slot], r.grad_in.at[expert - shift], r.d_sem.at[0, slot]),
            pltpu.make_async_copy(r.dout.at[slot], r.grad_out.at[expert - shift], r.d_sem.at[1, slot]),
        )

    def one_expert(expert, index):
        slot = expert % 2
        for copy in weights_of(expert):
            copy.wait()

        @pl.when(expert + 1 < first + pack)
        def _():
            for copy in weights_of(expert + 1):
                copy.start()

        @pl.when(expert >= first + 2)
        def _():
            for copy in out_of(expert - 2):
                copy.wait()

        for number in range(chunks):

            def one_tile(step, carry):
                span = pl.ds(pl.multiple_of(number * chunk + step * tile, tile), tile)
                here = pl.ds(pl.multiple_of(step * tile, tile), tile)
                gate = column_of(
                    r.compact_x[index, span, MODEL_WIDTH:], lane_of((tile, LANES)), own * local + expert
                )
                pair = dot_nn(r.compact_x[index, span, :MODEL_WIDTH], r.ein[slot])
                gate_part, up_part = pair[:, :FF], pair[:, FF:]
                sigmoid = 1.0 / (1.0 + jnp.exp(-gate_part))
                silu = gate_part * sigmoid
                r.activated[here] = (silu * up_part * gate).astype(BF16)
                grad_activated = dot_nt(r.compact_u[index, span], r.eout[slot]) * gate
                r.grad_pair[here, :FF] = (
                    grad_activated * up_part * sigmoid * (1.0 + gate_part * (1.0 - sigmoid))
                ).astype(BF16)
                r.grad_pair[here, FF:] = (grad_activated * silu).astype(BF16)
                return carry

            lax.fori_loop(0, chunk // tile, one_tile, 0)
            rows = slice(number * chunk, (number + 1) * chunk)
            left_in = r.compact_x[index, rows, pl.ds(pl.multiple_of(plane * slice_in, LANES), slice_in)]
            left_out = r.activated[:, pl.ds(pl.multiple_of(plane * slice_out, LANES), slice_out)]
            term_in = dot_tn(left_in, r.grad_pair[...])
            term_out = dot_tn(left_out, r.compact_u[index, rows])
            if number == 0:
                r.din[slot] = term_in
                r.dout[slot] = term_out
            else:
                r.din[slot] += term_in
                r.dout[slot] += term_out
        for copy in out_of(expert):
            copy.start()

    def run(low, high):
        def body(index, carry):
            one_expert(first + index, index)
            return carry

        if high > low:
            lax.fori_loop(low, high, body, 0)

    def start():
        for number in range(min(depth - 1, groups)):
            for copy in rows_of(number):
                copy.start()
        for copy in weights_of(first):
            copy.start()

    def finish():
        for expert in range(max(first, first + pack - 2), first + pack):
            for copy in out_of(expert):
                copy.wait()

    names = Names()
    names.load, names.gather, names.run, names.finish, names.pack = start, gather, run, finish, pack
    return names


def gradients_kernel(planes, owners, tokens, local, r):
    section = lax.axis_index("section")
    plane = lax.axis_index("dp")
    own = lax.axis_index("expert")
    partner = dict(section=1 - section)
    part = MODEL_WIDTH // (planes * owners)
    barrier = pltpu.get_barrier_semaphore()
    for step in range(1, owners):
        pl.semaphore_signal(barrier, inc=1, device_id=dict(expert=(own + step) % owners), device_id_type=MESH)
    for step in range(1, planes):
        pl.semaphore_signal(barrier, inc=1, device_id=dict(dp=(plane + step) % planes), device_id_type=MESH)
    pl.semaphore_signal(barrier, inc=1, device_id=partner, device_id_type=MESH)

    experts = ExpertGrads(planes, owners, tokens, local, 0, r)
    experts.load()

    def meet(source, target, index):
        here = pltpu.make_async_copy(source.at[section], target.at[section], r.m_local.at[index])
        there = remote(source.at[1 - section], target.at[section], r.m_send.at[index], r.m_recv.at[index], partner)
        return here, there

    meets = [
        meet(r.low, r.all_low.at[own], 0),
        meet(r.chosen, r.both_chosen, 1),
        meet(r.small, r.both_small, 2),
        meet(r.projected_grad, r.all_projected.at[own], 3),
    ]
    pl.semaphore_wait(barrier, owners - 1 + planes - 1 + 1)
    for here, there in meets:
        here.start()
        there.start()

    def piece_of(buffer):
        return lambda owner, half: buffer.at[owner] if half is None else buffer.at[owner, half]

    spreads = (
        PlaneBroadcast(owners, own, piece_of(r.all_low), r.f_send.at[0], r.f_recv.at[0]),
        PlaneBroadcast(owners, own, piece_of(r.all_projected), r.f_send.at[1], r.f_recv.at[1]),
    )
    width = planes * LANES

    def variant_of(owner):
        return owner * part // LANES

    def chosen_to(step, which):
        target = (own + step) % owners
        columns = pl.ds((1 - which) * width, width)
        return remote(
            r.both_chosen.at[:, variant_of(target), :, columns], r.all_chosen.at[own, :, :, columns],
            r.c_send.at[which, step], r.c_recv.at[which, step], dict(expert=target),
        )

    def small_to(step):
        return remote(
            r.small_out, r.small_in.at[step - 1], r.v_send.at[step], r.v_recv.at[step],
            dict(expert=(own + step) % owners),
        )

    halves = (
        (r.all_low, r.product_out, r.sums, r.leaving_out),
        (r.all_projected, r.product_in, r.partial, None),
    )

    def sums_over(step):
        return remote(
            r.leaving_out.at[step - 1], r.arriving_out.at[step - 1], r.z_send.at[step], r.z_recv.at[step],
            dict(dp=(plane + step) % planes),
        )

    def attention_start():
        for here, there in meets:
            here.wait()
            there.wait_recv()
        r.small_kept[...] = r.both_small[0] + r.both_small[1]
        r.small_out[...] = r.small_kept[...].astype(BF16)
        for step in range(1, owners):
            small_to(step).start()
        for which in range(2):
            spreads[which].start()
            for step in range(1, owners):
                chosen_to(step, which).start()
        r.all_chosen[own] = r.both_chosen[:, variant_of(own)]

    def attention_small():
        total = r.small_kept[...]
        for step in range(1, owners):
            small_to(step).wait_recv()
            total = total + r.small_in[step - 1].astype(F32)
        r.sums[part:] = total
        for step in range(1, planes):
            r.leaving_out[step - 1, part:] = total.astype(BF16)

    def attention_partial(which):
        factors, product, partial, leaving = halves[which]
        spreads[which].wait()
        for step in range(1, owners):
            chosen_to(step, which).wait_recv()
        within = own * part % LANES
        some = min(owners, 4)
        pile = some * 2 * tokens
        for step in list(range(1, planes)) + [0]:
            target = (plane + step) % planes
            columns = pl.ds(pl.multiple_of(((1 - which) * planes + target) * LANES, LANES), LANES)
            for first in range(0, owners, some):
                left = r.all_chosen[first : first + some, :, :, columns].reshape(pile, LANES)
                term = dot_tn(left, factors[first : first + some].reshape(pile, factors.shape[-1]))
                if first == 0:
                    product[...] = term
                else:
                    product[...] += term
            mine = product[pl.ds(pl.multiple_of(within, 16), part)]
            if step == 0:
                partial[:part] = mine
            else:
                if which == 0:
                    leaving[step - 1, :part] = mine.astype(BF16)
                    sums_over(step).start()
                else:
                    getattr(r, f"to{step}")[...] = mine.astype(BF16)

    def attention_last():
        total = r.sums[...]
        for step in range(1, planes):
            sums_over(step).wait()
            total = total + r.arriving_out[step - 1].astype(F32)
        r.sums[...] = total
        for here, there in meets:
            there.wait_send()
        for which in range(2):
            spreads[which].sent()
            for step in range(1, owners):
                chosen_to(step, which).wait_send()
        for step in range(1, owners):
            small_to(step).wait_send()

    attention_start()
    experts.gather()
    pack = experts.pack
    experts.run(0, pack // 6)
    attention_small()
    spreads[0].forward()
    experts.run(pack // 6, 2 * pack // 6)
    spreads[1].forward()
    attention_partial(0)
    experts.run(2 * pack // 6, pack)
    experts.finish()
    attention_partial(1)
    attention_last()


def rest_kernel(planes, owners, tokens, local, first, r):
    experts = ExpertGrads(planes, owners, tokens, local, first, r)
    experts.load()
    held = ((r.first_in, r.held_in, r.grad_in), (r.first_out, r.held_out, r.grad_out))
    entering = [
        pltpu.make_async_copy(source, here, r.move_sem.at[0, index]) for index, (source, here, _) in enumerate(held)
    ]
    moving = [
        pltpu.make_async_copy(here, target.at[pl.ds(0, first)], r.move_sem.at[1, index])
        for index, (_, here, target) in enumerate(held)
    ]
    for copy in entering:
        copy.start()
    part = r.grad_attn_out.shape[0]
    r.grad_attn_out[...] = r.sums[:part]
    r.grad_gain_one[...] = r.sums[part : part + 1]
    r.grad_gain_two[...] = r.sums[part + 1 : part + 2]
    r.grad_router[...] = r.sums[part + 16 :]
    r.hidden_out[...] = r.hidden[...]
    r.input_grad_out[...] = r.input_grad[...]
    experts.gather()
    for number in range(2):
        entering[number].wait()
        moving[number].start()
    experts.run(0, experts.pack)
    experts.finish()
    for copy in moving:
        copy.wait()


def grads_scratch(planes, owners, tokens, pack):
    group = 4 * tokens
    groups = 2 * planes * owners * tokens // group
    slots = group // 2
    chunk = min(groups * slots, 1024)
    dma = lambda *shape: pltpu.SemaphoreType.DMA(shape)
    vmem = lambda shape, dtype: pltpu.VMEM(shape, dtype)
    return dict(
        ein=vmem((2, MODEL_WIDTH, 2 * FF), BF16),
        eout=vmem((2, FF, MODEL_WIDTH), BF16),
        x_rows=vmem((4, group, PACKED), BF16),
        u_rows=vmem((4, group, MODEL_WIDTH), BF16),
        ranks=vmem((LANES, group), F32),
        picks=vmem((min(pack, 5) * slots, group), BF16),
        compact_x=vmem((pack, groups * slots, PACKED), BF16),
        compact_u=vmem((pack, groups * slots, MODEL_WIDTH), BF16),
        activated=vmem((chunk, FF), BF16),
        grad_pair=vmem((chunk, 2 * FF), BF16),
        din=vmem((2, MODEL_WIDTH // planes, 2 * FF), F32),
        dout=vmem((2, FF // planes, MODEL_WIDTH), F32),
        e_sem=dma(2, 2),
        t_sem=dma(2, 4),
        d_sem=dma(2, 2),
    )


def weight_gradients(done, experts_in, experts_out):
    planes, owners = lax.axis_size("dp"), lax.axis_size("expert")
    local = experts_in.shape[1]
    tokens = done.low.shape[1]
    part = MODEL_WIDTH // (planes * owners)
    first = max(1, 6 * local // 8)
    wide = 2 * planes * LANES
    variants = done.chosen.shape[1]
    small = done.small.shape[1:]
    dma = lambda *shape: pltpu.SemaphoreType.DMA(shape)
    vmem = lambda shape, dtype: pltpu.VMEM(shape, dtype)
    shape_in, shape_out = (MODEL_WIDTH // planes, 2 * FF), (FF // planes, MODEL_WIDTH)
    tables = dict(
        every_x=(done.every_x.reshape(-1, PACKED), any_spec()),
        every_u=(done.every_u.reshape(-1, MODEL_WIDTH), any_spec()),
        experts_in=(experts_in, any_spec()),
        experts_out=(experts_out, any_spec()),
    )
    exchanged = call(
        functools.partial(gradients_kernel, planes, owners, tokens, local),
        "weight_gradients",
        1,
        dict(
            projected_grad=(done.projected_grad, vmem_spec()),
            low=(done.low, vmem_spec()),
            chosen=(done.chosen, vmem_spec()),
            small=(done.small, vmem_spec()),
            **tables,
        ),
        dict(
            grad_in=((first,) + shape_in, F32, any_spec()),
            grad_out=((first,) + shape_out, F32, any_spec()),
            partial=((part, PROJECTED), F32, vmem_spec()),
            sums=((part + small[0], MODEL_WIDTH), F32, vmem_spec()),
            **{f"to{step}": ((part, PROJECTED), BF16, vmem_spec()) for step in range(1, planes)},
        ),
        dict(
            all_low=vmem((owners, 2, tokens, MODEL_WIDTH), BF16),
            all_projected=vmem((owners, 2, tokens, PROJECTED), BF16),
            both_chosen=vmem((2, variants, tokens, wide), BF16),
            all_chosen=vmem((owners, 2, tokens, wide), BF16),
            both_small=vmem((2,) + small, F32),
            small_kept=vmem(small, F32),
            small_out=vmem(small, BF16),
            small_in=vmem((owners - 1,) + small, BF16),
            product_in=vmem((LANES, PROJECTED), F32),
            product_out=vmem((LANES, MODEL_WIDTH), F32),
            leaving_out=vmem((planes - 1, part + small[0], MODEL_WIDTH), BF16),
            arriving_out=vmem((planes - 1, part + small[0], MODEL_WIDTH), BF16),
            z_send=dma(planes),
            z_recv=dma(planes),
            m_local=dma(4),
            m_send=dma(4),
            m_recv=dma(4),
            f_send=dma(2, owners),
            f_recv=dma(2, owners),
            c_send=dma(2, owners),
            c_recv=dma(2, owners),
            v_send=dma(owners),
            v_recv=dma(owners),
            **grads_scratch(planes, owners, tokens, first),
        ),
    )
    total = exchanged.partial
    arriving = [
        lax.ppermute(getattr(exchanged, f"to{step}"), "dp", [(i, (i + step) % planes) for i in range(planes)])
        for step in range(1, planes)
    ]
    count = local - first
    rows = 2 * planes * owners * tokens
    rest = call(
        functools.partial(rest_kernel, planes, owners, tokens, local, first),
        "other_experts",
        None,
        dict(
            first_in=(exchanged.grad_in, any_spec()),
            first_out=(exchanged.grad_out, any_spec()),
            sums=(exchanged.sums, vmem_spec()),
            hidden=(done.hidden, vmem_spec()),
            input_grad=(done.input_grad, vmem_spec()),
            **tables,
        ),
        dict(
            grad_in=((local,) + shape_in, F32, any_spec()),
            grad_out=((local,) + shape_out, F32, any_spec()),
            grad_attn_out=((part, MODEL_WIDTH), F32, vmem_spec()),
            grad_gain_one=((1, MODEL_WIDTH), F32, vmem_spec()),
            grad_gain_two=((1, MODEL_WIDTH), F32, vmem_spec()),
            grad_router=((EXPERTS, MODEL_WIDTH), F32, vmem_spec()),
            hidden_out=(done.hidden.shape, BF16, vmem_spec()),
            input_grad_out=(done.hidden.shape, BF16, vmem_spec()),
        ),
        dict(
            held_in=vmem((first,) + shape_in, F32),
            held_out=vmem((first,) + shape_out, F32),
            move_sem=dma(2, 2),
            **grads_scratch(planes, owners, tokens, count),
        ),
        pl.CostEstimate(flops=count * rows * 6 * MODEL_WIDTH * FF, bytes_accessed=rows * 4 * MODEL_WIDTH, transcendentals=0),
    )
    arriving, rest.grad_in = lax.optimization_barrier((arriving, rest.grad_in))
    for piece in arriving:
        total = total + piece.astype(F32)
    return rest, total


def shards(layer_input, cotangent, positions, routes, gain_one, attn_in, attn_out, gain_two, router,
           experts_in, experts_out):
    place = lax.dynamic_index_in_dim(positions, lax.axis_index("section"), 0, keepdims=False)
    lane = jnp.arange(LANES)
    frequency = jnp.power(rotary_base, -((lane % HALF).astype(F32) * (2.0 / HEAD_SIZE)))
    angles = place.astype(F32)[:, None] * frequency[None, :]
    cosine = jnp.cos(angles)
    sine = jnp.where(lane % HEAD_SIZE < HALF, -1.0, 1.0) * jnp.sin(angles)

    done = both_layers(
        layer_input, cotangent, routes, gain_one, attn_in, attn_out, gain_two, router, cosine, sine,
        experts_in, experts_out,
    )
    rest, grad_attn_in = weight_gradients(done, experts_in, experts_out)
    return (
        rest.hidden_out[None],
        rest.input_grad_out[None],
        rest.grad_gain_one,
        grad_attn_in[None],
        rest.grad_attn_out[None],
        rest.grad_gain_two,
        rest.grad_router.T[None],
        rest.grad_in[None],
        rest.grad_out[None],
    )


def solution(mesh):
    in_specs = (
        P(None, ("dp", "expert"), None),
        P(None, ("dp", "expert"), None),
        P(None, ("dp", "expert")),
        P("section", None, ("dp", "expert"), None),
        P("section", None),
        P("section", "dp", None),
        P("section", "dp", None),
        P("section", None),
        P("section", None, None),
        P("section", "expert", None, None),
        P("section", "expert", None, None),
    )
    out_specs = (
        P("section", None, ("dp", "expert"), None),
        P("section", None, ("dp", "expert"), None),
        P("section", None),
        P("section", ("dp", "expert"), None),
        P("section", ("dp", "expert"), None),
        P("section", None),
        P("section", None, None),
        P("section", "expert", "dp", None),
        P("section", "expert", "dp", None),
    )
    return jax.shard_map(shards, mesh=mesh, in_specs=in_specs, out_specs=out_specs, check_vma=False)
```
